32 devices in a mesh: strip: 8 (over z, x), chan: 4 (over y, core).
Axes of the slice: x: 2, y: 2, z: 4, core: 2. Of those that a mesh axis runs over, the one named last changes fastest.
Arguments:
- section_input: bfloat16 [48, 1024, 256], P(None, 'strip'), may hold values from -6 to 6
- conv_weight: bfloat16 [3, 3, 256, 256], replicated, may hold values from -0.125 to 0.125
- conv_bias: float32 [256], replicated, may hold values from -3 to 3
- deep_weight: bfloat16 [3, 3, 256, 512], P(None, None, None, 'chan'), may hold values from -0.125 to 0.125
- deep_bias: float32 [512], P('chan'), may hold values from -3 to 3
- labels: int32 [24, 512], P(None, 'strip'), may hold values from 0 to 32, as said below
- slot_ids: int32 [256], P('strip'), may hold values from 0 to 511, as said below
- embed_grad: float32 [512, 512], P('strip', 'chan'), may hold values from -0.8 to 0.8
Outputs:
- embeddings: float32 [512, 512], P('strip', 'chan')
- weight_grad: float32 [3, 3, 256, 512], P(None, None, None, 'chan')
- bias_grad: float32 [512], P('chan')
The draws below stay inside these ranges and needn't reach their ends.
Inputs may be any that keep to these rules, and one draw needn't show every extreme that they name: `labels`: the value 32 marks background; any other value v names entry v of the list of the strip that holds the pixel. `slot_ids`: A value s names slot s % 64 of owner s // 64 (an index of strip). The slots within one strip's list differ; a slot stands in the lists of at most two strips, which are neighbours (a crack across a strip border). Every owner holds at most 64 components and some owner holds exactly 64.
All inputs are finite; a program needn't handle non-finite values.
Results may differ from the reference program's by a relative error of at most 0.0035.
Values may be sent and summed in bfloat16 or wider, within the bound.
No kernel may reach another device: no remote copies, remote signals or barrier semaphores. Data moves between devices by JAX's collectives and lax.ppermute only.
A program may use at most 64 MiB of HBM per device.

```python
import jax
import jax.numpy as jnp
from jax import lax

CMID = 256
CDEEP = 512
ROWS = 48
LIST_DEV = 32
SHARED = 4
OWNED = 64
COLS = 1024
HALF_DEV = 64
HALF_COLS = 512
HALF_ROWS = 24
LISTS = 256
SLOTS = 512


def draw_labels(key, part):
    keys = jax.random.split(key, 4)
    column = jnp.arange(HALF_COLS, dtype=jnp.int32) % HALF_DEV
    quarter = max(HALF_DEV // 4, 1)
    left_lab = jax.random.randint(keys[0], (HALF_ROWS, HALF_COLS), 0, SHARED)
    right_lab = jax.random.randint(keys[1], (HALF_ROWS, HALF_COLS), LIST_DEV - SHARED, LIST_DEV)
    middle_lab = jax.random.randint(keys[2], (HALF_ROWS, HALF_COLS), SHARED, LIST_DEV - SHARED)
    backdrop = jax.random.randint(keys[3], (HALF_ROWS, HALF_COLS), 0, 4)
    chosen = jnp.where(column[None, :] < quarter, left_lab, jnp.where(column[None, :] >= HALF_DEV - quarter, right_lab, middle_lab))
    return jnp.where(backdrop == 0, LIST_DEV, chosen).astype(jnp.int32)


def draw_slot_ids(key, part):
    keys = jax.random.split(key, 3)
    strip_total = LISTS // LIST_DEV
    entries = jnp.arange(LISTS, dtype=jnp.int32)
    strip_of = entries // LIST_DEV
    within = entries % LIST_DEV
    step_size = LIST_DEV - SHARED
    own_id = jnp.where(strip_of == 0, within, LIST_DEV + (strip_of - 1) * step_size + (within - SHARED))
    prev_strip = strip_of - 1
    prev_entry = LIST_DEV - SHARED + within
    shared_id = jnp.where(prev_strip == 0, prev_entry, LIST_DEV + (prev_strip - 1) * step_size + (prev_entry - SHARED))
    component = jnp.where((strip_of >= 1) & (within < SHARED), shared_id, own_id)
    unique_total = LIST_DEV + (strip_total - 1) * step_size
    order_rank = jax.random.permutation(keys[0], unique_total)
    busiest = jax.random.randint(keys[1], (), 0, strip_total)
    spare_total = (strip_total - 1) * OWNED
    spare = jax.random.permutation(keys[2], spare_total)
    ranked = order_rank[component]
    picked = spare[jnp.clip(ranked - OWNED, 0, spare_total - 1)]
    other_owner = picked // OWNED
    other_owner = other_owner + (other_owner >= busiest).astype(jnp.int32)
    slot_value = jnp.where(ranked < OWNED, busiest * OWNED + ranked, other_owner * OWNED + picked % OWNED)
    return slot_value.astype(jnp.int32)


def shard_levels(rng, extent, cuts, low, top_value):
    level = 1.0
    for axis_at, parts in cuts:
        steps = jax.random.uniform(jax.random.fold_in(jax.random.fold_in(rng, 6), axis_at), (parts,), jnp.float32, low / len(cuts), top_value / len(cuts))
        level = level * jnp.repeat(jnp.exp(steps), extent[axis_at] // parts).reshape((-1,) + (1,) * (len(extent) - 1 - axis_at))
    return level


def noise(own_key, dims, scale, limit, cuts=(), held_as=jnp.bfloat16):
    values = scale * jax.random.normal(own_key, dims, jnp.float32)
    if cuts:
        values = values * shard_levels(own_key, dims, cuts, -0.22, 0.18)
    return jnp.clip(values, -limit, limit).astype(held_as)


def setup_inputs(seed: int = 0) -> dict:
    key_list = jax.random.split(jax.random.key(seed), 9)
    section_input = noise(key_list[0], (ROWS, COLS, CMID), 1.0, 6.0, ((1, 8),))
    conv_weight = noise(key_list[1], (3, 3, CMID, CMID), (9 * CMID) ** -0.5, 0.125)
    conv_bias = noise(key_list[2], (CMID,), 0.5, 3.0, (), jnp.float32)
    deep_weight = noise(key_list[3], (3, 3, CMID, CDEEP), (9 * CMID) ** -0.5, 0.125, ((3, 4),))
    deep_bias = noise(key_list[4], (CDEEP,), 0.5, 3.0, ((0, 4),), jnp.float32)
    labels = draw_labels(jax.random.fold_in(key_list[8], 71), 0)
    slot_ids = draw_slot_ids(jax.random.fold_in(key_list[8], 71), 0)
    embed_grad = noise(key_list[7], (SLOTS, CDEEP), 0.1, 0.8, ((0, 8), (1, 4)), jnp.float32)
    return dict(section_input=section_input, conv_weight=conv_weight, conv_bias=conv_bias, deep_weight=deep_weight, deep_bias=deep_bias, labels=labels, slot_ids=slot_ids, embed_grad=embed_grad)


def swish(value):
    return value * jax.nn.sigmoid(value)


def swish_slope(value):
    sigma = jax.nn.sigmoid(value)
    return sigma * (1.0 + value * (1.0 - sigma))


def convolve(padded, weight, row_count, col_count):
    channels = padded.shape[-1]
    running = None
    for shift_row in range(3):
        for shift_col in range(3):
            window = padded[shift_row:shift_row + row_count, shift_col:shift_col + col_count].reshape(row_count * col_count, channels)
            partial_term = jnp.dot(window, weight[shift_row, shift_col], preferred_element_type=jnp.float32)
            running = partial_term if running is None else running + partial_term
    return running.reshape(row_count, col_count, weight.shape[-1])


def pool_pairs(hidden):
    row_count, col_count, channels = hidden.shape
    return hidden.reshape(row_count // 2, 2, col_count // 2, 2, channels).mean(axis=(1, 3)).astype(jnp.bfloat16)


def reference(section_input, conv_weight, conv_bias, deep_weight, deep_bias, labels, slot_ids, embed_grad):
    padded = jnp.pad(section_input, ((1, 1), (1, 1), (0, 0)))

    def row_block(block_index):
        first_row = (block_index * 8).astype(jnp.int32)
        row_band = lax.dynamic_slice_in_dim(padded, first_row, 10, 0)
        hidden = swish(convolve(row_band, conv_weight, 8, COLS) + conv_bias)
        return pool_pairs(hidden)

    pooled = lax.map(row_block, jnp.arange(ROWS // 8, dtype=jnp.int32)).reshape(HALF_ROWS, HALF_COLS, CMID)
    padded_deep = jnp.pad(pooled, ((1, 1), (1, 1), (0, 0)))
    deep_pre = convolve(padded_deep, deep_weight, HALF_ROWS, HALF_COLS) + deep_bias
    features = swish(deep_pre).astype(jnp.bfloat16).reshape(-1, CDEEP)
    strip_of = jnp.arange(HALF_COLS, dtype=jnp.int32) // HALF_DEV
    entry_index = (strip_of[None, :] * LIST_DEV + jnp.minimum(labels, LIST_DEV - 1)).astype(jnp.int32)
    pixel_slot = jnp.where(labels < LIST_DEV, slot_ids[entry_index], SLOTS).reshape(-1).astype(jnp.int32)
    slot_sums = jax.ops.segment_sum(features.astype(jnp.float32), pixel_slot, num_segments=SLOTS + 1)[:SLOTS]
    counts = jax.ops.segment_sum(jnp.ones(pixel_slot.shape, jnp.float32), pixel_slot, num_segments=SLOTS + 1)[:SLOTS]
    divisor = jnp.maximum(counts, 1.0)[:, None]
    embeddings = slot_sums / divisor
    slot_grad = jnp.concatenate([embed_grad / divisor, jnp.zeros((1, CDEEP), jnp.float32)], axis=0)
    pixel_grad = slot_grad[pixel_slot] * swish_slope(deep_pre.reshape(-1, CDEEP))
    deep_grad = pixel_grad.astype(jnp.bfloat16)
    pieces = []
    for shift_row in range(3):
        for shift_col in range(3):
            window = padded_deep[shift_row:shift_row + HALF_ROWS, shift_col:shift_col + HALF_COLS].reshape(-1, CMID)
            pieces.append(lax.dot_general(window, deep_grad, (((0,), (0,)), ((), ())), preferred_element_type=jnp.float32))
    weight_grad = jnp.stack(pieces).reshape(3, 3, CMID, CDEEP)
    bias_grad = jnp.sum(deep_grad.astype(jnp.float32), axis=0)
    return embeddings, weight_grad, bias_grad
```

```python
import jax
import jax.numpy as jnp
from jax import lax
from jax.sharding import PartitionSpec as P


def with_halo(cells, sides, width):
    for axis, dim in sides:
        count = lax.axis_size(axis)
        ends = count - 1
        head = lax.slice_in_dim(cells, 0, width, axis=dim)
        tail = lax.slice_in_dim(cells, cells.shape[dim] - width, cells.shape[dim], axis=dim)
        cells = jnp.concatenate(
            [
                lax.ppermute(tail, axis, [(i, (i + 1) % count) for i in range(ends)]),
                cells,
                lax.ppermute(head, axis, [((i + 1) % count, i) for i in range(ends)]),
            ],
            axis=dim,
        )
    return cells


def swish(value):
    return value * jax.nn.sigmoid(value)


def swish_slope(value):
    sigma = jax.nn.sigmoid(value)
    return sigma * (1.0 + value * (1.0 - sigma))


def convolve(padded, weight, row_count, col_count):
    channels = padded.shape[-1]
    running = None
    for shift_row in range(3):
        for shift_col in range(3):
            window = padded[
                shift_row : shift_row + row_count, shift_col : shift_col + col_count
            ].reshape(row_count * col_count, channels)
            partial_term = jnp.dot(
                window, weight[shift_row, shift_col], preferred_element_type=jnp.float32
            )
            running = partial_term if running is None else running + partial_term
    return running.reshape(row_count, col_count, weight.shape[-1])


def pool_pairs(hidden):
    row_count, col_count, channels = hidden.shape
    return (
        hidden.reshape(row_count // 2, 2, col_count // 2, 2, channels)
        .mean(axis=(1, 3))
        .astype(jnp.bfloat16)
    )


def swap(value, axis, mask):
    count = lax.axis_size(axis)
    return lax.ppermute(value, axis, [(i, i ^ mask) for i in range(count)])


def bit_groups(count, first, most):
    bits = count.bit_length() - 1
    groups, at = [], 0
    while at < bits:
        size = min(first if at == 0 else most, bits - at)
        groups.append((at, size))
        at += size
    return groups


def gather_relative(value, axis, groups):
    held = value[None]
    for shift, size in groups:
        held = jnp.concatenate(
            [held] + [swap(held, axis, m << shift) for m in range(1, 1 << size)], axis=0
        )
    return held


def pack(block, extra):
    lanes = block.shape[-1]
    top = jnp.maximum(jnp.max(jnp.abs(block)), jnp.max(jnp.abs(extra)))
    power = jnp.ceil(jnp.log2(jnp.maximum(top, 1e-30)))
    up = jnp.exp2(12.0 - power)
    lead = block.shape[:-2]
    tail = jnp.concatenate(
        [extra * up, jnp.broadcast_to(power, (15, lanes))], axis=0
    )
    tail = jnp.broadcast_to(tail, lead + tail.shape)
    return jnp.concatenate([block * up, tail], axis=-2).astype(jnp.float16)


def unpack(packed):
    wide = packed.astype(jnp.float32)
    down = jnp.exp2(wide[..., -1:, :1] - 12.0)
    return wide[..., :-16, :] * down, wide[..., -16:-15, :] * down


def reduce_chunks(chunks, extra, axis, groups):
    me = lax.axis_index(axis)
    for shift, size in groups:
        ways = 1 << size
        digit = (me >> shift) & (ways - 1)
        packed = pack(chunks, extra)
        packed = packed.reshape((-1, ways) + packed.shape[1:])
        total, total_extra = unpack(lax.dynamic_index_in_dim(packed, digit, 1, False))
        for m in range(1, ways):
            part = swap(
                lax.dynamic_index_in_dim(packed, digit ^ m, 1, False), axis, m << shift
            )
            more, more_extra = unpack(part)
            total, total_extra = total + more, total_extra + more_extra
        chunks, extra = total, total_extra[0]
    return chunks[0], extra


def body(
    section_input, conv_weight, conv_bias, deep_weight, deep_bias, labels, slot_ids, embed_grad
):
    chan_count = lax.axis_size("chan")
    chan_pos = lax.axis_index("chan")
    strip_count = lax.axis_size("strip")
    strip_pos = lax.axis_index("strip")
    row_total, col_local, channels = section_input.shape
    row_part = row_total // chan_count
    half_cols = col_local // 2
    list_len = slot_ids.shape[0]
    owned, width_deep = embed_grad.shape

    flat_labels = labels.reshape(-1)
    member = flat_labels[None, :] == jnp.arange(list_len, dtype=jnp.int32)[:, None]
    part_counts = jnp.sum(member.astype(jnp.float32), axis=1)
    side = jnp.stack([slot_ids.astype(jnp.float32), part_counts])
    side = jnp.pad(side, ((0, 6), (0, width_deep - list_len)))
    small_groups = bit_groups(strip_count, 1, 2)
    shared = gather_relative(jnp.concatenate([embed_grad, side]), "strip", small_groups)
    every_id = shared[:, owned, :list_len].reshape(-1).astype(jnp.int32)
    every_count = shared[:, owned + 1, :list_len].reshape(-1)
    entry_count = jnp.sum(
        jnp.where(slot_ids[:, None] == every_id[None, :], every_count[None, :], 0.0), axis=1
    )
    own_slots = strip_pos * owned + jnp.arange(owned, dtype=jnp.int32)
    owner_hot = own_slots[:, None] == every_id[None, :]
    slot_counts = jnp.sum(jnp.where(owner_hot, every_count[None, :], 0.0), axis=1)
    place = ((slot_ids // owned) ^ strip_pos) * owned + slot_ids % owned
    entry_grad = shared[:, :owned].reshape(-1, width_deep)[place]
    entry_grad = entry_grad / jnp.maximum(entry_count, 1.0)[:, None]

    padded_rows = jnp.pad(section_input, ((1, 1), (0, 0), (0, 0)))
    own_rows = lax.dynamic_slice_in_dim(padded_rows, chan_pos * row_part, row_part + 2, 0)
    extended = with_halo(own_rows, (("strip", 1),), 3)
    hidden = swish(convolve(extended, conv_weight, row_part, col_local + 4) + conv_bias)
    pooled = pool_pairs(hidden)
    column = jnp.arange(half_cols + 2)
    outside = (column == 0) & (strip_pos == 0) | (column == half_cols + 1) & (
        strip_pos == strip_count - 1
    )
    pooled = jnp.where(outside[None, :, None], jnp.zeros_like(pooled), pooled)
    gathered = lax.all_gather(pooled, "chan", axis=0, tiled=True)
    padded_deep = jnp.pad(gathered, ((1, 1), (0, 0), (0, 0)))
    half_rows = gathered.shape[0]
    deep_pre = convolve(padded_deep, deep_weight, half_rows, half_cols) + deep_bias
    features = swish(deep_pre).astype(jnp.bfloat16).reshape(-1, width_deep)
    part_sums = jnp.dot(member.astype(jnp.bfloat16), features, preferred_element_type=jnp.float32)
    every_sum = gather_relative(part_sums, "strip", small_groups).reshape(-1, width_deep)
    slot_sums = jnp.dot(
        owner_hot.astype(jnp.float32), every_sum, precision=lax.Precision.HIGHEST
    )
    embeddings = slot_sums / jnp.maximum(slot_counts, 1.0)[:, None]

    pixel_grad = lax.dot_general(
        member.astype(jnp.float32),
        entry_grad,
        (((0,), (0,)), ((), ())),
        precision=lax.Precision.HIGHEST,
        preferred_element_type=jnp.float32,
    )
    deep_grad = (pixel_grad * swish_slope(deep_pre.reshape(-1, width_deep))).astype(jnp.bfloat16)
    pieces = []
    for shift_row in range(3):
        for shift_col in range(3):
            window = padded_deep[
                shift_row : shift_row + half_rows, shift_col : shift_col + half_cols
            ].reshape(-1, channels)
            pieces.append(
                lax.dot_general(
                    window, deep_grad, (((0,), (0,)), ((), ())), preferred_element_type=jnp.float32
                )
            )
    local_weight = jnp.stack(pieces).reshape(strip_count, -1, width_deep)
    local_bias = jnp.sum(deep_grad.astype(jnp.float32), axis=0, keepdims=True)
    groups = bit_groups(strip_count, 3, 3)
    chunk, bias_sum = reduce_chunks(local_weight, local_bias, "strip", groups)
    packed = gather_relative(pack(chunk, bias_sum), "strip", groups)
    weight_rows, bias_rows = unpack(packed[jnp.arange(strip_count) ^ strip_pos])
    weight_grad = weight_rows.reshape(3, 3, channels, width_deep)
    bias_grad = bias_rows[0, 0]
    return (embeddings, weight_grad, bias_grad)


def solution(mesh):
    placed = (
        P(None, "strip", None),
        P(),
        P(),
        P(None, None, None, "chan"),
        P("chan"),
        P(None, "strip"),
        P("strip"),
        P("strip", "chan"),
    )
    return jax.shard_map(
        body,
        mesh=mesh,
        in_specs=placed,
        out_specs=(P("strip", "chan"), P(None, None, None, "chan"), P("chan")),
        check_vma=False,
    )
```

```python
import functools

import jax
import jax.numpy as jnp
from jax import lax
from jax.experimental import pallas as pl
from jax.experimental.pallas import tpu as pltpu
from jax.sharding import PartitionSpec as P

F32, BF16, F16 = jnp.float32, jnp.bfloat16, jnp.float16
VMEM = pl.BlockSpec(memory_space=pltpu.VMEM)
SMEM = pl.BlockSpec(memory_space=pltpu.SMEM)
SIDE = 8
NOTE = 16


def params():
    return pltpu.CompilerParams(vmem_limit_bytes=48 << 20)


def swap(value, axis, mask):
    count = lax.axis_size(axis)
    return lax.ppermute(value, axis, [(i, i ^ mask) for i in range(count)])


def bit_groups(count, first, most):
    bits = count.bit_length() - 1
    groups, at = [], 0
    while at < bits:
        size = min(first if at == 0 else most, bits - at)
        groups.append((at, size))
        at += size
    return groups


def gather_relative(value, axis, groups):
    parts = [value[None]]
    for shift, size in groups:
        held = parts[0] if len(parts) == 1 else jnp.concatenate(parts, axis=0)
        parts = [held] + [swap(held, axis, m << shift) for m in range(1, 1 << size)]
    return parts


def conv_kernel(where_ref, x_ref, w_ref, b_ref, out_ref, wide, taps, *, block):
    rows, cols, chans = x_ref.shape
    half_cols = cols // 2
    out_rows = out_ref.shape[0]
    first = where_ref[0] * (2 * out_rows) - 1
    total = 2 * out_rows + 2
    lanes = chans // 128
    edge = jnp.zeros((8, 128), F32)
    for t in range(wide.shape[0]):
        wide[t, 0:8] = edge
        wide[t, cols + 8 : cols + 16] = edge

    def prepare(i, slot):
        r = first + i
        inside = (r >= 0) & (r < rows)
        x = x_ref[jnp.clip(r, 0, rows - 1)].astype(F32)
        x = jnp.where(inside, x, 0.0)
        for t in range(lanes):
            wide[slot * lanes + t, 8 : 8 + cols] = x[:, t * 128 : (t + 1) * 128]
        for tap in range(4):
            for t in range(lanes):
                piece = wide[slot * lanes + t, pl.ds(7 + tap, half_cols, stride=2), :]
                at = (tap * lanes + t) * 128
                taps[i, :, at : at + 128] = piece.astype(BF16)

    def prepare_two(k, carry):
        prepare(2 * k, 0)
        prepare(2 * k + 1, 1)
        return carry

    lax.fori_loop(0, total // 2, prepare_two, 0)
    bias = b_ref[...]

    def step(k, carry):
        r0 = k * 2 * block
        acc = None
        for phase in range(2):
            lhs = jnp.concatenate(
                [
                    taps[pl.ds(r0 + dr, 2 * block), :, phase * chans : (phase + 3) * chans]
                    for dr in range(3)
                ],
                axis=-1,
            ).reshape(2 * block * half_cols, 9 * chans)
            v = jnp.dot(lhs, w_ref[...], preferred_element_type=F32) + bias
            h = (v * jax.nn.sigmoid(v)).reshape(block, 2, half_cols, chans)
            h = h[:, 0] + h[:, 1]
            acc = h if acc is None else acc + h
        out_ref[pl.ds(k * block, block)] = (acc * 0.25).astype(BF16)
        return carry

    lax.fori_loop(0, out_rows // block, step, 0)


def conv_pool(where, x, w, b):
    rows, cols, chans = x.shape
    out_rows = rows // 4
    block = next(k for k in (6, 4, 3, 2, 1) if out_rows % k == 0)
    return pl.pallas_call(
        functools.partial(conv_kernel, block=block),
        out_shape=jax.ShapeDtypeStruct((out_rows, cols // 2, chans), BF16),
        in_specs=[SMEM, VMEM, VMEM, VMEM],
        out_specs=VMEM,
        scratch_shapes=[
            pltpu.VMEM((2 * (chans // 128), cols + 16, 128), F32),
            pltpu.VMEM((2 * out_rows + 2, cols // 2, 4 * chans), BF16),
        ],
        compiler_params=params(),
        cost_estimate=pl.CostEstimate(
            flops=4 * out_rows * cols * 9 * chans * chans * 2,
            bytes_accessed=rows * cols * chans * 2,
            transcendentals=0,
        ),
        name="conv_pool",
    )(where, x, w, b)


def edge_kernel(where_ref, left_ref, head_ref, tail_ref, right_ref, w_ref, b_ref, out_ref, wide, acc):
    rows, width, chans = head_ref.shape
    lanes = chans // 128
    count = 8 * rows
    for s, pair in enumerate(((left_ref, head_ref), (tail_ref, right_ref))):
        for k, ref in enumerate(pair):
            x = ref[...].astype(F32)
            for t in range(lanes):
                for r in range(rows):
                    at = r * 8 + k * width
                    wide[s * lanes + t, at : at + width] = x[r, :, t * 128 : (t + 1) * 128]
    column = [
        [
            jnp.concatenate(
                [wide[s * lanes + t, pl.ds(c, rows, stride=8), :] for t in range(lanes)], axis=-1
            ).astype(BF16)
            for c in range(2 * width)
        ]
        for s in range(2)
    ]
    lhs = jnp.concatenate(
        [
            jnp.concatenate(column[s][2 * j + phase : 2 * j + phase + 3], axis=-1)
            for s in range(2)
            for j in range(2)
            for phase in range(2)
        ],
        axis=0,
    )
    bias = b_ref[...]
    depth = 3 * chans
    pad = rows + 16
    for dr in range(3):
        part = jnp.dot(lhs, w_ref[dr * depth : (dr + 1) * depth], preferred_element_type=F32)
        for g in range(8):
            own = part[g * rows : (g + 1) * rows]
            for t in range(lanes):
                at = 9 - dr
                piece = own[:, t * 128 : (t + 1) * 128]
                if dr == 0:
                    acc[g * lanes + t, 0:8] = jnp.zeros((8, 128), F32)
                    acc[g * lanes + t, 8 + rows : pad] = jnp.zeros((8, 128), F32)
                    acc[g * lanes + t, 8:9] = jnp.zeros((1, 128), F32)
                    acc[g * lanes + t, at : at + rows] = piece
                else:
                    acc[g * lanes + t, at : at + rows] += piece
    for g in range(4):
        for t in range(lanes):
            total = None
            for phase in range(2):
                at = (2 * g + phase) * lanes + t
                v = acc[at, 8 : 8 + rows] + bias[:, t * 128 : (t + 1) * 128]
                acc[at, 8 : 8 + rows] = v * jax.nn.sigmoid(v)
                both = (
                    acc[at, pl.ds(8, rows // 2, stride=2), :]
                    + acc[at, pl.ds(9, rows // 2, stride=2), :]
                )
                total = both if total is None else total + both
            lost = jnp.where(g == 0, where_ref[1], jnp.where(g == 3, where_ref[2], 0))
            keep = jnp.where(lost > 0, 0.0, 0.25)
            out_ref[g, t] = (total * keep).astype(BF16).astype(F32)


def conv_edges(where, left, head, tail, right, w, b):
    rows, _, chans = head.shape
    lanes = chans // 128
    return pl.pallas_call(
        edge_kernel,
        out_shape=jax.ShapeDtypeStruct((4, lanes, rows // 2, 128), F32),
        in_specs=[SMEM] + [VMEM] * 6,
        out_specs=VMEM,
        scratch_shapes=[
            pltpu.VMEM((2 * lanes, 8 * rows, 128), F32),
            pltpu.VMEM((8 * lanes, rows + 16, 128), F32),
        ],
        compiler_params=params(),
        name="conv_edges",
    )(where, left, head, tail, right, w, b)


def scale_rows(block, note_rows, sums):
    def exponent(values):
        top = None
        for v in values:
            one = jnp.max(jnp.max(jnp.abs(v), axis=0, keepdims=True), axis=1, keepdims=True)
            top = one if top is None else jnp.maximum(top, one)
        return jnp.ceil(jnp.log2(jnp.maximum(top, 1e-30)))

    power = exponent([block, note_rows])
    power_sums = exponent([sums])
    return power, power_sums


def note_block(bias, power, power_sums, width):
    row = lax.broadcasted_iota(jnp.int32, (NOTE, width), 0)
    bias = jnp.broadcast_to(bias * jnp.exp2(12.0 - power), (NOTE, width))
    power = jnp.broadcast_to(power, (NOTE, width))
    power_sums = jnp.broadcast_to(power_sums, (NOTE, width))
    return jnp.where(row == 0, bias, jnp.where(row == 1, power, power_sums))


def read_note(part, at):
    note = part[at : at + NOTE]
    down = jnp.exp2(note[1:2] - 12.0)
    return note[0:1] * down, down, jnp.exp2(note[2:3] - 12.0)


def deep_kernel(
    where_ref, own_ref, other_ref, edge_ref, w_ref, b_ref, lab_ref, slots_ref, *refs, block, n_parts, chunk, ways
):
    part_refs = refs[:n_parts]
    out_refs = refs[n_parts : n_parts + ways]
    wide, taps, member, grad, weight = refs[n_parts + ways :]
    part, cols, chans = own_ref.shape
    rows = 2 * part
    lanes = chans // 128
    width = w_ref.shape[-1]
    half, me = where_ref[0], where_ref[3]
    entries = slots_ref.shape[0]
    owned = part_refs[0].shape[1] - SIDE
    taps[0] = jnp.zeros(taps.shape[1:], BF16)
    taps[rows + 1] = jnp.zeros(taps.shape[1:], BF16)

    def prepare(ref, base, i, slot):
        x = ref[i].astype(F32)
        r = base + i
        for t in range(lanes):
            s = slot * lanes + t
            at = t * 128
            wide[s, 8 : 8 + cols] = x[:, at : at + 128]
            for g, place in enumerate((7, 8, 7 + cols, 8 + cols)):
                wide[s, place : place + 1] = edge_ref[g, t, pl.ds(r, 1), :]
        for tap in range(3):
            for t in range(lanes):
                piece = wide[slot * lanes + t, 7 + tap : 7 + tap + cols, :]
                at = (tap * lanes + t) * 128
                taps[r + 1, :, at : at + 128] = piece.astype(BF16)

    def prepare_two(k, carry):
        prepare(own_ref, half * part, k, 0)
        prepare(other_ref, (1 - half) * part, k, 1)
        return carry

    lax.fori_loop(0, part, prepare_two, 0)
    ids = slots_ref[...]
    total = jnp.zeros((entries, 1), F32)
    entry_grad = jnp.zeros((entries, width), F32)
    owner, inner = ids // owned, ids % owned
    spot = lax.broadcasted_iota(jnp.int32, (entries, owned), 1)
    m = 0
    for ref in part_refs:
        for k in range(ref.shape[0]):
            there = ref[k, owned : owned + 1, :entries] == ids.astype(F32)
            counts = ref[k, owned + 1 : owned + 2, :entries]
            total += jnp.sum(jnp.where(there, counts, 0.0), axis=1, keepdims=True)
            hot = ((owner ^ me) == m) & (inner == spot)
            entry_grad += jnp.dot(
                hot.astype(F32), ref[k, :owned], precision=lax.Precision.HIGHEST, preferred_element_type=F32
            )
            m += 1
    entry_grad = entry_grad / jnp.maximum(total, 1.0)
    lab = jnp.transpose(lab_ref[...].astype(F32))
    lane = lax.broadcasted_iota(jnp.int32, (cols, 128), 1)
    want = jnp.where(lane < 3 * entries, lane % entries, -1).astype(F32)
    for r in range(rows):
        member[r] = (lab[:, r : r + 1] == want).astype(BF16)
    high = entry_grad.astype(BF16)
    rest = entry_grad - high.astype(F32)
    mid = rest.astype(BF16)
    low = (rest - mid.astype(F32)).astype(BF16)
    terms = jnp.concatenate([high, mid, low, jnp.zeros((128 - 3 * entries, width), BF16)], axis=0)
    bias = b_ref[...]
    size = block * cols

    def step(k, carry):
        sums, bias_sum = carry
        r0 = k * block
        lhs = jnp.concatenate([taps[pl.ds(r0 + dr, block)] for dr in range(3)], axis=-1)
        v = jnp.dot(lhs.reshape(size, 9 * chans), w_ref[...], preferred_element_type=F32) + bias
        sig = jax.nn.sigmoid(v)
        features = (v * sig).astype(BF16)
        mem = member[pl.ds(r0, block)].reshape(size, 128)
        pixel = jnp.dot(mem, terms, preferred_element_type=F32)
        dg = (pixel * (sig * (1.0 + v * (1.0 - sig)))).astype(BF16)
        grad[pl.ds(k * size, size)] = dg
        sums = sums + lax.dot_general(
            mem, features, (((0,), (0,)), ((), ())), preferred_element_type=F32
        )[:entries]
        bias_sum = bias_sum + jnp.sum(dg.astype(F32), axis=0, keepdims=True)
        return sums, bias_sum

    sums, bias_sum = lax.fori_loop(
        0, rows // block, step, (jnp.zeros((entries, width), F32), jnp.zeros((1, width), F32))
    )
    depth = 3 * chans
    for dr in range(3):
        window = taps[dr : dr + rows].reshape(rows * cols, depth)
        out = lax.dot_general(grad[...], window, (((0,), (0,)), ((), ())), preferred_element_type=F32)
        weight[dr * depth : (dr + 1) * depth] = jnp.transpose(out)
    if weight.shape[0] > 3 * depth:
        weight[3 * depth :] = jnp.zeros((weight.shape[0] - 3 * depth, width), F32)
    power, power_sums = scale_rows(weight[...], bias_sum, sums)
    up = jnp.exp2(12.0 - power)
    note = note_block(bias_sum, power, power_sums, width)
    sums = sums * jnp.exp2(12.0 - power_sums)
    digit = lax.rem(me, ways)
    heads = weight.shape[0] // chunk // ways
    for m in range(ways):
        for hi in range(heads):
            j = hi * ways + (digit ^ m)
            out_refs[m][hi * chunk : (hi + 1) * chunk] = (
                weight[pl.ds(pl.multiple_of(j * chunk, 8), chunk)] * up
            )
        out_refs[m][heads * chunk : heads * chunk + NOTE] = note
        out_refs[m][heads * chunk + NOTE :] = sums


def deep_part(where, own, other, edges, w, b, labels, slots, parts, chunk, count, ways):
    part, cols, chans = own.shape
    rows, width = 2 * part, w.shape[-1]
    entries = slots.shape[0]
    block = next(k for k in (8, 4, 2, 1) if rows % k == 0)
    out = jax.ShapeDtypeStruct((count // ways * chunk + NOTE + entries, width), F32)
    return pl.pallas_call(
        functools.partial(deep_kernel, block=block, n_parts=len(parts), chunk=chunk, ways=ways),
        out_shape=(out,) * ways,
        in_specs=[SMEM] + [VMEM] * (7 + len(parts)),
        out_specs=(VMEM,) * ways,
        scratch_shapes=[
            pltpu.VMEM((2 * (chans // 128), cols + 16, 128), F32),
            pltpu.VMEM((rows + 2, cols, 3 * chans), BF16),
            pltpu.VMEM((rows, cols, 128), BF16),
            pltpu.VMEM((rows * cols, width), BF16),
            pltpu.VMEM((count * chunk, width), F32),
        ],
        compiler_params=params(),
        cost_estimate=pl.CostEstimate(
            flops=8 * rows * cols * 9 * chans * width, bytes_accessed=4 << 20, transcendentals=0
        ),
        name="deep_part",
    )(where, own, other, edges, w, b, labels, slots, *parts)


def merge_kernel(where_ref, *refs, chunk, heads, held, entries, shift, next_ways):
    n_parts = len(refs) - next_ways - 1
    part_refs, out_refs, sums_ref = refs[:n_parts], refs[n_parts:-1], refs[-1]
    width = part_refs[0].shape[-1]
    size = heads * chunk
    total, bias = jnp.zeros((size, width), F32), jnp.zeros((1, width), F32)
    sums_rows = held * entries
    for m, ref in enumerate(part_refs):
        more, down, down_sums = read_note(ref, size)
        total, bias = total + ref[:size] * down, bias + more
        sums_ref[m * sums_rows : (m + 1) * sums_rows] = ref[size + NOTE :] * down_sums
    sums = sums_ref[...]
    power, power_sums = scale_rows(total, bias, sums)
    note = note_block(bias, power, power_sums, width)
    total = total * jnp.exp2(12.0 - power)
    if next_ways == 1:
        out_refs[0][:size] = total
        out_refs[0][size:] = note
        return
    sums = sums * jnp.exp2(12.0 - power_sums)
    digit = lax.rem(where_ref[3] >> shift, next_ways)
    for m in range(next_ways):
        for hi in range(heads // next_ways):
            piece = jnp.zeros((chunk, width), F32)
            for d in range(next_ways):
                at = (hi * next_ways + d) * chunk
                piece = jnp.where((digit ^ m) == d, total[at : at + chunk], piece)
            out_refs[m][hi * chunk : (hi + 1) * chunk] = piece
        at = heads // next_ways * chunk
        out_refs[m][at : at + NOTE] = note
        out_refs[m][at + NOTE :] = sums


def merge(where, parts, chunk, heads, held, entries, shift, next_ways):
    width = parts[0].shape[-1]
    sums_rows = len(parts) * held * entries
    if next_ways == 1:
        outs = (jax.ShapeDtypeStruct((heads * chunk + NOTE, width), F32),)
    else:
        rows = heads // next_ways * chunk + NOTE + sums_rows
        outs = (jax.ShapeDtypeStruct((rows, width), F32),) * next_ways
    outs = outs + (jax.ShapeDtypeStruct((sums_rows, width), F32),)
    out = pl.pallas_call(
        functools.partial(
            merge_kernel, chunk=chunk, heads=heads, held=held, entries=entries, shift=shift, next_ways=next_ways
        ),
        out_shape=outs,
        in_specs=[SMEM] + [VMEM] * len(parts),
        out_specs=(VMEM,) * len(outs),
        compiler_params=params(),
        name="merge",
    )(where, *parts)
    return out[:-1], out[-1]


def embed_kernel(where_ref, sums_ref, *refs, entries):
    part_refs, out_ref = refs[:-1], refs[-1]
    owned, width = out_ref.shape
    own = (where_ref[3] * owned + lax.broadcasted_iota(jnp.int32, (owned, entries), 0)).astype(F32)
    sums, counts = jnp.zeros((owned, width), F32), jnp.zeros((owned, 1), F32)
    m = 0
    for ref in part_refs:
        for k in range(ref.shape[0]):
            there = ref[k, owned : owned + 1, :entries] == own
            count = ref[k, owned + 1 : owned + 2, :entries]
            counts += jnp.sum(jnp.where(there, count, 0.0), axis=1, keepdims=True)
            sums += jnp.dot(
                there.astype(F32),
                sums_ref[m * entries : (m + 1) * entries],
                precision=lax.Precision.HIGHEST,
                preferred_element_type=F32,
            )
            m += 1
    out_ref[...] = sums / jnp.maximum(counts, 1.0)


def spread_kernel(where_ref, *refs, chunk, rows):
    part_refs, weight_ref, bias_ref, place = refs[:-3], refs[-3], refs[-2], refs[-1]
    me = where_ref[3]
    m = 0
    for ref in part_refs:
        for k in range(ref.shape[0]):
            bias, down, _ = read_note(ref[k], chunk)
            j = me ^ m
            place[pl.ds(pl.multiple_of(j * chunk, 8), chunk)] = ref[k, :chunk] * down

            @pl.when(j == 0)
            def _():
                bias_ref[...] = bias

            m += 1
    weight_ref[...] = place[:rows]


def spread(where, parts, chunk, count, rows):
    width = parts[0].shape[-1]
    return pl.pallas_call(
        functools.partial(spread_kernel, chunk=chunk, rows=rows),
        out_shape=(jax.ShapeDtypeStruct((rows, width), F32), jax.ShapeDtypeStruct((1, width), F32)),
        in_specs=[SMEM] + [VMEM] * len(parts),
        out_specs=(VMEM, VMEM),
        scratch_shapes=[pltpu.VMEM((count * chunk, width), F32)],
        compiler_params=params(),
        name="spread",
    )(where, *parts)


def body(
    section_input, conv_weight, conv_bias, deep_weight, deep_bias, labels, slot_ids, embed_grad
):
    chan_count = lax.axis_size("chan")
    strip_count = lax.axis_size("strip")
    chan_pos = lax.axis_index("chan")
    strip_pos = lax.axis_index("strip")
    half = chan_pos & 1
    channels = section_input.shape[-1]
    entries = slot_ids.shape[0]
    owned, width = embed_grad.shape
    where = jnp.stack(
        [half, (strip_pos == 0).astype(jnp.int32), (strip_pos == strip_count - 1).astype(jnp.int32), strip_pos]
    ).astype(jnp.int32)
    conv_w = conv_weight.reshape(9 * channels, -1)
    conv_b = conv_bias.reshape(1, -1)

    head, tail = section_input[:, :3], section_input[:, -3:]
    pairs = []
    for s in range(strip_count):
        for c in range(chan_count):
            to = s + 1 - 2 * (c & 1)
            if 0 <= to < strip_count:
                pairs.append((s * chan_count + c, to * chan_count + c))
    got = lax.ppermute(jnp.where(half == 0, tail, head), ("strip", "chan"), pairs)
    traded = swap(got, "chan", 1)
    left = jnp.where(half == 0, got, traded)
    right = jnp.where(half == 0, traded, got)

    member = labels.reshape(1, -1) == jnp.arange(entries, dtype=jnp.int32)[:, None]
    counts = jnp.sum(member.astype(F32), axis=1)
    side = jnp.pad(
        jnp.stack([slot_ids.astype(F32), counts]), ((0, SIDE - 2), (0, width - entries))
    )
    shared = gather_relative(
        jnp.concatenate([embed_grad, side]), "strip", bit_groups(strip_count, 1, 2)
    )

    pooled = conv_pool(where, section_input, conv_w, conv_b)
    other = swap(pooled, "chan", 1)
    edges = conv_edges(where, left, head, tail, right, conv_w, conv_b)

    groups = bit_groups(strip_count, 3, 3)
    chunk = -(-9 * channels // strip_count // 8) * 8
    send = deep_part(
        where,
        pooled,
        other,
        edges,
        deep_weight.reshape(9 * channels, width),
        deep_bias.reshape(1, width),
        labels,
        slot_ids.reshape(entries, 1),
        shared,
        chunk,
        strip_count,
        1 << groups[0][1],
    )
    heads, held = strip_count, 1
    for k, (shift, size) in enumerate(groups):
        ways = 1 << size
        heads //= ways
        parts = [send[0]] + [
            swap(send[m].astype(F16), "strip", m << shift).astype(F32) for m in range(1, ways)
        ]
        after, next_size = groups[k + 1] if k + 1 < len(groups) else (0, 0)
        send, sums = merge(where, parts, chunk, heads, held, entries, after, 1 << next_size)
        held *= ways
    embeddings = pl.pallas_call(
        functools.partial(embed_kernel, entries=entries),
        out_shape=jax.ShapeDtypeStruct((owned, width), F32),
        in_specs=[SMEM] + [VMEM] * (1 + len(shared)),
        out_specs=VMEM,
        compiler_params=params(),
        name="embed",
    )(where, sums, *shared)
    gathered = gather_relative(send[0].astype(F16), "strip", groups)
    weight_rows, bias_row = spread(
        where, [g.astype(F32) for g in gathered], chunk, strip_count, 9 * channels
    )
    return (embeddings, weight_rows.reshape(3, 3, channels, width), bias_row[0])


def solution(mesh):
    placed = (
        P(None, "strip", None),
        P(),
        P(),
        P(None, None, None, "chan"),
        P("chan"),
        P(None, "strip"),
        P("strip"),
        P("strip", "chan"),
    )
    return jax.shard_map(
        body,
        mesh=mesh,
        in_specs=placed,
        out_specs=(P("strip", "chan"), P(None, None, None, "chan"), P("chan")),
        check_vma=False,
    )
```

```python
import functools

import jax
import jax.numpy as jnp
from jax import lax
from jax.experimental import pallas as pl
from jax.experimental.pallas import tpu as pltpu
from jax.sharding import PartitionSpec as P

F32, BF16, F16 = jnp.float32, jnp.bfloat16, jnp.float16
VMEM = pl.BlockSpec(memory_space=pltpu.VMEM)
SMEM = pl.BlockSpec(memory_space=pltpu.SMEM)
ANY = pl.BlockSpec(memory_space=pl.ANY)
SIDE = 8
NOTE = 16


def params():
    return pltpu.CompilerParams(vmem_limit_bytes=48 << 20)


def swap(value, axis, mask):
    count = lax.axis_size(axis)
    return lax.ppermute(value, axis, [(i, i ^ mask) for i in range(count)])


def bit_groups(count, first, most):
    bits = count.bit_length() - 1
    groups, at = [], 0
    while at < bits:
        size = min(first if at == 0 else most, bits - at)
        groups.append((at, size))
        at += size
    return groups


def gather_groups(value, axis, groups):
    parts = [value]
    for shift, size in groups:
        held = parts[0] if len(parts) == 1 else jnp.concatenate(parts, axis=0)
        parts = [held] + [swap(held, axis, m << shift) for m in range(1, 1 << size)]
    return parts


def high_groups(count):
    return [(at + 1, size) for at, size in bit_groups(count // 2, 2, 2)]


def conv_kernel(
    where_ref, x_hbm, w_hbm, b_ref, *refs, part, parts, block
):
    out_ref, rows_ref, w_ref, wide, taps, sems = refs[-6:]
    rows, cols, chans = x_hbm.shape
    half_cols = cols // 2
    out_rows = out_ref.shape[0]
    total = 2 * out_rows + 2
    first = (where_ref[0] * parts + part) * (2 * out_rows) - 1
    start = jnp.clip(first, 0, rows - total)
    offset = first - start
    early = total // 2
    copies = [
        pltpu.make_async_copy(x_hbm.at[pl.ds(start, early)], rows_ref.at[pl.ds(0, early)], sems.at[0]),
        pltpu.make_async_copy(
            x_hbm.at[pl.ds(start + early, total - early)],
            rows_ref.at[pl.ds(early, total - early)],
            sems.at[1],
        ),
        pltpu.make_async_copy(w_hbm, w_ref, sems.at[2]),
    ]
    for copy in copies:
        copy.start()
    lanes = chans // 128
    edge = jnp.zeros((8, 128), F32)
    for t in range(wide.shape[0]):
        wide[t, 0:8] = edge
        wide[t, cols + 8 : cols + 16] = edge

    def prepare(i, slot):
        r = i + offset
        inside = (r >= 0) & (r < total)
        x = rows_ref[jnp.clip(r, 0, total - 1)].astype(F32)
        x = jnp.where(inside, x, 0.0)
        for t in range(lanes):
            wide[slot * lanes + t, 8 : 8 + cols] = x[:, t * 128 : (t + 1) * 128]
        for tap in range(4):
            for t in range(lanes):
                piece = wide[slot * lanes + t, pl.ds(7 + tap, half_cols, stride=2), :]
                at = (tap * lanes + t) * 128
                taps[i, :, at : at + 128] = piece.astype(BF16)

    def prepare_two(k, carry):
        prepare(2 * k, 0)
        prepare(2 * k + 1, 1)
        return carry

    copies[0].wait()
    ready = (early - 1) // 2
    lax.fori_loop(0, ready, prepare_two, 0)
    copies[1].wait()
    lax.fori_loop(ready, total // 2, prepare_two, 0)
    copies[2].wait()
    bias = b_ref[...]

    def step(k, carry):
        r0 = k * 2 * block
        acc = None
        for phase in range(2):
            lhs = jnp.concatenate(
                [
                    taps[pl.ds(r0 + dr, 2 * block), :, phase * chans : (phase + 3) * chans]
                    for dr in range(3)
                ],
                axis=-1,
            ).reshape(2 * block * half_cols, 9 * chans)
            v = jnp.dot(lhs, w_ref[...], preferred_element_type=F32) + bias
            h = (v * jax.nn.sigmoid(v)).reshape(block, 2, half_cols, chans)
            h = h[:, 0] + h[:, 1]
            acc = h if acc is None else acc + h
        out_ref[pl.ds(k * block, block)] = (acc * 0.25).astype(BF16)
        return carry

    lax.fori_loop(0, out_rows // block, step, 0)


def conv_pool(where, x, w, b, part, parts, after=()):
    rows, cols, chans = x.shape
    out_rows = rows // 4 // parts
    block = next(k for k in (6, 4, 3, 2, 1) if out_rows % k == 0)
    total = 2 * out_rows + 2
    return pl.pallas_call(
        functools.partial(conv_kernel, part=part, parts=parts, block=block),
        out_shape=jax.ShapeDtypeStruct((out_rows, cols // 2, chans), BF16),
        in_specs=[SMEM, ANY, ANY, VMEM] + [ANY] * len(after),
        out_specs=VMEM,
        scratch_shapes=[
            pltpu.VMEM((total, cols, chans), BF16),
            pltpu.VMEM(w.shape, BF16),
            pltpu.VMEM((2 * (chans // 128), cols + 16, 128), F32),
            pltpu.VMEM((total, cols // 2, 4 * chans), BF16),
            pltpu.SemaphoreType.DMA((3,)),
        ],
        compiler_params=params(),
        cost_estimate=pl.CostEstimate(
            flops=4 * out_rows * cols * 9 * chans * chans * 2,
            bytes_accessed=2 * total * cols * chans,
            transcendentals=0,
        ),
        name="conv_pool",
    )(where, x, w, b, *after)


def edge_kernel(where_ref, left_ref, head_ref, tail_ref, right_ref, w_hbm, b_ref, *refs):
    out_ref, w_ref, wide, acc, sem = refs[-5:]
    copy = pltpu.make_async_copy(w_hbm, w_ref, sem)
    copy.start()
    rows, width, chans = head_ref.shape
    lanes = chans // 128
    count = 8 * rows
    for s, pair in enumerate(((left_ref, head_ref), (tail_ref, right_ref))):
        for k, ref in enumerate(pair):
            x = ref[...].astype(F32)
            for t in range(lanes):
                for r in range(rows):
                    at = r * 8 + k * width
                    wide[s * lanes + t, at : at + width] = x[r, :, t * 128 : (t + 1) * 128]
    column = [
        [
            jnp.concatenate(
                [wide[s * lanes + t, pl.ds(c, rows, stride=8), :] for t in range(lanes)], axis=-1
            ).astype(BF16)
            for c in range(2 * width)
        ]
        for s in range(2)
    ]
    lhs = jnp.concatenate(
        [
            jnp.concatenate(column[s][2 * j + phase : 2 * j + phase + 3], axis=-1)
            for s in range(2)
            for j in range(2)
            for phase in range(2)
        ],
        axis=0,
    )
    bias = b_ref[...]
    depth = 3 * chans
    pad = rows + 16
    copy.wait()
    for dr in range(3):
        part = jnp.dot(lhs, w_ref[dr * depth : (dr + 1) * depth], preferred_element_type=F32)
        for g in range(8):
            own = part[g * rows : (g + 1) * rows]
            for t in range(lanes):
                at = 9 - dr
                piece = own[:, t * 128 : (t + 1) * 128]
                if dr == 0:
                    acc[g * lanes + t, 0:8] = jnp.zeros((8, 128), F32)
                    acc[g * lanes + t, 8 + rows : pad] = jnp.zeros((8, 128), F32)
                    acc[g * lanes + t, 8:9] = jnp.zeros((1, 128), F32)
                    acc[g * lanes + t, at : at + rows] = piece
                else:
                    acc[g * lanes + t, at : at + rows] += piece
    for g in range(4):
        for t in range(lanes):
            total = None
            for phase in range(2):
                at = (2 * g + phase) * lanes + t
                v = acc[at, 8 : 8 + rows] + bias[:, t * 128 : (t + 1) * 128]
                acc[at, 8 : 8 + rows] = v * jax.nn.sigmoid(v)
                both = (
                    acc[at, pl.ds(8, rows // 2, stride=2), :]
                    + acc[at, pl.ds(9, rows // 2, stride=2), :]
                )
                total = both if total is None else total + both
            lost = jnp.where(g == 0, where_ref[1], jnp.where(g == 3, where_ref[2], 0))
            keep = jnp.where(lost > 0, 0.0, 0.25)
            out_ref[g, t] = (total * keep).astype(BF16).astype(F32)


def conv_edges(where, left, head, tail, right, w, b, after):
    rows, _, chans = head.shape
    lanes = chans // 128
    return pl.pallas_call(
        edge_kernel,
        out_shape=jax.ShapeDtypeStruct((4, lanes, rows // 2, 128), F32),
        in_specs=[SMEM] + [VMEM] * 4 + [ANY, VMEM] + [ANY] * len(after),
        out_specs=VMEM,
        scratch_shapes=[
            pltpu.VMEM(w.shape, BF16),
            pltpu.VMEM((2 * lanes, 8 * rows, 128), F32),
            pltpu.VMEM((8 * lanes, rows + 16, 128), F32),
            pltpu.SemaphoreType.DMA,
        ],
        compiler_params=params(),
        name="conv_edges",
    )(where, left, head, tail, right, w, b, *after)


def scale_rows(block, note_rows, sums):
    def exponent(values):
        top = None
        for v in values:
            one = jnp.max(jnp.max(jnp.abs(v), axis=0, keepdims=True), axis=1, keepdims=True)
            top = one if top is None else jnp.maximum(top, one)
        return jnp.ceil(jnp.log2(jnp.maximum(top, 1e-30)))

    power = exponent([block, note_rows])
    power_sums = exponent([sums])
    return power, power_sums


def note_block(bias, power, power_sums, width):
    row = lax.broadcasted_iota(jnp.int32, (NOTE, width), 0)
    bias = jnp.broadcast_to(bias * jnp.exp2(12.0 - power), (NOTE, width))
    power = jnp.broadcast_to(power, (NOTE, width))
    power_sums = jnp.broadcast_to(power_sums, (NOTE, width))
    return jnp.where(row == 0, bias, jnp.where(row == 1, power, power_sums))


def read_note(part, at):
    note = part[at : at + NOTE]
    down = jnp.exp2(note[1:2] - 12.0)
    return note[0:1] * down, down, jnp.exp2(note[2:3] - 12.0)


def deep_kernel(
    where_ref, edge_ref, w_ref, b_ref, lab_ref, slots_ref, *refs, block, n_maps, n_parts, chunk, ways
):
    map_refs, refs = refs[: 2 * n_maps], refs[2 * n_maps :]
    part_refs = refs[:n_parts]
    out_refs = refs[n_parts : n_parts + ways]
    wide, taps, member, grad, weight = refs[n_parts + ways :]
    part, cols, chans = map_refs[0].shape
    rows = 2 * n_maps * part
    lanes = chans // 128
    width = w_ref.shape[-1]
    half, me = where_ref[0], where_ref[3]
    entries = slots_ref.shape[0]
    owned = part_refs[0].shape[1] - SIDE
    taps[0] = jnp.zeros(taps.shape[1:], BF16)
    taps[rows + 1] = jnp.zeros(taps.shape[1:], BF16)

    def prepare(ref, base, i, slot):
        x = ref[i].astype(F32)
        r = base + i
        for t in range(lanes):
            s = slot * lanes + t
            at = t * 128
            wide[s, 8 : 8 + cols] = x[:, at : at + 128]
            for g, place in enumerate((7, 8, 7 + cols, 8 + cols)):
                wide[s, place : place + 1] = edge_ref[g, t, pl.ds(r, 1), :]
        for tap in range(3):
            for t in range(lanes):
                piece = wide[slot * lanes + t, 7 + tap : 7 + tap + cols, :]
                at = (tap * lanes + t) * 128
                taps[r + 1, :, at : at + 128] = piece.astype(BF16)

    def prepare_rows(k, carry):
        for q in range(n_maps):
            prepare(map_refs[q], (half * n_maps + q) * part, k, 2 * q)
            prepare(map_refs[n_maps + q], ((1 - half) * n_maps + q) * part, k, 2 * q + 1)
        return carry

    lax.fori_loop(0, part, prepare_rows, 0)
    ids = slots_ref[...]
    total = jnp.zeros((entries, 1), F32)
    entry_grad = jnp.zeros((entries, width), F32)
    owner, inner = ids // owned, ids % owned
    spot = lax.broadcasted_iota(jnp.int32, (entries, owned), 1)
    m = 0
    for ref in part_refs:
        for k in range(ref.shape[0]):
            there = ref[k, owned : owned + 1, :entries] == ids.astype(F32)
            counts = ref[k, owned + 1 : owned + 2, :entries]
            total += jnp.sum(jnp.where(there, counts, 0.0), axis=1, keepdims=True)
            hot = ((owner ^ me) == m) & (inner == spot)
            entry_grad += jnp.dot(
                hot.astype(F32), ref[k, :owned], precision=lax.Precision.HIGHEST, preferred_element_type=F32
            )
            m += 1
    entry_grad = entry_grad / jnp.maximum(total, 1.0)
    lab = jnp.transpose(lab_ref[...].astype(F32))
    lane = lax.broadcasted_iota(jnp.int32, (cols, 128), 1)
    want = jnp.where(lane < 3 * entries, lane % entries, -1).astype(F32)
    for r in range(rows):
        member[r] = (lab[:, r : r + 1] == want).astype(BF16)
    high = entry_grad.astype(BF16)
    rest = entry_grad - high.astype(F32)
    mid = rest.astype(BF16)
    low = (rest - mid.astype(F32)).astype(BF16)
    terms = jnp.concatenate([high, mid, low, jnp.zeros((128 - 3 * entries, width), BF16)], axis=0)
    bias = b_ref[...]
    size = block * cols

    def step(k, carry):
        sums, bias_sum = carry
        r0 = k * block
        lhs = jnp.concatenate([taps[pl.ds(r0 + dr, block)] for dr in range(3)], axis=-1)
        v = jnp.dot(lhs.reshape(size, 9 * chans), w_ref[...], preferred_element_type=F32) + bias
        sig = jax.nn.sigmoid(v)
        features = (v * sig).astype(BF16)
        mem = member[pl.ds(r0, block)].reshape(size, 128)
        pixel = jnp.dot(mem, terms, preferred_element_type=F32)
        dg = (pixel * (sig * (1.0 + v * (1.0 - sig)))).astype(BF16)
        grad[pl.ds(k * size, size)] = dg
        sums = sums + lax.dot_general(
            mem, features, (((0,), (0,)), ((), ())), preferred_element_type=F32
        )[:entries]
        bias_sum = bias_sum + jnp.sum(dg.astype(F32), axis=0, keepdims=True)
        return sums, bias_sum

    sums, bias_sum = lax.fori_loop(
        0, rows // block, step, (jnp.zeros((entries, width), F32), jnp.zeros((1, width), F32))
    )
    depth = 3 * chans
    for dr in range(3):
        window = taps[dr : dr + rows].reshape(rows * cols, depth)
        out = lax.dot_general(grad[...], window, (((0,), (0,)), ((), ())), preferred_element_type=F32)
        weight[dr * depth : (dr + 1) * depth] = jnp.transpose(out)
    if weight.shape[0] > 3 * depth:
        weight[3 * depth :] = jnp.zeros((weight.shape[0] - 3 * depth, width), F32)
    power, power_sums = scale_rows(weight[...], bias_sum, sums)
    up = jnp.exp2(12.0 - power)
    note = note_block(bias_sum, power, power_sums, width)
    sums = sums * jnp.exp2(12.0 - power_sums)
    digit = lax.rem(me, ways)
    heads = weight.shape[0] // chunk // ways
    for m in range(ways):
        for hi in range(heads):
            j = hi * ways + (digit ^ m)
            out_refs[m][hi * chunk : (hi + 1) * chunk] = (
                weight[pl.ds(pl.multiple_of(j * chunk, 8), chunk)] * up
            )
        out_refs[m][heads * chunk : heads * chunk + NOTE] = note
        out_refs[m][heads * chunk + NOTE :] = sums


def deep_part(where, own, other, edges, w, b, labels, slots, parts, chunk, count, ways):
    part, cols, chans = own[0].shape
    rows, width = 2 * len(own) * part, w.shape[-1]
    entries = slots.shape[0]
    block = next(k for k in (8, 4, 2, 1) if rows % k == 0)
    out = jax.ShapeDtypeStruct((count // ways * chunk + NOTE + entries, width), F32)
    return pl.pallas_call(
        functools.partial(
            deep_kernel, block=block, n_maps=len(own), n_parts=len(parts), chunk=chunk, ways=ways
        ),
        out_shape=(out,) * ways,
        in_specs=[SMEM] + [VMEM] * (5 + 2 * len(own) + len(parts)),
        out_specs=(VMEM,) * ways,
        scratch_shapes=[
            pltpu.VMEM((2 * len(own) * (chans // 128), cols + 16, 128), F32),
            pltpu.VMEM((rows + 2, cols, 3 * chans), BF16),
            pltpu.VMEM((rows, cols, 128), BF16),
            pltpu.VMEM((rows * cols, width), BF16),
            pltpu.VMEM((count * chunk, width), F32),
        ],
        compiler_params=params(),
        cost_estimate=pl.CostEstimate(
            flops=8 * rows * cols * 9 * chans * width, bytes_accessed=4 << 20, transcendentals=0
        ),
        name="deep_part",
    )(where, edges, w, b, labels, slots, *own, *other, *parts)


def merge_kernel(where_ref, *refs, chunk, heads, held, entries, shift, next_ways):
    n_parts = len(refs) - next_ways - 1
    part_refs, out_refs, sums_ref = refs[:n_parts], refs[n_parts:-1], refs[-1]
    width = part_refs[0].shape[-1]
    size = heads * chunk
    total, bias = jnp.zeros((size, width), F32), jnp.zeros((1, width), F32)
    sums_rows = held * entries
    for m, ref in enumerate(part_refs):
        more, down, down_sums = read_note(ref, size)
        total, bias = total + ref[:size] * down, bias + more
        sums_ref[m * sums_rows : (m + 1) * sums_rows] = ref[size + NOTE :] * down_sums
    sums = sums_ref[...]
    power, power_sums = scale_rows(total, bias, sums)
    note = note_block(bias, power, power_sums, width)
    total = total * jnp.exp2(12.0 - power)
    if next_ways == 1:
        out_refs[0][:size] = total
        out_refs[0][size:] = note
        return
    sums = sums * jnp.exp2(12.0 - power_sums)
    digit = lax.rem(where_ref[3] >> shift, next_ways)
    for m in range(next_ways):
        for hi in range(heads // next_ways):
            piece = jnp.zeros((chunk, width), F32)
            for d in range(next_ways):
                at = (hi * next_ways + d) * chunk
                piece = jnp.where((digit ^ m) == d, total[at : at + chunk], piece)
            out_refs[m][hi * chunk : (hi + 1) * chunk] = piece
        at = heads // next_ways * chunk
        out_refs[m][at : at + NOTE] = note
        out_refs[m][at + NOTE :] = sums


def merge(where, parts, chunk, heads, held, entries, shift, next_ways):
    width = parts[0].shape[-1]
    sums_rows = len(parts) * held * entries
    if next_ways == 1:
        outs = (jax.ShapeDtypeStruct((heads * chunk + NOTE, width), F32),)
    else:
        rows = heads // next_ways * chunk + NOTE + sums_rows
        outs = (jax.ShapeDtypeStruct((rows, width), F32),) * next_ways
    outs = outs + (jax.ShapeDtypeStruct((sums_rows, width), F32),)
    out = pl.pallas_call(
        functools.partial(
            merge_kernel, chunk=chunk, heads=heads, held=held, entries=entries, shift=shift, next_ways=next_ways
        ),
        out_shape=outs,
        in_specs=[SMEM] + [VMEM] * len(parts),
        out_specs=(VMEM,) * len(outs),
        compiler_params=params(),
        name="merge",
    )(where, *parts)
    return out[:-1], out[-1]


def embed_kernel(where_ref, sums_ref, *refs, entries):
    part_refs, out_ref = refs[:-1], refs[-1]
    owned, width = out_ref.shape
    own = (where_ref[3] * owned + lax.broadcasted_iota(jnp.int32, (owned, entries), 0)).astype(F32)
    sums, counts = jnp.zeros((owned, width), F32), jnp.zeros((owned, 1), F32)
    m = 0
    for ref in part_refs:
        for k in range(ref.shape[0]):
            there = ref[k, owned : owned + 1, :entries] == own
            count = ref[k, owned + 1 : owned + 2, :entries]
            counts += jnp.sum(jnp.where(there, count, 0.0), axis=1, keepdims=True)
            sums += jnp.dot(
                there.astype(F32),
                sums_ref[m * entries : (m + 1) * entries],
                precision=lax.Precision.HIGHEST,
                preferred_element_type=F32,
            )
            m += 1
    out_ref[...] = sums / jnp.maximum(counts, 1.0)


def spread_kernel(where_ref, *refs, chunk, rows):
    part_refs, weight_ref, bias_ref, place = refs[:-3], refs[-3], refs[-2], refs[-1]
    me = where_ref[3]
    m = 0
    for p, ref in enumerate(part_refs):
        m = 1 if p == len(part_refs) // 2 else m
        for k in range(ref.shape[0]):
            bias, down, _ = read_note(ref[k], chunk)
            j = me ^ m
            place[pl.ds(pl.multiple_of(j * chunk, 8), chunk)] = ref[k, :chunk] * down

            @pl.when(j == 0)
            def _():
                bias_ref[...] = bias

            m += 2
    weight_ref[...] = place[:rows]


def spread(where, parts, chunk, count, rows):
    width = parts[0].shape[-1]
    return pl.pallas_call(
        functools.partial(spread_kernel, chunk=chunk, rows=rows),
        out_shape=(jax.ShapeDtypeStruct((rows, width), F32), jax.ShapeDtypeStruct((1, width), F32)),
        in_specs=[SMEM] + [VMEM] * len(parts),
        out_specs=(VMEM, VMEM),
        scratch_shapes=[pltpu.VMEM((count * chunk, width), F32)],
        compiler_params=params(),
        name="spread",
    )(where, *parts)


def body(
    section_input, conv_weight, conv_bias, deep_weight, deep_bias, labels, slot_ids, embed_grad
):
    chan_count = lax.axis_size("chan")
    strip_count = lax.axis_size("strip")
    chan_pos = lax.axis_index("chan")
    strip_pos = lax.axis_index("strip")
    half = chan_pos & 1
    channels = section_input.shape[-1]
    entries = slot_ids.shape[0]
    owned, width = embed_grad.shape
    where = jnp.stack(
        [half, (strip_pos == 0).astype(jnp.int32), (strip_pos == strip_count - 1).astype(jnp.int32), strip_pos]
    ).astype(jnp.int32)
    conv_w = conv_weight.reshape(9 * channels, -1)
    conv_b = conv_bias.reshape(1, -1)

    head, tail = section_input[:, :3], section_input[:, -3:]
    pairs = []
    for s in range(strip_count):
        for c in range(chan_count):
            to = s + 1 - 2 * (c & 1)
            if 0 <= to < strip_count:
                pairs.append((s * chan_count + c, to * chan_count + c))
    got = lax.ppermute(jnp.where(half == 0, tail, head), ("strip", "chan"), pairs)
    traded = swap(got, "chan", 1)
    left = jnp.where(half == 0, got, traded)
    right = jnp.where(half == 0, traded, got)

    member = labels.reshape(1, -1) == jnp.arange(entries, dtype=jnp.int32)[:, None]
    counts = jnp.sum(member.astype(F32), axis=1)
    side = jnp.pad(
        jnp.stack([slot_ids.astype(F32), counts]), ((0, SIDE - 2), (0, width - entries))
    )
    packed = jnp.concatenate([embed_grad, side])
    near = swap(packed, "strip", 1)
    shared = gather_groups(jnp.stack([packed, near]), "strip", bit_groups(strip_count, 1, 2)[1:])

    own_a = conv_pool(where, section_input, conv_w, conv_b, 0, 2)
    own_b = conv_pool(where, section_input, conv_w, conv_b, 1, 2, (near,))
    pooled = [own_a, own_b]
    other = [swap(p, "chan", 1) for p in pooled]
    edges = conv_edges(where, left, head, tail, right, conv_w, conv_b, shared[1:])

    groups = bit_groups(strip_count, 3, 3)
    chunk = -(-9 * channels // strip_count // 8) * 8
    send = deep_part(
        where,
        pooled,
        other,
        edges,
        deep_weight.reshape(9 * channels, width),
        deep_bias.reshape(1, width),
        labels,
        slot_ids.reshape(entries, 1),
        shared,
        chunk,
        strip_count,
        1 << groups[0][1],
    )
    heads, held = strip_count, 1
    for k, (shift, size) in enumerate(groups):
        ways = 1 << size
        heads //= ways
        parts = [send[0]] + [
            swap(send[m].astype(F16), "strip", m << shift).astype(F32) for m in range(1, ways)
        ]
        after, next_size = groups[k + 1] if k + 1 < len(groups) else (0, 0)
        send, sums = merge(where, parts, chunk, heads, held, entries, after, 1 << next_size)
        held *= ways
    embeddings = pl.pallas_call(
        functools.partial(embed_kernel, entries=entries),
        out_shape=jax.ShapeDtypeStruct((owned, width), F32),
        in_specs=[SMEM] + [VMEM] * (1 + len(shared)),
        out_specs=VMEM,
        compiler_params=params(),
        name="embed",
    )(where, sums, *shared)
    gathered = gather_groups(send[0].astype(F16)[None], "strip", high_groups(strip_count))
    gathered = gathered + [swap(g, "strip", 1) for g in gathered]
    weight_rows, bias_row = spread(
        where, [g.astype(F32) for g in gathered], chunk, strip_count, 9 * channels
    )
    return (embeddings, weight_rows.reshape(3, 3, channels, width), bias_row[0])


def solution(mesh):
    placed = (
        P(None, "strip", None),
        P(),
        P(),
        P(None, None, None, "chan"),
        P("chan"),
        P(None, "strip"),
        P("strip"),
        P("strip", "chan"),
    )
    return jax.shard_map(
        body,
        mesh=mesh,
        in_specs=placed,
        out_specs=(P("strip", "chan"), P(None, None, None, "chan"), P("chan")),
        check_vma=False,
    )
```

```python
import functools

import jax
import jax.numpy as jnp
from jax import lax
from jax.experimental import pallas as pl
from jax.experimental.pallas import tpu as pltpu
from jax.sharding import PartitionSpec as P

F32, BF16, F16 = jnp.float32, jnp.bfloat16, jnp.float16
VMEM = pl.BlockSpec(memory_space=pltpu.VMEM)
SMEM = pl.BlockSpec(memory_space=pltpu.SMEM)
HBM = pl.BlockSpec(memory_space=pltpu.HBM)
ANY = pl.BlockSpec(memory_space=pl.ANY)
SIDE = 8
NOTE = 16


def params(mib=8):
    return pltpu.CompilerParams(vmem_limit_bytes=mib << 20)


def swap(value, axis, mask):
    count = lax.axis_size(axis)
    return lax.ppermute(value, axis, [(i, i ^ mask) for i in range(count)])


def bit_groups(count, first, most):
    bits = count.bit_length() - 1
    groups, at = [], 0
    while at < bits:
        size = min(first if at == 0 else most, bits - at)
        groups.append((at, size))
        at += size
    return groups


def gather_groups(value, axis, groups):
    parts = [value]
    for shift, size in groups:
        held = parts[0] if len(parts) == 1 else jnp.concatenate(parts, axis=0)
        parts = [held] + [swap(held, axis, m << shift) for m in range(1, 1 << size)]
    return parts


def relative(refs):
    half = len(refs) // 2
    for low in range(2):
        m = low
        for ref in refs[low * half : (low + 1) * half]:
            for k in range(ref.shape[0]):
                yield m, ref, k
                m += 2


def high_groups(count):
    return [(at + 1, size) for at, size in bit_groups(count // 2, 2, 2)]


def window_kernel(where_ref, x_hbm, taps, rows_ref, wide, sems):
    rows, cols, chans = x_hbm.shape
    half_cols = cols // 2
    total = taps.shape[0]
    first = where_ref[0] * (total - 2) - 1
    start = jnp.clip(first, 0, rows - total)
    offset = first - start
    steps = sems.shape[0]
    cuts = [k * total // steps for k in range(steps + 1)]
    copies = []
    for k in range(steps):
        at, size = cuts[k], cuts[k + 1] - cuts[k]
        copies.append(
            pltpu.make_async_copy(
                x_hbm.at[pl.ds(start + at, size)], rows_ref.at[pl.ds(at, size)], sems.at[k]
            )
        )
        copies[k].start()
    lanes = chans // 128
    border = jnp.zeros((8, 128), F32)
    for t in range(wide.shape[0]):
        wide[t, 0:8] = border
        wide[t, cols + 8 : cols + 16] = border

    def prepare(i, slot):
        r = i + offset
        inside = (r >= 0) & (r < total)
        x = rows_ref[jnp.clip(r, 0, total - 1)].astype(F32)
        x = jnp.where(inside, x, 0.0)
        for t in range(lanes):
            wide[slot * lanes + t, 8 : 8 + cols] = x[:, t * 128 : (t + 1) * 128]
        for tap in range(4):
            for t in range(lanes):
                piece = wide[slot * lanes + t, pl.ds(7 + tap, half_cols, stride=2), :]
                at = (tap * lanes + t) * 128
                taps[i, :, at : at + 128] = piece.astype(BF16)

    def prepare_two(k, carry):
        prepare(2 * k, 0)
        prepare(2 * k + 1, 1)
        return carry

    done = 0
    for k in range(steps):
        copies[k].wait()
        ready = (cuts[k + 1] - 1) // 2 if k + 1 < steps else total // 2
        lax.fori_loop(done, ready, prepare_two, 0)
        done = ready


def windows(where, x):
    rows, cols, chans = x.shape
    total = rows // 2 + 2
    return pl.pallas_call(
        window_kernel,
        out_shape=jax.ShapeDtypeStruct((total, cols // 2, 4 * chans), BF16),
        in_specs=[SMEM, HBM],
        out_specs=VMEM,
        scratch_shapes=[
            pltpu.VMEM((total, cols, chans), BF16),
            pltpu.VMEM((2 * (chans // 128), cols + 16, 128), F32),
            pltpu.SemaphoreType.DMA((4,)),
        ],
        compiler_params=params(12),
        cost_estimate=pl.CostEstimate(flops=0, bytes_accessed=12 << 20, transcendentals=0),
        name="windows",
    )(where, pltpu.with_memory_space_constraint(x, pltpu.HBM))


def edge_part(where_ref, pairs, w_ref, bias, edge_ref, wide, acc):
    rows, width, chans = pairs[0][0].shape
    lanes = chans // 128
    for s, pair in enumerate(pairs):
        for k, ref in enumerate(pair):
            x = ref[...].astype(F32)
            for t in range(lanes):
                for r in range(rows):
                    at = r * 8 + k * width
                    wide[s * lanes + t, at : at + width] = x[r, :, t * 128 : (t + 1) * 128]
    column = [
        [
            jnp.concatenate(
                [wide[s * lanes + t, pl.ds(c, rows, stride=8), :] for t in range(lanes)], axis=-1
            ).astype(BF16)
            for c in range(2 * width)
        ]
        for s in range(2)
    ]
    lhs = jnp.concatenate(
        [
            jnp.concatenate(column[s][2 * j + phase : 2 * j + phase + 3], axis=-1)
            for s in range(2)
            for j in range(2)
            for phase in range(2)
        ],
        axis=0,
    )
    depth = 3 * chans
    pad = rows + 16
    for dr in range(3):
        part = jnp.dot(lhs, w_ref[dr * depth : (dr + 1) * depth], preferred_element_type=F32)
        for g in range(8):
            own = part[g * rows : (g + 1) * rows]
            for t in range(lanes):
                at = 9 - dr
                piece = own[:, t * 128 : (t + 1) * 128]
                if dr == 0:
                    acc[g * lanes + t, 0:8] = jnp.zeros((8, 128), F32)
                    acc[g * lanes + t, 8 + rows : pad] = jnp.zeros((8, 128), F32)
                    acc[g * lanes + t, 8:9] = jnp.zeros((1, 128), F32)
                    acc[g * lanes + t, at : at + rows] = piece
                else:
                    acc[g * lanes + t, at : at + rows] += piece
    for g in range(4):
        for t in range(lanes):
            total = None
            for phase in range(2):
                at = (2 * g + phase) * lanes + t
                v = acc[at, 8 : 8 + rows] + bias[:, t * 128 : (t + 1) * 128]
                acc[at, 8 : 8 + rows] = v * jax.nn.sigmoid(v)
                both = (
                    acc[at, pl.ds(8, rows // 2, stride=2), :]
                    + acc[at, pl.ds(9, rows // 2, stride=2), :]
                )
                total = both if total is None else total + both
            lost = jnp.where(g == 0, where_ref[1], jnp.where(g == 3, where_ref[2], 0))
            keep = jnp.where(lost > 0, 0.0, 0.25)
            edge_ref[g, t] = (total * keep).astype(BF16).astype(F32)


def conv_kernel(
    where_ref, taps, w_ref, b_ref, left_ref, head_ref, tail_ref, right_ref, *refs, block
):
    out_ref, edge_ref, wide, acc = refs[-4:]
    half_cols, chans = taps.shape[1], taps.shape[2] // 4
    out_rows = out_ref.shape[0]
    bias = b_ref[...]

    def step(k, carry):
        r0 = k * 2 * block
        total = None
        for phase in range(2):
            lhs = jnp.concatenate(
                [
                    taps[pl.ds(r0 + dr, 2 * block), :, phase * chans : (phase + 3) * chans]
                    for dr in range(3)
                ],
                axis=-1,
            ).reshape(2 * block * half_cols, 9 * chans)
            v = jnp.dot(lhs, w_ref[...], preferred_element_type=F32) + bias
            h = (v * jax.nn.sigmoid(v)).reshape(block, 2, half_cols, chans)
            h = h[:, 0] + h[:, 1]
            total = h if total is None else total + h
        out_ref[pl.ds(k * block, block)] = (total * 0.25).astype(BF16)
        return carry

    lax.fori_loop(0, out_rows // block, step, 0)
    pairs = ((left_ref, head_ref), (tail_ref, right_ref))
    edge_part(where_ref, pairs, w_ref, bias, edge_ref, wide, acc)


def conv_pool(where, taps, w, b, left, head, tail, right, after):
    total, half_cols, width = taps.shape
    chans, rows = width // 4, head.shape[0]
    out_rows, lanes = (total - 2) // 2, chans // 128
    block = next(k for k in (6, 4, 3, 2, 1) if out_rows % k == 0)
    return pl.pallas_call(
        functools.partial(conv_kernel, block=block),
        out_shape=(
            jax.ShapeDtypeStruct((out_rows, half_cols, chans), BF16),
            jax.ShapeDtypeStruct((4, lanes, rows // 2, 128), F32),
        ),
        in_specs=[SMEM] + [VMEM] * 7 + [ANY] * len(after),
        out_specs=(VMEM, VMEM),
        scratch_shapes=[
            pltpu.VMEM((2 * lanes, 8 * rows, 128), F32),
            pltpu.VMEM((8 * lanes, rows + 16, 128), F32),
        ],
        compiler_params=params(24),
        cost_estimate=pl.CostEstimate(
            flops=8 * out_rows * half_cols * 9 * chans * chans,
            bytes_accessed=8 << 20,
            transcendentals=0,
        ),
        name="conv_pool",
    )(where, taps, w, b, left, head, tail, right, *after)


def side_kernel(grad_ref, slots_ref, labels_ref, out_ref):
    owned, width = grad_ref.shape
    entries = slots_ref.shape[1]
    out_ref[:owned] = grad_ref[...]
    lane = lax.broadcasted_iota(jnp.int32, (1, width), 1)
    labels = labels_ref[...]
    counts = jnp.zeros((1, width), F32)
    for e in range(entries):
        hit = jnp.where(labels == e, 1.0, 0.0)
        hit = jnp.sum(jnp.sum(hit, axis=0, keepdims=True), axis=1, keepdims=True)
        counts = jnp.where(lane == e, hit, counts)
    ids = jnp.concatenate(
        [slots_ref[...].astype(F32), jnp.zeros((1, width - entries), F32)], axis=1
    )
    row = lax.broadcasted_iota(jnp.int32, (SIDE, width), 0)
    out_ref[owned:] = jnp.where(row == 0, ids, jnp.where(row == 1, counts, 0.0))


def pack_side(grad, slots, labels):
    owned, width = grad.shape
    return pl.pallas_call(
        side_kernel,
        out_shape=jax.ShapeDtypeStruct((owned + SIDE, width), F32),
        in_specs=[VMEM] * 3,
        out_specs=VMEM,
        compiler_params=params(),
        name="pack_side",
    )(grad, slots.reshape(1, -1), labels)


def join_kernel(*refs):
    at = 0
    for ref in refs[:-1]:
        refs[-1][at : at + ref.shape[0]] = ref[...]
        at += ref.shape[0]


def join(parts):
    shape = (sum(p.shape[0] for p in parts),) + parts[0].shape[1:]
    return pl.pallas_call(
        join_kernel,
        out_shape=jax.ShapeDtypeStruct(shape, F32),
        in_specs=[VMEM] * len(parts),
        out_specs=VMEM,
        compiler_params=params(),
        name="join",
    )(*parts)


def scale_rows(block, note_rows, sums):
    def exponent(values):
        top = None
        for v in values:
            one = jnp.max(jnp.max(jnp.abs(v), axis=0, keepdims=True), axis=1, keepdims=True)
            top = one if top is None else jnp.maximum(top, one)
        return jnp.ceil(jnp.log2(jnp.maximum(top, 1e-30)))

    power = exponent([block, note_rows])
    power_sums = exponent([sums])
    return power, power_sums


def note_block(bias, power, power_sums, width):
    row = lax.broadcasted_iota(jnp.int32, (NOTE, width), 0)
    bias = jnp.broadcast_to(bias, (NOTE, width))
    power = jnp.broadcast_to(power, (NOTE, width))
    power_sums = jnp.broadcast_to(power_sums, (NOTE, width))
    return jnp.where(row == 0, bias, jnp.where(row == 1, power, power_sums))


def read_note(part, at):
    note = part[at : at + NOTE]
    down = jnp.exp2(note[1:2] - 12.0)
    return note[0:1] * down, down, jnp.exp2(note[2:3] - 12.0)


def deep_kernel(where_ref, edge_ref, w_ref, b_ref, lab_ref, *refs, block, n_maps, entries):
    map_refs = refs[: 2 * n_maps]
    taps, member, slope, sums_ref, wide = refs[2 * n_maps :]
    part, cols, chans = map_refs[0].shape
    rows = 2 * n_maps * part
    lanes = chans // 128
    width = w_ref.shape[-1]
    half = where_ref[0]
    taps[0] = jnp.zeros(taps.shape[1:], BF16)
    taps[rows + 1] = jnp.zeros(taps.shape[1:], BF16)

    def prepare(ref, base, i, slot):
        x = ref[i].astype(F32)
        r = base + i
        for t in range(lanes):
            s = slot * lanes + t
            at = t * 128
            wide[s, 8 : 8 + cols] = x[:, at : at + 128]
            for g, place in enumerate((7, 8, 7 + cols, 8 + cols)):
                wide[s, place : place + 1] = edge_ref[g, t, pl.ds(r, 1), :]
        for tap in range(3):
            for t in range(lanes):
                piece = wide[slot * lanes + t, 7 + tap : 7 + tap + cols, :]
                at = (tap * lanes + t) * 128
                taps[r + 1, :, at : at + 128] = piece.astype(BF16)

    def prepare_rows(k, carry):
        for q in range(n_maps):
            prepare(map_refs[q], (half * n_maps + q) * part, k, 2 * q)
            prepare(map_refs[n_maps + q], ((1 - half) * n_maps + q) * part, k, 2 * q + 1)
        return carry

    lax.fori_loop(0, part, prepare_rows, 0)
    lab = jnp.transpose(lab_ref[...].astype(F32))
    lane = lax.broadcasted_iota(jnp.int32, (cols, 128), 1)
    want = jnp.where(lane < 3 * entries, lane % entries, -1).astype(F32)
    for r in range(rows):
        member[r] = (lab[:, r : r + 1] == want).astype(BF16)
    bias = b_ref[...]
    size = block * cols

    def step(k, sums):
        r0 = k * block
        lhs = jnp.concatenate([taps[pl.ds(r0 + dr, block)] for dr in range(3)], axis=-1)
        v = jnp.dot(lhs.reshape(size, 9 * chans), w_ref[...], preferred_element_type=F32) + bias
        sig = jax.nn.sigmoid(v)
        features = (v * sig).astype(BF16)
        slope[pl.ds(k * size, size)] = sig * (1.0 + v * (1.0 - sig))
        mem = member[pl.ds(r0, block)].reshape(size, 128)
        return sums + lax.dot_general(
            mem, features, (((0,), (0,)), ((), ())), preferred_element_type=F32
        )[:entries]

    sums_ref[...] = lax.fori_loop(0, rows // block, step, jnp.zeros((entries, width), F32))


def deep_forward(where, own, other, edges, w, b, labels, entries):
    part, cols, chans = own[0].shape
    rows, width = 2 * len(own) * part, w.shape[-1]
    block = next(k for k in (8, 4, 2, 1) if rows % k == 0)
    return pl.pallas_call(
        functools.partial(deep_kernel, block=block, n_maps=len(own), entries=entries),
        out_shape=(
            jax.ShapeDtypeStruct((rows + 2, cols, 3 * chans), BF16),
            jax.ShapeDtypeStruct((rows, cols, 128), BF16),
            jax.ShapeDtypeStruct((rows * cols, width), F32),
            jax.ShapeDtypeStruct((entries, width), F32),
        ),
        in_specs=[SMEM] + [VMEM] * (4 + 2 * len(own)),
        out_specs=(VMEM,) * 4,
        scratch_shapes=[pltpu.VMEM((2 * len(own) * (chans // 128), cols + 16, 128), F32)],
        compiler_params=params(16),
        cost_estimate=pl.CostEstimate(
            flops=4 * rows * cols * 9 * chans * width, bytes_accessed=8 << 20, transcendentals=0
        ),
        name="deep_forward",
    )(where, edges, w, b, labels, *own, *other)


def grad_kernel(
    where_ref, taps, member, slope, sums_ref, slots_ref, *refs, n_parts, chunk, ways, with_sums
):
    part_refs = refs[:n_parts]
    out_refs = refs[n_parts : n_parts + ways]
    grad, weight = refs[n_parts + ways :]
    rows, cols, depth = member.shape[0], taps.shape[1], taps.shape[2]
    width = slope.shape[-1]
    me = where_ref[3]
    entries = slots_ref.shape[0]
    owned = part_refs[0].shape[1] - SIDE
    ids = slots_ref[...]
    total = jnp.zeros((entries, 1), F32)
    entry_grad = jnp.zeros((entries, width), F32)
    owner, inner = ids // owned, ids % owned
    spot = lax.broadcasted_iota(jnp.int32, (entries, owned), 1)
    for m, ref, k in relative(part_refs):
        there = ref[k, owned : owned + 1, :entries] == ids.astype(F32)
        counts = ref[k, owned + 1 : owned + 2, :entries]
        total += jnp.sum(jnp.where(there, counts, 0.0), axis=1, keepdims=True)
        hot = ((owner ^ me) == m) & (inner == spot)
        entry_grad += jnp.dot(
            hot.astype(F32), ref[k, :owned], precision=lax.Precision.HIGHEST, preferred_element_type=F32
        )
    entry_grad = entry_grad / jnp.maximum(total, 1.0)
    high = entry_grad.astype(BF16)
    rest = entry_grad - high.astype(F32)
    mid = rest.astype(BF16)
    low = (rest - mid.astype(F32)).astype(BF16)
    terms = jnp.concatenate([high, mid, low, jnp.zeros((128 - 3 * entries, width), BF16)], axis=0)
    pixel = jnp.dot(member[...].reshape(rows * cols, 128), terms, preferred_element_type=F32)
    dg = (pixel * slope[...]).astype(BF16)
    grad[...] = dg
    bias_sum = jnp.sum(dg.astype(F32), axis=0, keepdims=True)
    for dr in range(3):
        window = taps[dr : dr + rows].reshape(rows * cols, depth)
        out = lax.dot_general(grad[...], window, (((0,), (0,)), ((), ())), preferred_element_type=F32)
        weight[dr * depth : (dr + 1) * depth] = jnp.transpose(out)
    if weight.shape[0] > 3 * depth:
        weight[3 * depth :] = jnp.zeros((weight.shape[0] - 3 * depth, width), F32)
    sums = sums_ref[...]
    power, power_sums = scale_rows(weight[...], bias_sum, sums)
    up = jnp.exp2(12.0 - power)
    note = note_block(bias_sum * up, power, power_sums, width)
    digit = lax.rem(me, ways)
    heads = weight.shape[0] // chunk // ways
    for m in range(ways):
        for hi in range(heads):
            j = hi * ways + (digit ^ m)
            out_refs[m][hi * chunk : (hi + 1) * chunk] = (
                weight[pl.ds(pl.multiple_of(j * chunk, 8), chunk)] * up
            )
        out_refs[m][heads * chunk : heads * chunk + NOTE] = note
    out_refs[with_sums][heads * chunk + NOTE :] = sums * jnp.exp2(12.0 - power_sums)


def deep_backward(where, forward, slots, parts, chunk, count, ways, with_sums):
    taps, _, slope, sums = forward
    width, entries = slope.shape[-1], sums.shape[0]
    size = count // ways * chunk + NOTE
    return pl.pallas_call(
        functools.partial(
            grad_kernel, n_parts=len(parts), chunk=chunk, ways=ways, with_sums=with_sums
        ),
        out_shape=tuple(
            jax.ShapeDtypeStruct((size + (entries if m == with_sums else 0), width), F32)
            for m in range(ways)
        ),
        in_specs=[SMEM] + [VMEM] * (5 + len(parts)),
        out_specs=(VMEM,) * ways,
        scratch_shapes=[
            pltpu.VMEM(slope.shape, BF16),
            pltpu.VMEM((count * chunk, width), F32),
        ],
        compiler_params=params(16),
        cost_estimate=pl.CostEstimate(
            flops=4 * slope.shape[0] * 3 * taps.shape[2] * width, bytes_accessed=8 << 20, transcendentals=0
        ),
        name="deep_backward",
    )(where, *forward, slots, *parts)


def pair_kernel(own_ref, got_ref, own_sums_ref, got_sums_ref, *refs, size, entries):
    out_ref = refs[-1]
    own, got = own_ref[size : size + NOTE], got_ref[size : size + NOTE]
    power = jnp.maximum(own[1:2], got[1:2]) + 1.0
    power_sums = jnp.maximum(own[2:3], got[2:3])
    own_down, got_down = jnp.exp2(own[1:2] - power), jnp.exp2(got[1:2] - power)
    out_ref[:size] = own_ref[:size] * own_down + got_ref[:size] * got_down
    bias = own[0:1] * own_down + got[0:1] * got_down
    out_ref[size : size + NOTE] = note_block(bias, power, power_sums, own.shape[-1])
    at = size + NOTE
    sums = own_sums_ref[at : at + entries] * jnp.exp2(own[2:3] - power_sums)
    out_ref[at : at + entries] = sums
    sums = got_sums_ref[at : at + entries] * jnp.exp2(got[2:3] - power_sums)
    out_ref[at + entries : at + 2 * entries] = sums


def merge_pair(own, got, own_sums, got_sums, size, entries, after):
    width = own.shape[-1]
    return pl.pallas_call(
        functools.partial(pair_kernel, size=size, entries=entries),
        out_shape=jax.ShapeDtypeStruct((size + NOTE + 2 * entries, width), F32),
        in_specs=[VMEM] * 4 + [ANY] * len(after),
        out_specs=VMEM,
        compiler_params=params(),
        name="merge_pair",
    )(own, got, own_sums, got_sums, *after)


def merge_kernel(where_ref, *refs, chunk, heads, held, entries, shift, next_ways):
    n_parts = len(refs) - next_ways - 1
    part_refs, out_refs, sums_ref = refs[:n_parts], refs[n_parts:-1], refs[-1]
    width = part_refs[0].shape[-1]
    size = heads * chunk
    total, bias = jnp.zeros((size, width), F32), jnp.zeros((1, width), F32)
    sums_rows = held * entries
    for m, ref in enumerate(part_refs):
        more, down, down_sums = read_note(ref, size)
        total, bias = total + ref[:size] * down, bias + more
        sums_ref[m * sums_rows : (m + 1) * sums_rows] = ref[size + NOTE :] * down_sums
    sums = sums_ref[...]
    power, power_sums = scale_rows(total, bias, sums)
    up = jnp.exp2(12.0 - power)
    note = note_block(bias * up, power, power_sums, width)
    total = total * up
    if next_ways == 1:
        out_refs[0][:size] = total
        out_refs[0][size:] = note
        return
    sums = sums * jnp.exp2(12.0 - power_sums)
    digit = lax.rem(where_ref[3] >> shift, next_ways)
    for m in range(next_ways):
        for hi in range(heads // next_ways):
            piece = jnp.zeros((chunk, width), F32)
            for d in range(next_ways):
                at = (hi * next_ways + d) * chunk
                piece = jnp.where((digit ^ m) == d, total[at : at + chunk], piece)
            out_refs[m][hi * chunk : (hi + 1) * chunk] = piece
        at = heads // next_ways * chunk
        out_refs[m][at : at + NOTE] = note
        out_refs[m][at + NOTE :] = sums


def merge(where, parts, chunk, heads, held, entries, shift, next_ways):
    width = parts[0].shape[-1]
    sums_rows = len(parts) * held * entries
    if next_ways == 1:
        outs = (jax.ShapeDtypeStruct((heads * chunk + NOTE, width), F32),)
    else:
        rows = heads // next_ways * chunk + NOTE + sums_rows
        outs = (jax.ShapeDtypeStruct((rows, width), F32),) * next_ways
    outs = outs + (jax.ShapeDtypeStruct((sums_rows, width), F32),)
    out = pl.pallas_call(
        functools.partial(
            merge_kernel, chunk=chunk, heads=heads, held=held, entries=entries, shift=shift, next_ways=next_ways
        ),
        out_shape=outs,
        in_specs=[SMEM] + [VMEM] * len(parts),
        out_specs=(VMEM,) * len(outs),
        compiler_params=params(),
        name="merge",
    )(where, *parts)
    return out[:-1], out[-1]


def embed_kernel(where_ref, sums_ref, *refs, entries):
    part_refs, out_ref = refs[:-1], refs[-1]
    owned, width = out_ref.shape
    own = (where_ref[3] * owned + lax.broadcasted_iota(jnp.int32, (owned, entries), 0)).astype(F32)
    sums, counts = jnp.zeros((owned, width), F32), jnp.zeros((owned, 1), F32)
    for m, ref, k in relative(part_refs):
        there = ref[k, owned : owned + 1, :entries] == own
        count = ref[k, owned + 1 : owned + 2, :entries]
        counts += jnp.sum(jnp.where(there, count, 0.0), axis=1, keepdims=True)
        sums += jnp.dot(
            there.astype(F32),
            sums_ref[m * entries : (m + 1) * entries],
            precision=lax.Precision.HIGHEST,
            preferred_element_type=F32,
        )
    out_ref[...] = sums / jnp.maximum(counts, 1.0)


def spread_kernel(where_ref, *refs, chunk, rows):
    part_refs, weight_ref, bias_ref, place = refs[:-3], refs[-3], refs[-2], refs[-1]
    me = where_ref[3]
    for m, ref, k in relative(part_refs):
        bias, down, _ = read_note(ref[k], chunk)
        j = me ^ m
        place[pl.ds(pl.multiple_of(j * chunk, 8), chunk)] = ref[k, :chunk] * down

        @pl.when(j == 0)
        def _():
            bias_ref[...] = bias

    weight_ref[...] = place[:rows]


def spread(where, parts, chunk, count, rows):
    width = parts[0].shape[-1]
    return pl.pallas_call(
        functools.partial(spread_kernel, chunk=chunk, rows=rows),
        out_shape=(jax.ShapeDtypeStruct((rows, width), F32), jax.ShapeDtypeStruct((1, width), F32)),
        in_specs=[SMEM] + [VMEM] * len(parts),
        out_specs=(VMEM, VMEM),
        scratch_shapes=[pltpu.VMEM((count * chunk, width), F32)],
        compiler_params=params(),
        name="spread",
    )(where, *parts)


def body(
    section_input, conv_weight, conv_bias, deep_weight, deep_bias, labels, slot_ids, embed_grad
):
    chan_count = lax.axis_size("chan")
    strip_count = lax.axis_size("strip")
    chan_pos = lax.axis_index("chan")
    strip_pos = lax.axis_index("strip")
    half = chan_pos & 1
    channels = section_input.shape[-1]
    entries = slot_ids.shape[0]
    owned, width = embed_grad.shape
    where = jnp.stack(
        [half, (strip_pos == 0).astype(jnp.int32), (strip_pos == strip_count - 1).astype(jnp.int32), strip_pos]
    ).astype(jnp.int32)
    conv_w = conv_weight.reshape(9 * channels, -1)
    conv_b = conv_bias.reshape(1, -1)

    head, tail = section_input[:, :3], section_input[:, -3:]
    pairs = []
    for s in range(strip_count):
        for c in range(chan_count):
            to = s + 1 - 2 * (c & 1)
            if 0 <= to < strip_count:
                pairs.append((s * chan_count + c, to * chan_count + c))
    got = lax.ppermute(jnp.where(half == 0, tail, head), ("strip", "chan"), pairs)
    traded = swap(got, "chan", 1)
    left = jnp.where(half == 0, got, traded)
    right = jnp.where(half == 0, traded, got)

    shared = gather_groups(
        pack_side(embed_grad, slot_ids, labels)[None], "strip", high_groups(strip_count)
    )

    taps = windows(where, section_input)
    joined = join(shared)
    shared = [joined, swap(joined, "strip", 1)]
    pooled, edges = conv_pool(where, taps, conv_w, conv_b, left, head, tail, right, [joined])
    other = swap(pooled, "chan", 1)

    chunk = -(-9 * channels // strip_count // 8) * 8
    bits = min(2, strip_count.bit_length() - 2)
    pieces = 1 << bits
    order = list(range(pieces // 2, pieces)) + list(range(pieces // 2))[::-1]
    with_sums = 2 * order[0] + 1
    forward = deep_forward(
        where,
        [pooled],
        [other],
        edges,
        deep_weight.reshape(9 * channels, width),
        deep_bias.reshape(1, width),
        labels,
        entries,
    )
    send = deep_backward(
        where, forward, slot_ids.reshape(entries, 1), shared, chunk, strip_count, 2 * pieces, with_sums
    )
    heads, held = strip_count // (2 * pieces), 2
    got = {k: swap(send[2 * k + 1].astype(F16), "strip", 1).astype(F32) for k in order}
    pair, parts, before = {}, {}, []
    for k in order:
        pair[k] = merge_pair(
            send[2 * k], got[k], send[with_sums], got[order[0]], heads * chunk, entries, before
        )
        parts[k] = swap(pair[k].astype(F16), "strip", 2 * k).astype(F32) if k else pair[k]
        before = [pair[k]] if k < pieces // 2 or k + 1 < pieces else [pair[k], parts[order[0]]]
    parts = [parts[k] for k in range(pieces)]
    held *= pieces
    send, sums = parts, None
    shift = bits + 1
    while True:
        left_bits = strip_count.bit_length() - 1 - shift
        size = min(3, left_bits)
        send, sums = merge(
            where, parts, chunk, heads, held // len(parts), entries, shift, 1 << size
        )
        if size == 0:
            break
        ways = 1 << size
        heads //= ways
        parts = [send[0]] + [
            swap(send[m].astype(F16), "strip", m << shift).astype(F32) for m in range(1, ways)
        ]
        held *= ways
        shift += size
    embeddings = pl.pallas_call(
        functools.partial(embed_kernel, entries=entries),
        out_shape=jax.ShapeDtypeStruct((owned, width), F32),
        in_specs=[SMEM] + [VMEM] * (1 + len(shared)),
        out_specs=VMEM,
        compiler_params=params(),
        name="embed",
    )(where, sums, *shared)
    gathered = gather_groups(send[0].astype(F16)[None], "strip", high_groups(strip_count))
    gathered = gathered + [swap(g, "strip", 1) for g in gathered]
    weight_rows, bias_row = spread(
        where, [g.astype(F32) for g in gathered], chunk, strip_count, 9 * channels
    )
    return (embeddings, weight_rows.reshape(3, 3, channels, width), bias_row[0])


def solution(mesh):
    placed = (
        P(None, "strip", None),
        P(),
        P(),
        P(None, None, None, "chan"),
        P("chan"),
        P(None, "strip"),
        P("strip"),
        P("strip", "chan"),
    )
    return jax.shard_map(
        body,
        mesh=mesh,
        in_specs=placed,
        out_specs=(P("strip", "chan"), P(None, None, None, "chan"), P("chan")),
        check_vma=False,
    )
```

```python
import functools
import math

import jax
import jax.numpy as jnp
from jax import lax
from jax.experimental import pallas as pl
from jax.experimental.pallas import tpu as pltpu
from jax.sharding import PartitionSpec as P

F32, BF16, F16 = jnp.float32, jnp.bfloat16, jnp.float16
VMEM = pl.BlockSpec(memory_space=pltpu.VMEM)
SMEM = pl.BlockSpec(memory_space=pltpu.SMEM)
HBM = pl.BlockSpec(memory_space=pltpu.HBM)
ANY = pl.BlockSpec(memory_space=pl.ANY)
SIDE = 8
WIDTH = 3
PIECE = 4
STEP = 4
NOTE = 16


def params(mib=8):
    return pltpu.CompilerParams(vmem_limit_bytes=mib << 20)


def swap(value, axis, mask):
    count = lax.axis_size(axis)
    return lax.ppermute(value, axis, [(i, i ^ mask) for i in range(count)])


def bit_groups(count, first, most):
    bits = count.bit_length() - 1
    groups, at = [], 0
    while at < bits:
        size = min(first if at == 0 else most, bits - at)
        groups.append((at, size))
        at += size
    return groups


def gather_groups(value, axis, groups):
    parts = [value]
    for shift, size in groups:
        held = parts[0] if len(parts) == 1 else jnp.concatenate(parts, axis=0)
        parts = [held] + [swap(held, axis, m << shift) for m in range(1, 1 << size)]
    return parts


def relative(refs):
    half = len(refs) // 2
    for low in range(2):
        m = low
        for ref in refs[low * half : (low + 1) * half]:
            for k in range(ref.shape[0]):
                yield m, ref, k
                m += 2


def high_groups(count):
    return [(at + 1, size) for at, size in bit_groups(count // 2, 2, 2)]


def shares(pooled_rows):
    first = pooled_rows * 2 // 3 // STEP * STEP
    return first, pooled_rows - first


def pick(half, pair):
    return jnp.where(half == 0, pair[0], pair[1])


def window_kernel(where_ref, x_hbm, w_hbm, taps, w_ref, rows_ref, wide, sems):
    rows, cols, chans = x_hbm.shape
    half_cols = cols // 2
    half = where_ref[0]
    first, second = shares(rows // 2)
    counts = [-(-(2 * n + 1) // PIECE) for n in (first, second)]
    pieces = pick(half, counts)
    start = pick(half, (0, rows - counts[1] * PIECE))
    shift = pick(half, (PIECE + 1, PIECE - (2 * first - 1 - (rows - counts[1] * PIECE))))

    def piece(k):
        at = pl.ds(k * PIECE, PIECE)
        return pltpu.make_async_copy(
            x_hbm.at[pl.ds(start + k * PIECE, PIECE)], rows_ref.at[at], sems.at[k]
        )

    def begin(k, carry):
        piece(k).start()
        return carry

    lax.fori_loop(0, pieces, begin, 0)
    weights = pltpu.make_async_copy(w_hbm, w_ref, sems.at[sems.shape[0] - 1])
    weights.start()
    lanes = chans // 128
    border = jnp.zeros((8, 128), F32)
    for t in range(wide.shape[0]):
        wide[t, 0:8] = border
        wide[t, cols + 8 : cols + 16] = border

    def prepare(k, carry):
        piece(k).wait()
        for slot in range(PIECE):
            r = k * PIECE + slot
            x = rows_ref[r].astype(F32)
            for t in range(lanes):
                wide[slot * lanes + t, 8 : 8 + cols] = x[:, t * 128 : (t + 1) * 128]
            for tap in range(4):
                for t in range(lanes):
                    part = wide[slot * lanes + t, pl.ds(7 + tap, half_cols, stride=2), :]
                    at = (tap * lanes + t) * 128
                    taps[r + shift, :, at : at + 128] = part.astype(BF16)
        return carry

    lax.fori_loop(0, pieces, prepare, 0)
    outside = pick(half, (PIECE, PIECE + 2 * second + 1))
    taps[outside] = jnp.zeros(taps.shape[1:], BF16)
    weights.wait()


def windows(where, x, w):
    rows, cols, chans = x.shape
    first, _ = shares(rows // 2)
    most = -(-(2 * first + 1) // PIECE)
    return pl.pallas_call(
        window_kernel,
        out_shape=(
            jax.ShapeDtypeStruct(((most + 2) * PIECE, cols // 2, 4 * chans), BF16),
            jax.ShapeDtypeStruct(w.shape, BF16),
        ),
        in_specs=[SMEM, HBM, HBM],
        out_specs=(VMEM, VMEM),
        scratch_shapes=[
            pltpu.VMEM((most * PIECE, cols, chans), BF16),
            pltpu.VMEM((PIECE * (chans // 128), cols + 16, 128), F32),
            pltpu.SemaphoreType.DMA((most + 1,)),
        ],
        compiler_params=params(16),
        cost_estimate=pl.CostEstimate(flops=0, bytes_accessed=12 << 20, transcendentals=0),
        name="windows",
    )(where, *(pltpu.with_memory_space_constraint(a, pltpu.HBM) for a in (x, w)))


def edge_part(where_ref, pairs, w_ref, bias, edge_ref, acc):
    rows = pairs[0].shape[0]
    chans = w_ref.shape[1]
    lanes = chans // 128
    depth = 3 * chans
    lhs = jnp.concatenate(
        [
            pairs[s][:, (2 * j + phase) * chans : (2 * j + phase + 3) * chans]
            for s in range(2)
            for j in range(2)
            for phase in range(2)
        ],
        axis=0,
    )
    pad = rows + 16
    for dr in range(3):
        part = jnp.dot(lhs, w_ref[dr * depth : (dr + 1) * depth], preferred_element_type=F32)
        for g in range(8):
            own = part[g * rows : (g + 1) * rows]
            for t in range(lanes):
                at = 9 - dr
                piece = own[:, t * 128 : (t + 1) * 128]
                if dr == 0:
                    acc[g * lanes + t, 0:8] = jnp.zeros((8, 128), F32)
                    acc[g * lanes + t, 8 + rows : pad] = jnp.zeros((8, 128), F32)
                    acc[g * lanes + t, 8:9] = jnp.zeros((1, 128), F32)
                    acc[g * lanes + t, at : at + rows] = piece
                else:
                    acc[g * lanes + t, at : at + rows] += piece
    for g in range(4):
        for t in range(lanes):
            total = None
            for phase in range(2):
                at = (2 * g + phase) * lanes + t
                v = acc[at, 8 : 8 + rows] + bias[:, t * 128 : (t + 1) * 128]
                acc[at, 8 : 8 + rows] = v * jax.nn.sigmoid(v)
                both = (
                    acc[at, pl.ds(8, rows // 2, stride=2), :]
                    + acc[at, pl.ds(9, rows // 2, stride=2), :]
                )
                total = both if total is None else total + both
            lost = jnp.where(g == 0, where_ref[1], jnp.where(g == 3, where_ref[2], 0))
            keep = jnp.where(lost > 0, 0.0, 0.25)
            edge_ref[g, t] = (total * keep).astype(BF16).astype(F32)


def conv_kernel(where_ref, taps, w_ref, b_ref, got_ref, traded_ref, head_ref, tail_ref, *refs):
    out_ref, edge_ref, acc = refs[-3:]
    half_cols, chans = taps.shape[1], taps.shape[2] // 4
    half = where_ref[0]
    first, second = shares(head_ref.shape[0] // 2)
    bias = b_ref[...]

    def step(k, carry):
        r0 = PIECE + k * 2 * STEP
        total = None
        for phase in range(2):
            lhs = jnp.concatenate(
                [
                    taps[pl.ds(r0 + dr, 2 * STEP), :, phase * chans : (phase + 3) * chans]
                    for dr in range(3)
                ],
                axis=-1,
            ).reshape(2 * STEP * half_cols, 9 * chans)
            v = jnp.dot(lhs, w_ref[...], preferred_element_type=F32) + bias
            h = (v * jax.nn.sigmoid(v)).reshape(STEP, 2, half_cols, chans)
            h = h[:, 0] + h[:, 1]
            total = h if total is None else total + h
        out_ref[pl.ds(k * STEP, STEP)] = (total * 0.25).astype(BF16)
        return carry

    lax.fori_loop(0, pick(half, (first // STEP, second // STEP)), step, 0)
    got, traded = got_ref[...], traded_ref[...]
    left = jnp.concatenate([jnp.where(half == 0, got, traded), head_ref[...]], axis=-1)
    right = jnp.concatenate([tail_ref[...], jnp.where(half == 0, traded, got)], axis=-1)
    edge_part(where_ref, (left, right), w_ref, bias, edge_ref, acc)


def conv_pool(where, taps, w, b, got, traded, head, tail, after):
    _, half_cols, width = taps.shape
    chans, rows = width // 4, head.shape[0]
    first, lanes = shares(rows // 2)[0], chans // 128
    return pl.pallas_call(
        conv_kernel,
        out_shape=(
            jax.ShapeDtypeStruct((first, half_cols, chans), BF16),
            jax.ShapeDtypeStruct((4, lanes, rows // 2, 128), F32),
        ),
        in_specs=[SMEM] + [VMEM] * 7 + [ANY] * len(after),
        out_specs=(VMEM, VMEM),
        scratch_shapes=[pltpu.VMEM((8 * lanes, rows + 16, 128), F32)],
        compiler_params=params(24),
        cost_estimate=pl.CostEstimate(
            flops=8 * first * half_cols * 9 * chans * chans,
            bytes_accessed=8 << 20,
            transcendentals=0,
        ),
        name="conv_pool",
    )(where, taps, w, b, got, traded, head, tail, *after)


def start_kernel(
    where_ref, x_hbm, grad_hbm, labels_hbm, slots_hbm, side_ref, head_ref, tail_ref, send_ref,
    labels_ref, slots_ref, left, right, wide, sems,
):
    owned, width = grad_hbm.shape
    rows, cols, chans = x_hbm.shape
    entries = slots_ref.shape[1]
    reach = left.shape[1]
    half = where_ref[0]
    copies = [
        pltpu.make_async_copy(labels_hbm, labels_ref, sems.at[0]),
        pltpu.make_async_copy(grad_hbm, side_ref.at[0, pl.ds(0, owned)], sems.at[1]),
        pltpu.make_async_copy(x_hbm.at[:, pl.ds(0, reach)], left, sems.at[2]),
        pltpu.make_async_copy(x_hbm.at[:, pl.ds(cols - reach, reach)], right, sems.at[3]),
        pltpu.make_async_copy(slots_hbm, slots_ref, sems.at[4]),
    ]
    for copy in copies:
        copy.start()
    lane = lax.broadcasted_iota(jnp.int32, (1, width), 1)
    copies[0].wait()
    copies[4].wait()
    ids = jnp.concatenate(
        [slots_ref[...].astype(F32), jnp.zeros((1, width - entries), F32)], axis=1
    )
    labels = labels_ref[...]
    counts = jnp.zeros((1, width), F32)
    for e in range(entries):
        hit = jnp.where(labels == e, 1.0, 0.0)
        hit = jnp.sum(jnp.sum(hit, axis=0, keepdims=True), axis=1, keepdims=True)
        counts = jnp.where(lane == e, hit, counts)
    row = lax.broadcasted_iota(jnp.int32, (SIDE, width), 0)
    side_ref[0, owned:] = jnp.where(row == 0, ids, jnp.where(row == 1, counts, 0.0))
    lanes = chans // 128
    copies[2].wait()
    copies[3].wait()
    for ref, out_ref, at, sent in ((left, head_ref, 0, 1), (right, tail_ref, reach - WIDTH, 0)):
        x = ref[...].astype(F32).reshape(rows * reach, chans)
        for t in range(lanes):
            wide[t] = x[:, t * 128 : (t + 1) * 128]
        for c in range(WIDTH):
            for t in range(lanes):
                part = wide[t, pl.ds(at + c, rows, stride=reach), :].astype(BF16)
                place = (c * lanes + t) * 128
                out_ref[:, place : place + 128] = part
    send_ref[...] = jnp.where(half == 0, tail_ref[...], head_ref[...])
    copies[1].wait()


def start(where, x, grad, slots, labels):
    owned, width = grad.shape
    rows, _, chans = x.shape
    reach = 16
    columns = jax.ShapeDtypeStruct((rows, WIDTH * chans), BF16)
    fixed = [
        pltpu.with_memory_space_constraint(a, pltpu.HBM)
        for a in (x, grad, labels, slots.reshape(1, -1))
    ]
    return pl.pallas_call(
        start_kernel,
        out_shape=(jax.ShapeDtypeStruct((1, owned + SIDE, width), F32),) + (columns,) * 3,
        in_specs=[SMEM, HBM, HBM, HBM, HBM],
        out_specs=(VMEM,) * 4,
        scratch_shapes=[
            pltpu.VMEM(labels.shape, jnp.int32),
            pltpu.VMEM((1, slots.shape[0]), jnp.int32),
            pltpu.VMEM((rows, reach, chans), BF16),
            pltpu.VMEM((rows, reach, chans), BF16),
            pltpu.VMEM((chans // 128, rows * reach, 128), F32),
            pltpu.SemaphoreType.DMA((5,)),
        ],
        compiler_params=params(),
        name="start",
    )(where, *fixed)


def join_kernel(*refs, count):
    at = 0
    for ref in refs[:count]:
        refs[-1][at : at + ref.shape[0]] = ref[...]
        at += ref.shape[0]


def join(parts, after):
    shape = (sum(p.shape[0] for p in parts),) + parts[0].shape[1:]
    return pl.pallas_call(
        functools.partial(join_kernel, count=len(parts)),
        out_shape=jax.ShapeDtypeStruct(shape, F32),
        in_specs=[VMEM] * len(parts) + [ANY] * len(after),
        out_specs=VMEM,
        compiler_params=params(),
        name="join",
    )(*parts, *after)


def scale_rows(block, note_rows, sums):
    def exponent(values):
        top = None
        for v in values:
            one = jnp.max(jnp.max(jnp.abs(v), axis=0, keepdims=True), axis=1, keepdims=True)
            top = one if top is None else jnp.maximum(top, one)
        return jnp.ceil(jnp.log2(jnp.maximum(top, 1e-30)))

    power = exponent([block, note_rows])
    power_sums = exponent([sums])
    return power, power_sums


def note_block(bias, power, power_sums, width):
    row = lax.broadcasted_iota(jnp.int32, (NOTE, width), 0)
    bias = jnp.broadcast_to(bias, (NOTE, width))
    power = jnp.broadcast_to(power, (NOTE, width))
    power_sums = jnp.broadcast_to(power_sums, (NOTE, width))
    return jnp.where(row == 0, bias, jnp.where(row == 1, power, power_sums))


def read_note(part, at):
    note = part[at : at + NOTE]
    down = jnp.exp2(note[1:2] - 12.0)
    return note[0:1] * down, down, jnp.exp2(note[2:3] - 12.0)


def deep_kernel(
    where_ref, own_ref, other_ref, edge_ref, w_ref, b_ref, lab_ref, taps, member, slope, sums_ref, wide,
    *, block, entries
):
    _, cols, chans = own_ref.shape
    rows = lab_ref.shape[0]
    lanes = chans // 128
    width = w_ref.shape[-1]
    half = where_ref[0]
    taps[0] = jnp.zeros(taps.shape[1:], BF16)
    taps[rows + 1] = jnp.zeros(taps.shape[1:], BF16)

    def prepare(ref, base, i, slot):
        x = ref[i].astype(F32)
        r = base + i
        for t in range(lanes):
            s = slot * lanes + t
            at = t * 128
            wide[s, 8 : 8 + cols] = x[:, at : at + 128]
            for g, place in enumerate((7, 8, 7 + cols, 8 + cols)):
                wide[s, place : place + 1] = edge_ref[g, t, pl.ds(r, 1), :]
        for tap in range(3):
            for t in range(lanes):
                piece = wide[slot * lanes + t, 7 + tap : 7 + tap + cols, :]
                at = (tap * lanes + t) * 128
                taps[r + 1, :, at : at + 128] = piece.astype(BF16)

    first, second = shares(rows)
    times = math.gcd(first, second)

    def prepare_all(even_ref, odd_ref):
        def prepare_rows(k, carry):
            for q in range(rows // times):
                ref, base = (even_ref, 0) if q < first // times else (odd_ref, first)
                prepare(ref, base, q * times - base + k, q)
            return carry

        lax.fori_loop(0, times, prepare_rows, 0)

    @pl.when(half == 0)
    def _():
        prepare_all(own_ref, other_ref)

    @pl.when(half != 0)
    def _():
        prepare_all(other_ref, own_ref)

    lab = jnp.transpose(lab_ref[...].astype(F32))
    lane = lax.broadcasted_iota(jnp.int32, (cols, 128), 1)
    want = jnp.where(lane < 3 * entries, lane % entries, -1).astype(F32)
    for r in range(rows):
        member[r] = (lab[:, r : r + 1] == want).astype(BF16)
    bias = b_ref[...]
    size = block * cols

    def step(k, sums):
        r0 = k * block
        lhs = jnp.concatenate([taps[pl.ds(r0 + dr, block)] for dr in range(3)], axis=-1)
        v = jnp.dot(lhs.reshape(size, 9 * chans), w_ref[...], preferred_element_type=F32) + bias
        sig = jax.nn.sigmoid(v)
        features = (v * sig).astype(BF16)
        slope[pl.ds(k * size, size)] = sig * (1.0 + v * (1.0 - sig))
        mem = member[pl.ds(r0, block)].reshape(size, 128)
        return sums + lax.dot_general(
            mem, features, (((0,), (0,)), ((), ())), preferred_element_type=F32
        )[:entries]

    sums_ref[...] = lax.fori_loop(0, rows // block, step, jnp.zeros((entries, width), F32))


def deep_forward(where, own, other, edges, w, b, labels, entries):
    _, cols, chans = own.shape
    rows, width = labels.shape[0], w.shape[-1]
    block = next(k for k in (8, 4, 2, 1) if rows % k == 0)
    first, second = shares(rows)
    slots = rows // math.gcd(first, second)
    return pl.pallas_call(
        functools.partial(deep_kernel, block=block, entries=entries),
        out_shape=(
            jax.ShapeDtypeStruct((rows + 2, cols, 3 * chans), BF16),
            jax.ShapeDtypeStruct((rows, cols, 128), BF16),
            jax.ShapeDtypeStruct((rows * cols, width), F32),
            jax.ShapeDtypeStruct((entries, width), F32),
        ),
        in_specs=[SMEM] + [VMEM] * 6,
        out_specs=(VMEM,) * 4,
        scratch_shapes=[pltpu.VMEM((slots * (chans // 128), cols + 16, 128), F32)],
        compiler_params=params(16),
        cost_estimate=pl.CostEstimate(
            flops=4 * rows * cols * 9 * chans * width, bytes_accessed=8 << 20, transcendentals=0
        ),
        name="deep_forward",
    )(where, own, other, edges, w, b, labels)


def grad_kernel(
    where_ref, taps, member, slope, sums_ref, *refs, n_parts, chunk, ways, with_sums
):
    part_refs = refs[:n_parts]
    out_refs = refs[n_parts : n_parts + ways]
    grad, weight = refs[n_parts + ways :]
    rows, cols, depth = member.shape[0], taps.shape[1], taps.shape[2]
    width = slope.shape[-1]
    me = where_ref[3]
    entries = sums_ref.shape[0]
    owned = part_refs[0].shape[1] - SIDE
    own_ids = jnp.broadcast_to(part_refs[0][0, owned : owned + 1, :entries], (entries, entries))
    across = lax.broadcasted_iota(jnp.int32, (entries, entries), 1)
    down = lax.broadcasted_iota(jnp.int32, (entries, entries), 0)
    ids = jnp.sum(jnp.where(across == down, own_ids, 0.0), axis=1, keepdims=True).astype(jnp.int32)
    total = jnp.zeros((entries, 1), F32)
    entry_grad = jnp.zeros((entries, width), F32)
    owner, inner = ids // owned, ids % owned
    spot = lax.broadcasted_iota(jnp.int32, (entries, owned), 1)
    for m, ref, k in relative(part_refs):
        there = ref[k, owned : owned + 1, :entries] == ids.astype(F32)
        counts = ref[k, owned + 1 : owned + 2, :entries]
        total += jnp.sum(jnp.where(there, counts, 0.0), axis=1, keepdims=True)
        hot = ((owner ^ me) == m) & (inner == spot)
        entry_grad += jnp.dot(
            hot.astype(F32), ref[k, :owned], precision=lax.Precision.HIGHEST, preferred_element_type=F32
        )
    entry_grad = entry_grad / jnp.maximum(total, 1.0)
    high = entry_grad.astype(BF16)
    rest = entry_grad - high.astype(F32)
    mid = rest.astype(BF16)
    low = (rest - mid.astype(F32)).astype(BF16)
    terms = jnp.concatenate([high, mid, low, jnp.zeros((128 - 3 * entries, width), BF16)], axis=0)
    pixel = jnp.dot(member[...].reshape(rows * cols, 128), terms, preferred_element_type=F32)
    dg = (pixel * slope[...]).astype(BF16)
    grad[...] = dg
    bias_sum = jnp.sum(dg.astype(F32), axis=0, keepdims=True)
    for dr in range(3):
        window = taps[dr : dr + rows].reshape(rows * cols, depth)
        out = lax.dot_general(grad[...], window, (((0,), (0,)), ((), ())), preferred_element_type=F32)
        weight[dr * depth : (dr + 1) * depth] = jnp.transpose(out)
    if weight.shape[0] > 3 * depth:
        weight[3 * depth :] = jnp.zeros((weight.shape[0] - 3 * depth, width), F32)
    sums = sums_ref[...]
    power, power_sums = scale_rows(weight[...], bias_sum, sums)
    up = jnp.exp2(12.0 - power)
    note = note_block(bias_sum * up, power, power_sums, width)
    digit = lax.rem(me, ways)
    heads = weight.shape[0] // chunk // ways
    for m in range(ways):
        for hi in range(heads):
            j = hi * ways + (digit ^ m)
            out_refs[m][hi * chunk : (hi + 1) * chunk] = (
                weight[pl.ds(pl.multiple_of(j * chunk, 8), chunk)] * up
            )
        out_refs[m][heads * chunk : heads * chunk + NOTE] = note
    out_refs[with_sums][heads * chunk + NOTE :] = sums * jnp.exp2(12.0 - power_sums)


def deep_backward(where, forward, parts, chunk, count, ways, with_sums):
    taps, _, slope, sums = forward
    width, entries = slope.shape[-1], sums.shape[0]
    size = count // ways * chunk + NOTE
    return pl.pallas_call(
        functools.partial(
            grad_kernel, n_parts=len(parts), chunk=chunk, ways=ways, with_sums=with_sums
        ),
        out_shape=tuple(
            jax.ShapeDtypeStruct((size + (entries if m == with_sums else 0), width), F32)
            for m in range(ways)
        ),
        in_specs=[SMEM] + [VMEM] * (4 + len(parts)),
        out_specs=(VMEM,) * ways,
        scratch_shapes=[
            pltpu.VMEM(slope.shape, BF16),
            pltpu.VMEM((count * chunk, width), F32),
        ],
        compiler_params=params(16),
        cost_estimate=pl.CostEstimate(
            flops=4 * slope.shape[0] * 3 * taps.shape[2] * width, bytes_accessed=8 << 20, transcendentals=0
        ),
        name="deep_backward",
    )(where, *forward, *parts)


def pair_kernel(own_ref, got_ref, own_sums_ref, got_sums_ref, *refs, size, entries):
    out_ref = refs[-1]
    own, got = own_ref[size : size + NOTE], got_ref[size : size + NOTE]
    power = jnp.maximum(own[1:2], got[1:2]) + 1.0
    power_sums = jnp.maximum(own[2:3], got[2:3])
    own_down, got_down = jnp.exp2(own[1:2] - power), jnp.exp2(got[1:2] - power)
    out_ref[:size] = own_ref[:size] * own_down + got_ref[:size] * got_down
    bias = own[0:1] * own_down + got[0:1] * got_down
    out_ref[size : size + NOTE] = note_block(bias, power, power_sums, own.shape[-1])
    at = size + NOTE
    sums = own_sums_ref[at : at + entries] * jnp.exp2(own[2:3] - power_sums)
    out_ref[at : at + entries] = sums
    sums = got_sums_ref[at : at + entries] * jnp.exp2(got[2:3] - power_sums)
    out_ref[at + entries : at + 2 * entries] = sums


def merge_pair(own, got, own_sums, got_sums, size, entries, after):
    width = own.shape[-1]
    return pl.pallas_call(
        functools.partial(pair_kernel, size=size, entries=entries),
        out_shape=jax.ShapeDtypeStruct((size + NOTE + 2 * entries, width), F32),
        in_specs=[VMEM] * 4 + [ANY] * len(after),
        out_specs=VMEM,
        compiler_params=params(),
        name="merge_pair",
    )(own, got, own_sums, got_sums, *after)


def merge_kernel(where_ref, *refs, chunk, heads, held, entries, shift, next_ways):
    n_parts = len(refs) - next_ways - 1
    part_refs, out_refs, sums_ref = refs[:n_parts], refs[n_parts:-1], refs[-1]
    width = part_refs[0].shape[-1]
    size = heads * chunk
    total, bias = jnp.zeros((size, width), F32), jnp.zeros((1, width), F32)
    sums_rows = held * entries
    for m, ref in enumerate(part_refs):
        more, down, down_sums = read_note(ref, size)
        total, bias = total + ref[:size] * down, bias + more
        sums_ref[m * sums_rows : (m + 1) * sums_rows] = ref[size + NOTE :] * down_sums
    sums = sums_ref[...]
    power, power_sums = scale_rows(total, bias, sums)
    up = jnp.exp2(12.0 - power)
    note = note_block(bias * up, power, power_sums, width)
    total = total * up
    if next_ways == 1:
        out_refs[0][:size] = total
        out_refs[0][size:] = note
        return
    sums = sums * jnp.exp2(12.0 - power_sums)
    digit = lax.rem(where_ref[3] >> shift, next_ways)
    for m in range(next_ways):
        for hi in range(heads // next_ways):
            piece = jnp.zeros((chunk, width), F32)
            for d in range(next_ways):
                at = (hi * next_ways + d) * chunk
                piece = jnp.where((digit ^ m) == d, total[at : at + chunk], piece)
            out_refs[m][hi * chunk : (hi + 1) * chunk] = piece
        at = heads // next_ways * chunk
        out_refs[m][at : at + NOTE] = note
        out_refs[m][at + NOTE :] = sums


def merge(where, parts, chunk, heads, held, entries, shift, next_ways):
    width = parts[0].shape[-1]
    sums_rows = len(parts) * held * entries
    if next_ways == 1:
        outs = (jax.ShapeDtypeStruct((heads * chunk + NOTE, width), F32),)
    else:
        rows = heads // next_ways * chunk + NOTE + sums_rows
        outs = (jax.ShapeDtypeStruct((rows, width), F32),) * next_ways
    outs = outs + (jax.ShapeDtypeStruct((sums_rows, width), F32),)
    out = pl.pallas_call(
        functools.partial(
            merge_kernel, chunk=chunk, heads=heads, held=held, entries=entries, shift=shift, next_ways=next_ways
        ),
        out_shape=outs,
        in_specs=[SMEM] + [VMEM] * len(parts),
        out_specs=(VMEM,) * len(outs),
        compiler_params=params(),
        name="merge",
    )(where, *parts)
    return out[:-1], out[-1]


def embed_kernel(where_ref, sums_ref, *refs, entries):
    part_refs, out_ref = refs[:-1], refs[-1]
    owned, width = out_ref.shape
    own = (where_ref[3] * owned + lax.broadcasted_iota(jnp.int32, (owned, entries), 0)).astype(F32)
    sums, counts = jnp.zeros((owned, width), F32), jnp.zeros((owned, 1), F32)
    for m, ref, k in relative(part_refs):
        there = ref[k, owned : owned + 1, :entries] == own
        count = ref[k, owned + 1 : owned + 2, :entries]
        counts += jnp.sum(jnp.where(there, count, 0.0), axis=1, keepdims=True)
        sums += jnp.dot(
            there.astype(F32),
            sums_ref[m * entries : (m + 1) * entries],
            precision=lax.Precision.HIGHEST,
            preferred_element_type=F32,
        )
    out_ref[...] = sums / jnp.maximum(counts, 1.0)


def spread_kernel(where_ref, *refs, chunk, rows):
    part_refs, weight_hbm, bias_ref, place, sems = refs[:-4], refs[-4], refs[-3], refs[-2], refs[-1]
    me = where_ref[3]
    whole = rows == place.shape[0]
    copies = []
    for m, ref, k in relative(part_refs):
        bias, down, _ = read_note(ref[k], chunk)
        j = me ^ m
        at = pl.ds(pl.multiple_of(j * chunk, 8), chunk)
        place[at] = ref[k, :chunk] * down
        if whole:
            copies.append(pltpu.make_async_copy(place.at[at], weight_hbm.at[at], sems.at[m]))
            copies[-1].start()

        @pl.when(j == 0)
        def _():
            bias_ref[...] = bias

    if not whole:
        copies.append(pltpu.make_async_copy(place.at[pl.ds(0, rows)], weight_hbm, sems.at[0]))
        copies[-1].start()
    for copy in copies:
        copy.wait()


def spread(where, parts, chunk, count, rows):
    width = parts[0].shape[-1]
    return pl.pallas_call(
        functools.partial(spread_kernel, chunk=chunk, rows=rows),
        out_shape=(jax.ShapeDtypeStruct((rows, width), F32), jax.ShapeDtypeStruct((1, width), F32)),
        in_specs=[SMEM] + [VMEM] * len(parts),
        out_specs=(HBM, VMEM),
        scratch_shapes=[
            pltpu.VMEM((count * chunk, width), F32),
            pltpu.SemaphoreType.DMA((count,)),
        ],
        compiler_params=params(),
        name="spread",
    )(where, *parts)


def body(
    section_input, conv_weight, conv_bias, deep_weight, deep_bias, labels, slot_ids, embed_grad
):
    chan_count = lax.axis_size("chan")
    strip_count = lax.axis_size("strip")
    chan_pos = lax.axis_index("chan")
    strip_pos = lax.axis_index("strip")
    half = chan_pos & 1
    channels = section_input.shape[-1]
    entries = slot_ids.shape[0]
    owned, width = embed_grad.shape
    where = jnp.stack(
        [half, (strip_pos == 0).astype(jnp.int32), (strip_pos == strip_count - 1).astype(jnp.int32), strip_pos]
    ).astype(jnp.int32)
    conv_w = conv_weight.reshape(9 * channels, -1)
    conv_b = conv_bias.reshape(1, -1)

    side, head, tail, sent = start(where, section_input, embed_grad, slot_ids, labels)
    pairs = []
    for s in range(strip_count):
        for c in range(chan_count):
            to = s + 1 - 2 * (c & 1)
            if 0 <= to < strip_count:
                pairs.append((s * chan_count + c, to * chan_count + c))
    got = lax.ppermute(sent, ("strip", "chan"), pairs)

    shared = gather_groups(side, "strip", high_groups(strip_count))

    taps, near_w = windows(where, section_input, conv_w)
    got, joined = lax.optimization_barrier((got, join(shared, [taps])))
    traded = swap(got, "chan", 1)
    shared = [joined, swap(joined, "strip", 1)]
    pooled, edges = conv_pool(where, taps, near_w, conv_b, got, traded, head, tail, [joined])
    other = swap(pooled, "chan", 1)

    chunk = -(-9 * channels // strip_count // 8) * 8
    bits = min(2, strip_count.bit_length() - 2)
    pieces = 1 << bits
    order = list(range(pieces // 2, pieces)) + list(range(pieces // 2))[::-1]
    with_sums = 2 * order[0] + 1
    forward = deep_forward(
        where,
        pooled,
        other,
        edges,
        deep_weight.reshape(9 * channels, width),
        deep_bias.reshape(1, width),
        labels,
        entries,
    )
    send = deep_backward(
        where, forward, shared, chunk, strip_count, 2 * pieces, with_sums
    )
    heads, held = strip_count // (2 * pieces), 2
    got = {k: swap(send[2 * k + 1].astype(F16), "strip", 1).astype(F32) for k in order}
    pair, parts, before = {}, {}, []
    for k in order:
        pair[k] = merge_pair(
            send[2 * k], got[k], send[with_sums], got[order[0]], heads * chunk, entries, before
        )
        parts[k] = swap(pair[k].astype(F16), "strip", 2 * k).astype(F32) if k else pair[k]
        before = [pair[k]] if k < pieces // 2 or k + 1 < pieces else [pair[k], parts[order[0]]]
    parts = [parts[k] for k in range(pieces)]
    held *= pieces
    send, sums = parts, None
    shift = bits + 1
    while True:
        left_bits = strip_count.bit_length() - 1 - shift
        size = min(3, left_bits)
        send, sums = merge(
            where, parts, chunk, heads, held // len(parts), entries, shift, 1 << size
        )
        if size == 0:
            break
        ways = 1 << size
        heads //= ways
        parts = [send[0]] + [
            swap(send[m].astype(F16), "strip", m << shift).astype(F32) for m in range(1, ways)
        ]
        held *= ways
        shift += size
    embeddings = pl.pallas_call(
        functools.partial(embed_kernel, entries=entries),
        out_shape=jax.ShapeDtypeStruct((owned, width), F32),
        in_specs=[SMEM] + [VMEM] * (1 + len(shared)),
        out_specs=VMEM,
        compiler_params=params(),
        name="embed",
    )(where, sums, *shared)
    gathered = gather_groups(send[0].astype(F16)[None], "strip", high_groups(strip_count))
    gathered = gathered + [swap(g, "strip", 1) for g in gathered]
    weight_rows, bias_row = spread(
        where, [g.astype(F32) for g in gathered], chunk, strip_count, 9 * channels
    )
    return (embeddings, weight_rows.reshape(3, 3, channels, width), bias_row[0])


def solution(mesh):
    placed = (
        P(None, "strip", None),
        P(),
        P(),
        P(None, None, None, "chan"),
        P("chan"),
        P(None, "strip"),
        P("strip"),
        P("strip", "chan"),
    )
    return jax.shard_map(
        body,
        mesh=mesh,
        in_specs=placed,
        out_specs=(P("strip", "chan"), P(None, None, None, "chan"), P("chan")),
        check_vma=False,
    )
```

```python
import functools
import math

import jax
import jax.numpy as jnp
from jax import lax
from jax.experimental import pallas as pl
from jax.experimental.pallas import tpu as pltpu
from jax.sharding import PartitionSpec as P

F32, BF16, F16 = jnp.float32, jnp.bfloat16, jnp.float16
VMEM = pl.BlockSpec(memory_space=pltpu.VMEM)
SMEM = pl.BlockSpec(memory_space=pltpu.SMEM)
HBM = pl.BlockSpec(memory_space=pltpu.HBM)
ANY = pl.BlockSpec(memory_space=pl.ANY)
SIDE = 8
WIDTH = 3
PIECE = 4
STEP = 4
NOTE = 16


def params(mib=8):
    return pltpu.CompilerParams(vmem_limit_bytes=mib << 20)


def swap(value, axis, mask):
    count = lax.axis_size(axis)
    return lax.ppermute(value, axis, [(i, i ^ mask) for i in range(count)])


def bit_groups(count, first, most):
    bits = count.bit_length() - 1
    groups, at = [], 0
    while at < bits:
        size = min(first if at == 0 else most, bits - at)
        groups.append((at, size))
        at += size
    return groups


def gather_groups(value, axis, groups):
    parts = [value]
    for shift, size in groups:
        held = parts[0] if len(parts) == 1 else jnp.concatenate(parts, axis=0)
        parts = [held] + [swap(held, axis, m << shift) for m in range(1, 1 << size)]
    return parts


def relative(refs):
    half = len(refs) // 2
    for low in range(2):
        m = low
        for ref in refs[low * half : (low + 1) * half]:
            for k in range(ref.shape[0]):
                yield m, ref, k
                m += 2


def high_groups(count):
    return [(at + 1, size) for at, size in bit_groups(count // 2, 2, 2)]


def shares(pooled_rows):
    first = pooled_rows // 2
    return first, pooled_rows - first


def pick(half, pair):
    return jnp.where(half == 0, pair[0], pair[1])


def window_kernel(where_ref, x_hbm, w_hbm, taps, w_ref, rows_ref, wide, sems):
    rows, cols, chans = x_hbm.shape
    half_cols = cols // 2
    half = where_ref[0]
    first, second = shares(rows // 2)
    counts = [-(-(2 * n + 1) // PIECE) for n in (first, second)]
    pieces = pick(half, counts)
    start = pick(half, (0, rows - counts[1] * PIECE))
    shift = pick(half, (PIECE + 1, PIECE - (2 * first - 1 - (rows - counts[1] * PIECE))))

    def piece(k):
        at = pl.ds(k * PIECE, PIECE)
        return pltpu.make_async_copy(
            x_hbm.at[pl.ds(start + k * PIECE, PIECE)], rows_ref.at[at], sems.at[k]
        )

    def begin(k, carry):
        piece(k).start()
        return carry

    lax.fori_loop(0, pieces, begin, 0)
    weights = pltpu.make_async_copy(w_hbm, w_ref, sems.at[sems.shape[0] - 1])
    weights.start()
    lanes = chans // 128
    border = jnp.zeros((8, 128), F32)
    for t in range(wide.shape[0]):
        wide[t, 0:8] = border
        wide[t, cols + 8 : cols + 16] = border

    def prepare(k, carry):
        piece(k).wait()
        for slot in range(PIECE):
            r = k * PIECE + slot
            x = rows_ref[r].astype(F32)
            for t in range(lanes):
                wide[slot * lanes + t, 8 : 8 + cols] = x[:, t * 128 : (t + 1) * 128]
            for tap in range(4):
                for t in range(lanes):
                    part = wide[slot * lanes + t, pl.ds(7 + tap, half_cols, stride=2), :]
                    at = (tap * lanes + t) * 128
                    taps[r + shift, :, at : at + 128] = part.astype(BF16)
        return carry

    lax.fori_loop(0, pieces, prepare, 0)
    outside = pick(half, (PIECE, PIECE + 2 * second + 1))
    taps[outside] = jnp.zeros(taps.shape[1:], BF16)
    weights.wait()


def windows(where, x, w):
    rows, cols, chans = x.shape
    first, _ = shares(rows // 2)
    most = -(-(2 * first + 1) // PIECE)
    return pl.pallas_call(
        window_kernel,
        out_shape=(
            jax.ShapeDtypeStruct(((most + 2) * PIECE, cols // 2, 4 * chans), BF16),
            jax.ShapeDtypeStruct(w.shape, BF16),
        ),
        in_specs=[SMEM, HBM, HBM],
        out_specs=(VMEM, VMEM),
        scratch_shapes=[
            pltpu.VMEM((most * PIECE, cols, chans), BF16),
            pltpu.VMEM((PIECE * (chans // 128), cols + 16, 128), F32),
            pltpu.SemaphoreType.DMA((most + 1,)),
        ],
        compiler_params=params(16),
        cost_estimate=pl.CostEstimate(flops=0, bytes_accessed=12 << 20, transcendentals=0),
        name="windows",
    )(where, *(pltpu.with_memory_space_constraint(a, pltpu.HBM) for a in (x, w)))


def edge_part(where_ref, pairs, w_ref, bias, edge_ref, acc):
    rows = pairs[0].shape[0]
    chans = w_ref.shape[1]
    lanes = chans // 128
    depth = 3 * chans
    lhs = jnp.concatenate(
        [
            pairs[s][:, (2 * j + phase) * chans : (2 * j + phase + 3) * chans]
            for s in range(2)
            for j in range(2)
            for phase in range(2)
        ],
        axis=0,
    )
    pad = rows + 16
    for dr in range(3):
        part = jnp.dot(lhs, w_ref[dr * depth : (dr + 1) * depth], preferred_element_type=F32)
        for g in range(8):
            own = part[g * rows : (g + 1) * rows]
            for t in range(lanes):
                at = 9 - dr
                piece = own[:, t * 128 : (t + 1) * 128]
                if dr == 0:
                    acc[g * lanes + t, 0:8] = jnp.zeros((8, 128), F32)
                    acc[g * lanes + t, 8 + rows : pad] = jnp.zeros((8, 128), F32)
                    acc[g * lanes + t, 8:9] = jnp.zeros((1, 128), F32)
                    acc[g * lanes + t, at : at + rows] = piece
                else:
                    acc[g * lanes + t, at : at + rows] += piece
    for g in range(4):
        for t in range(lanes):
            total = None
            for phase in range(2):
                at = (2 * g + phase) * lanes + t
                v = acc[at, 8 : 8 + rows] + bias[:, t * 128 : (t + 1) * 128]
                acc[at, 8 : 8 + rows] = v * jax.nn.sigmoid(v)
                both = (
                    acc[at, pl.ds(8, rows // 2, stride=2), :]
                    + acc[at, pl.ds(9, rows // 2, stride=2), :]
                )
                total = both if total is None else total + both
            lost = jnp.where(g == 0, where_ref[1], jnp.where(g == 3, where_ref[2], 0))
            keep = jnp.where(lost > 0, 0.0, 0.25)
            edge_ref[g, t] = (total * keep).astype(BF16).astype(F32)


def conv_kernel(where_ref, taps, w_ref, b_ref, *refs):
    out_ref = refs[-1]
    half_cols, chans = taps.shape[1], taps.shape[2] // 4
    bias = b_ref[...]

    def step(k, carry):
        r0 = PIECE + k * 2 * STEP
        total = None
        for phase in range(2):
            lhs = jnp.concatenate(
                [
                    taps[pl.ds(r0 + dr, 2 * STEP), :, phase * chans : (phase + 3) * chans]
                    for dr in range(3)
                ],
                axis=-1,
            ).reshape(2 * STEP * half_cols, 9 * chans)
            v = jnp.dot(lhs, w_ref[...], preferred_element_type=F32) + bias
            h = (v * jax.nn.sigmoid(v)).reshape(STEP, 2, half_cols, chans)
            h = h[:, 0] + h[:, 1]
            total = h if total is None else total + h
        out_ref[pl.ds(k * STEP, STEP)] = (total * 0.25).astype(BF16)
        return carry

    lax.fori_loop(0, out_ref.shape[0] // STEP, step, 0)


def conv_pool(where, taps, w, b, pooled_rows, after):
    _, half_cols, width = taps.shape
    chans = width // 4
    return pl.pallas_call(
        conv_kernel,
        out_shape=jax.ShapeDtypeStruct((pooled_rows, half_cols, chans), BF16),
        in_specs=[SMEM] + [VMEM] * 3 + [ANY] * len(after),
        out_specs=VMEM,
        compiler_params=params(16),
        cost_estimate=pl.CostEstimate(
            flops=8 * pooled_rows * half_cols * 9 * chans * chans,
            bytes_accessed=8 << 20,
            transcendentals=0,
        ),
        name="conv_pool",
    )(where, taps, w, b, *after)


def edge_kernel(where_ref, w_ref, b_ref, got_ref, traded_ref, head_ref, tail_ref, *refs):
    edge_ref, acc = refs[-2:]
    half = where_ref[0]
    got, traded = got_ref[...], traded_ref[...]
    left = jnp.concatenate([jnp.where(half == 0, got, traded), head_ref[...]], axis=-1)
    right = jnp.concatenate([tail_ref[...], jnp.where(half == 0, traded, got)], axis=-1)
    edge_part(where_ref, (left, right), w_ref, b_ref[...], edge_ref, acc)


def conv_edges(where, w, b, got, traded, head, tail, after):
    rows, lanes = head.shape[0], w.shape[1] // 128
    return pl.pallas_call(
        edge_kernel,
        out_shape=jax.ShapeDtypeStruct((4, lanes, rows // 2, 128), F32),
        in_specs=[SMEM] + [VMEM] * 6 + [ANY] * len(after),
        out_specs=VMEM,
        scratch_shapes=[pltpu.VMEM((8 * lanes, rows + 16, 128), F32)],
        compiler_params=params(),
        cost_estimate=pl.CostEstimate(flops=0, bytes_accessed=4 << 20, transcendentals=0),
        name="conv_edges",
    )(where, w, b, got, traded, head, tail, *after)


def start_kernel(
    where_ref, x_hbm, grad_hbm, labels_hbm, slots_hbm, side_ref, head_ref, tail_ref, send_ref,
    labels_ref, slots_ref, left, right, wide, sems,
):
    owned, width = grad_hbm.shape
    rows, cols, chans = x_hbm.shape
    entries = slots_ref.shape[1]
    reach = left.shape[1]
    half = where_ref[0]
    copies = [
        pltpu.make_async_copy(labels_hbm, labels_ref, sems.at[0]),
        pltpu.make_async_copy(grad_hbm, side_ref.at[0, pl.ds(0, owned)], sems.at[1]),
        pltpu.make_async_copy(x_hbm.at[:, pl.ds(0, reach)], left, sems.at[2]),
        pltpu.make_async_copy(x_hbm.at[:, pl.ds(cols - reach, reach)], right, sems.at[3]),
        pltpu.make_async_copy(slots_hbm, slots_ref, sems.at[4]),
    ]
    for copy in copies:
        copy.start()
    lane = lax.broadcasted_iota(jnp.int32, (1, width), 1)
    copies[0].wait()
    copies[4].wait()
    ids = jnp.concatenate(
        [slots_ref[...].astype(F32), jnp.zeros((1, width - entries), F32)], axis=1
    )
    labels = labels_ref[...]
    counts = jnp.zeros((1, width), F32)
    for e in range(entries):
        hit = jnp.where(labels == e, 1.0, 0.0)
        hit = jnp.sum(jnp.sum(hit, axis=0, keepdims=True), axis=1, keepdims=True)
        counts = jnp.where(lane == e, hit, counts)
    row = lax.broadcasted_iota(jnp.int32, (SIDE, width), 0)
    side_ref[0, owned:] = jnp.where(row == 0, ids, jnp.where(row == 1, counts, 0.0))
    lanes = chans // 128
    copies[2].wait()
    copies[3].wait()
    for ref, out_ref, at, sent in ((left, head_ref, 0, 1), (right, tail_ref, reach - WIDTH, 0)):
        x = ref[...].astype(F32).reshape(rows * reach, chans)
        for t in range(lanes):
            wide[t] = x[:, t * 128 : (t + 1) * 128]
        for c in range(WIDTH):
            for t in range(lanes):
                part = wide[t, pl.ds(at + c, rows, stride=reach), :].astype(BF16)
                place = (c * lanes + t) * 128
                out_ref[:, place : place + 128] = part
    send_ref[...] = jnp.where(half == 0, tail_ref[...], head_ref[...])
    copies[1].wait()


def start(where, x, grad, slots, labels):
    owned, width = grad.shape
    rows, _, chans = x.shape
    reach = 16
    columns = jax.ShapeDtypeStruct((rows, WIDTH * chans), BF16)
    fixed = [
        pltpu.with_memory_space_constraint(a, pltpu.HBM)
        for a in (x, grad, labels, slots.reshape(1, -1))
    ]
    return pl.pallas_call(
        start_kernel,
        out_shape=(jax.ShapeDtypeStruct((1, owned + SIDE, width), F32),) + (columns,) * 3,
        in_specs=[SMEM, HBM, HBM, HBM, HBM],
        out_specs=(VMEM,) * 4,
        scratch_shapes=[
            pltpu.VMEM(labels.shape, jnp.int32),
            pltpu.VMEM((1, slots.shape[0]), jnp.int32),
            pltpu.VMEM((rows, reach, chans), BF16),
            pltpu.VMEM((rows, reach, chans), BF16),
            pltpu.VMEM((chans // 128, rows * reach, 128), F32),
            pltpu.SemaphoreType.DMA((5,)),
        ],
        compiler_params=params(),
        name="start",
    )(where, *fixed)


def join_kernel(*refs, count):
    at = 0
    for ref in refs[:count]:
        refs[-1][at : at + ref.shape[0]] = ref[...]
        at += ref.shape[0]


def join(parts, after):
    shape = (sum(p.shape[0] for p in parts),) + parts[0].shape[1:]
    return pl.pallas_call(
        functools.partial(join_kernel, count=len(parts)),
        out_shape=jax.ShapeDtypeStruct(shape, F32),
        in_specs=[VMEM] * len(parts) + [ANY] * len(after),
        out_specs=VMEM,
        compiler_params=params(),
        name="join",
    )(*parts, *after)


def scale_rows(block, note_rows, sums):
    def exponent(values):
        top = None
        for v in values:
            one = jnp.max(jnp.max(jnp.abs(v), axis=0, keepdims=True), axis=1, keepdims=True)
            top = one if top is None else jnp.maximum(top, one)
        return jnp.ceil(jnp.log2(jnp.maximum(top, 1e-30)))

    power = exponent([block, note_rows])
    power_sums = exponent([sums])
    return power, power_sums


def note_block(bias, power, power_sums, width):
    row = lax.broadcasted_iota(jnp.int32, (NOTE, width), 0)
    bias = jnp.broadcast_to(bias, (NOTE, width))
    power = jnp.broadcast_to(power, (NOTE, width))
    power_sums = jnp.broadcast_to(power_sums, (NOTE, width))
    return jnp.where(row == 0, bias, jnp.where(row == 1, power, power_sums))


def read_note(part, at):
    note = part[at : at + NOTE]
    down = jnp.exp2(note[1:2] - 12.0)
    return note[0:1] * down, down, jnp.exp2(note[2:3] - 12.0)


def deep_kernel(
    where_ref, own_ref, other_ref, edge_ref, w_ref, b_ref, lab_ref, taps, member, slope, sums_ref, wide,
    *, block, entries
):
    _, cols, chans = own_ref.shape
    rows = lab_ref.shape[0]
    lanes = chans // 128
    width = w_ref.shape[-1]
    half = where_ref[0]
    taps[0] = jnp.zeros(taps.shape[1:], BF16)
    taps[rows + 1] = jnp.zeros(taps.shape[1:], BF16)

    def prepare(ref, base, i, slot):
        x = ref[i].astype(F32)
        r = base + i
        for t in range(lanes):
            s = slot * lanes + t
            at = t * 128
            wide[s, 8 : 8 + cols] = x[:, at : at + 128]
            for g, place in enumerate((7, 8, 7 + cols, 8 + cols)):
                wide[s, place : place + 1] = edge_ref[g, t, pl.ds(r, 1), :]
        for tap in range(3):
            for t in range(lanes):
                piece = wide[slot * lanes + t, 7 + tap : 7 + tap + cols, :]
                at = (tap * lanes + t) * 128
                taps[r + 1, :, at : at + 128] = piece.astype(BF16)

    first, second = shares(rows)
    times = math.gcd(first, second)

    def prepare_all(even_ref, odd_ref):
        def prepare_rows(k, carry):
            for q in range(rows // times):
                ref, base = (even_ref, 0) if q < first // times else (odd_ref, first)
                prepare(ref, base, q * times - base + k, q)
            return carry

        lax.fori_loop(0, times, prepare_rows, 0)

    @pl.when(half == 0)
    def _():
        prepare_all(own_ref, other_ref)

    @pl.when(half != 0)
    def _():
        prepare_all(other_ref, own_ref)

    lab = jnp.transpose(lab_ref[...].astype(F32))
    lane = lax.broadcasted_iota(jnp.int32, (cols, 128), 1)
    want = jnp.where(lane < 3 * entries, lane % entries, -1).astype(F32)
    for r in range(rows):
        member[r] = (lab[:, r : r + 1] == want).astype(BF16)
    bias = b_ref[...]
    size = block * cols

    def step(k, sums):
        r0 = k * block
        lhs = jnp.concatenate([taps[pl.ds(r0 + dr, block)] for dr in range(3)], axis=-1)
        v = jnp.dot(lhs.reshape(size, 9 * chans), w_ref[...], preferred_element_type=F32) + bias
        sig = jax.nn.sigmoid(v)
        features = (v * sig).astype(BF16)
        slope[pl.ds(k * size, size)] = sig * (1.0 + v * (1.0 - sig))
        mem = member[pl.ds(r0, block)].reshape(size, 128)
        return sums + lax.dot_general(
            mem, features, (((0,), (0,)), ((), ())), preferred_element_type=F32
        )[:entries]

    sums_ref[...] = lax.fori_loop(0, rows // block, step, jnp.zeros((entries, width), F32))


def deep_forward(where, own, other, edges, w, b, labels, entries):
    _, cols, chans = own.shape
    rows, width = labels.shape[0], w.shape[-1]
    block = next(k for k in (8, 4, 2, 1) if rows % k == 0)
    first, second = shares(rows)
    slots = rows // math.gcd(first, second)
    return pl.pallas_call(
        functools.partial(deep_kernel, block=block, entries=entries),
        out_shape=(
            jax.ShapeDtypeStruct((rows + 2, cols, 3 * chans), BF16),
            jax.ShapeDtypeStruct((rows, cols, 128), BF16),
            jax.ShapeDtypeStruct((rows * cols, width), F32),
            jax.ShapeDtypeStruct((entries, width), F32),
        ),
        in_specs=[SMEM] + [VMEM] * 6,
        out_specs=(VMEM,) * 4,
        scratch_shapes=[pltpu.VMEM((slots * (chans // 128), cols + 16, 128), F32)],
        compiler_params=params(16),
        cost_estimate=pl.CostEstimate(
            flops=4 * rows * cols * 9 * chans * width, bytes_accessed=8 << 20, transcendentals=0
        ),
        name="deep_forward",
    )(where, own, other, edges, w, b, labels)


def grad_kernel(
    where_ref, taps, member, slope, sums_ref, *refs, n_parts, chunk, ways, with_sums
):
    part_refs = refs[:n_parts]
    out_refs = refs[n_parts : n_parts + ways]
    grad, weight = refs[n_parts + ways :]
    rows, cols, depth = member.shape[0], taps.shape[1], taps.shape[2]
    width = slope.shape[-1]
    me = where_ref[3]
    entries = sums_ref.shape[0]
    owned = part_refs[0].shape[1] - SIDE
    own_ids = jnp.broadcast_to(part_refs[0][0, owned : owned + 1, :entries], (entries, entries))
    across = lax.broadcasted_iota(jnp.int32, (entries, entries), 1)
    down = lax.broadcasted_iota(jnp.int32, (entries, entries), 0)
    ids = jnp.sum(jnp.where(across == down, own_ids, 0.0), axis=1, keepdims=True).astype(jnp.int32)
    total = jnp.zeros((entries, 1), F32)
    entry_grad = jnp.zeros((entries, width), F32)
    owner, inner = ids // owned, ids % owned
    spot = lax.broadcasted_iota(jnp.int32, (entries, owned), 1)
    for m, ref, k in relative(part_refs):
        there = ref[k, owned : owned + 1, :entries] == ids.astype(F32)
        counts = ref[k, owned + 1 : owned + 2, :entries]
        total += jnp.sum(jnp.where(there, counts, 0.0), axis=1, keepdims=True)
        hot = ((owner ^ me) == m) & (inner == spot)
        entry_grad += jnp.dot(
            hot.astype(F32), ref[k, :owned], precision=lax.Precision.HIGHEST, preferred_element_type=F32
        )
    entry_grad = entry_grad / jnp.maximum(total, 1.0)
    high = entry_grad.astype(BF16)
    rest = entry_grad - high.astype(F32)
    mid = rest.astype(BF16)
    low = (rest - mid.astype(F32)).astype(BF16)
    terms = jnp.concatenate([high, mid, low, jnp.zeros((128 - 3 * entries, width), BF16)], axis=0)
    pixel = jnp.dot(member[...].reshape(rows * cols, 128), terms, preferred_element_type=F32)
    dg = (pixel * slope[...]).astype(BF16)
    grad[...] = dg
    bias_sum = jnp.sum(dg.astype(F32), axis=0, keepdims=True)
    for dr in range(3):
        window = taps[dr : dr + rows].reshape(rows * cols, depth)
        out = lax.dot_general(grad[...], window, (((0,), (0,)), ((), ())), preferred_element_type=F32)
        weight[dr * depth : (dr + 1) * depth] = jnp.transpose(out)
    if weight.shape[0] > 3 * depth:
        weight[3 * depth :] = jnp.zeros((weight.shape[0] - 3 * depth, width), F32)
    sums = sums_ref[...]
    power, power_sums = scale_rows(weight[...], bias_sum, sums)
    up = jnp.exp2(12.0 - power)
    note = note_block(bias_sum * up, power, power_sums, width)
    digit = lax.rem(me, ways)
    heads = weight.shape[0] // chunk // ways
    for m in range(ways):
        for hi in range(heads):
            j = hi * ways + (digit ^ m)
            out_refs[m][hi * chunk : (hi + 1) * chunk] = (
                weight[pl.ds(pl.multiple_of(j * chunk, 8), chunk)] * up
            )
        out_refs[m][heads * chunk : heads * chunk + NOTE] = note
    out_refs[with_sums][heads * chunk + NOTE :] = sums * jnp.exp2(12.0 - power_sums)


def deep_backward(where, forward, parts, chunk, count, ways, with_sums):
    taps, _, slope, sums = forward
    width, entries = slope.shape[-1], sums.shape[0]
    size = count // ways * chunk + NOTE
    return pl.pallas_call(
        functools.partial(
            grad_kernel, n_parts=len(parts), chunk=chunk, ways=ways, with_sums=with_sums
        ),
        out_shape=tuple(
            jax.ShapeDtypeStruct((size + (entries if m == with_sums else 0), width), F32)
            for m in range(ways)
        ),
        in_specs=[SMEM] + [VMEM] * (4 + len(parts)),
        out_specs=(VMEM,) * ways,
        scratch_shapes=[
            pltpu.VMEM(slope.shape, BF16),
            pltpu.VMEM((count * chunk, width), F32),
        ],
        compiler_params=params(16),
        cost_estimate=pl.CostEstimate(
            flops=4 * slope.shape[0] * 3 * taps.shape[2] * width, bytes_accessed=8 << 20, transcendentals=0
        ),
        name="deep_backward",
    )(where, *forward, *parts)


def pair_kernel(own_ref, got_ref, own_sums_ref, got_sums_ref, *refs, size, entries):
    out_ref = refs[-1]
    own, got = own_ref[size : size + NOTE], got_ref[size : size + NOTE]
    power = jnp.maximum(own[1:2], got[1:2]) + 1.0
    power_sums = jnp.maximum(own[2:3], got[2:3])
    own_down, got_down = jnp.exp2(own[1:2] - power), jnp.exp2(got[1:2] - power)
    out_ref[:size] = own_ref[:size] * own_down + got_ref[:size] * got_down
    bias = own[0:1] * own_down + got[0:1] * got_down
    out_ref[size : size + NOTE] = note_block(bias, power, power_sums, own.shape[-1])
    at = size + NOTE
    sums = own_sums_ref[at : at + entries] * jnp.exp2(own[2:3] - power_sums)
    out_ref[at : at + entries] = sums
    sums = got_sums_ref[at : at + entries] * jnp.exp2(got[2:3] - power_sums)
    out_ref[at + entries : at + 2 * entries] = sums


def merge_pair(own, got, own_sums, got_sums, size, entries, after):
    width = own.shape[-1]
    return pl.pallas_call(
        functools.partial(pair_kernel, size=size, entries=entries),
        out_shape=jax.ShapeDtypeStruct((size + NOTE + 2 * entries, width), F32),
        in_specs=[VMEM] * 4 + [ANY] * len(after),
        out_specs=VMEM,
        compiler_params=params(),
        cost_estimate=pl.CostEstimate(flops=0, bytes_accessed=32 << 20, transcendentals=0),
        name="merge_pair",
    )(own, got, own_sums, got_sums, *after)


def merge_kernel(where_ref, *refs, chunk, heads, held, entries, shift, next_ways):
    n_parts = len(refs) - next_ways - 1
    part_refs, out_refs, sums_ref = refs[:n_parts], refs[n_parts:-1], refs[-1]
    width = part_refs[0].shape[-1]
    size = heads * chunk
    total, bias = jnp.zeros((size, width), F32), jnp.zeros((1, width), F32)
    sums_rows = held * entries
    for m, ref in enumerate(part_refs):
        more, down, down_sums = read_note(ref, size)
        total, bias = total + ref[:size] * down, bias + more
        sums_ref[m * sums_rows : (m + 1) * sums_rows] = ref[size + NOTE :] * down_sums
    sums = sums_ref[...]
    power, power_sums = scale_rows(total, bias, sums)
    up = jnp.exp2(12.0 - power)
    note = note_block(bias * up, power, power_sums, width)
    total = total * up
    if next_ways == 1:
        out_refs[0][:size] = total
        out_refs[0][size:] = note
        return
    sums = sums * jnp.exp2(12.0 - power_sums)
    digit = lax.rem(where_ref[3] >> shift, next_ways)
    for m in range(next_ways):
        for hi in range(heads // next_ways):
            piece = jnp.zeros((chunk, width), F32)
            for d in range(next_ways):
                at = (hi * next_ways + d) * chunk
                piece = jnp.where((digit ^ m) == d, total[at : at + chunk], piece)
            out_refs[m][hi * chunk : (hi + 1) * chunk] = piece
        at = heads // next_ways * chunk
        out_refs[m][at : at + NOTE] = note
        out_refs[m][at + NOTE :] = sums


def merge(where, parts, chunk, heads, held, entries, shift, next_ways):
    width = parts[0].shape[-1]
    sums_rows = len(parts) * held * entries
    if next_ways == 1:
        outs = (jax.ShapeDtypeStruct((heads * chunk + NOTE, width), F32),)
    else:
        rows = heads // next_ways * chunk + NOTE + sums_rows
        outs = (jax.ShapeDtypeStruct((rows, width), F32),) * next_ways
    outs = outs + (jax.ShapeDtypeStruct((sums_rows, width), F32),)
    out = pl.pallas_call(
        functools.partial(
            merge_kernel, chunk=chunk, heads=heads, held=held, entries=entries, shift=shift, next_ways=next_ways
        ),
        out_shape=outs,
        in_specs=[SMEM] + [VMEM] * len(parts),
        out_specs=(VMEM,) * len(outs),
        compiler_params=params(),
        name="merge",
    )(where, *parts)
    return out[:-1], out[-1]


def embed_kernel(where_ref, sums_ref, *refs, entries):
    part_refs, out_ref = refs[:-1], refs[-1]
    owned, width = out_ref.shape
    own = (where_ref[3] * owned + lax.broadcasted_iota(jnp.int32, (owned, entries), 0)).astype(F32)
    sums, counts = jnp.zeros((owned, width), F32), jnp.zeros((owned, 1), F32)
    for m, ref, k in relative(part_refs):
        there = ref[k, owned : owned + 1, :entries] == own
        count = ref[k, owned + 1 : owned + 2, :entries]
        counts += jnp.sum(jnp.where(there, count, 0.0), axis=1, keepdims=True)
        sums += jnp.dot(
            there.astype(F32),
            sums_ref[m * entries : (m + 1) * entries],
            precision=lax.Precision.HIGHEST,
            preferred_element_type=F32,
        )
    out_ref[...] = sums / jnp.maximum(counts, 1.0)


def spread_kernel(where_ref, *refs, chunk, rows):
    part_refs, weight_ref, bias_ref, place = refs[:-3], refs[-3], refs[-2], refs[-1]
    me = where_ref[3]
    whole = rows == place.shape[0]
    for m, ref, k in relative(part_refs):
        bias, down, _ = read_note(ref[k], chunk)
        j = me ^ m
        target = weight_ref if whole else place
        target[pl.ds(pl.multiple_of(j * chunk, 8), chunk)] = ref[k, :chunk] * down

        @pl.when(j == 0)
        def _():
            bias_ref[...] = bias

    if not whole:
        weight_ref[...] = place[:rows]


def spread(where, parts, chunk, count, rows):
    width = parts[0].shape[-1]
    return pl.pallas_call(
        functools.partial(spread_kernel, chunk=chunk, rows=rows),
        out_shape=(jax.ShapeDtypeStruct((rows, width), F32), jax.ShapeDtypeStruct((1, width), F32)),
        in_specs=[SMEM] + [VMEM] * len(parts),
        out_specs=(VMEM, VMEM),
        scratch_shapes=[pltpu.VMEM((count * chunk, width), F32)],
        compiler_params=params(),
        name="spread",
    )(where, *parts)


def body(
    section_input, conv_weight, conv_bias, deep_weight, deep_bias, labels, slot_ids, embed_grad
):
    chan_count = lax.axis_size("chan")
    strip_count = lax.axis_size("strip")
    chan_pos = lax.axis_index("chan")
    strip_pos = lax.axis_index("strip")
    half = chan_pos & 1
    channels = section_input.shape[-1]
    entries = slot_ids.shape[0]
    owned, width = embed_grad.shape
    where = jnp.stack(
        [half, (strip_pos == 0).astype(jnp.int32), (strip_pos == strip_count - 1).astype(jnp.int32), strip_pos]
    ).astype(jnp.int32)
    conv_w = conv_weight.reshape(9 * channels, -1)
    conv_b = conv_bias.reshape(1, -1)

    side, head, tail, sent = start(where, section_input, embed_grad, slot_ids, labels)
    pairs = []
    for s in range(strip_count):
        for c in range(chan_count):
            to = s + 1 - 2 * (c & 1)
            if 0 <= to < strip_count:
                pairs.append((s * chan_count + c, to * chan_count + c))
    got = lax.ppermute(sent, ("strip", "chan"), pairs)

    shared = gather_groups(side, "strip", high_groups(strip_count))

    taps, near_w = windows(where, section_input, conv_w)
    got, joined = lax.optimization_barrier((got, join(shared, [taps])))
    traded = swap(got, "chan", 1)
    shared = [joined, swap(joined, "strip", 1)]
    pooled = conv_pool(where, taps, near_w, conv_b, section_input.shape[0] // 4, [joined, got])
    other = swap(pooled, "chan", 1)
    edges = conv_edges(where, near_w, conv_b, got, traded, head, tail, [pooled])

    chunk = -(-9 * channels // strip_count // 8) * 8
    bits = min(2, strip_count.bit_length() - 2)
    pieces = 1 << bits
    order = list(range(pieces // 2, pieces)) + list(range(pieces // 2))[::-1]
    with_sums = 2 * order[0] + 1
    forward = deep_forward(
        where,
        pooled,
        other,
        edges,
        deep_weight.reshape(9 * channels, width),
        deep_bias.reshape(1, width),
        labels,
        entries,
    )
    send = deep_backward(
        where, forward, shared, chunk, strip_count, 2 * pieces, with_sums
    )
    heads, held = strip_count // (2 * pieces), 2
    leaving = lax.optimization_barrier([send[2 * k + 1].astype(F16) for k in order])
    got = {k: swap(part, "strip", 1).astype(F32) for k, part in zip(order, leaving)}
    pair, parts, before = {}, {}, []
    for k in order:
        pair[k] = merge_pair(
            send[2 * k], got[k], send[with_sums], got[order[0]], heads * chunk, entries, before
        )
        parts[k] = swap(pair[k].astype(F16), "strip", 2 * k).astype(F32) if k else pair[k]
        before = [pair[k]] if k < pieces // 2 or k + 1 < pieces else [pair[k], parts[order[0]]]
    parts = [parts[k] for k in range(pieces)]
    held *= pieces
    send, sums = parts, None
    shift = bits + 1
    while True:
        left_bits = strip_count.bit_length() - 1 - shift
        size = min(3, left_bits)
        send, sums = merge(
            where, parts, chunk, heads, held // len(parts), entries, shift, 1 << size
        )
        if size == 0:
            break
        ways = 1 << size
        heads //= ways
        parts = [send[0]] + [
            swap(send[m].astype(F16), "strip", m << shift).astype(F32) for m in range(1, ways)
        ]
        held *= ways
        shift += size
    embeddings = pl.pallas_call(
        functools.partial(embed_kernel, entries=entries),
        out_shape=jax.ShapeDtypeStruct((owned, width), F32),
        in_specs=[SMEM] + [VMEM] * (1 + len(shared)),
        out_specs=VMEM,
        compiler_params=params(),
        name="embed",
    )(where, sums, *shared)
    gathered = gather_groups(send[0].astype(F16)[None], "strip", high_groups(strip_count))
    gathered = gathered + [swap(g, "strip", 1) for g in gathered]
    weight_rows, bias_row = spread(
        where, [g.astype(F32) for g in gathered], chunk, strip_count, 9 * channels
    )
    return (embeddings, weight_rows.reshape(3, 3, channels, width), bias_row[0])


def solution(mesh):
    placed = (
        P(None, "strip", None),
        P(),
        P(),
        P(None, None, None, "chan"),
        P("chan"),
        P(None, "strip"),
        P("strip"),
        P("strip", "chan"),
    )
    return jax.shard_map(
        body,
        mesh=mesh,
        in_specs=placed,
        out_specs=(P("strip", "chan"), P(None, None, None, "chan"), P("chan")),
        check_vma=False,
    )
```

```python
import functools
import itertools
import math

import jax
import jax.numpy as jnp
from jax import lax
from jax.experimental import pallas as pl
from jax.experimental.pallas import tpu as pltpu
from jax.sharding import PartitionSpec as P

F32, BF16, F16 = jnp.float32, jnp.bfloat16, jnp.float16
VMEM = pl.BlockSpec(memory_space=pltpu.VMEM)
SMEM = pl.BlockSpec(memory_space=pltpu.SMEM)
HBM = pl.BlockSpec(memory_space=pltpu.HBM)
ANY = pl.BlockSpec(memory_space=pl.ANY)
SIDE = 8
WIDTH = 3
PIECE = 4
STEP = 6
NOTE = 16


def params(mib=8):
    return pltpu.CompilerParams(vmem_limit_bytes=mib << 20)


def swap(value, axis, mask):
    count = lax.axis_size(axis)
    return lax.ppermute(value, axis, [(i, i ^ mask) for i in range(count)])


def bit_groups(count, first, most):
    bits = count.bit_length() - 1
    groups, at = [], 0
    while at < bits:
        size = min(first if at == 0 else most, bits - at)
        groups.append((at, size))
        at += size
    return groups


def gather_groups(value, axis, groups):
    parts = [value]
    for shift, size in groups:
        held = parts[0] if len(parts) == 1 else jnp.concatenate(parts, axis=0)
        parts = [held] + [swap(held, axis, m << shift) for m in range(1, 1 << size)]
    return parts


def relative(refs):
    half = len(refs) // 2
    for low in range(2):
        m = low
        for ref in refs[low * half : (low + 1) * half]:
            for k in range(ref.shape[0]):
                yield m, ref, k
                m += 2


def high_groups(count):
    return [(at + 1, size) for at, size in bit_groups(count // 2, 2, 2)]


def shares(pooled_rows):
    first = pooled_rows // 2
    return first, pooled_rows - first


def pick(half, pair):
    return jnp.where(half == 0, pair[0], pair[1])


def window_kernel(where_ref, x_hbm, w_hbm, taps, w_ref, rows_ref, wide, sems):
    rows, cols, chans = x_hbm.shape
    half_cols = cols // 2
    half = where_ref[0]
    first, second = shares(rows // 2)
    counts = [-(-(2 * n + 1) // PIECE) for n in (first, second)]
    pieces = pick(half, counts)
    start = pick(half, (0, rows - counts[1] * PIECE))
    shift = pick(half, (PIECE + 1, PIECE - (2 * first - 1 - (rows - counts[1] * PIECE))))

    def piece(k):
        at = pl.ds(k * PIECE, PIECE)
        return pltpu.make_async_copy(
            x_hbm.at[pl.ds(start + k * PIECE, PIECE)], rows_ref.at[at], sems.at[k]
        )

    def begin(k, carry):
        piece(k).start()
        return carry

    lax.fori_loop(0, pieces, begin, 0)
    weights = pltpu.make_async_copy(w_hbm, w_ref, sems.at[sems.shape[0] - 1])
    weights.start()
    lanes = chans // 128
    border = jnp.zeros((8, 128), F32)
    for t in range(wide.shape[0]):
        wide[t, 0:8] = border
        wide[t, cols + 8 : cols + 16] = border

    def prepare(k, carry):
        piece(k).wait()
        for slot in range(PIECE):
            r = k * PIECE + slot
            x = rows_ref[r].astype(F32)
            for t in range(lanes):
                wide[slot * lanes + t, 8 : 8 + cols] = x[:, t * 128 : (t + 1) * 128]
            for tap in range(4):
                for t in range(lanes):
                    part = wide[slot * lanes + t, pl.ds(7 + tap, half_cols, stride=2), :]
                    at = (tap * lanes + t) * 128
                    taps[r + shift, :, at : at + 128] = part.astype(BF16)
        return carry

    lax.fori_loop(0, pieces, prepare, 0)
    outside = pick(half, (PIECE, PIECE + 2 * second + 1))
    taps[outside] = jnp.zeros(taps.shape[1:], BF16)
    weights.wait()


def windows(where, x, w):
    rows, cols, chans = x.shape
    first, _ = shares(rows // 2)
    most = -(-(2 * first + 1) // PIECE)
    return pl.pallas_call(
        window_kernel,
        out_shape=(
            jax.ShapeDtypeStruct(((most + 2) * PIECE, cols // 2, 4 * chans), BF16),
            jax.ShapeDtypeStruct(w.shape, BF16),
        ),
        in_specs=[SMEM, HBM, HBM],
        out_specs=(VMEM, VMEM),
        scratch_shapes=[
            pltpu.VMEM((most * PIECE, cols, chans), BF16),
            pltpu.VMEM((PIECE * (chans // 128), cols + 16, 128), F32),
            pltpu.SemaphoreType.DMA((most + 1,)),
        ],
        compiler_params=params(16),
        cost_estimate=pl.CostEstimate(flops=0, bytes_accessed=12 << 20, transcendentals=0),
        name="windows",
    )(where, *(pltpu.with_memory_space_constraint(a, pltpu.HBM) for a in (x, w)))


def edge_part(where_ref, pairs, w_ref, bias, edge_ref, acc):
    rows = pairs[0].shape[0]
    chans = w_ref.shape[1]
    lanes = chans // 128
    depth = 3 * chans
    lhs = jnp.concatenate(
        [
            pairs[s][:, (2 * j + phase) * chans : (2 * j + phase + 3) * chans]
            for s in range(2)
            for j in range(2)
            for phase in range(2)
        ],
        axis=0,
    )
    pad = rows + 16
    for dr in range(3):
        part = jnp.dot(lhs, w_ref[dr * depth : (dr + 1) * depth], preferred_element_type=F32)
        for g in range(8):
            own = part[g * rows : (g + 1) * rows]
            for t in range(lanes):
                at = 9 - dr
                piece = own[:, t * 128 : (t + 1) * 128]
                if dr == 0:
                    acc[g * lanes + t, 0:8] = jnp.zeros((8, 128), F32)
                    acc[g * lanes + t, 8 + rows : pad] = jnp.zeros((8, 128), F32)
                    acc[g * lanes + t, 8:9] = jnp.zeros((1, 128), F32)
                    acc[g * lanes + t, at : at + rows] = piece
                else:
                    acc[g * lanes + t, at : at + rows] += piece
    for g in range(4):
        for t in range(lanes):
            total = None
            for phase in range(2):
                at = (2 * g + phase) * lanes + t
                v = acc[at, 8 : 8 + rows] + bias[:, t * 128 : (t + 1) * 128]
                acc[at, 8 : 8 + rows] = v * jax.nn.sigmoid(v)
                both = (
                    acc[at, pl.ds(8, rows // 2, stride=2), :]
                    + acc[at, pl.ds(9, rows // 2, stride=2), :]
                )
                total = both if total is None else total + both
            lost = jnp.where(g == 0, where_ref[1], jnp.where(g == 3, where_ref[2], 0))
            keep = jnp.where(lost > 0, 0.0, 0.25)
            edge_ref[g, t] = (total * keep).astype(BF16).astype(F32)


def conv_kernel(where_ref, taps, w_ref, b_ref, *refs):
    out_ref = refs[-1]
    assert out_ref.shape[0] % STEP == 0
    half_cols, chans = taps.shape[1], taps.shape[2] // 4
    bias = b_ref[...]

    def step(k, carry):
        r0 = PIECE + k * 2 * STEP
        total = None
        for phase in range(2):
            lhs = jnp.concatenate(
                [
                    taps[pl.ds(r0 + dr, 2 * STEP), :, phase * chans : (phase + 3) * chans]
                    for dr in range(3)
                ],
                axis=-1,
            ).reshape(2 * STEP * half_cols, 9 * chans)
            v = jnp.dot(lhs, w_ref[...], preferred_element_type=F32) + bias
            h = (v * jax.nn.sigmoid(v)).reshape(STEP, 2, half_cols, chans)
            h = h[:, 0] + h[:, 1]
            total = h if total is None else total + h
        out_ref[pl.ds(k * STEP, STEP)] = (total * 0.25).astype(BF16)
        return carry

    lax.fori_loop(0, out_ref.shape[0] // STEP, step, 0)


def conv_pool(where, taps, w, b, pooled_rows, after):
    _, half_cols, width = taps.shape
    chans = width // 4
    return pl.pallas_call(
        conv_kernel,
        out_shape=jax.ShapeDtypeStruct((pooled_rows, half_cols, chans), BF16),
        in_specs=[SMEM] + [VMEM] * 3 + [ANY] * len(after),
        out_specs=VMEM,
        compiler_params=params(16),
        cost_estimate=pl.CostEstimate(
            flops=8 * pooled_rows * half_cols * 9 * chans * chans,
            bytes_accessed=8 << 20,
            transcendentals=0,
        ),
        name="conv_pool",
    )(where, taps, w, b, *after)


def edge_kernel(where_ref, w_ref, b_ref, got_ref, traded_ref, head_ref, tail_ref, *refs):
    edge_ref, acc = refs[-2:]
    half = where_ref[0]
    got, traded = got_ref[...], traded_ref[...]
    left = jnp.concatenate([jnp.where(half == 0, got, traded), head_ref[...]], axis=-1)
    right = jnp.concatenate([tail_ref[...], jnp.where(half == 0, traded, got)], axis=-1)
    edge_part(where_ref, (left, right), w_ref, b_ref[...], edge_ref, acc)


def conv_edges(where, w, b, got, traded, head, tail, after):
    rows, lanes = head.shape[0], w.shape[1] // 128
    return pl.pallas_call(
        edge_kernel,
        out_shape=jax.ShapeDtypeStruct((4, lanes, rows // 2, 128), F32),
        in_specs=[SMEM] + [VMEM] * 6 + [ANY] * len(after),
        out_specs=VMEM,
        scratch_shapes=[pltpu.VMEM((8 * lanes, rows + 16, 128), F32)],
        compiler_params=params(),
        cost_estimate=pl.CostEstimate(flops=0, bytes_accessed=4 << 20, transcendentals=0),
        name="conv_edges",
    )(where, w, b, got, traded, head, tail, *after)


def start_kernel(
    where_ref, x_hbm, grad_hbm, labels_hbm, slots_hbm, side_ref, head_ref, tail_ref, send_ref,
    labels_ref, slots_ref, left, right, wide, sems,
):
    owned, width = grad_hbm.shape
    rows, cols, chans = x_hbm.shape
    entries = slots_ref.shape[1]
    reach = left.shape[1]
    half = where_ref[0]
    copies = [
        pltpu.make_async_copy(labels_hbm, labels_ref, sems.at[0]),
        pltpu.make_async_copy(grad_hbm, side_ref.at[0, pl.ds(0, owned)], sems.at[1]),
        pltpu.make_async_copy(x_hbm.at[:, pl.ds(0, reach)], left, sems.at[2]),
        pltpu.make_async_copy(x_hbm.at[:, pl.ds(cols - reach, reach)], right, sems.at[3]),
        pltpu.make_async_copy(slots_hbm, slots_ref, sems.at[4]),
    ]
    for copy in copies:
        copy.start()
    lane = lax.broadcasted_iota(jnp.int32, (1, width), 1)
    copies[0].wait()
    copies[4].wait()
    ids = jnp.concatenate(
        [slots_ref[...].astype(F32), jnp.zeros((1, width - entries), F32)], axis=1
    )
    labels = labels_ref[...]
    counts = jnp.zeros((1, width), F32)
    for e in range(entries):
        hit = jnp.where(labels == e, 1.0, 0.0)
        hit = jnp.sum(jnp.sum(hit, axis=0, keepdims=True), axis=1, keepdims=True)
        counts = jnp.where(lane == e, hit, counts)
    row = lax.broadcasted_iota(jnp.int32, (SIDE, width), 0)
    side_ref[0, owned:] = jnp.where(row == 0, ids, jnp.where(row == 1, counts, 0.0))
    lanes = chans // 128
    copies[2].wait()
    copies[3].wait()
    for ref, out_ref, at, sent in ((left, head_ref, 0, 1), (right, tail_ref, reach - WIDTH, 0)):
        x = ref[...].astype(F32).reshape(rows * reach, chans)
        for t in range(lanes):
            wide[t] = x[:, t * 128 : (t + 1) * 128]
        for c in range(WIDTH):
            for t in range(lanes):
                part = wide[t, pl.ds(at + c, rows, stride=reach), :].astype(BF16)
                place = (c * lanes + t) * 128
                out_ref[:, place : place + 128] = part
    send_ref[...] = jnp.where(half == 0, tail_ref[...], head_ref[...])
    copies[1].wait()


def start(where, x, grad, slots, labels):
    owned, width = grad.shape
    rows, _, chans = x.shape
    reach = 16
    columns = jax.ShapeDtypeStruct((rows, WIDTH * chans), BF16)
    fixed = [
        pltpu.with_memory_space_constraint(a, pltpu.HBM)
        for a in (x, grad, labels, slots.reshape(1, -1))
    ]
    return pl.pallas_call(
        start_kernel,
        out_shape=(jax.ShapeDtypeStruct((1, owned + SIDE, width), F32),) + (columns,) * 3,
        in_specs=[SMEM, HBM, HBM, HBM, HBM],
        out_specs=(VMEM,) * 4,
        scratch_shapes=[
            pltpu.VMEM(labels.shape, jnp.int32),
            pltpu.VMEM((1, slots.shape[0]), jnp.int32),
            pltpu.VMEM((rows, reach, chans), BF16),
            pltpu.VMEM((rows, reach, chans), BF16),
            pltpu.VMEM((chans // 128, rows * reach, 128), F32),
            pltpu.SemaphoreType.DMA((5,)),
        ],
        compiler_params=params(),
        name="start",
    )(where, *fixed)


def join_kernel(*refs, count):
    at = 0
    for ref in refs[:count]:
        refs[-1][at : at + ref.shape[0]] = ref[...]
        at += ref.shape[0]


def join(parts, after):
    shape = (sum(p.shape[0] for p in parts),) + parts[0].shape[1:]
    return pl.pallas_call(
        functools.partial(join_kernel, count=len(parts)),
        out_shape=jax.ShapeDtypeStruct(shape, F32),
        in_specs=[VMEM] * len(parts) + [ANY] * len(after),
        out_specs=VMEM,
        compiler_params=params(),
        name="join",
    )(*parts, *after)


def scale_rows(block, note_rows, sums):
    def exponent(values):
        top = None
        for v in values:
            one = jnp.max(jnp.max(jnp.abs(v), axis=0, keepdims=True), axis=1, keepdims=True)
            top = one if top is None else jnp.maximum(top, one)
        return jnp.ceil(jnp.log2(jnp.maximum(top, 1e-30)))

    power = exponent([block, note_rows])
    power_sums = exponent([sums])
    return power, power_sums


def note_block(bias, power, power_sums, width):
    row = lax.broadcasted_iota(jnp.int32, (NOTE, width), 0)
    bias = jnp.broadcast_to(bias, (NOTE, width))
    power = jnp.broadcast_to(power, (NOTE, width))
    power_sums = jnp.broadcast_to(power_sums, (NOTE, width))
    return jnp.where(row == 0, bias, jnp.where(row == 1, power, power_sums))


def read_note(part, at):
    note = part[at : at + NOTE]
    down = jnp.exp2(note[1:2] - 12.0)
    return note[0:1] * down, down, jnp.exp2(note[2:3] - 12.0)


def deep_kernel(
    where_ref, own_ref, other_ref, edge_ref, w_ref, b_ref, lab_ref, taps, member, slope, sums_ref, wide,
    *, block, entries
):
    _, cols, chans = own_ref.shape
    rows = lab_ref.shape[0]
    lanes = chans // 128
    width = w_ref.shape[-1]
    half = where_ref[0]
    taps[0] = jnp.zeros(taps.shape[1:], BF16)
    taps[rows + 1] = jnp.zeros(taps.shape[1:], BF16)

    def prepare(ref, base, i, slot):
        x = ref[i].astype(F32)
        r = base + i
        for t in range(lanes):
            s = slot * lanes + t
            at = t * 128
            wide[s, 8 : 8 + cols] = x[:, at : at + 128]
            for g, place in enumerate((7, 8, 7 + cols, 8 + cols)):
                wide[s, place : place + 1] = edge_ref[g, t, pl.ds(r, 1), :]
        for tap in range(3):
            for t in range(lanes):
                piece = wide[slot * lanes + t, 7 + tap : 7 + tap + cols, :]
                at = (tap * lanes + t) * 128
                taps[r + 1, :, at : at + 128] = piece.astype(BF16)

    first, second = shares(rows)
    times = math.gcd(first, second)

    def prepare_all(even_ref, odd_ref):
        def prepare_rows(k, carry):
            for q in range(rows // times):
                ref, base = (even_ref, 0) if q < first // times else (odd_ref, first)
                prepare(ref, base, q * times - base + k, q)
            return carry

        lax.fori_loop(0, times, prepare_rows, 0)

    @pl.when(half == 0)
    def _():
        prepare_all(own_ref, other_ref)

    @pl.when(half != 0)
    def _():
        prepare_all(other_ref, own_ref)

    lab = jnp.transpose(lab_ref[...].astype(F32))
    lane = lax.broadcasted_iota(jnp.int32, (cols, 128), 1)
    want = jnp.where(lane < 3 * entries, lane % entries, -1).astype(F32)
    for r in range(rows):
        member[r] = (lab[:, r : r + 1] == want).astype(BF16)
    bias = b_ref[...]
    size = block * cols

    def step(k, sums):
        r0 = k * block
        lhs = jnp.concatenate([taps[pl.ds(r0 + dr, block)] for dr in range(3)], axis=-1)
        v = jnp.dot(lhs.reshape(size, 9 * chans), w_ref[...], preferred_element_type=F32) + bias
        sig = jax.nn.sigmoid(v)
        features = (v * sig).astype(BF16)
        slope[pl.ds(k * size, size)] = sig * (1.0 + v * (1.0 - sig))
        mem = member[pl.ds(r0, block)].reshape(size, 128)
        return sums + lax.dot_general(
            mem, features, (((0,), (0,)), ((), ())), preferred_element_type=F32
        )[:entries]

    sums_ref[...] = lax.fori_loop(0, rows // block, step, jnp.zeros((entries, width), F32))


def deep_forward(where, own, other, edges, w, b, labels, entries):
    _, cols, chans = own.shape
    rows, width = labels.shape[0], w.shape[-1]
    block = next(k for k in (8, 4, 2, 1) if rows % k == 0)
    first, second = shares(rows)
    slots = rows // math.gcd(first, second)
    return pl.pallas_call(
        functools.partial(deep_kernel, block=block, entries=entries),
        out_shape=(
            jax.ShapeDtypeStruct((rows + 2, cols, 3 * chans), BF16),
            jax.ShapeDtypeStruct((rows, cols, 128), BF16),
            jax.ShapeDtypeStruct((rows * cols, width), F32),
            jax.ShapeDtypeStruct((entries, width), F32),
        ),
        in_specs=[SMEM] + [VMEM] * 6,
        out_specs=(VMEM,) * 4,
        scratch_shapes=[pltpu.VMEM((slots * (chans // 128), cols + 16, 128), F32)],
        compiler_params=params(16),
        cost_estimate=pl.CostEstimate(
            flops=4 * rows * cols * 9 * chans * width, bytes_accessed=8 << 20, transcendentals=0
        ),
        name="deep_forward",
    )(where, own, other, edges, w, b, labels)


def grad_kernel(
    where_ref, taps, member, slope, sums_ref, *refs, n_parts, chunk, ways, with_sums
):
    part_refs = refs[:n_parts]
    out_refs = refs[n_parts : n_parts + ways]
    grad, weight = refs[n_parts + ways :]
    rows, cols, depth = member.shape[0], taps.shape[1], taps.shape[2]
    width = slope.shape[-1]
    me = where_ref[3]
    entries = sums_ref.shape[0]
    owned = part_refs[0].shape[1] - SIDE
    own_ids = jnp.broadcast_to(part_refs[0][0, owned : owned + 1, :entries], (entries, entries))
    across = lax.broadcasted_iota(jnp.int32, (entries, entries), 1)
    down = lax.broadcasted_iota(jnp.int32, (entries, entries), 0)
    ids = jnp.sum(jnp.where(across == down, own_ids, 0.0), axis=1, keepdims=True).astype(jnp.int32)
    total = jnp.zeros((entries, 1), F32)
    entry_grad = jnp.zeros((entries, width), F32)
    owner, inner = ids // owned, ids % owned
    spot = lax.broadcasted_iota(jnp.int32, (entries, owned), 1)
    for m, ref, k in relative(part_refs):
        there = ref[k, owned : owned + 1, :entries] == ids.astype(F32)
        counts = ref[k, owned + 1 : owned + 2, :entries]
        total += jnp.sum(jnp.where(there, counts, 0.0), axis=1, keepdims=True)
        hot = ((owner ^ me) == m) & (inner == spot)
        entry_grad += jnp.dot(
            hot.astype(F32), ref[k, :owned], precision=lax.Precision.HIGHEST, preferred_element_type=F32
        )
    entry_grad = entry_grad / jnp.maximum(total, 1.0)
    high = entry_grad.astype(BF16)
    rest = entry_grad - high.astype(F32)
    mid = rest.astype(BF16)
    low = (rest - mid.astype(F32)).astype(BF16)
    terms = jnp.concatenate([high, mid, low, jnp.zeros((128 - 3 * entries, width), BF16)], axis=0)
    pixel = jnp.dot(member[...].reshape(rows * cols, 128), terms, preferred_element_type=F32)
    dg = (pixel * slope[...]).astype(BF16)
    grad[...] = dg
    bias_sum = jnp.sum(dg.astype(F32), axis=0, keepdims=True)
    for dr in range(3):
        window = taps[dr : dr + rows].reshape(rows * cols, depth)
        out = lax.dot_general(grad[...], window, (((0,), (0,)), ((), ())), preferred_element_type=F32)
        weight[dr * depth : (dr + 1) * depth] = jnp.transpose(out)
    if weight.shape[0] > 3 * depth:
        weight[3 * depth :] = jnp.zeros((weight.shape[0] - 3 * depth, width), F32)
    sums = sums_ref[...]
    power, power_sums = scale_rows(weight[...], bias_sum, sums)
    up = jnp.exp2(12.0 - power)
    note = note_block(bias_sum * up, power, power_sums, width)
    digit = lax.rem(me, ways)
    heads = weight.shape[0] // chunk // ways
    for m in range(ways):
        for hi in range(heads):
            j = hi * ways + (digit ^ m)
            out_refs[m][hi * chunk : (hi + 1) * chunk] = (
                weight[pl.ds(pl.multiple_of(j * chunk, 8), chunk)] * up
            )
        out_refs[m][heads * chunk : heads * chunk + NOTE] = note
    sums = sums * jnp.exp2(12.0 - power_sums)
    for m in with_sums:
        out_refs[m][heads * chunk + NOTE :] = sums


def deep_backward(where, forward, parts, chunk, count, ways, with_sums):
    taps, _, slope, sums = forward
    width, entries = slope.shape[-1], sums.shape[0]
    size = count // ways * chunk + NOTE
    return pl.pallas_call(
        functools.partial(
            grad_kernel, n_parts=len(parts), chunk=chunk, ways=ways, with_sums=with_sums
        ),
        out_shape=tuple(
            jax.ShapeDtypeStruct((size + (entries if m in with_sums else 0), width), F32)
            for m in range(ways)
        ),
        in_specs=[SMEM] + [VMEM] * (4 + len(parts)),
        out_specs=(VMEM,) * ways,
        scratch_shapes=[
            pltpu.VMEM(slope.shape, BF16),
            pltpu.VMEM((count * chunk, width), F32),
        ],
        compiler_params=params(16),
        cost_estimate=pl.CostEstimate(
            flops=4 * slope.shape[0] * 3 * taps.shape[2] * width, bytes_accessed=8 << 20, transcendentals=0
        ),
        name="deep_backward",
    )(where, *forward, *parts)


def pair_kernel(own_ref, got_ref, own_sums_ref, got_sums_ref, *refs, size, entries):
    out_ref = refs[-1]
    own, got = own_ref[size : size + NOTE], got_ref[size : size + NOTE]
    power = jnp.maximum(own[1:2], got[1:2]) + 1.0
    power_sums = jnp.maximum(own[2:3], got[2:3])
    own_down, got_down = jnp.exp2(own[1:2] - power), jnp.exp2(got[1:2] - power)
    out_ref[:size] = own_ref[:size] * own_down + got_ref[:size] * got_down
    bias = own[0:1] * own_down + got[0:1] * got_down
    out_ref[size : size + NOTE] = note_block(bias, power, power_sums, own.shape[-1])
    at = size + NOTE
    sums = own_sums_ref[at : at + entries] * jnp.exp2(own[2:3] - power_sums)
    out_ref[at : at + entries] = sums
    sums = got_sums_ref[at : at + entries] * jnp.exp2(got[2:3] - power_sums)
    out_ref[at + entries : at + 2 * entries] = sums


def merge_pair(own, got, own_sums, got_sums, size, entries, after):
    width = own.shape[-1]
    return pl.pallas_call(
        functools.partial(pair_kernel, size=size, entries=entries),
        out_shape=jax.ShapeDtypeStruct((size + NOTE + 2 * entries, width), F32),
        in_specs=[VMEM] * 4 + [ANY] * len(after),
        out_specs=VMEM,
        compiler_params=params(),
        cost_estimate=pl.CostEstimate(flops=0, bytes_accessed=32 << 20, transcendentals=0),
        name="merge_pair",
    )(own, got, own_sums, got_sums, *after)


def merge_kernel(where_ref, *refs, plan, chunk, heads, entries, shift, next_ways):
    n_parts = len(plan)
    part_refs, out_refs, sums_ref = refs[:n_parts], refs[n_parts:-1], refs[-1]
    width = part_refs[0].shape[-1]
    size = heads * chunk
    total, bias = jnp.zeros((size, width), F32), jnp.zeros((1, width), F32)
    for ref, (added, members) in zip(part_refs, plan):
        more, down, down_sums = read_note(ref, size)
        if added:
            total, bias = total + ref[:size] * down, bias + more
        for k, m in enumerate(members):
            at = size + NOTE + k * entries
            sums_ref[m * entries : (m + 1) * entries] = ref[at : at + entries] * down_sums
    sums = sums_ref[...]
    power, power_sums = scale_rows(total, bias, sums)
    up = jnp.exp2(12.0 - power)
    note = note_block(bias * up, power, power_sums, width)
    total = total * up
    if next_ways == 1:
        out_refs[0][:size] = total
        out_refs[0][size:] = note
        return
    sums = sums * jnp.exp2(12.0 - power_sums)
    digit = lax.rem(where_ref[3] >> shift, next_ways)
    for m in range(next_ways):
        for hi in range(heads // next_ways):
            piece = jnp.zeros((chunk, width), F32)
            for d in range(next_ways):
                at = (hi * next_ways + d) * chunk
                piece = jnp.where((digit ^ m) == d, total[at : at + chunk], piece)
            out_refs[m][hi * chunk : (hi + 1) * chunk] = piece
        at = heads // next_ways * chunk
        out_refs[m][at : at + NOTE] = note
        out_refs[m][at + NOTE :] = sums


def merge(where, parts, chunk, heads, entries, shift, next_ways):
    width = parts[0][0].shape[-1]
    sums_rows = sum(len(members) for _, _, members in parts) * entries
    if next_ways == 1:
        outs = (jax.ShapeDtypeStruct((heads * chunk + NOTE, width), F32),)
    else:
        rows = heads // next_ways * chunk + NOTE + sums_rows
        outs = (jax.ShapeDtypeStruct((rows, width), F32),) * next_ways
    outs = outs + (jax.ShapeDtypeStruct((sums_rows, width), F32),)
    out = pl.pallas_call(
        functools.partial(
            merge_kernel,
            plan=tuple((added, tuple(members)) for _, added, members in parts),
            chunk=chunk,
            heads=heads,
            entries=entries,
            shift=shift,
            next_ways=next_ways,
        ),
        out_shape=outs,
        in_specs=[SMEM] + [VMEM] * len(parts),
        out_specs=(VMEM,) * len(outs),
        compiler_params=params(),
        name="merge",
    )(where, *(part for part, _, _ in parts))
    return out[:-1], out[-1]


def embed_kernel(where_ref, sums_ref, *refs, entries):
    part_refs, out_ref = refs[:-1], refs[-1]
    owned, width = out_ref.shape
    own = (where_ref[3] * owned + lax.broadcasted_iota(jnp.int32, (owned, entries), 0)).astype(F32)
    sums, counts = jnp.zeros((owned, width), F32), jnp.zeros((owned, 1), F32)
    for m, ref, k in relative(part_refs):
        there = ref[k, owned : owned + 1, :entries] == own
        count = ref[k, owned + 1 : owned + 2, :entries]
        counts += jnp.sum(jnp.where(there, count, 0.0), axis=1, keepdims=True)
        sums += jnp.dot(
            there.astype(F32),
            sums_ref[m * entries : (m + 1) * entries],
            precision=lax.Precision.HIGHEST,
            preferred_element_type=F32,
        )
    out_ref[...] = sums / jnp.maximum(counts, 1.0)


def spread_kernel(where_ref, *refs, chunk, rows):
    part_refs, weight_ref, bias_ref, place = refs[:-3], refs[-3], refs[-2], refs[-1]
    me = where_ref[3]
    whole = rows == place.shape[0]
    count = len(part_refs)
    for k, m in itertools.product(range(part_refs[0].shape[0]), range(count)):
        ref = part_refs[m]
        bias, down, _ = read_note(ref[k], chunk)
        j = me ^ (m + k * count)
        target = weight_ref if whole else place
        target[pl.ds(pl.multiple_of(j * chunk, 8), chunk)] = ref[k, :chunk] * down

        @pl.when(j == 0)
        def _():
            bias_ref[...] = bias

    if not whole:
        weight_ref[...] = place[:rows]


def spread(where, parts, chunk, count, rows):
    width = parts[0].shape[-1]
    return pl.pallas_call(
        functools.partial(spread_kernel, chunk=chunk, rows=rows),
        out_shape=(jax.ShapeDtypeStruct((rows, width), F32), jax.ShapeDtypeStruct((1, width), F32)),
        in_specs=[SMEM] + [VMEM] * len(parts),
        out_specs=(VMEM, VMEM),
        scratch_shapes=[pltpu.VMEM((count * chunk, width), F32)],
        compiler_params=params(),
        name="spread",
    )(where, *parts)


def body(
    section_input, conv_weight, conv_bias, deep_weight, deep_bias, labels, slot_ids, embed_grad
):
    chan_count = lax.axis_size("chan")
    strip_count = lax.axis_size("strip")
    chan_pos = lax.axis_index("chan")
    strip_pos = lax.axis_index("strip")
    half = chan_pos & 1
    channels = section_input.shape[-1]
    entries = slot_ids.shape[0]
    owned, width = embed_grad.shape
    where = jnp.stack(
        [half, (strip_pos == 0).astype(jnp.int32), (strip_pos == strip_count - 1).astype(jnp.int32), strip_pos]
    ).astype(jnp.int32)
    conv_w = conv_weight.reshape(9 * channels, -1)
    conv_b = conv_bias.reshape(1, -1)

    side, head, tail, sent = start(where, section_input, embed_grad, slot_ids, labels)
    pairs = []
    for s in range(strip_count):
        for c in range(chan_count):
            to = s + 1 - 2 * (c & 1)
            if 0 <= to < strip_count:
                pairs.append((s * chan_count + c, to * chan_count + c))
    got = lax.ppermute(sent, ("strip", "chan"), pairs)

    shared = gather_groups(side, "strip", high_groups(strip_count))

    taps, near_w = windows(where, section_input, conv_w)
    got, joined = lax.optimization_barrier((got, join(shared, [taps])))
    traded = swap(got, "chan", 1)
    shared = [joined, swap(joined, "strip", 1)]
    pooled = conv_pool(where, taps, near_w, conv_b, section_input.shape[0] // 4, [joined, got])
    other = swap(pooled, "chan", 1)
    edges = conv_edges(where, near_w, conv_b, got, traded, head, tail, [pooled])

    chunk = -(-9 * channels // strip_count // 8) * 8
    bits = strip_count.bit_length() - 1
    pieces = 1 << min(2, bits - 1)
    ways = 2 * pieces
    far = list(range(2, pieces))
    with_sums = {2, 3} | {2 * k + 1 for k in far[:1]}
    forward = deep_forward(
        where,
        pooled,
        other,
        edges,
        deep_weight.reshape(9 * channels, width),
        deep_bias.reshape(1, width),
        labels,
        entries,
    )
    send = deep_backward(where, forward, shared, chunk, strip_count, ways, with_sums)
    heads = strip_count // ways
    got = {k: swap(send[2 * k + 1].astype(F16), "strip", 1).astype(F32) for k in far}
    parts = [(send[0], True, [])]
    for m in range(1, min(4, ways)):
        sent = swap(send[m].astype(F16), "strip", m).astype(F32)
        parts.append((sent, True, [m] if m in with_sums else []))
    before = [part for part, _, members in parts if members == [2]]
    for k in far:
        own_sums, got_sums = send[2 * far[0] + 1], got[far[0]]
        pair = merge_pair(send[2 * k], got[k], own_sums, got_sums, heads * chunk, entries, before)
        before = [pair]
        sent = swap(pair.astype(F16), "strip", 2 * k).astype(F32)
        parts.append((sent, True, [2 * k, 2 * k + 1]))
        if k == far[0]:
            parts += [(own_sums, False, [0]), (got_sums, False, [1])]
    held, shift = ways, ways.bit_length() - 1
    while True:
        size = min(3, bits - shift)
        send, sums = merge(where, parts, chunk, heads, entries, shift, 1 << size)
        if size == 0:
            break
        more = 1 << size
        heads //= more
        arrived = [send[0]] + [
            swap(send[m].astype(F16), "strip", m << shift).astype(F32) for m in range(1, more)
        ]
        parts = [
            (part, True, list(range(m * held, (m + 1) * held))) for m, part in enumerate(arrived)
        ]
        held *= more
        shift += size
    embeddings = pl.pallas_call(
        functools.partial(embed_kernel, entries=entries),
        out_shape=jax.ShapeDtypeStruct((owned, width), F32),
        in_specs=[SMEM] + [VMEM] * (1 + len(shared)),
        out_specs=VMEM,
        compiler_params=params(),
        name="embed",
    )(where, sums, *shared)
    high = [(at, min(3, bits - at)) for at in range(ways.bit_length() - 1, bits, 3)]
    own = gather_groups(send[0].astype(F16)[None], "strip", high)
    own = own[0] if len(own) == 1 else jnp.concatenate(own, axis=0)
    gathered = [own] + [swap(own, "strip", m) for m in range(1, min(4, ways))]
    for k in far:
        direct = swap(own, "strip", 2 * k)
        gathered += [direct, swap(direct, "strip", 1)]
    weight_rows, bias_row = spread(
        where, [g.astype(F32) for g in gathered], chunk, strip_count, 9 * channels
    )
    return (embeddings, weight_rows.reshape(3, 3, channels, width), bias_row[0])


def solution(mesh):
    placed = (
        P(None, "strip", None),
        P(),
        P(),
        P(None, None, None, "chan"),
        P("chan"),
        P(None, "strip"),
        P("strip"),
        P("strip", "chan"),
    )
    return jax.shard_map(
        body,
        mesh=mesh,
        in_specs=placed,
        out_specs=(P("strip", "chan"), P(None, None, None, "chan"), P("chan")),
        check_vma=False,
    )
```

```python
import functools
import itertools
import math

import jax
import jax.numpy as jnp
from jax import lax
from jax.experimental import pallas as pl
from jax.experimental.pallas import tpu as pltpu
from jax.sharding import PartitionSpec as P

F32, BF16, F16 = jnp.float32, jnp.bfloat16, jnp.float16
VMEM = pl.BlockSpec(memory_space=pltpu.VMEM)
SMEM = pl.BlockSpec(memory_space=pltpu.SMEM)
HBM = pl.BlockSpec(memory_space=pltpu.HBM)
ANY = pl.BlockSpec(memory_space=pl.ANY)
SIDE = 8
WIDTH = 3
PIECE = 4
STEP = 6
NOTE = 16


def params(mib=8):
    return pltpu.CompilerParams(vmem_limit_bytes=mib << 20)


def swap(value, axis, mask):
    count = lax.axis_size(axis)
    return lax.ppermute(value, axis, [(i, i ^ mask) for i in range(count)])


def gather_step(held, axis, step):
    shift, size = step
    return [held] + [swap(held, axis, m << shift) for m in range(1, 1 << size)]


def relative(refs):
    half = len(refs) // 2
    for low in range(2):
        m = low
        for ref in refs[low * half : (low + 1) * half]:
            for k in range(ref.shape[0]):
                yield m, ref, k
                m += 2


def shares(pooled_rows):
    first = pooled_rows // 2
    return first, pooled_rows - first


def pick(half, pair):
    return jnp.where(half == 0, pair[0], pair[1])


def window_kernel(where_ref, x_hbm, w_hbm, taps, w_ref, rows_ref, wide, sems):
    rows, cols, chans = x_hbm.shape
    half_cols = cols // 2
    half = where_ref[0]
    first, second = shares(rows // 2)
    counts = [-(-(2 * n + 1) // PIECE) for n in (first, second)]
    pieces = pick(half, counts)
    start = pick(half, (0, rows - counts[1] * PIECE))
    shift = pick(half, (PIECE + 1, PIECE - (2 * first - 1 - (rows - counts[1] * PIECE))))

    def piece(k):
        at = pl.ds(k * PIECE, PIECE)
        return pltpu.make_async_copy(
            x_hbm.at[pl.ds(start + k * PIECE, PIECE)], rows_ref.at[at], sems.at[k]
        )

    def begin(k, carry):
        piece(k).start()
        return carry

    lax.fori_loop(0, pieces, begin, 0)
    weights = pltpu.make_async_copy(w_hbm, w_ref, sems.at[sems.shape[0] - 1])
    weights.start()
    lanes = chans // 128
    border = jnp.zeros((8, 128), F32)
    for t in range(wide.shape[0]):
        wide[t, 0:8] = border
        wide[t, cols + 8 : cols + 16] = border

    def prepare(k, carry):
        piece(k).wait()
        for slot in range(PIECE):
            r = k * PIECE + slot
            x = rows_ref[r].astype(F32)
            for t in range(lanes):
                wide[slot * lanes + t, 8 : 8 + cols] = x[:, t * 128 : (t + 1) * 128]
            for tap in range(4):
                for t in range(lanes):
                    part = wide[slot * lanes + t, pl.ds(7 + tap, half_cols, stride=2), :]
                    at = (tap * lanes + t) * 128
                    taps[r + shift, :, at : at + 128] = part.astype(BF16)
        return carry

    lax.fori_loop(0, pieces, prepare, 0)
    outside = pick(half, (PIECE, PIECE + 2 * second + 1))
    taps[outside] = jnp.zeros(taps.shape[1:], BF16)
    weights.wait()


def windows(where, x, w):
    rows, cols, chans = x.shape
    first, _ = shares(rows // 2)
    most = -(-(2 * first + 1) // PIECE)
    return pl.pallas_call(
        window_kernel,
        out_shape=(
            jax.ShapeDtypeStruct(((most + 2) * PIECE, cols // 2, 4 * chans), BF16),
            jax.ShapeDtypeStruct(w.shape, BF16),
        ),
        in_specs=[SMEM, HBM, HBM],
        out_specs=(VMEM, VMEM),
        scratch_shapes=[
            pltpu.VMEM((most * PIECE, cols, chans), BF16),
            pltpu.VMEM((PIECE * (chans // 128), cols + 16, 128), F32),
            pltpu.SemaphoreType.DMA((most + 1,)),
        ],
        compiler_params=params(16),
        cost_estimate=pl.CostEstimate(flops=0, bytes_accessed=12 << 20, transcendentals=0),
        name="windows",
    )(where, *(pltpu.with_memory_space_constraint(a, pltpu.HBM) for a in (x, w)))


def edge_part(where_ref, pairs, w_ref, bias, edge_ref, acc):
    rows = pairs[0].shape[0]
    chans = w_ref.shape[1]
    lanes = chans // 128
    depth = 3 * chans
    lhs = jnp.concatenate(
        [
            pairs[s][:, (2 * j + phase) * chans : (2 * j + phase + 3) * chans]
            for s in range(2)
            for j in range(2)
            for phase in range(2)
        ],
        axis=0,
    )
    pad = rows + 16
    for dr in range(3):
        part = jnp.dot(lhs, w_ref[dr * depth : (dr + 1) * depth], preferred_element_type=F32)
        for g in range(8):
            own = part[g * rows : (g + 1) * rows]
            for t in range(lanes):
                at = 9 - dr
                piece = own[:, t * 128 : (t + 1) * 128]
                if dr == 0:
                    acc[g * lanes + t, 0:8] = jnp.zeros((8, 128), F32)
                    acc[g * lanes + t, 8 + rows : pad] = jnp.zeros((8, 128), F32)
                    acc[g * lanes + t, 8:9] = jnp.zeros((1, 128), F32)
                    acc[g * lanes + t, at : at + rows] = piece
                else:
                    acc[g * lanes + t, at : at + rows] += piece
    for g in range(4):
        for t in range(lanes):
            total = None
            for phase in range(2):
                at = (2 * g + phase) * lanes + t
                v = acc[at, 8 : 8 + rows] + bias[:, t * 128 : (t + 1) * 128]
                acc[at, 8 : 8 + rows] = v * jax.nn.sigmoid(v)
                both = (
                    acc[at, pl.ds(8, rows // 2, stride=2), :]
                    + acc[at, pl.ds(9, rows // 2, stride=2), :]
                )
                total = both if total is None else total + both
            lost = jnp.where(g == 0, where_ref[1], jnp.where(g == 3, where_ref[2], 0))
            keep = jnp.where(lost > 0, 0.0, 0.25)
            edge_ref[g, t] = (total * keep).astype(BF16).astype(F32)


def conv_kernel(where_ref, taps, w_ref, b_ref, *refs):
    out_ref = refs[-1]
    assert out_ref.shape[0] % STEP == 0
    half_cols, chans = taps.shape[1], taps.shape[2] // 4
    bias = b_ref[...]

    def step(k, carry):
        r0 = PIECE + k * 2 * STEP
        total = None
        for phase in range(2):
            lhs = jnp.concatenate(
                [
                    taps[pl.ds(r0 + dr, 2 * STEP), :, phase * chans : (phase + 3) * chans]
                    for dr in range(3)
                ],
                axis=-1,
            ).reshape(2 * STEP * half_cols, 9 * chans)
            v = jnp.dot(lhs, w_ref[...], preferred_element_type=F32) + bias
            h = (v * jax.nn.sigmoid(v)).reshape(STEP, 2, half_cols, chans)
            h = h[:, 0] + h[:, 1]
            total = h if total is None else total + h
        out_ref[pl.ds(k * STEP, STEP)] = (total * 0.25).astype(BF16)
        return carry

    lax.fori_loop(0, out_ref.shape[0] // STEP, step, 0)


def conv_pool(where, taps, w, b, pooled_rows, after):
    _, half_cols, width = taps.shape
    chans = width // 4
    return pl.pallas_call(
        conv_kernel,
        out_shape=jax.ShapeDtypeStruct((pooled_rows, half_cols, chans), BF16),
        in_specs=[SMEM] + [VMEM] * 3 + [ANY] * len(after),
        out_specs=VMEM,
        compiler_params=params(16),
        cost_estimate=pl.CostEstimate(
            flops=8 * pooled_rows * half_cols * 9 * chans * chans,
            bytes_accessed=8 << 20,
            transcendentals=0,
        ),
        name="conv_pool",
    )(where, taps, w, b, *after)


def edge_kernel(where_ref, w_ref, b_ref, got_ref, traded_ref, head_ref, tail_ref, *refs):
    edge_ref, acc = refs[-2:]
    half = where_ref[0]
    got, traded = got_ref[...], traded_ref[...]
    left = jnp.concatenate([jnp.where(half == 0, got, traded), head_ref[...]], axis=-1)
    right = jnp.concatenate([tail_ref[...], jnp.where(half == 0, traded, got)], axis=-1)
    edge_part(where_ref, (left, right), w_ref, b_ref[...], edge_ref, acc)


def conv_edges(where, w, b, got, traded, head, tail, after):
    rows, lanes = head.shape[0], w.shape[1] // 128
    return pl.pallas_call(
        edge_kernel,
        out_shape=jax.ShapeDtypeStruct((4, lanes, rows // 2, 128), F32),
        in_specs=[SMEM] + [VMEM] * 6 + [ANY] * len(after),
        out_specs=VMEM,
        scratch_shapes=[pltpu.VMEM((8 * lanes, rows + 16, 128), F32)],
        compiler_params=params(),
        cost_estimate=pl.CostEstimate(flops=0, bytes_accessed=4 << 20, transcendentals=0),
        name="conv_edges",
    )(where, w, b, got, traded, head, tail, *after)


def start_kernel(
    where_ref, x_hbm, grad_hbm, labels_hbm, slots_hbm, side_ref, head_ref, tail_ref, send_ref,
    labels_ref, slots_ref, left, right, wide, sems,
):
    owned, width = grad_hbm.shape
    rows, cols, chans = x_hbm.shape
    entries = slots_ref.shape[1]
    reach = left.shape[1]
    half = where_ref[0]
    copies = [
        pltpu.make_async_copy(labels_hbm, labels_ref, sems.at[0]),
        pltpu.make_async_copy(grad_hbm, side_ref.at[0, pl.ds(0, owned)], sems.at[1]),
        pltpu.make_async_copy(x_hbm.at[:, pl.ds(0, reach)], left, sems.at[2]),
        pltpu.make_async_copy(x_hbm.at[:, pl.ds(cols - reach, reach)], right, sems.at[3]),
        pltpu.make_async_copy(slots_hbm, slots_ref, sems.at[4]),
    ]
    for copy in copies:
        copy.start()
    lane = lax.broadcasted_iota(jnp.int32, (1, width), 1)
    copies[0].wait()
    copies[4].wait()
    ids = jnp.concatenate(
        [slots_ref[...].astype(F32), jnp.zeros((1, width - entries), F32)], axis=1
    )
    labels = labels_ref[...]
    counts = jnp.zeros((1, width), F32)
    for e in range(entries):
        hit = jnp.where(labels == e, 1.0, 0.0)
        hit = jnp.sum(jnp.sum(hit, axis=0, keepdims=True), axis=1, keepdims=True)
        counts = jnp.where(lane == e, hit, counts)
    row = lax.broadcasted_iota(jnp.int32, (SIDE, width), 0)
    side_ref[0, owned:] = jnp.where(row == 0, ids, jnp.where(row == 1, counts, 0.0))
    lanes = chans // 128
    copies[2].wait()
    copies[3].wait()
    for ref, out_ref, at, sent in ((left, head_ref, 0, 1), (right, tail_ref, reach - WIDTH, 0)):
        x = ref[...].astype(F32).reshape(rows * reach, chans)
        for t in range(lanes):
            wide[t] = x[:, t * 128 : (t + 1) * 128]
        for c in range(WIDTH):
            for t in range(lanes):
                part = wide[t, pl.ds(at + c, rows, stride=reach), :].astype(BF16)
                place = (c * lanes + t) * 128
                out_ref[:, place : place + 128] = part
    send_ref[...] = jnp.where(half == 0, tail_ref[...], head_ref[...])
    copies[1].wait()


def start(where, x, grad, slots, labels):
    owned, width = grad.shape
    rows, _, chans = x.shape
    reach = 16
    columns = jax.ShapeDtypeStruct((rows, WIDTH * chans), BF16)
    fixed = [
        pltpu.with_memory_space_constraint(a, pltpu.HBM)
        for a in (x, grad, labels, slots.reshape(1, -1))
    ]
    return pl.pallas_call(
        start_kernel,
        out_shape=(jax.ShapeDtypeStruct((1, owned + SIDE, width), F32),) + (columns,) * 3,
        in_specs=[SMEM, HBM, HBM, HBM, HBM],
        out_specs=(VMEM,) * 4,
        scratch_shapes=[
            pltpu.VMEM(labels.shape, jnp.int32),
            pltpu.VMEM((1, slots.shape[0]), jnp.int32),
            pltpu.VMEM((rows, reach, chans), BF16),
            pltpu.VMEM((rows, reach, chans), BF16),
            pltpu.VMEM((chans // 128, rows * reach, 128), F32),
            pltpu.SemaphoreType.DMA((5,)),
        ],
        compiler_params=params(),
        name="start",
    )(where, *fixed)


def join_kernel(*refs, count):
    at = 0
    for ref in refs[:count]:
        refs[-1][at : at + ref.shape[0]] = ref[...]
        at += ref.shape[0]


def join(parts, after):
    shape = (sum(p.shape[0] for p in parts),) + parts[0].shape[1:]
    return pl.pallas_call(
        functools.partial(join_kernel, count=len(parts)),
        out_shape=jax.ShapeDtypeStruct(shape, F32),
        in_specs=[VMEM] * len(parts) + [ANY] * len(after),
        out_specs=VMEM,
        compiler_params=params(),
        name="join",
    )(*parts, *after)


def scale_rows(block, note_rows, sums):
    def exponent(values):
        top = None
        for v in values:
            one = jnp.max(jnp.max(jnp.abs(v), axis=0, keepdims=True), axis=1, keepdims=True)
            top = one if top is None else jnp.maximum(top, one)
        return jnp.ceil(jnp.log2(jnp.maximum(top, 1e-30)))

    power = exponent([block, note_rows])
    power_sums = exponent([sums])
    return power, power_sums


def note_block(bias, power, power_sums, width):
    row = lax.broadcasted_iota(jnp.int32, (NOTE, width), 0)
    bias = jnp.broadcast_to(bias, (NOTE, width))
    power = jnp.broadcast_to(power, (NOTE, width))
    power_sums = jnp.broadcast_to(power_sums, (NOTE, width))
    return jnp.where(row == 0, bias, jnp.where(row == 1, power, power_sums))


def read_note(part, at):
    note = part[at : at + NOTE]
    down = jnp.exp2(note[1:2] - 12.0)
    return note[0:1] * down, down, jnp.exp2(note[2:3] - 12.0)


def deep_kernel(
    where_ref, own_ref, other_ref, edge_ref, w_ref, b_ref, lab_ref, taps, member, slope, sums_ref, wide,
    *, block, entries
):
    _, cols, chans = own_ref.shape
    rows = lab_ref.shape[0]
    lanes = chans // 128
    width = w_ref.shape[-1]
    half = where_ref[0]
    taps[0] = jnp.zeros(taps.shape[1:], BF16)
    taps[rows + 1] = jnp.zeros(taps.shape[1:], BF16)

    def prepare(ref, base, i, slot):
        x = ref[i].astype(F32)
        r = base + i
        for t in range(lanes):
            s = slot * lanes + t
            at = t * 128
            wide[s, 8 : 8 + cols] = x[:, at : at + 128]
            for g, place in enumerate((7, 8, 7 + cols, 8 + cols)):
                wide[s, place : place + 1] = edge_ref[g, t, pl.ds(r, 1), :]
        for tap in range(3):
            for t in range(lanes):
                piece = wide[slot * lanes + t, 7 + tap : 7 + tap + cols, :]
                at = (tap * lanes + t) * 128
                taps[r + 1, :, at : at + 128] = piece.astype(BF16)

    first, second = shares(rows)
    times = math.gcd(first, second)

    def prepare_all(even_ref, odd_ref):
        def prepare_rows(k, carry):
            for q in range(rows // times):
                ref, base = (even_ref, 0) if q < first // times else (odd_ref, first)
                prepare(ref, base, q * times - base + k, q)
            return carry

        lax.fori_loop(0, times, prepare_rows, 0)

    @pl.when(half == 0)
    def _():
        prepare_all(own_ref, other_ref)

    @pl.when(half != 0)
    def _():
        prepare_all(other_ref, own_ref)

    lab = jnp.transpose(lab_ref[...].astype(F32))
    lane = lax.broadcasted_iota(jnp.int32, (cols, 128), 1)
    want = jnp.where(lane < 3 * entries, lane % entries, -1).astype(F32)
    for r in range(rows):
        member[r] = (lab[:, r : r + 1] == want).astype(BF16)
    bias = b_ref[...]
    size = block * cols

    def step(k, sums):
        r0 = k * block
        lhs = jnp.concatenate([taps[pl.ds(r0 + dr, block)] for dr in range(3)], axis=-1)
        v = jnp.dot(lhs.reshape(size, 9 * chans), w_ref[...], preferred_element_type=F32) + bias
        sig = jax.nn.sigmoid(v)
        features = (v * sig).astype(BF16)
        slope[pl.ds(k * size, size)] = sig * (1.0 + v * (1.0 - sig))
        mem = member[pl.ds(r0, block)].reshape(size, 128)
        return sums + lax.dot_general(
            mem, features, (((0,), (0,)), ((), ())), preferred_element_type=F32
        )[:entries]

    sums_ref[...] = lax.fori_loop(0, rows // block, step, jnp.zeros((entries, width), F32))


def deep_forward(where, own, other, edges, w, b, labels, entries):
    _, cols, chans = own.shape
    rows, width = labels.shape[0], w.shape[-1]
    block = next(k for k in (8, 4, 2, 1) if rows % k == 0)
    first, second = shares(rows)
    slots = rows // math.gcd(first, second)
    return pl.pallas_call(
        functools.partial(deep_kernel, block=block, entries=entries),
        out_shape=(
            jax.ShapeDtypeStruct((rows + 2, cols, 3 * chans), BF16),
            jax.ShapeDtypeStruct((rows, cols, 128), BF16),
            jax.ShapeDtypeStruct((rows * cols, width), F32),
            jax.ShapeDtypeStruct((entries, width), F32),
        ),
        in_specs=[SMEM] + [VMEM] * 6,
        out_specs=(VMEM,) * 4,
        scratch_shapes=[pltpu.VMEM((slots * (chans // 128), cols + 16, 128), F32)],
        compiler_params=params(16),
        cost_estimate=pl.CostEstimate(
            flops=4 * rows * cols * 9 * chans * width, bytes_accessed=8 << 20, transcendentals=0
        ),
        name="deep_forward",
    )(where, own, other, edges, w, b, labels)


def grad_kernel(
    where_ref, taps, member, slope, sums_ref, *refs, n_parts, chunk, ways, with_sums
):
    part_refs = refs[:n_parts]
    out_refs = refs[n_parts : n_parts + ways]
    grad, weight = refs[n_parts + ways :]
    rows, cols, depth = member.shape[0], taps.shape[1], taps.shape[2]
    width = slope.shape[-1]
    me = where_ref[3]
    entries = sums_ref.shape[0]
    owned = part_refs[0].shape[1] - SIDE
    own_ids = jnp.broadcast_to(part_refs[0][0, owned : owned + 1, :entries], (entries, entries))
    across = lax.broadcasted_iota(jnp.int32, (entries, entries), 1)
    down = lax.broadcasted_iota(jnp.int32, (entries, entries), 0)
    ids = jnp.sum(jnp.where(across == down, own_ids, 0.0), axis=1, keepdims=True).astype(jnp.int32)
    total = jnp.zeros((entries, 1), F32)
    entry_grad = jnp.zeros((entries, width), F32)
    owner, inner = ids // owned, ids % owned
    spot = lax.broadcasted_iota(jnp.int32, (entries, owned), 1)
    for m, ref, k in relative(part_refs):
        there = ref[k, owned : owned + 1, :entries] == ids.astype(F32)
        counts = ref[k, owned + 1 : owned + 2, :entries]
        total += jnp.sum(jnp.where(there, counts, 0.0), axis=1, keepdims=True)
        hot = ((owner ^ me) == m) & (inner == spot)
        entry_grad += jnp.dot(
            hot.astype(F32), ref[k, :owned], precision=lax.Precision.HIGHEST, preferred_element_type=F32
        )
    entry_grad = entry_grad / jnp.maximum(total, 1.0)
    high = entry_grad.astype(BF16)
    rest = entry_grad - high.astype(F32)
    mid = rest.astype(BF16)
    low = (rest - mid.astype(F32)).astype(BF16)
    terms = jnp.concatenate([high, mid, low, jnp.zeros((128 - 3 * entries, width), BF16)], axis=0)
    pixel = jnp.dot(member[...].reshape(rows * cols, 128), terms, preferred_element_type=F32)
    dg = (pixel * slope[...]).astype(BF16)
    grad[...] = dg
    bias_sum = jnp.sum(dg.astype(F32), axis=0, keepdims=True)
    for dr in range(3):
        window = taps[dr : dr + rows].reshape(rows * cols, depth)
        out = lax.dot_general(grad[...], window, (((0,), (0,)), ((), ())), preferred_element_type=F32)
        weight[dr * depth : (dr + 1) * depth] = jnp.transpose(out)
    if weight.shape[0] > 3 * depth:
        weight[3 * depth :] = jnp.zeros((weight.shape[0] - 3 * depth, width), F32)
    sums = sums_ref[...]
    power, power_sums = scale_rows(weight[...], bias_sum, sums)
    up = jnp.exp2(12.0 - power)
    note = note_block(bias_sum * up, power, power_sums, width)
    digit = lax.rem(me, ways)
    heads = weight.shape[0] // chunk // ways
    for m in range(ways):
        for hi in range(heads):
            j = hi * ways + (digit ^ m)
            out_refs[m][hi * chunk : (hi + 1) * chunk] = (
                weight[pl.ds(pl.multiple_of(j * chunk, 8), chunk)] * up
            )
        out_refs[m][heads * chunk : heads * chunk + NOTE] = note
    sums = sums * jnp.exp2(12.0 - power_sums)
    for m in with_sums:
        out_refs[m][heads * chunk + NOTE :] = sums


def deep_backward(where, forward, parts, chunk, count, ways, with_sums):
    taps, _, slope, sums = forward
    width, entries = slope.shape[-1], sums.shape[0]
    size = count // ways * chunk + NOTE
    return pl.pallas_call(
        functools.partial(
            grad_kernel, n_parts=len(parts), chunk=chunk, ways=ways, with_sums=with_sums
        ),
        out_shape=tuple(
            jax.ShapeDtypeStruct((size + (entries if m in with_sums else 0), width), F32)
            for m in range(ways)
        ),
        in_specs=[SMEM] + [VMEM] * (4 + len(parts)),
        out_specs=(VMEM,) * ways,
        scratch_shapes=[
            pltpu.VMEM(slope.shape, BF16),
            pltpu.VMEM((count * chunk, width), F32),
        ],
        compiler_params=params(16),
        cost_estimate=pl.CostEstimate(
            flops=4 * slope.shape[0] * 3 * taps.shape[2] * width, bytes_accessed=8 << 20, transcendentals=0
        ),
        name="deep_backward",
    )(where, *forward, *parts)


def pair_kernel(own_ref, got_ref, own_sums_ref, got_sums_ref, *refs, size, entries):
    out_ref = refs[-1]
    own, got = own_ref[size : size + NOTE], got_ref[size : size + NOTE]
    power = jnp.maximum(own[1:2], got[1:2]) + 1.0
    power_sums = jnp.maximum(own[2:3], got[2:3])
    own_down, got_down = jnp.exp2(own[1:2] - power), jnp.exp2(got[1:2] - power)
    out_ref[:size] = own_ref[:size] * own_down + got_ref[:size] * got_down
    bias = own[0:1] * own_down + got[0:1] * got_down
    out_ref[size : size + NOTE] = note_block(bias, power, power_sums, own.shape[-1])
    at = size + NOTE
    sums = own_sums_ref[at : at + entries] * jnp.exp2(own[2:3] - power_sums)
    out_ref[at : at + entries] = sums
    sums = got_sums_ref[at : at + entries] * jnp.exp2(got[2:3] - power_sums)
    out_ref[at + entries : at + 2 * entries] = sums


def merge_pair(own, got, own_sums, got_sums, size, entries, after):
    width = own.shape[-1]
    return pl.pallas_call(
        functools.partial(pair_kernel, size=size, entries=entries),
        out_shape=jax.ShapeDtypeStruct((size + NOTE + 2 * entries, width), F32),
        in_specs=[VMEM] * 4 + [ANY] * len(after),
        out_specs=VMEM,
        compiler_params=params(),
        cost_estimate=pl.CostEstimate(flops=0, bytes_accessed=32 << 20, transcendentals=0),
        name="merge_pair",
    )(own, got, own_sums, got_sums, *after)


def merge_kernel(where_ref, *refs, plan, chunk, heads, entries, shift, next_ways):
    n_parts = len(plan)
    part_refs, out_refs, sums_ref = refs[:n_parts], refs[n_parts:-1], refs[-1]
    width = part_refs[0].shape[-1]
    size = heads * chunk
    total, bias = jnp.zeros((size, width), F32), jnp.zeros((1, width), F32)
    for ref, (added, members) in zip(part_refs, plan):
        more, down, down_sums = read_note(ref, size)
        if added:
            total, bias = total + ref[:size] * down, bias + more
        for k, m in enumerate(members):
            at = size + NOTE + k * entries
            sums_ref[m * entries : (m + 1) * entries] = ref[at : at + entries] * down_sums
    sums = sums_ref[...]
    power, power_sums = scale_rows(total, bias, sums)
    up = jnp.exp2(12.0 - power)
    note = note_block(bias * up, power, power_sums, width)
    total = total * up
    if next_ways == 1:
        out_refs[0][:size] = total
        out_refs[0][size:] = note
        return
    sums = sums * jnp.exp2(12.0 - power_sums)
    digit = lax.rem(where_ref[3] >> shift, next_ways)
    for m in range(next_ways):
        for hi in range(heads // next_ways):
            piece = jnp.zeros((chunk, width), F32)
            for d in range(next_ways):
                at = (hi * next_ways + d) * chunk
                piece = jnp.where((digit ^ m) == d, total[at : at + chunk], piece)
            out_refs[m][hi * chunk : (hi + 1) * chunk] = piece
        at = heads // next_ways * chunk
        out_refs[m][at : at + NOTE] = note
        out_refs[m][at + NOTE :] = sums


def merge(where, parts, chunk, heads, entries, shift, next_ways):
    width = parts[0][0].shape[-1]
    sums_rows = sum(len(members) for _, _, members in parts) * entries
    if next_ways == 1:
        outs = (jax.ShapeDtypeStruct((heads * chunk + NOTE, width), F32),)
    else:
        rows = heads // next_ways * chunk + NOTE + sums_rows
        outs = (jax.ShapeDtypeStruct((rows, width), F32),) * next_ways
    outs = outs + (jax.ShapeDtypeStruct((sums_rows, width), F32),)
    out = pl.pallas_call(
        functools.partial(
            merge_kernel,
            plan=tuple((added, tuple(members)) for _, added, members in parts),
            chunk=chunk,
            heads=heads,
            entries=entries,
            shift=shift,
            next_ways=next_ways,
        ),
        out_shape=outs,
        in_specs=[SMEM] + [VMEM] * len(parts),
        out_specs=(VMEM,) * len(outs),
        compiler_params=params(),
        name="merge",
    )(where, *(part for part, _, _ in parts))
    return out[:-1], out[-1]


def embed_kernel(where_ref, sums_ref, *refs, entries):
    part_refs, out_ref = refs[:-1], refs[-1]
    owned, width = out_ref.shape
    own = (where_ref[3] * owned + lax.broadcasted_iota(jnp.int32, (owned, entries), 0)).astype(F32)
    sums, counts = jnp.zeros((owned, width), F32), jnp.zeros((owned, 1), F32)
    for m, ref, k in relative(part_refs):
        there = ref[k, owned : owned + 1, :entries] == own
        count = ref[k, owned + 1 : owned + 2, :entries]
        counts += jnp.sum(jnp.where(there, count, 0.0), axis=1, keepdims=True)
        sums += jnp.dot(
            there.astype(F32),
            sums_ref[m * entries : (m + 1) * entries],
            precision=lax.Precision.HIGHEST,
            preferred_element_type=F32,
        )
    out_ref[...] = sums / jnp.maximum(counts, 1.0)


def spread_kernel(where_ref, *refs, chunk, members):
    count = len(members)
    part_refs, before = refs[:count], refs[count:-4]
    weight_hbm, bias_ref, place, sems = refs[-4:]
    me = where_ref[3]
    bias_ref[...] = before[1][...] if before else jnp.zeros_like(bias_ref)
    copies = []
    for p, m in enumerate(members):
        bias, down, _ = read_note(part_refs[p][0], chunk)
        place[p * chunk : (p + 1) * chunk] = part_refs[p][0, :chunk] * down
        j = me ^ m
        copies.append(
            pltpu.make_async_copy(
                place.at[pl.ds(p * chunk, chunk)],
                weight_hbm.at[pl.ds(pl.multiple_of(j * chunk, 8), chunk)],
                sems.at[p],
            )
        )
        copies[p].start()

        @pl.when(j == 0)
        def _():
            bias_ref[...] = bias

    for copy in copies:
        copy.wait()


def spread(where, parts, before, chunk, count, rows):
    parts = {m: part.astype(F32) for m, part in parts.items()}
    width = next(iter(parts.values())).shape[-1]
    before = list(before)
    return pl.pallas_call(
        functools.partial(spread_kernel, chunk=chunk, members=tuple(parts)),
        out_shape=(jax.ShapeDtypeStruct((rows, width), F32), jax.ShapeDtypeStruct((1, width), F32)),
        in_specs=[SMEM] + [VMEM] * len(parts) + ([HBM, VMEM] if before else []),
        out_specs=(HBM, VMEM),
        scratch_shapes=[
            pltpu.VMEM((len(parts) * chunk, width), F32),
            pltpu.SemaphoreType.DMA((len(parts),)),
        ],
        input_output_aliases={1 + len(parts): 0} if before else {},
        compiler_params=params(),
        name="spread",
    )(where, *parts.values(), *before)


def spread_all_kernel(where_ref, *refs, chunk, rows, members):
    part_refs, weight_ref, bias_ref, place = refs[:-3], refs[-3], refs[-2], refs[-1]
    me = where_ref[3]
    count = len(members)
    for p, k in itertools.product(range(count), range(part_refs[0].shape[0])):
        bias, down, _ = read_note(part_refs[p][k], chunk)
        j = me ^ (members[p] + k * count)
        place[pl.ds(pl.multiple_of(j * chunk, 8), chunk)] = part_refs[p][k, :chunk] * down

        @pl.when(j == 0)
        def _():
            bias_ref[...] = bias

    weight_ref[...] = place[:rows]


def spread_all(where, parts, chunk, count, rows):
    parts = {m: part.astype(F32) for m, part in parts.items()}
    width = parts[0].shape[-1]
    return pl.pallas_call(
        functools.partial(spread_all_kernel, chunk=chunk, rows=rows, members=tuple(parts)),
        out_shape=(jax.ShapeDtypeStruct((rows, width), F32), jax.ShapeDtypeStruct((1, width), F32)),
        in_specs=[SMEM] + [VMEM] * len(parts),
        out_specs=(VMEM, VMEM),
        scratch_shapes=[pltpu.VMEM((count * chunk, width), F32)],
        compiler_params=params(),
        name="spread_all",
    )(where, *parts.values())


def body(
    section_input, conv_weight, conv_bias, deep_weight, deep_bias, labels, slot_ids, embed_grad
):
    chan_count = lax.axis_size("chan")
    strip_count = lax.axis_size("strip")
    chan_pos = lax.axis_index("chan")
    strip_pos = lax.axis_index("strip")
    half = chan_pos & 1
    channels = section_input.shape[-1]
    entries = slot_ids.shape[0]
    owned, width = embed_grad.shape
    where = jnp.stack(
        [half, (strip_pos == 0).astype(jnp.int32), (strip_pos == strip_count - 1).astype(jnp.int32), strip_pos]
    ).astype(jnp.int32)
    conv_w = conv_weight.reshape(9 * channels, -1)
    conv_b = conv_bias.reshape(1, -1)

    side, head, tail, sent = start(where, section_input, embed_grad, slot_ids, labels)
    pairs = []
    for s in range(strip_count):
        for c in range(chan_count):
            to = s + 1 - 2 * (c & 1)
            if 0 <= to < strip_count:
                pairs.append((s * chan_count + c, to * chan_count + c))
    got = lax.ppermute(sent, ("strip", "chan"), pairs)

    steps = [(at + 1, 1) for at in range(min(2, strip_count.bit_length() - 2))]
    steps += [(at, min(3, strip_count.bit_length() - 1 - at)) for at in range(3, strip_count.bit_length() - 1, 3)]
    ahead = gather_step(side, "strip", steps[0])
    taps, near_w = windows(where, section_input, conv_w)
    shared = join(ahead, [taps])
    got, shared = lax.optimization_barrier((got, shared))
    traded = swap(got, "chan", 1)
    ahead = gather_step(shared, "strip", steps[1])
    pooled = conv_pool(where, taps, near_w, conv_b, section_input.shape[0] // 4, [shared, got])
    pooled, shared = lax.optimization_barrier((pooled, join(ahead, [pooled])))
    other = swap(pooled, "chan", 1)
    for step in steps[2:]:
        shared = join(gather_step(shared, "strip", step), [])
    shared = [shared, swap(shared, "strip", 1)]
    edges = conv_edges(where, near_w, conv_b, got, traded, head, tail, [pooled])

    chunk = -(-9 * channels // strip_count // 8) * 8
    bits = strip_count.bit_length() - 1
    pieces = 1 << min(2, bits - 1)
    ways = 2 * pieces
    far = list(range(2, pieces))
    with_sums = {2, 3} | {2 * k + 1 for k in far[:1]}
    forward = deep_forward(
        where,
        pooled,
        other,
        edges,
        deep_weight.reshape(9 * channels, width),
        deep_bias.reshape(1, width),
        labels,
        entries,
    )
    send = deep_backward(where, forward, shared, chunk, strip_count, ways, with_sums)
    heads = strip_count // ways
    got = {k: swap(send[2 * k + 1].astype(F16), "strip", 1).astype(F32) for k in far}
    parts = [(send[0], True, [])]
    for m in range(1, min(4, ways)):
        sent = swap(send[m].astype(F16), "strip", m).astype(F32)
        parts.append((sent, True, [m] if m in with_sums else []))
    before = [part for part, _, members in parts if members == [2]]
    for k in far:
        own_sums, got_sums = send[2 * far[0] + 1], got[far[0]]
        pair = merge_pair(send[2 * k], got[k], own_sums, got_sums, heads * chunk, entries, before)
        before = [pair]
        sent = swap(pair.astype(F16), "strip", 2 * k).astype(F32)
        parts.append((sent, True, [2 * k, 2 * k + 1]))
        if k == far[0]:
            parts += [(own_sums, False, [0]), (got_sums, False, [1])]
    held, shift = ways, ways.bit_length() - 1
    while True:
        size = min(3, bits - shift)
        send, sums = merge(where, parts, chunk, heads, entries, shift, 1 << size)
        if size == 0:
            break
        more = 1 << size
        heads //= more
        arrived = [send[0]] + [
            swap(send[m].astype(F16), "strip", m << shift).astype(F32) for m in range(1, more)
        ]
        parts = [
            (part, True, list(range(m * held, (m + 1) * held))) for m, part in enumerate(arrived)
        ]
        held *= more
        shift += size
    embeddings = pl.pallas_call(
        functools.partial(embed_kernel, entries=entries),
        out_shape=jax.ShapeDtypeStruct((owned, width), F32),
        in_specs=[SMEM] + [VMEM] * (1 + len(shared)),
        out_specs=VMEM,
        compiler_params=params(),
        name="embed",
    )(where, sums, *shared)
    own = send[0].astype(F16)[None]
    for at in range(ways.bit_length() - 1, bits, 3):
        own = jnp.concatenate(gather_step(own, "strip", (at, min(3, bits - at))), axis=0)
    gathered = {m: swap(own, "strip", m) if m else own for m in range(min(4, ways))}
    for k in far:
        gathered[2 * k] = swap(own, "strip", 2 * k)
    late = {2 * k + 1: swap(gathered[2 * k], "strip", 1) for k in far}
    rows = 9 * channels
    if strip_count * chunk == rows and late:
        result = spread(where, gathered, [], chunk, strip_count, rows)
        weight_rows, bias_row = spread(where, late, result, chunk, strip_count, rows)
    else:
        weight_rows, bias_row = spread_all(where, {**gathered, **late}, chunk, strip_count, rows)
    return (embeddings, weight_rows.reshape(3, 3, channels, width), bias_row[0])


def solution(mesh):
    placed = (
        P(None, "strip", None),
        P(),
        P(),
        P(None, None, None, "chan"),
        P("chan"),
        P(None, "strip"),
        P("strip"),
        P("strip", "chan"),
    )
    return jax.shard_map(
        body,
        mesh=mesh,
        in_specs=placed,
        out_specs=(P("strip", "chan"), P(None, None, None, "chan"), P("chan")),
        check_vma=False,
    )
```

```python
import functools
import itertools
import math

import jax
import jax.numpy as jnp
from jax import lax
from jax.experimental import pallas as pl
from jax.experimental.pallas import tpu as pltpu
from jax.sharding import PartitionSpec as P

F32, BF16, F16 = jnp.float32, jnp.bfloat16, jnp.float16
VMEM = pl.BlockSpec(memory_space=pltpu.VMEM)
SMEM = pl.BlockSpec(memory_space=pltpu.SMEM)
HBM = pl.BlockSpec(memory_space=pltpu.HBM)
ANY = pl.BlockSpec(memory_space=pl.ANY)
SIDE = 8
WIDTH = 3
PIECE = 4
STEP = 6
NOTE = 16


def params(mib=8):
    return pltpu.CompilerParams(vmem_limit_bytes=mib << 20)


def swap(value, axis, mask):
    count = lax.axis_size(axis)
    return lax.ppermute(value, axis, [(i, i ^ mask) for i in range(count)])


def gather_step(held, axis, step):
    shift, size = step
    return [held] + [swap(held, axis, m << shift) for m in range(1, 1 << size)]


def relative(refs):
    half = len(refs) // 2
    for low in range(2):
        m = low
        for ref in refs[low * half : (low + 1) * half]:
            for k in range(ref.shape[0]):
                yield m, ref, k
                m += 2


def sigmoid(v):
    return jax.nn.sigmoid(v)


def shares(pooled_rows):
    first = pooled_rows // 2
    return first, pooled_rows - first


def pick(half, pair):
    return jnp.where(half == 0, pair[0], pair[1])


def share_rows(half, rows):
    first, second = shares(rows // 2)
    most = -(-(2 * max(first, second) + 1) // PIECE) * PIECE
    return most, pick(half, (0, rows - most)), pick(half, (-1, 2 * first - 1 - (rows - most)))


def window_kernel(where_ref, rows_ref, taps, wide, *, rows):
    most, cols, chans = rows_ref.shape
    half_cols = cols // 2
    half = where_ref[0]
    _, _, before = share_rows(half, rows)
    shift = PIECE - before
    lanes = chans // 128
    border = jnp.zeros((8, 128), F32)
    for t in range(wide.shape[0]):
        wide[t, 0:8] = border
        wide[t, cols + 8 : cols + 16] = border

    def prepare(k, carry):
        for slot in range(PIECE):
            r = k * PIECE + slot
            x = rows_ref[r].astype(F32)
            for t in range(lanes):
                wide[slot * lanes + t, 8 : 8 + cols] = x[:, t * 128 : (t + 1) * 128]
            for tap in range(4):
                for t in range(lanes):
                    part = wide[slot * lanes + t, pl.ds(7 + tap, half_cols, stride=2), :]
                    at = (tap * lanes + t) * 128
                    taps[r + shift, :, at : at + 128] = part.astype(BF16)
        return carry

    lax.fori_loop(0, most // PIECE, prepare, 0)
    second = shares(rows // 2)[1]
    outside = pick(half, (PIECE, PIECE + 2 * second + 1))
    taps[outside] = jnp.zeros(taps.shape[1:], BF16)


def windows(where, near_rows, rows):
    most, cols, chans = near_rows.shape
    return pl.pallas_call(
        functools.partial(window_kernel, rows=rows),
        out_shape=jax.ShapeDtypeStruct((most + 2 * PIECE, cols // 2, 4 * chans), BF16),
        in_specs=[SMEM, VMEM],
        out_specs=VMEM,
        scratch_shapes=[pltpu.VMEM((PIECE * (chans // 128), cols + 16, 128), F32)],
        compiler_params=params(16),
        cost_estimate=pl.CostEstimate(flops=0, bytes_accessed=12 << 20, transcendentals=0),
        name="windows",
    )(where, near_rows)


def edge_part(where_ref, pairs, w_ref, bias, edge_ref, acc):
    rows = pairs[0].shape[0]
    chans = w_ref.shape[1]
    lanes = chans // 128
    depth = 3 * chans
    lhs = jnp.concatenate(
        [
            pairs[s][:, (2 * j + phase) * chans : (2 * j + phase + 3) * chans]
            for s in range(2)
            for j in range(2)
            for phase in range(2)
        ],
        axis=0,
    )
    pad = rows + 16
    for dr in range(3):
        part = jnp.dot(lhs, w_ref[dr * depth : (dr + 1) * depth], preferred_element_type=F32)
        for g in range(8):
            own = part[g * rows : (g + 1) * rows]
            for t in range(lanes):
                at = 9 - dr
                piece = own[:, t * 128 : (t + 1) * 128]
                if dr == 0:
                    acc[g * lanes + t, 0:8] = jnp.zeros((8, 128), F32)
                    acc[g * lanes + t, 8 + rows : pad] = jnp.zeros((8, 128), F32)
                    acc[g * lanes + t, 8:9] = jnp.zeros((1, 128), F32)
                    acc[g * lanes + t, at : at + rows] = piece
                else:
                    acc[g * lanes + t, at : at + rows] += piece
    for g in range(4):
        for t in range(lanes):
            total = None
            for phase in range(2):
                at = (2 * g + phase) * lanes + t
                v = acc[at, 8 : 8 + rows] + bias[:, t * 128 : (t + 1) * 128]
                acc[at, 8 : 8 + rows] = v * sigmoid(v)
                both = (
                    acc[at, pl.ds(8, rows // 2, stride=2), :]
                    + acc[at, pl.ds(9, rows // 2, stride=2), :]
                )
                total = both if total is None else total + both
            lost = jnp.where(g == 0, where_ref[1], jnp.where(g == 3, where_ref[2], 0))
            keep = jnp.where(lost > 0, 0.0, 0.25)
            edge_ref[g, t] = (total * keep).astype(BF16).astype(F32)


def conv_kernel(where_ref, taps, w_ref, b_ref, *refs):
    out_ref = refs[-1]
    assert out_ref.shape[0] % STEP == 0
    half_cols, chans = taps.shape[1], taps.shape[2] // 4
    bias = b_ref[...]

    def step(k, carry):
        r0 = PIECE + k * 2 * STEP
        total = None
        for phase in range(2):
            lhs = jnp.concatenate(
                [
                    taps[pl.ds(r0 + dr, 2 * STEP), :, phase * chans : (phase + 3) * chans]
                    for dr in range(3)
                ],
                axis=-1,
            ).reshape(2 * STEP * half_cols, 9 * chans)
            v = jnp.dot(lhs, w_ref[...], preferred_element_type=F32) + bias
            h = (v * sigmoid(v)).reshape(STEP, 2, half_cols, chans)
            h = h[:, 0] + h[:, 1]
            total = h if total is None else total + h
        out_ref[pl.ds(k * STEP, STEP)] = (total * 0.25).astype(BF16)
        return carry

    for k in range(out_ref.shape[0] // STEP):
        step(k, 0)


def conv_pool(where, taps, w, b, pooled_rows, after):
    _, half_cols, width = taps.shape
    chans = width // 4
    return pl.pallas_call(
        conv_kernel,
        out_shape=jax.ShapeDtypeStruct((pooled_rows, half_cols, chans), BF16),
        in_specs=[SMEM] + [VMEM] * 3 + [ANY] * len(after),
        out_specs=VMEM,
        compiler_params=params(16),
        cost_estimate=pl.CostEstimate(
            flops=8 * pooled_rows * half_cols * 9 * chans * chans,
            bytes_accessed=8 << 20,
            transcendentals=0,
        ),
        name="conv_pool",
    )(where, taps, w, b, *after)


def edge_kernel(where_ref, w_ref, b_ref, got_ref, traded_ref, head_ref, tail_ref, *refs):
    edge_ref, acc = refs[-2:]
    half = where_ref[0]
    got, traded = got_ref[...], traded_ref[...]
    left = jnp.concatenate([jnp.where(half == 0, got, traded), head_ref[...]], axis=-1)
    right = jnp.concatenate([tail_ref[...], jnp.where(half == 0, traded, got)], axis=-1)
    edge_part(where_ref, (left, right), w_ref, b_ref[...], edge_ref, acc)


def conv_edges(where, w, b, got, traded, head, tail, after):
    rows, lanes = head.shape[0], w.shape[1] // 128
    return pl.pallas_call(
        edge_kernel,
        out_shape=jax.ShapeDtypeStruct((4, lanes, rows // 2, 128), F32),
        in_specs=[SMEM] + [VMEM] * 6 + [ANY] * len(after),
        out_specs=VMEM,
        scratch_shapes=[pltpu.VMEM((8 * lanes, rows + 16, 128), F32)],
        compiler_params=params(),
        cost_estimate=pl.CostEstimate(flops=0, bytes_accessed=4 << 20, transcendentals=0),
        name="conv_edges",
    )(where, w, b, got, traded, head, tail, *after)


def start_kernel(
    where_ref, x_hbm, w_hbm, grad_hbm, labels_hbm, slots_hbm,
    side_ref, head_ref, tail_ref, send_ref, near_ref, w_ref,
    labels_ref, slots_ref, left, right, wide, sems,
):
    owned, width = grad_hbm.shape
    rows, cols, chans = x_hbm.shape
    entries = slots_ref.shape[1]
    reach = left.shape[1]
    half = where_ref[0]
    copies = [
        pltpu.make_async_copy(labels_hbm, labels_ref, sems.at[0]),
        pltpu.make_async_copy(grad_hbm, side_ref.at[0, pl.ds(0, owned)], sems.at[1]),
        pltpu.make_async_copy(x_hbm.at[:, pl.ds(0, reach)], left, sems.at[2]),
        pltpu.make_async_copy(x_hbm.at[:, pl.ds(cols - reach, reach)], right, sems.at[3]),
        pltpu.make_async_copy(slots_hbm, slots_ref, sems.at[4]),
    ]
    most, first, _ = share_rows(half, rows)
    size = most // 4
    for k in range(4):
        source = x_hbm.at[pl.ds(first + k * size, size)]
        copies.append(
            pltpu.make_async_copy(source, near_ref.at[pl.ds(k * size, size)], sems.at[5 + k])
        )
    copies.append(pltpu.make_async_copy(w_hbm, w_ref, sems.at[9]))
    for copy in copies:
        copy.start()
    lane = lax.broadcasted_iota(jnp.int32, (1, width), 1)
    copies[0].wait()
    copies[4].wait()
    ids = jnp.concatenate(
        [slots_ref[...].astype(F32), jnp.zeros((1, width - entries), F32)], axis=1
    )
    labels = labels_ref[...]
    counts = jnp.zeros((1, width), F32)
    for e in range(entries):
        hit = jnp.where(labels == e, 1.0, 0.0)
        hit = jnp.sum(jnp.sum(hit, axis=0, keepdims=True), axis=1, keepdims=True)
        counts = jnp.where(lane == e, hit, counts)
    row = lax.broadcasted_iota(jnp.int32, (SIDE, width), 0)
    side_ref[0, owned:] = jnp.where(row == 0, ids, jnp.where(row == 1, counts, 0.0))
    lanes = chans // 128
    copies[2].wait()
    copies[3].wait()
    for ref, out_ref, at, sent in ((left, head_ref, 0, 1), (right, tail_ref, reach - WIDTH, 0)):
        x = ref[...].astype(F32).reshape(rows * reach, chans)
        for t in range(lanes):
            wide[t] = x[:, t * 128 : (t + 1) * 128]
        for c in range(WIDTH):
            for t in range(lanes):
                part = wide[t, pl.ds(at + c, rows, stride=reach), :].astype(BF16)
                place = (c * lanes + t) * 128
                out_ref[:, place : place + 128] = part
    send_ref[...] = jnp.where(half == 0, tail_ref[...], head_ref[...])
    copies[1].wait()
    for copy in copies[5:]:
        copy.wait()


def start(where, x, w, grad, slots, labels):
    owned, width = grad.shape
    rows, cols, chans = x.shape
    reach = 16
    most = share_rows(0, rows)[0]
    columns = jax.ShapeDtypeStruct((rows, WIDTH * chans), BF16)
    fixed = [
        pltpu.with_memory_space_constraint(a, pltpu.HBM)
        for a in (x, w, grad, labels, slots.reshape(1, -1))
    ]
    return pl.pallas_call(
        start_kernel,
        out_shape=(jax.ShapeDtypeStruct((1, owned + SIDE, width), F32),)
        + (columns,) * 3
        + (jax.ShapeDtypeStruct((most, cols, chans), BF16), jax.ShapeDtypeStruct(w.shape, BF16)),
        in_specs=[SMEM] + [HBM] * 5,
        out_specs=(VMEM,) * 6,
        scratch_shapes=[
            pltpu.VMEM(labels.shape, jnp.int32),
            pltpu.VMEM((1, slots.shape[0]), jnp.int32),
            pltpu.VMEM((rows, reach, chans), BF16),
            pltpu.VMEM((rows, reach, chans), BF16),
            pltpu.VMEM((chans // 128, rows * reach, 128), F32),
            pltpu.SemaphoreType.DMA((10,)),
        ],
        compiler_params=params(16),
        name="start",
    )(where, *fixed)


def join_kernel(*refs, count):
    at = 0
    for ref in refs[:count]:
        refs[-1][at : at + ref.shape[0]] = ref[...]
        at += ref.shape[0]


def join(parts, after):
    shape = (sum(p.shape[0] for p in parts),) + parts[0].shape[1:]
    return pl.pallas_call(
        functools.partial(join_kernel, count=len(parts)),
        out_shape=jax.ShapeDtypeStruct(shape, F32),
        in_specs=[VMEM] * len(parts) + [ANY] * len(after),
        out_specs=VMEM,
        compiler_params=params(),
        name="join",
    )(*parts, *after)


def scale_rows(block, note_rows, sums):
    def exponent(values):
        top = None
        for v in values:
            one = jnp.max(jnp.max(jnp.abs(v), axis=0, keepdims=True), axis=1, keepdims=True)
            top = one if top is None else jnp.maximum(top, one)
        return jnp.ceil(jnp.log2(jnp.maximum(top, 1e-30)))

    power = exponent([block, note_rows])
    power_sums = exponent([sums])
    return power, power_sums


def note_block(bias, power, power_sums, width):
    row = lax.broadcasted_iota(jnp.int32, (NOTE, width), 0)
    bias = jnp.broadcast_to(bias, (NOTE, width))
    power = jnp.broadcast_to(power, (NOTE, width))
    power_sums = jnp.broadcast_to(power_sums, (NOTE, width))
    return jnp.where(row == 0, bias, jnp.where(row == 1, power, power_sums))


def read_note(part, at):
    note = part[at : at + NOTE]
    down = jnp.exp2(note[1:2] - 12.0)
    return note[0:1] * down, down, jnp.exp2(note[2:3] - 12.0)


def deep_kernel(
    where_ref, own_ref, other_ref, edge_ref, w_ref, b_ref, lab_ref, taps, member, slope, sums_ref, wide,
    inside, *, block, entries
):
    _, cols, chans = own_ref.shape
    rows = lab_ref.shape[0]
    lanes = chans // 128
    width = w_ref.shape[-1]
    half = where_ref[0]
    taps[0] = jnp.zeros(taps.shape[1:], BF16)
    taps[rows + 1] = jnp.zeros(taps.shape[1:], BF16)

    def prepare(ref, base, i, slot):
        x = ref[i].astype(F32)
        r = base + i
        for t in range(lanes):
            s = slot * lanes + t
            at = t * 128
            wide[s, 8 : 8 + cols] = x[:, at : at + 128]
            for g, place in enumerate((7, 8, 7 + cols, 8 + cols)):
                wide[s, place : place + 1] = edge_ref[g, t, pl.ds(r, 1), :]
        for tap in range(3):
            for t in range(lanes):
                piece = wide[slot * lanes + t, 7 + tap : 7 + tap + cols, :]
                at = (tap * lanes + t) * 128
                taps[r + 1, :, at : at + 128] = piece.astype(BF16)

    first, second = shares(rows)
    times = math.gcd(first, second)

    def prepare_all(even_ref, odd_ref):
        def prepare_rows(k, carry):
            for q in range(rows // times):
                ref, base = (even_ref, 0) if q < first // times else (odd_ref, first)
                prepare(ref, base, q * times - base + k, q)
            return carry

        lax.fori_loop(0, times, prepare_rows, 0)

    @pl.when(half == 0)
    def _():
        prepare_all(own_ref, other_ref)

    @pl.when(half != 0)
    def _():
        prepare_all(other_ref, own_ref)

    lab = jnp.transpose(lab_ref[...].astype(F32))
    lane = lax.broadcasted_iota(jnp.int32, (cols, 128), 1)
    want = jnp.where(lane < 3 * entries, lane % entries, -1).astype(F32)
    for r in range(rows):
        member[r] = (lab[:, r : r + 1] == want).astype(BF16)
    bias = b_ref[...]
    size = block * cols

    flat = jnp.concatenate([lab_ref[r : r + 1, :] for r in range(rows)], axis=1)
    entry = lax.broadcasted_iota(jnp.int32, (entries, rows * cols), 0)
    inside[...] = jnp.where(jnp.broadcast_to(flat, entry.shape) == entry, 1.0, 0.0).astype(BF16)

    def step(k, sums):
        r0 = k * block
        lhs = jnp.concatenate([taps[pl.ds(r0 + dr, block)] for dr in range(3)], axis=-1)
        v = jnp.dot(lhs.reshape(size, 9 * chans), w_ref[...], preferred_element_type=F32) + bias
        sig = sigmoid(v)
        features = (v * sig).astype(BF16)
        slope[pl.ds(k * size, size)] = sig * (1.0 + v * (1.0 - sig))
        mine = inside[:, pl.ds(pl.multiple_of(k * size, 128), size)]
        return sums + jnp.dot(mine, features, preferred_element_type=F32)

    sums_ref[...] = lax.fori_loop(0, rows // block, step, jnp.zeros((entries, width), F32))


def deep_forward(where, own, other, edges, w, b, labels, entries):
    _, cols, chans = own.shape
    rows, width = labels.shape[0], w.shape[-1]
    block = next(k for k in (8, 4, 2, 1) if rows % k == 0)
    first, second = shares(rows)
    slots = rows // math.gcd(first, second)
    return pl.pallas_call(
        functools.partial(deep_kernel, block=block, entries=entries),
        out_shape=(
            jax.ShapeDtypeStruct((rows + 2, cols, 3 * chans), BF16),
            jax.ShapeDtypeStruct((rows, cols, 128), BF16),
            jax.ShapeDtypeStruct((rows * cols, width), F32),
            jax.ShapeDtypeStruct((entries, width), F32),
        ),
        in_specs=[SMEM] + [VMEM] * 6,
        out_specs=(VMEM,) * 4,
        scratch_shapes=[
            pltpu.VMEM((slots * (chans // 128), cols + 16, 128), F32),
            pltpu.VMEM((entries, rows * cols), BF16),
        ],
        compiler_params=params(16),
        cost_estimate=pl.CostEstimate(
            flops=4 * rows * cols * 9 * chans * width, bytes_accessed=8 << 20, transcendentals=0
        ),
        name="deep_forward",
    )(where, own, other, edges, w, b, labels)


def grad_kernel(
    where_ref, taps, member, slope, sums_ref, *refs, n_parts, chunk, ways, with_sums
):
    part_refs = refs[:n_parts]
    out_refs = refs[n_parts : n_parts + ways]
    (weight,) = refs[n_parts + ways :]
    rows, cols, depth = member.shape[0], taps.shape[1], taps.shape[2]
    width = slope.shape[-1]
    me = where_ref[3]
    entries = sums_ref.shape[0]
    owned = part_refs[0].shape[1] - SIDE
    own_ids = jnp.broadcast_to(part_refs[0][0, owned : owned + 1, :entries], (entries, entries))
    across = lax.broadcasted_iota(jnp.int32, (entries, entries), 1)
    down = lax.broadcasted_iota(jnp.int32, (entries, entries), 0)
    ids = jnp.sum(jnp.where(across == down, own_ids, 0.0), axis=1, keepdims=True).astype(jnp.int32)
    total = jnp.zeros((entries, 1), F32)
    entry_grad = jnp.zeros((entries, width), F32)
    owner, inner = ids // owned, ids % owned
    spot = lax.broadcasted_iota(jnp.int32, (entries, owned), 1)
    for m, ref, k in relative(part_refs):
        there = ref[k, owned : owned + 1, :entries] == ids.astype(F32)
        counts = ref[k, owned + 1 : owned + 2, :entries]
        total += jnp.sum(jnp.where(there, counts, 0.0), axis=1, keepdims=True)
        hot = ((owner ^ me) == m) & (inner == spot)
        entry_grad += jnp.dot(
            hot.astype(F32), ref[k, :owned], precision=lax.Precision.HIGHEST, preferred_element_type=F32
        )
    entry_grad = entry_grad / jnp.maximum(total, 1.0)
    high = entry_grad.astype(BF16)
    rest = entry_grad - high.astype(F32)
    mid = rest.astype(BF16)
    low = (rest - mid.astype(F32)).astype(BF16)
    terms = jnp.concatenate([high, mid, low, jnp.zeros((128 - 3 * entries, width), BF16)], axis=0)
    pixel = jnp.dot(member[...].reshape(rows * cols, 128), terms, preferred_element_type=F32)
    dg = (pixel * slope[...]).astype(BF16)
    turned = jnp.transpose(dg)
    bias_sum = jnp.sum(dg.astype(F32), axis=0, keepdims=True)
    for dr in range(3):
        window = taps[dr : dr + rows].reshape(rows * cols, depth)
        out = jnp.dot(turned, window, preferred_element_type=F32)
        weight[dr * depth : (dr + 1) * depth] = jnp.transpose(out)
    if weight.shape[0] > 3 * depth:
        weight[3 * depth :] = jnp.zeros((weight.shape[0] - 3 * depth, width), F32)
    sums = sums_ref[...]
    power, power_sums = scale_rows(weight[...], bias_sum, sums)
    up = jnp.exp2(12.0 - power)
    note = note_block(bias_sum * up, power, power_sums, width)
    digit = lax.rem(me, ways)
    heads = weight.shape[0] // chunk // ways
    for m in range(ways):
        for hi in range(heads):
            j = hi * ways + (digit ^ m)
            out_refs[m][hi * chunk : (hi + 1) * chunk] = (
                weight[pl.ds(pl.multiple_of(j * chunk, 8), chunk)] * up
            )
        out_refs[m][heads * chunk : heads * chunk + NOTE] = note
    sums = sums * jnp.exp2(12.0 - power_sums)
    for m in with_sums:
        out_refs[m][heads * chunk + NOTE :] = sums


def deep_backward(where, forward, parts, chunk, count, ways, with_sums):
    taps, _, slope, sums = forward
    width, entries = slope.shape[-1], sums.shape[0]
    size = count // ways * chunk + NOTE
    return pl.pallas_call(
        functools.partial(
            grad_kernel, n_parts=len(parts), chunk=chunk, ways=ways, with_sums=with_sums
        ),
        out_shape=tuple(
            jax.ShapeDtypeStruct((size + (entries if m in with_sums else 0), width), F32)
            for m in range(ways)
        ),
        in_specs=[SMEM] + [VMEM] * (4 + len(parts)),
        out_specs=(VMEM,) * ways,
        scratch_shapes=[pltpu.VMEM((count * chunk, width), F32)],
        compiler_params=params(16),
        cost_estimate=pl.CostEstimate(
            flops=4 * slope.shape[0] * 3 * taps.shape[2] * width, bytes_accessed=8 << 20, transcendentals=0
        ),
        name="deep_backward",
    )(where, *forward, *parts)


def pair_kernel(own_ref, got_ref, own_sums_ref, got_sums_ref, *refs, size, entries):
    out_ref = refs[-1]
    own, got = own_ref[size : size + NOTE], got_ref[size : size + NOTE]
    power = jnp.maximum(own[1:2], got[1:2]) + 1.0
    power_sums = jnp.maximum(own[2:3], got[2:3])
    own_down, got_down = jnp.exp2(own[1:2] - power), jnp.exp2(got[1:2] - power)
    out_ref[:size] = own_ref[:size] * own_down + got_ref[:size] * got_down
    bias = own[0:1] * own_down + got[0:1] * got_down
    out_ref[size : size + NOTE] = note_block(bias, power, power_sums, own.shape[-1])
    at = size + NOTE
    sums = own_sums_ref[at : at + entries] * jnp.exp2(own[2:3] - power_sums)
    out_ref[at : at + entries] = sums
    sums = got_sums_ref[at : at + entries] * jnp.exp2(got[2:3] - power_sums)
    out_ref[at + entries : at + 2 * entries] = sums


def merge_pair(own, got, own_sums, got_sums, size, entries, after):
    width = own.shape[-1]
    return pl.pallas_call(
        functools.partial(pair_kernel, size=size, entries=entries),
        out_shape=jax.ShapeDtypeStruct((size + NOTE + 2 * entries, width), F32),
        in_specs=[VMEM] * 4 + [ANY] * len(after),
        out_specs=VMEM,
        compiler_params=params(),
        cost_estimate=pl.CostEstimate(flops=0, bytes_accessed=32 << 20, transcendentals=0),
        name="merge_pair",
    )(own, got, own_sums, got_sums, *after)


def merge_kernel(where_ref, *refs, plan, chunk, heads, entries, shift, next_ways):
    n_parts = len(plan)
    part_refs, out_refs, sums_ref = refs[:n_parts], refs[n_parts:-1], refs[-1]
    width = part_refs[0].shape[-1]
    size = heads * chunk
    total, bias = jnp.zeros((size, width), F32), jnp.zeros((1, width), F32)
    for ref, (added, members) in zip(part_refs, plan):
        more, down, down_sums = read_note(ref, size)
        if added:
            total, bias = total + ref[:size] * down, bias + more
        for k, m in enumerate(members):
            at = size + NOTE + k * entries
            sums_ref[m * entries : (m + 1) * entries] = ref[at : at + entries] * down_sums
    sums = sums_ref[...]
    power, power_sums = scale_rows(total, bias, sums)
    up = jnp.exp2(12.0 - power)
    note = note_block(bias * up, power, power_sums, width)
    total = total * up
    if next_ways == 1:
        out_refs[0][:size] = total
        out_refs[0][size:] = note
        return
    sums = sums * jnp.exp2(12.0 - power_sums)
    digit = lax.rem(where_ref[3] >> shift, next_ways)
    for m in range(next_ways):
        for hi in range(heads // next_ways):
            piece = jnp.zeros((chunk, width), F32)
            for d in range(next_ways):
                at = (hi * next_ways + d) * chunk
                piece = jnp.where((digit ^ m) == d, total[at : at + chunk], piece)
            out_refs[m][hi * chunk : (hi + 1) * chunk] = piece
        at = heads // next_ways * chunk
        out_refs[m][at : at + NOTE] = note
        out_refs[m][at + NOTE :] = sums


def merge(where, parts, chunk, heads, entries, shift, next_ways):
    width = parts[0][0].shape[-1]
    sums_rows = sum(len(members) for _, _, members in parts) * entries
    if next_ways == 1:
        outs = (jax.ShapeDtypeStruct((heads * chunk + NOTE, width), F32),)
    else:
        rows = heads // next_ways * chunk + NOTE + sums_rows
        outs = (jax.ShapeDtypeStruct((rows, width), F32),) * next_ways
    outs = outs + (jax.ShapeDtypeStruct((sums_rows, width), F32),)
    out = pl.pallas_call(
        functools.partial(
            merge_kernel,
            plan=tuple((added, tuple(members)) for _, added, members in parts),
            chunk=chunk,
            heads=heads,
            entries=entries,
            shift=shift,
            next_ways=next_ways,
        ),
        out_shape=outs,
        in_specs=[SMEM] + [VMEM] * len(parts),
        out_specs=(VMEM,) * len(outs),
        compiler_params=params(),
        name="merge",
    )(where, *(part for part, _, _ in parts))
    return out[:-1], out[-1]


def embed_kernel(where_ref, sums_ref, *refs, entries):
    part_refs, out_ref = refs[:-1], refs[-1]
    owned, width = out_ref.shape
    own = (where_ref[3] * owned + lax.broadcasted_iota(jnp.int32, (owned, entries), 0)).astype(F32)
    sums, counts = jnp.zeros((owned, width), F32), jnp.zeros((owned, 1), F32)
    for m, ref, k in relative(part_refs):
        there = ref[k, owned : owned + 1, :entries] == own
        count = ref[k, owned + 1 : owned + 2, :entries]
        counts += jnp.sum(jnp.where(there, count, 0.0), axis=1, keepdims=True)
        sums += jnp.dot(
            there.astype(F32),
            sums_ref[m * entries : (m + 1) * entries],
            precision=lax.Precision.HIGHEST,
            preferred_element_type=F32,
        )
    out_ref[...] = sums / jnp.maximum(counts, 1.0)


def spread_kernel(where_ref, *refs, chunk, rows, members):
    part_refs, weight_ref, bias_ref, place = refs[:-3], refs[-3], refs[-2], refs[-1]
    me = where_ref[3]
    count = len(members)
    for p, k in itertools.product(range(count), range(part_refs[0].shape[0])):
        bias, down, _ = read_note(part_refs[p][k], chunk)
        j = me ^ (members[p] + k * count)
        target = weight_ref if rows == place.shape[0] else place
        target[pl.ds(pl.multiple_of(j * chunk, 8), chunk)] = part_refs[p][k, :chunk] * down

        @pl.when(j == 0)
        def _():
            bias_ref[...] = bias

    if rows != place.shape[0]:
        weight_ref[...] = place[:rows]


def spread(where, parts, chunk, count, rows):
    parts = {m: part.astype(F32) for m, part in parts.items()}
    width = parts[0].shape[-1]
    return pl.pallas_call(
        functools.partial(spread_kernel, chunk=chunk, rows=rows, members=tuple(parts)),
        out_shape=(jax.ShapeDtypeStruct((rows, width), F32), jax.ShapeDtypeStruct((1, width), F32)),
        in_specs=[SMEM] + [VMEM] * len(parts),
        out_specs=(VMEM, VMEM),
        scratch_shapes=[pltpu.VMEM((count * chunk, width), F32)],
        compiler_params=params(),
        name="spread",
    )(where, *parts.values())


def body(
    section_input, conv_weight, conv_bias, deep_weight, deep_bias, labels, slot_ids, embed_grad
):
    chan_count = lax.axis_size("chan")
    strip_count = lax.axis_size("strip")
    chan_pos = lax.axis_index("chan")
    strip_pos = lax.axis_index("strip")
    half = chan_pos & 1
    channels = section_input.shape[-1]
    entries = slot_ids.shape[0]
    owned, width = embed_grad.shape
    where = jnp.stack(
        [half, (strip_pos == 0).astype(jnp.int32), (strip_pos == strip_count - 1).astype(jnp.int32), strip_pos]
    ).astype(jnp.int32)
    conv_w = conv_weight.reshape(9 * channels, -1)
    conv_b = conv_bias.reshape(1, -1)

    side, head, tail, sent, near_rows, near_w = start(
        where, section_input, conv_w, embed_grad, slot_ids, labels
    )
    pairs = []
    for s in range(strip_count):
        for c in range(chan_count):
            to = s + 1 - 2 * (c & 1)
            if 0 <= to < strip_count:
                pairs.append((s * chan_count + c, to * chan_count + c))
    got = lax.ppermute(sent, ("strip", "chan"), pairs)

    steps = [(at + 1, 1) for at in range(min(2, strip_count.bit_length() - 2))]
    steps += [(at, min(3, strip_count.bit_length() - 1 - at)) for at in range(3, strip_count.bit_length() - 1, 3)]
    ahead = gather_step(side, "strip", steps[0])
    taps = windows(where, near_rows, section_input.shape[0])
    shared = join(ahead, [taps])
    got, shared = lax.optimization_barrier((got, shared))
    traded = swap(got, "chan", 1)
    ahead = gather_step(shared, "strip", steps[1])
    pooled = conv_pool(where, taps, near_w, conv_b, section_input.shape[0] // 4, [shared, got])
    pooled, shared = lax.optimization_barrier((pooled, join(ahead, [pooled])))
    other = swap(pooled, "chan", 1)
    for step in steps[2:]:
        shared = join(gather_step(shared, "strip", step), [])
    shared = [shared, swap(shared, "strip", 1)]
    edges = conv_edges(where, near_w, conv_b, got, traded, head, tail, [pooled])

    chunk = -(-9 * channels // strip_count // 8) * 8
    bits = strip_count.bit_length() - 1
    pieces = 1 << min(2, bits - 1)
    ways = 2 * pieces
    far = list(range(2, pieces))
    with_sums = {2, 3} | {2 * k + 1 for k in far[:1]}
    forward = deep_forward(
        where,
        pooled,
        other,
        edges,
        deep_weight.reshape(9 * channels, width),
        deep_bias.reshape(1, width),
        labels,
        entries,
    )
    send = deep_backward(where, forward, shared, chunk, strip_count, ways, with_sums)
    heads = strip_count // ways
    got = {k: swap(send[2 * k + 1].astype(F16), "strip", 1).astype(F32) for k in far}
    parts = [(send[0], True, [])]
    for m in range(1, min(4, ways)):
        sent = swap(send[m].astype(F16), "strip", m).astype(F32)
        parts.append((sent, True, [m] if m in with_sums else []))
    before = [part for part, _, members in parts if members == [2]]
    for k in far:
        own_sums, got_sums = send[2 * far[0] + 1], got[far[0]]
        pair = merge_pair(send[2 * k], got[k], own_sums, got_sums, heads * chunk, entries, before)
        before = [pair]
        sent = swap(pair.astype(F16), "strip", 2 * k).astype(F32)
        parts.append((sent, True, [2 * k, 2 * k + 1]))
        if k == far[0]:
            parts += [(own_sums, False, [0]), (got_sums, False, [1])]
    held, shift = ways, ways.bit_length() - 1
    while True:
        size = min(3, bits - shift)
        send, sums = merge(where, parts, chunk, heads, entries, shift, 1 << size)
        if size == 0:
            break
        more = 1 << size
        heads //= more
        arrived = [send[0]] + [
            swap(send[m].astype(F16), "strip", m << shift).astype(F32) for m in range(1, more)
        ]
        parts = [
            (part, True, list(range(m * held, (m + 1) * held))) for m, part in enumerate(arrived)
        ]
        held *= more
        shift += size
    embeddings = pl.pallas_call(
        functools.partial(embed_kernel, entries=entries),
        out_shape=jax.ShapeDtypeStruct((owned, width), F32),
        in_specs=[SMEM] + [VMEM] * (1 + len(shared)),
        out_specs=VMEM,
        compiler_params=params(),
        name="embed",
    )(where, sums, *shared)
    own = send[0].astype(F16)[None]
    for at in range(ways.bit_length() - 1, bits, 3):
        own = jnp.concatenate(gather_step(own, "strip", (at, min(3, bits - at))), axis=0)
    gathered = {m: swap(own, "strip", m) if m else own for m in range(min(4, ways))}
    for k in far:
        gathered[2 * k] = swap(own, "strip", 2 * k)
    late = {2 * k + 1: swap(gathered[2 * k], "strip", 1) for k in far}
    weight_rows, bias_row = spread(
        where, {**gathered, **late}, chunk, strip_count, 9 * channels
    )
    return (embeddings, weight_rows.reshape(3, 3, channels, width), bias_row[0])


def solution(mesh):
    placed = (
        P(None, "strip", None),
        P(),
        P(),
        P(None, None, None, "chan"),
        P("chan"),
        P(None, "strip"),
        P("strip"),
        P("strip", "chan"),
    )
    return jax.shard_map(
        body,
        mesh=mesh,
        in_specs=placed,
        out_specs=(P("strip", "chan"), P(None, None, None, "chan"), P("chan")),
        check_vma=False,
    )
```

```python
import functools
import itertools
import math

import jax
import jax.numpy as jnp
from jax import lax
from jax.experimental import pallas as pl
from jax.experimental.pallas import tpu as pltpu
from jax.sharding import PartitionSpec as P

F32, BF16, F16 = jnp.float32, jnp.bfloat16, jnp.float16
VMEM = pl.BlockSpec(memory_space=pltpu.VMEM)
SMEM = pl.BlockSpec(memory_space=pltpu.SMEM)
HBM = pl.BlockSpec(memory_space=pltpu.HBM)
ANY = pl.BlockSpec(memory_space=pl.ANY)
SIDE = 8
WIDTH = 3
PIECE = 4
STEP = 6
PAYLOADS = (((0,), 0), ((1,), 0), ((2,), 1), ((3,), 1), ((4,), 0), ((5,), 1), ((6, 7), 1))
NOTE = 16


def params(mib=8):
    return pltpu.CompilerParams(vmem_limit_bytes=mib << 20)


def swap(value, axis, mask):
    count = lax.axis_size(axis)
    return lax.ppermute(value, axis, [(i, i ^ mask) for i in range(count)])


def gather_step(held, axis, step):
    shift, size = step
    return [held] + [swap(held, axis, m << shift) for m in range(1, 1 << size)]


def relative(refs):
    half = len(refs) // 2
    for low in range(2):
        m = low
        for ref in refs[low * half : (low + 1) * half]:
            for k in range(ref.shape[0]):
                yield m, ref, k
                m += 2


def sigmoid(v):
    return jax.nn.sigmoid(v)


def shares(pooled_rows):
    first = pooled_rows // 2
    return first, pooled_rows - first


def pick(half, pair):
    return jnp.where(half == 0, pair[0], pair[1])


def share_rows(half, rows):
    first, second = shares(rows // 2)
    most = -(-(2 * max(first, second) + 1) // PIECE) * PIECE
    return most, pick(half, (0, rows - most)), pick(half, (-1, 2 * first - 1 - (rows - most)))


def window_kernel(where_ref, rows_ref, taps, wide, *, rows):
    most, cols, chans = rows_ref.shape
    half_cols = cols // 2
    half = where_ref[0]
    _, _, before = share_rows(half, rows)
    shift = PIECE - before
    lanes = chans // 128
    border = jnp.zeros((8, 128), F32)
    for t in range(wide.shape[0]):
        wide[t, 0:8] = border
        wide[t, cols + 8 : cols + 16] = border

    def prepare(k, carry):
        for slot in range(PIECE):
            r = k * PIECE + slot
            x = rows_ref[r].astype(F32)
            for t in range(lanes):
                wide[slot * lanes + t, 8 : 8 + cols] = x[:, t * 128 : (t + 1) * 128]
            for tap in range(4):
                for t in range(lanes):
                    part = wide[slot * lanes + t, pl.ds(7 + tap, half_cols, stride=2), :]
                    at = (tap * lanes + t) * 128
                    taps[r + shift, :, at : at + 128] = part.astype(BF16)
        return carry

    lax.fori_loop(0, most // PIECE, prepare, 0)
    second = shares(rows // 2)[1]
    outside = pick(half, (PIECE, PIECE + 2 * second + 1))
    taps[outside] = jnp.zeros(taps.shape[1:], BF16)


def windows(where, near_rows, rows):
    most, cols, chans = near_rows.shape
    return pl.pallas_call(
        functools.partial(window_kernel, rows=rows),
        out_shape=jax.ShapeDtypeStruct((most + 2 * PIECE, cols // 2, 4 * chans), BF16),
        in_specs=[SMEM, VMEM],
        out_specs=VMEM,
        scratch_shapes=[pltpu.VMEM((PIECE * (chans // 128), cols + 16, 128), F32)],
        compiler_params=params(16),
        cost_estimate=pl.CostEstimate(flops=0, bytes_accessed=12 << 20, transcendentals=0),
        name="windows",
    )(where, near_rows)


def edge_part(where_ref, pairs, w_ref, bias, edge_ref, acc):
    rows = pairs[0].shape[0]
    chans = w_ref.shape[1]
    lanes = chans // 128
    depth = 3 * chans
    lhs = jnp.concatenate(
        [
            pairs[s][:, (2 * j + phase) * chans : (2 * j + phase + 3) * chans]
            for s in range(2)
            for j in range(2)
            for phase in range(2)
        ],
        axis=0,
    )
    pad = rows + 16
    for dr in range(3):
        part = jnp.dot(lhs, w_ref[dr * depth : (dr + 1) * depth], preferred_element_type=F32)
        for g in range(8):
            own = part[g * rows : (g + 1) * rows]
            for t in range(lanes):
                at = 9 - dr
                piece = own[:, t * 128 : (t + 1) * 128]
                if dr == 0:
                    acc[g * lanes + t, 0:8] = jnp.zeros((8, 128), F32)
                    acc[g * lanes + t, 8 + rows : pad] = jnp.zeros((8, 128), F32)
                    acc[g * lanes + t, 8:9] = jnp.zeros((1, 128), F32)
                    acc[g * lanes + t, at : at + rows] = piece
                else:
                    acc[g * lanes + t, at : at + rows] += piece
    for g in range(4):
        for t in range(lanes):
            total = None
            for phase in range(2):
                at = (2 * g + phase) * lanes + t
                v = acc[at, 8 : 8 + rows] + bias[:, t * 128 : (t + 1) * 128]
                acc[at, 8 : 8 + rows] = v * sigmoid(v)
                both = (
                    acc[at, pl.ds(8, rows // 2, stride=2), :]
                    + acc[at, pl.ds(9, rows // 2, stride=2), :]
                )
                total = both if total is None else total + both
            lost = jnp.where(g == 0, where_ref[1], jnp.where(g == 3, where_ref[2], 0))
            keep = jnp.where(lost > 0, 0.0, 0.25)
            edge_ref[g, t] = (total * keep).astype(BF16).astype(F32)


def conv_kernel(where_ref, taps, w_ref, b_ref, *refs):
    out_ref = refs[-1]
    assert out_ref.shape[0] % STEP == 0
    half_cols, chans = taps.shape[1], taps.shape[2] // 4
    bias = b_ref[...]

    def step(k, carry):
        r0 = PIECE + k * 2 * STEP
        total = None
        for phase in range(2):
            lhs = jnp.concatenate(
                [
                    taps[pl.ds(r0 + dr, 2 * STEP), :, phase * chans : (phase + 3) * chans]
                    for dr in range(3)
                ],
                axis=-1,
            ).reshape(2 * STEP * half_cols, 9 * chans)
            v = jnp.dot(lhs, w_ref[...], preferred_element_type=F32) + bias
            h = (v * sigmoid(v)).reshape(STEP, 2, half_cols, chans)
            h = h[:, 0] + h[:, 1]
            total = h if total is None else total + h
        out_ref[pl.ds(k * STEP, STEP)] = (total * 0.25).astype(BF16)
        return carry

    for k in range(out_ref.shape[0] // STEP):
        step(k, 0)


def conv_pool(where, taps, w, b, pooled_rows, after):
    _, half_cols, width = taps.shape
    chans = width // 4
    return pl.pallas_call(
        conv_kernel,
        out_shape=jax.ShapeDtypeStruct((pooled_rows, half_cols, chans), BF16),
        in_specs=[SMEM] + [VMEM] * 3 + [ANY] * len(after),
        out_specs=VMEM,
        compiler_params=params(16),
        cost_estimate=pl.CostEstimate(
            flops=8 * pooled_rows * half_cols * 9 * chans * chans,
            bytes_accessed=8 << 20,
            transcendentals=0,
        ),
        name="conv_pool",
    )(where, taps, w, b, *after)


def edge_kernel(where_ref, w_ref, b_ref, got_ref, traded_ref, head_ref, tail_ref, *refs):
    edge_ref, acc = refs[-2:]
    half = where_ref[0]
    got, traded = got_ref[...], traded_ref[...]
    left = jnp.concatenate([jnp.where(half == 0, got, traded), head_ref[...]], axis=-1)
    right = jnp.concatenate([tail_ref[...], jnp.where(half == 0, traded, got)], axis=-1)
    edge_part(where_ref, (left, right), w_ref, b_ref[...], edge_ref, acc)


def conv_edges(where, w, b, got, traded, head, tail, after):
    rows, lanes = head.shape[0], w.shape[1] // 128
    return pl.pallas_call(
        edge_kernel,
        out_shape=jax.ShapeDtypeStruct((4, lanes, rows // 2, 128), F32),
        in_specs=[SMEM] + [VMEM] * 6 + [ANY] * len(after),
        out_specs=VMEM,
        scratch_shapes=[pltpu.VMEM((8 * lanes, rows + 16, 128), F32)],
        compiler_params=params(),
        cost_estimate=pl.CostEstimate(flops=0, bytes_accessed=4 << 20, transcendentals=0),
        name="conv_edges",
    )(where, w, b, got, traded, head, tail, *after)


def start_kernel(
    where_ref, x_hbm, w_hbm, grad_hbm, labels_hbm, slots_hbm,
    side_ref, head_ref, tail_ref, send_ref, near_ref, w_ref,
    labels_ref, slots_ref, left, right, wide, sems,
):
    owned, width = grad_hbm.shape
    rows, cols, chans = x_hbm.shape
    entries = slots_ref.shape[1]
    reach = left.shape[1]
    half = where_ref[0]
    copies = [
        pltpu.make_async_copy(labels_hbm, labels_ref, sems.at[0]),
        pltpu.make_async_copy(grad_hbm, side_ref.at[0, pl.ds(0, owned)], sems.at[1]),
        pltpu.make_async_copy(x_hbm.at[:, pl.ds(0, reach)], left, sems.at[2]),
        pltpu.make_async_copy(x_hbm.at[:, pl.ds(cols - reach, reach)], right, sems.at[3]),
        pltpu.make_async_copy(slots_hbm, slots_ref, sems.at[4]),
    ]
    most, first, _ = share_rows(half, rows)
    size = most // 4
    for k in range(4):
        source = x_hbm.at[pl.ds(first + k * size, size)]
        copies.append(
            pltpu.make_async_copy(source, near_ref.at[pl.ds(k * size, size)], sems.at[5 + k])
        )
    copies.append(pltpu.make_async_copy(w_hbm, w_ref, sems.at[9]))
    for copy in copies:
        copy.start()
    lane = lax.broadcasted_iota(jnp.int32, (1, width), 1)
    copies[0].wait()
    copies[4].wait()
    ids = jnp.concatenate(
        [slots_ref[...].astype(F32), jnp.zeros((1, width - entries), F32)], axis=1
    )
    labels = labels_ref[...]
    counts = jnp.zeros((1, width), F32)
    for e in range(entries):
        hit = jnp.where(labels == e, 1.0, 0.0)
        hit = jnp.sum(jnp.sum(hit, axis=0, keepdims=True), axis=1, keepdims=True)
        counts = jnp.where(lane == e, hit, counts)
    row = lax.broadcasted_iota(jnp.int32, (SIDE, width), 0)
    side_ref[0, owned:] = jnp.where(row == 0, ids, jnp.where(row == 1, counts, 0.0))
    lanes = chans // 128
    copies[2].wait()
    copies[3].wait()
    for ref, out_ref, at, sent in ((left, head_ref, 0, 1), (right, tail_ref, reach - WIDTH, 0)):
        x = ref[...].astype(F32).reshape(rows * reach, chans)
        for t in range(lanes):
            wide[t] = x[:, t * 128 : (t + 1) * 128]
        for c in range(WIDTH):
            for t in range(lanes):
                part = wide[t, pl.ds(at + c, rows, stride=reach), :].astype(BF16)
                place = (c * lanes + t) * 128
                out_ref[:, place : place + 128] = part
    send_ref[...] = jnp.where(half == 0, tail_ref[...], head_ref[...])
    copies[1].wait()
    for copy in copies[5:]:
        copy.wait()


def start(where, x, w, grad, slots, labels):
    owned, width = grad.shape
    rows, cols, chans = x.shape
    reach = 16
    most = share_rows(0, rows)[0]
    columns = jax.ShapeDtypeStruct((rows, WIDTH * chans), BF16)
    fixed = [
        pltpu.with_memory_space_constraint(a, pltpu.HBM)
        for a in (x, w, grad, labels, slots.reshape(1, -1))
    ]
    return pl.pallas_call(
        start_kernel,
        out_shape=(jax.ShapeDtypeStruct((1, owned + SIDE, width), F32),)
        + (columns,) * 3
        + (jax.ShapeDtypeStruct((most, cols, chans), BF16), jax.ShapeDtypeStruct(w.shape, BF16)),
        in_specs=[SMEM] + [HBM] * 5,
        out_specs=(VMEM,) * 6,
        scratch_shapes=[
            pltpu.VMEM(labels.shape, jnp.int32),
            pltpu.VMEM((1, slots.shape[0]), jnp.int32),
            pltpu.VMEM((rows, reach, chans), BF16),
            pltpu.VMEM((rows, reach, chans), BF16),
            pltpu.VMEM((chans // 128, rows * reach, 128), F32),
            pltpu.SemaphoreType.DMA((10,)),
        ],
        compiler_params=params(16),
        name="start",
    )(where, *fixed)


def join_kernel(*refs, count):
    at = 0
    for ref in refs[:count]:
        refs[-1][at : at + ref.shape[0]] = ref[...]
        at += ref.shape[0]


def join(parts, after):
    shape = (sum(p.shape[0] for p in parts),) + parts[0].shape[1:]
    return pl.pallas_call(
        functools.partial(join_kernel, count=len(parts)),
        out_shape=jax.ShapeDtypeStruct(shape, F32),
        in_specs=[VMEM] * len(parts) + [ANY] * len(after),
        out_specs=VMEM,
        compiler_params=params(),
        name="join",
    )(*parts, *after)


def scale_rows(block, note_rows, sums):
    def exponent(values):
        top = None
        for v in values:
            one = jnp.max(jnp.max(jnp.abs(v), axis=0, keepdims=True), axis=1, keepdims=True)
            top = one if top is None else jnp.maximum(top, one)
        return jnp.ceil(jnp.log2(jnp.maximum(top, 1e-30)))

    power = exponent([block, note_rows])
    power_sums = exponent([sums])
    return power, power_sums


def note_block(bias, power, power_sums, width):
    row = lax.broadcasted_iota(jnp.int32, (NOTE, width), 0)
    bias = jnp.broadcast_to(bias, (NOTE, width))
    power = jnp.broadcast_to(power, (NOTE, width))
    power_sums = jnp.broadcast_to(power_sums, (NOTE, width))
    return jnp.where(row == 0, bias, jnp.where(row == 1, power, power_sums))


def read_note(part, at):
    note = part[at : at + NOTE]
    down = jnp.exp2(note[1:2] - 12.0)
    return note[0:1] * down, down, jnp.exp2(note[2:3] - 12.0)


def deep_kernel(
    where_ref, own_ref, other_ref, edge_ref, w_ref, b_ref, lab_ref, taps, member, slope, sums_ref, wide,
    inside, *, block, entries
):
    _, cols, chans = own_ref.shape
    rows = lab_ref.shape[0]
    lanes = chans // 128
    width = w_ref.shape[-1]
    half = where_ref[0]
    taps[0] = jnp.zeros(taps.shape[1:], BF16)
    taps[rows + 1] = jnp.zeros(taps.shape[1:], BF16)

    def prepare(ref, base, i, slot):
        x = ref[i].astype(F32)
        r = base + i
        for t in range(lanes):
            s = slot * lanes + t
            at = t * 128
            wide[s, 8 : 8 + cols] = x[:, at : at + 128]
            for g, place in enumerate((7, 8, 7 + cols, 8 + cols)):
                wide[s, place : place + 1] = edge_ref[g, t, pl.ds(r, 1), :]
        for tap in range(3):
            for t in range(lanes):
                piece = wide[slot * lanes + t, 7 + tap : 7 + tap + cols, :]
                at = (tap * lanes + t) * 128
                taps[r + 1, :, at : at + 128] = piece.astype(BF16)

    first, second = shares(rows)
    times = math.gcd(first, second)

    def prepare_all(even_ref, odd_ref):
        def prepare_rows(k, carry):
            for q in range(rows // times):
                ref, base = (even_ref, 0) if q < first // times else (odd_ref, first)
                prepare(ref, base, q * times - base + k, q)
            return carry

        lax.fori_loop(0, times, prepare_rows, 0)

    @pl.when(half == 0)
    def _():
        prepare_all(own_ref, other_ref)

    @pl.when(half != 0)
    def _():
        prepare_all(other_ref, own_ref)

    lab = jnp.transpose(lab_ref[...].astype(F32))
    lane = lax.broadcasted_iota(jnp.int32, (cols, 128), 1)
    want = jnp.where(lane < 3 * entries, lane % entries, -1).astype(F32)
    for r in range(rows):
        member[r] = (lab[:, r : r + 1] == want).astype(BF16)
    bias = b_ref[...]
    size = block * cols

    flat = jnp.concatenate([lab_ref[r : r + 1, :] for r in range(rows)], axis=1)
    entry = lax.broadcasted_iota(jnp.int32, (entries, rows * cols), 0)
    inside[...] = jnp.where(jnp.broadcast_to(flat, entry.shape) == entry, 1.0, 0.0).astype(BF16)

    def step(k, sums):
        r0 = k * block
        lhs = jnp.concatenate([taps[pl.ds(r0 + dr, block)] for dr in range(3)], axis=-1)
        v = jnp.dot(lhs.reshape(size, 9 * chans), w_ref[...], preferred_element_type=F32) + bias
        sig = sigmoid(v)
        features = (v * sig).astype(BF16)
        slope[pl.ds(k * size, size)] = sig * (1.0 + v * (1.0 - sig))
        mine = inside[:, pl.ds(pl.multiple_of(k * size, 128), size)]
        return sums + jnp.dot(mine, features, preferred_element_type=F32)

    sums_ref[...] = lax.fori_loop(0, rows // block, step, jnp.zeros((entries, width), F32))


def deep_forward(where, own, other, edges, w, b, labels, entries):
    _, cols, chans = own.shape
    rows, width = labels.shape[0], w.shape[-1]
    block = next(k for k in (8, 4, 2, 1) if rows % k == 0)
    first, second = shares(rows)
    slots = rows // math.gcd(first, second)
    return pl.pallas_call(
        functools.partial(deep_kernel, block=block, entries=entries),
        out_shape=(
            jax.ShapeDtypeStruct((rows + 2, cols, 3 * chans), BF16),
            jax.ShapeDtypeStruct((rows, cols, 128), BF16),
            jax.ShapeDtypeStruct((rows * cols, width), F32),
            jax.ShapeDtypeStruct((entries, width), F32),
        ),
        in_specs=[SMEM] + [VMEM] * 6,
        out_specs=(VMEM,) * 4,
        scratch_shapes=[
            pltpu.VMEM((slots * (chans // 128), cols + 16, 128), F32),
            pltpu.VMEM((entries, rows * cols), BF16),
        ],
        compiler_params=params(16),
        cost_estimate=pl.CostEstimate(
            flops=4 * rows * cols * 9 * chans * width, bytes_accessed=8 << 20, transcendentals=0
        ),
        name="deep_forward",
    )(where, own, other, edges, w, b, labels)


def grad_kernel(
    where_ref, taps, member, slope, sums_ref, *refs, n_parts, chunk
):
    part_refs = refs[:n_parts]
    out_refs, weight = refs[n_parts:-1], refs[-1]
    rows, cols, depth = member.shape[0], taps.shape[1], taps.shape[2]
    width = slope.shape[-1]
    me = where_ref[3]
    entries = sums_ref.shape[0]
    owned = part_refs[0].shape[1] - SIDE
    own_ids = jnp.broadcast_to(part_refs[0][0, owned : owned + 1, :entries], (entries, entries))
    across = lax.broadcasted_iota(jnp.int32, (entries, entries), 1)
    down = lax.broadcasted_iota(jnp.int32, (entries, entries), 0)
    ids = jnp.sum(jnp.where(across == down, own_ids, 0.0), axis=1, keepdims=True).astype(jnp.int32)
    total = jnp.zeros((entries, 1), F32)
    entry_grad = jnp.zeros((entries, width), F32)
    owner, inner = ids // owned, ids % owned
    spot = lax.broadcasted_iota(jnp.int32, (entries, owned), 1)
    for m, ref, k in relative(part_refs):
        there = ref[k, owned : owned + 1, :entries] == ids.astype(F32)
        counts = ref[k, owned + 1 : owned + 2, :entries]
        total += jnp.sum(jnp.where(there, counts, 0.0), axis=1, keepdims=True)
        hot = ((owner ^ me) == m) & (inner == spot)
        entry_grad += jnp.dot(
            hot.astype(F32), ref[k, :owned], precision=lax.Precision.HIGHEST, preferred_element_type=F32
        )
    entry_grad = entry_grad / jnp.maximum(total, 1.0)
    high = entry_grad.astype(BF16)
    rest = entry_grad - high.astype(F32)
    mid = rest.astype(BF16)
    low = (rest - mid.astype(F32)).astype(BF16)
    terms = jnp.concatenate([high, mid, low, jnp.zeros((128 - 3 * entries, width), BF16)], axis=0)
    pixel = jnp.dot(member[...].reshape(rows * cols, 128), terms, preferred_element_type=F32)
    dg = (pixel * slope[...]).astype(BF16)
    turned = jnp.transpose(dg)
    bias_sum = jnp.sum(dg.astype(F32), axis=0, keepdims=True)
    for dr in range(3):
        window = taps[dr : dr + rows].reshape(rows * cols, depth)
        out = jnp.dot(turned, window, preferred_element_type=F32)
        weight[dr * depth : (dr + 1) * depth] = jnp.transpose(out)
    if weight.shape[0] > 3 * depth:
        weight[3 * depth :] = jnp.zeros((weight.shape[0] - 3 * depth, width), F32)
    sums = sums_ref[...]
    power, power_sums = scale_rows(weight[...], bias_sum, sums)
    up = jnp.exp2(12.0 - power)
    note = note_block(bias_sum * up, power, power_sums, width)
    ways = 8
    digit = lax.rem(me, ways)
    heads = weight.shape[0] // chunk // ways
    sums = sums * jnp.exp2(12.0 - power_sums)
    for out_ref, (members, with_sums) in zip(out_refs, PAYLOADS):
        at = 0
        for m, hi in itertools.product(members, range(heads)):
            j = hi * ways + (digit ^ m)
            out_ref[at : at + chunk] = weight[pl.ds(pl.multiple_of(j * chunk, 8), chunk)] * up
            at += chunk
        out_ref[at : at + NOTE] = note
        if with_sums:
            out_ref[at + NOTE :] = sums


def deep_backward(where, forward, parts, chunk, count):
    taps, _, slope, sums = forward
    width, entries = slope.shape[-1], sums.shape[0]
    size = count // 8 * chunk
    return pl.pallas_call(
        functools.partial(grad_kernel, n_parts=len(parts), chunk=chunk),
        out_shape=tuple(
            jax.ShapeDtypeStruct((len(members) * size + NOTE + with_sums * entries, width), F32)
            for members, with_sums in PAYLOADS
        ),
        in_specs=[SMEM] + [VMEM] * (4 + len(parts)),
        out_specs=(VMEM,) * len(PAYLOADS),
        scratch_shapes=[pltpu.VMEM((count * chunk, width), F32)],
        compiler_params=params(16),
        cost_estimate=pl.CostEstimate(
            flops=4 * slope.shape[0] * 3 * taps.shape[2] * width, bytes_accessed=8 << 20, transcendentals=0
        ),
        name="deep_backward",
    )(where, *forward, *parts)


def pair_kernel(own_ref, got_ref, *refs, size, entries, got_at, got_note, with_own):
    out_ref = refs[-1]
    own, got = own_ref[size : size + NOTE], got_ref[got_note : got_note + NOTE]
    power = jnp.maximum(own[1:2], got[1:2]) + 1.0
    power_sums = jnp.maximum(own[2:3], got[2:3])
    own_down, got_down = jnp.exp2(own[1:2] - power), jnp.exp2(got[1:2] - power)
    out_ref[:size] = own_ref[:size] * own_down + got_ref[got_at : got_at + size] * got_down
    bias = own[0:1] * own_down + got[0:1] * got_down
    out_ref[size : size + NOTE] = note_block(bias, power, power_sums, own.shape[-1])
    at = size + NOTE
    if with_own:
        sums = refs[0][at : at + entries] * jnp.exp2(own[2:3] - power_sums)
        out_ref[at : at + entries] = sums
        at += entries
    sums = got_ref[got_note + NOTE : got_note + NOTE + entries] * jnp.exp2(got[2:3] - power_sums)
    out_ref[at : at + entries] = sums


def merge_pair(own, got, own_sums, size, entries, got_at, got_note, after):
    width = own.shape[-1]
    rows = size + NOTE + (1 + len(own_sums)) * entries
    return pl.pallas_call(
        functools.partial(
            pair_kernel,
            size=size,
            entries=entries,
            got_at=got_at,
            got_note=got_note,
            with_own=bool(own_sums),
        ),
        out_shape=jax.ShapeDtypeStruct((rows, width), F32),
        in_specs=[VMEM] * (2 + len(own_sums)) + [ANY] * len(after),
        out_specs=VMEM,
        compiler_params=params(),
        name="merge_pair",
    )(own, got, *own_sums, *after)


def merge_kernel(where_ref, *refs, plan, chunk, heads, entries, shift, next_ways):
    n_parts = len(plan)
    part_refs, out_refs, sums_ref = refs[:n_parts], refs[n_parts:-1], refs[-1]
    width = part_refs[0].shape[-1]
    size = heads * chunk
    total, bias = jnp.zeros((size, width), F32), jnp.zeros((1, width), F32)
    for ref, (added, note_at, members) in zip(part_refs, plan):
        more, down, down_sums = read_note(ref, note_at)
        if added:
            total, bias = total + ref[:size] * down, bias + more
        for k, m in enumerate(members):
            at = note_at + NOTE + k * entries
            sums_ref[m * entries : (m + 1) * entries] = ref[at : at + entries] * down_sums
    sums = sums_ref[...]
    power, power_sums = scale_rows(total, bias, sums)
    up = jnp.exp2(12.0 - power)
    note = note_block(bias * up, power, power_sums, width)
    total = total * up
    if next_ways == 1:
        out_refs[0][:size] = total
        out_refs[0][size:] = note
        return
    sums = sums * jnp.exp2(12.0 - power_sums)
    digit = lax.rem(where_ref[3] >> shift, next_ways)
    for m in range(next_ways):
        for hi in range(heads // next_ways):
            piece = jnp.zeros((chunk, width), F32)
            for d in range(next_ways):
                at = (hi * next_ways + d) * chunk
                piece = jnp.where((digit ^ m) == d, total[at : at + chunk], piece)
            out_refs[m][hi * chunk : (hi + 1) * chunk] = piece
        at = heads // next_ways * chunk
        out_refs[m][at : at + NOTE] = note
        out_refs[m][at + NOTE :] = sums


def merge(where, parts, chunk, heads, entries, shift, next_ways):
    width = parts[0][0].shape[-1]
    sums_rows = sum(len(members) for _, _, _, members in parts) * entries
    if next_ways == 1:
        outs = (jax.ShapeDtypeStruct((heads * chunk + NOTE, width), F32),)
    else:
        rows = heads // next_ways * chunk + NOTE + sums_rows
        outs = (jax.ShapeDtypeStruct((rows, width), F32),) * next_ways
    outs = outs + (jax.ShapeDtypeStruct((sums_rows, width), F32),)
    out = pl.pallas_call(
        functools.partial(
            merge_kernel,
            plan=tuple((added, at, tuple(members)) for _, added, at, members in parts),
            chunk=chunk,
            heads=heads,
            entries=entries,
            shift=shift,
            next_ways=next_ways,
        ),
        out_shape=outs,
        in_specs=[SMEM] + [VMEM] * len(parts),
        out_specs=(VMEM,) * len(outs),
        compiler_params=params(),
        name="merge",
    )(where, *(part for part, _, _, _ in parts))
    return out[:-1], out[-1]


def embed_kernel(where_ref, sums_ref, *refs, entries):
    part_refs, out_ref = refs[:-1], refs[-1]
    owned, width = out_ref.shape
    own = (where_ref[3] * owned + lax.broadcasted_iota(jnp.int32, (owned, entries), 0)).astype(F32)
    sums, counts = jnp.zeros((owned, width), F32), jnp.zeros((owned, 1), F32)
    for m, ref, k in relative(part_refs):
        there = ref[k, owned : owned + 1, :entries] == own
        count = ref[k, owned + 1 : owned + 2, :entries]
        counts += jnp.sum(jnp.where(there, count, 0.0), axis=1, keepdims=True)
        sums += jnp.dot(
            there.astype(F32),
            sums_ref[m * entries : (m + 1) * entries],
            precision=lax.Precision.HIGHEST,
            preferred_element_type=F32,
        )
    out_ref[...] = sums / jnp.maximum(counts, 1.0)


def spread_kernel(where_ref, *refs, chunk, rows, members):
    part_refs, weight_ref, bias_ref, place = refs[:-3], refs[-3], refs[-2], refs[-1]
    me = where_ref[3]
    count = len(members)
    for p, k in itertools.product(range(count), range(part_refs[0].shape[0])):
        bias, down, _ = read_note(part_refs[p][k], chunk)
        j = me ^ (members[p] + k * count)
        target = weight_ref if rows == place.shape[0] else place
        target[pl.ds(pl.multiple_of(j * chunk, 8), chunk)] = part_refs[p][k, :chunk] * down

        @pl.when(j == 0)
        def _():
            bias_ref[...] = bias

    if rows != place.shape[0]:
        weight_ref[...] = place[:rows]


def spread(where, parts, chunk, count, rows):
    parts = {m: part.astype(F32) for m, part in parts.items()}
    width = parts[0].shape[-1]
    return pl.pallas_call(
        functools.partial(spread_kernel, chunk=chunk, rows=rows, members=tuple(parts)),
        out_shape=(jax.ShapeDtypeStruct((rows, width), F32), jax.ShapeDtypeStruct((1, width), F32)),
        in_specs=[SMEM] + [VMEM] * len(parts),
        out_specs=(VMEM, VMEM),
        scratch_shapes=[pltpu.VMEM((count * chunk, width), F32)],
        compiler_params=params(),
        name="spread",
    )(where, *parts.values())


def body(
    section_input, conv_weight, conv_bias, deep_weight, deep_bias, labels, slot_ids, embed_grad
):
    chan_count = lax.axis_size("chan")
    strip_count = lax.axis_size("strip")
    chan_pos = lax.axis_index("chan")
    strip_pos = lax.axis_index("strip")
    half = chan_pos & 1
    channels = section_input.shape[-1]
    entries = slot_ids.shape[0]
    owned, width = embed_grad.shape
    where = jnp.stack(
        [half, (strip_pos == 0).astype(jnp.int32), (strip_pos == strip_count - 1).astype(jnp.int32), strip_pos]
    ).astype(jnp.int32)
    conv_w = conv_weight.reshape(9 * channels, -1)
    conv_b = conv_bias.reshape(1, -1)

    side, head, tail, sent, near_rows, near_w = start(
        where, section_input, conv_w, embed_grad, slot_ids, labels
    )
    pairs = []
    for s in range(strip_count):
        for c in range(chan_count):
            to = s + 1 - 2 * (c & 1)
            if 0 <= to < strip_count:
                pairs.append((s * chan_count + c, to * chan_count + c))
    got = lax.ppermute(sent, ("strip", "chan"), pairs)

    steps = [(at + 1, 1) for at in range(min(2, strip_count.bit_length() - 2))]
    steps += [(at, min(3, strip_count.bit_length() - 1 - at)) for at in range(3, strip_count.bit_length() - 1, 3)]
    ahead = gather_step(side, "strip", steps[0])
    taps = windows(where, near_rows, section_input.shape[0])
    shared = join(ahead, [taps])
    got, shared = lax.optimization_barrier((got, shared))
    traded = swap(got, "chan", 1)
    ahead = gather_step(shared, "strip", steps[1])
    pooled = conv_pool(where, taps, near_w, conv_b, section_input.shape[0] // 4, [shared, got])
    pooled, shared = lax.optimization_barrier((pooled, join(ahead, [pooled])))
    other = swap(pooled, "chan", 1)
    for step in steps[2:]:
        shared = join(gather_step(shared, "strip", step), [])
    shared = [shared, swap(shared, "strip", 1)]
    edges = conv_edges(where, near_w, conv_b, got, traded, head, tail, [pooled])

    chunk = -(-9 * channels // strip_count // 8) * 8
    bits = strip_count.bit_length() - 1
    ways = 8
    forward = deep_forward(
        where,
        pooled,
        other,
        edges,
        deep_weight.reshape(9 * channels, width),
        deep_bias.reshape(1, width),
        labels,
        entries,
    )
    heads = strip_count // ways
    size = heads * chunk

    def sent(part, mask):
        return swap(part.astype(F16), "strip", mask).astype(F32)

    kept, beside, near, across, paired, pair, far = deep_backward(
        where, forward, shared, chunk, strip_count
    )
    got_far, got_pair = sent(far, 6), sent(pair, 1)
    onward = merge_pair(paired, got_pair, [pair], size, entries, 0, size, [])
    beside = merge_pair(beside, got_far, [], size, entries, size, 2 * size, [onward])
    parts = [
        (kept, True, size, []),
        (sent(beside, 1), True, size, [7]),
        (sent(near, 2), True, size, [2]),
        (sent(across, 3), True, size, [3]),
        (sent(onward, 4), True, size, [4, 5]),
        (got_far, True, 2 * size, [6]),
        (pair, False, size, [0]),
        (got_pair, False, size, [1]),
    ]
    held, shift = ways, 3
    while True:
        step = min(3, bits - shift)
        send, sums = merge(where, parts, chunk, heads, entries, shift, 1 << step)
        if step == 0:
            break
        more = 1 << step
        heads //= more
        arrived = [send[0]] + [sent(send[m], m << shift) for m in range(1, more)]
        parts = [
            (part, True, heads * chunk, list(range(m * held, (m + 1) * held)))
            for m, part in enumerate(arrived)
        ]
        held *= more
        shift += step
    embeddings = pl.pallas_call(
        functools.partial(embed_kernel, entries=entries),
        out_shape=jax.ShapeDtypeStruct((owned, width), F32),
        in_specs=[SMEM] + [VMEM] * (1 + len(shared)),
        out_specs=VMEM,
        compiler_params=params(),
        name="embed",
    )(where, sums, *shared)
    own = send[0].astype(F16)[None]
    for at in range(3, bits, 3):
        own = jnp.concatenate(gather_step(own, "strip", (at, min(3, bits - at))), axis=0)
    gathered = {m: swap(own, "strip", m) if m else own for m in range(4)}
    for k in (2, 3):
        gathered[2 * k] = swap(own, "strip", 2 * k)
    late = {2 * k + 1: swap(gathered[2 * k], "strip", 1) for k in (2, 3)}
    weight_rows, bias_row = spread(
        where, {**gathered, **late}, chunk, strip_count, 9 * channels
    )
    return (embeddings, weight_rows.reshape(3, 3, channels, width), bias_row[0])


def solution(mesh):
    placed = (
        P(None, "strip", None),
        P(),
        P(),
        P(None, None, None, "chan"),
        P("chan"),
        P(None, "strip"),
        P("strip"),
        P("strip", "chan"),
    )
    return jax.shard_map(
        body,
        mesh=mesh,
        in_specs=placed,
        out_specs=(P("strip", "chan"), P(None, None, None, "chan"), P("chan")),
        check_vma=False,
    )
```

```python
import functools
import itertools
import math

import jax
import jax.numpy as jnp
from jax import lax
from jax.experimental import pallas as pl
from jax.experimental.pallas import tpu as pltpu
from jax.sharding import PartitionSpec as P

F32, BF16, F16 = jnp.float32, jnp.bfloat16, jnp.float16
VMEM = pl.BlockSpec(memory_space=pltpu.VMEM)
HBM = pl.BlockSpec(memory_space=pltpu.HBM)
ANY = pl.BlockSpec(memory_space=pl.ANY)
SIDE = 8
WIDTH = 3
PIECE = 4
STEP = 6
PAYLOADS = (((0,), 0), ((1,), 0), ((2,), 1), ((3,), 1), ((4,), 0), ((5,), 1), ((6, 7), 1))
NOTE = 16


def params(mib=8):
    return pltpu.CompilerParams(vmem_limit_bytes=mib << 20)


def position():
    strip = lax.axis_index("strip")
    last = lax.axis_size("strip") - 1
    return (
        lax.axis_index("chan") & 1,
        (strip == 0).astype(jnp.int32),
        (strip == last).astype(jnp.int32),
        strip,
    )


def swap(value, axis, mask):
    count = lax.axis_size(axis)
    return lax.ppermute(value, axis, [(i, i ^ mask) for i in range(count)])


def gather_step(held, axis, step):
    shift, size = step
    return [held] + [swap(held, axis, m << shift) for m in range(1, 1 << size)]


def relative(refs):
    half = len(refs) // 2
    for low in range(2):
        m = low
        for ref in refs[low * half : (low + 1) * half]:
            for k in range(ref.shape[0]):
                yield m, ref, k
                m += 2


def sigmoid(v):
    return jax.nn.sigmoid(v)


def shares(pooled_rows):
    first = pooled_rows // 2
    return first, pooled_rows - first


def pick(half, pair):
    return jnp.where(half == 0, pair[0], pair[1])


def share_rows(half, rows):
    first, second = shares(rows // 2)
    most = -(-(2 * max(first, second) + 1) // PIECE) * PIECE
    return most, pick(half, (0, rows - most)), pick(half, (-1, 2 * first - 1 - (rows - most)))


def window_kernel(rows_ref, taps, wide, *, rows):
    most, cols, chans = rows_ref.shape
    half_cols = cols // 2
    half = position()[0]
    _, _, before = share_rows(half, rows)
    shift = PIECE - before
    lanes = chans // 128
    border = jnp.zeros((8, 128), F32)
    for t in range(wide.shape[0]):
        wide[t, 0:8] = border
        wide[t, cols + 8 : cols + 16] = border

    def prepare(k, carry):
        for slot in range(PIECE):
            r = k * PIECE + slot
            x = rows_ref[r].astype(F32)
            for t in range(lanes):
                wide[slot * lanes + t, 8 : 8 + cols] = x[:, t * 128 : (t + 1) * 128]
            for tap in range(4):
                for t in range(lanes):
                    part = wide[slot * lanes + t, pl.ds(7 + tap, half_cols, stride=2), :]
                    at = (tap * lanes + t) * 128
                    taps[r + shift, :, at : at + 128] = part.astype(BF16)
        return carry

    lax.fori_loop(0, most // PIECE, prepare, 0)
    second = shares(rows // 2)[1]
    outside = pick(half, (PIECE, PIECE + 2 * second + 1))
    taps[outside] = jnp.zeros(taps.shape[1:], BF16)


def windows(near_rows, rows):
    most, cols, chans = near_rows.shape
    return pl.pallas_call(
        functools.partial(window_kernel, rows=rows),
        out_shape=jax.ShapeDtypeStruct((most + 2 * PIECE, cols // 2, 4 * chans), BF16),
        in_specs=[VMEM],
        out_specs=VMEM,
        scratch_shapes=[pltpu.VMEM((PIECE * (chans // 128), cols + 16, 128), F32)],
        compiler_params=params(16),
        cost_estimate=pl.CostEstimate(flops=0, bytes_accessed=12 << 20, transcendentals=0),
        name="windows",
    )(near_rows)


def edge_part(pairs, w_ref, bias, edge_ref, acc):
    rows = pairs[0].shape[0]
    chans = w_ref.shape[1]
    lanes = chans // 128
    depth = 3 * chans
    lhs = jnp.concatenate(
        [
            pairs[s][:, (2 * j + phase) * chans : (2 * j + phase + 3) * chans]
            for s in range(2)
            for j in range(2)
            for phase in range(2)
        ],
        axis=0,
    )
    pad = rows + 16
    for dr in range(3):
        part = jnp.dot(lhs, w_ref[dr * depth : (dr + 1) * depth], preferred_element_type=F32)
        for g in range(8):
            own = part[g * rows : (g + 1) * rows]
            for t in range(lanes):
                at = 9 - dr
                piece = own[:, t * 128 : (t + 1) * 128]
                if dr == 0:
                    acc[g * lanes + t, 0:8] = jnp.zeros((8, 128), F32)
                    acc[g * lanes + t, 8 + rows : pad] = jnp.zeros((8, 128), F32)
                    acc[g * lanes + t, 8:9] = jnp.zeros((1, 128), F32)
                    acc[g * lanes + t, at : at + rows] = piece
                else:
                    acc[g * lanes + t, at : at + rows] += piece
    for g in range(4):
        for t in range(lanes):
            total = None
            for phase in range(2):
                at = (2 * g + phase) * lanes + t
                v = acc[at, 8 : 8 + rows] + bias[:, t * 128 : (t + 1) * 128]
                acc[at, 8 : 8 + rows] = v * sigmoid(v)
                both = (
                    acc[at, pl.ds(8, rows // 2, stride=2), :]
                    + acc[at, pl.ds(9, rows // 2, stride=2), :]
                )
                total = both if total is None else total + both
            lost = jnp.where(g == 0, position()[1], jnp.where(g == 3, position()[2], 0))
            keep = jnp.where(lost > 0, 0.0, 0.25)
            edge_ref[g, t] = (total * keep).astype(BF16).astype(F32)


def conv_kernel(taps, w_ref, b_ref, *refs):
    out_ref = refs[-1]
    assert out_ref.shape[0] % STEP == 0
    half_cols, chans = taps.shape[1], taps.shape[2] // 4
    bias = b_ref[...]

    def step(k, carry):
        r0 = PIECE + k * 2 * STEP
        total = None
        for phase in range(2):
            lhs = jnp.concatenate(
                [
                    taps[pl.ds(r0 + dr, 2 * STEP), :, phase * chans : (phase + 3) * chans]
                    for dr in range(3)
                ],
                axis=-1,
            ).reshape(2 * STEP * half_cols, 9 * chans)
            v = jnp.dot(lhs, w_ref[...], preferred_element_type=F32) + bias
            h = (v * sigmoid(v)).reshape(STEP, 2, half_cols, chans)
            h = h[:, 0] + h[:, 1]
            total = h if total is None else total + h
        out_ref[pl.ds(k * STEP, STEP)] = (total * 0.25).astype(BF16)
        return carry

    for k in range(out_ref.shape[0] // STEP):
        step(k, 0)


def conv_pool(taps, w, b, pooled_rows, after):
    _, half_cols, width = taps.shape
    chans = width // 4
    return pl.pallas_call(
        conv_kernel,
        out_shape=jax.ShapeDtypeStruct((pooled_rows, half_cols, chans), BF16),
        in_specs=[VMEM] * 3 + [ANY] * len(after),
        out_specs=VMEM,
        compiler_params=params(16),
        cost_estimate=pl.CostEstimate(
            flops=8 * pooled_rows * half_cols * 9 * chans * chans,
            bytes_accessed=8 << 20,
            transcendentals=0,
        ),
        name="conv_pool",
    )(taps, w, b, *after)


def edge_kernel(w_ref, b_ref, got_ref, traded_ref, head_ref, tail_ref, *refs):
    edge_ref, acc = refs[-2:]
    half = position()[0]
    got, traded = got_ref[...], traded_ref[...]
    left = jnp.concatenate([jnp.where(half == 0, got, traded), head_ref[...]], axis=-1)
    right = jnp.concatenate([tail_ref[...], jnp.where(half == 0, traded, got)], axis=-1)
    edge_part((left, right), w_ref, b_ref[...], edge_ref, acc)


def conv_edges(w, b, got, traded, head, tail, after):
    rows, lanes = head.shape[0], w.shape[1] // 128
    return pl.pallas_call(
        edge_kernel,
        out_shape=jax.ShapeDtypeStruct((4, lanes, rows // 2, 128), F32),
        in_specs=[VMEM] * 6 + [ANY] * len(after),
        out_specs=VMEM,
        scratch_shapes=[pltpu.VMEM((8 * lanes, rows + 16, 128), F32)],
        compiler_params=params(),
        cost_estimate=pl.CostEstimate(flops=0, bytes_accessed=4 << 20, transcendentals=0),
        name="conv_edges",
    )(w, b, got, traded, head, tail, *after)


def start_kernel(
    x_hbm, w_hbm, grad_hbm, labels_hbm, slots_hbm,
    side_ref, head_ref, tail_ref, send_ref, near_ref, w_ref,
    labels_ref, slots_ref, left, right, wide, sems,
):
    owned, width = grad_hbm.shape
    rows, cols, chans = x_hbm.shape
    entries = slots_ref.shape[1]
    reach = left.shape[1]
    half = position()[0]
    copies = [
        pltpu.make_async_copy(labels_hbm, labels_ref, sems.at[0]),
        pltpu.make_async_copy(grad_hbm, side_ref.at[0, pl.ds(0, owned)], sems.at[1]),
        pltpu.make_async_copy(x_hbm.at[:, pl.ds(0, reach)], left, sems.at[2]),
        pltpu.make_async_copy(x_hbm.at[:, pl.ds(cols - reach, reach)], right, sems.at[3]),
        pltpu.make_async_copy(slots_hbm, slots_ref, sems.at[4]),
    ]
    most, first, _ = share_rows(half, rows)
    size = most // 4
    for k in range(4):
        source = x_hbm.at[pl.ds(first + k * size, size)]
        copies.append(
            pltpu.make_async_copy(source, near_ref.at[pl.ds(k * size, size)], sems.at[5 + k])
        )
    copies.append(pltpu.make_async_copy(w_hbm, w_ref, sems.at[9]))
    for copy in copies:
        copy.start()
    lane = lax.broadcasted_iota(jnp.int32, (1, width), 1)
    copies[0].wait()
    copies[4].wait()
    ids = jnp.concatenate(
        [slots_ref[...].astype(F32), jnp.zeros((1, width - entries), F32)], axis=1
    )
    labels = labels_ref[...]
    counts = jnp.zeros((1, width), F32)
    for e in range(entries):
        hit = jnp.where(labels == e, 1.0, 0.0)
        hit = jnp.sum(jnp.sum(hit, axis=0, keepdims=True), axis=1, keepdims=True)
        counts = jnp.where(lane == e, hit, counts)
    row = lax.broadcasted_iota(jnp.int32, (SIDE, width), 0)
    side_ref[0, owned:] = jnp.where(row == 0, ids, jnp.where(row == 1, counts, 0.0))
    lanes = chans // 128
    copies[2].wait()
    copies[3].wait()
    for ref, out_ref, at, sent in ((left, head_ref, 0, 1), (right, tail_ref, reach - WIDTH, 0)):
        x = ref[...].astype(F32).reshape(rows * reach, chans)
        for t in range(lanes):
            wide[t] = x[:, t * 128 : (t + 1) * 128]
        for c in range(WIDTH):
            for t in range(lanes):
                part = wide[t, pl.ds(at + c, rows, stride=reach), :].astype(BF16)
                place = (c * lanes + t) * 128
                out_ref[:, place : place + 128] = part
    send_ref[...] = jnp.where(half == 0, tail_ref[...], head_ref[...])
    copies[1].wait()
    for copy in copies[5:]:
        copy.wait()


def start(x, w, grad, slots, labels):
    owned, width = grad.shape
    rows, cols, chans = x.shape
    reach = 16
    most = share_rows(0, rows)[0]
    columns = jax.ShapeDtypeStruct((rows, WIDTH * chans), BF16)
    fixed = [
        pltpu.with_memory_space_constraint(a, pltpu.HBM)
        for a in (x, w, grad, labels, slots.reshape(1, -1))
    ]
    return pl.pallas_call(
        start_kernel,
        out_shape=(jax.ShapeDtypeStruct((1, owned + SIDE, width), F32),)
        + (columns,) * 3
        + (jax.ShapeDtypeStruct((most, cols, chans), BF16), jax.ShapeDtypeStruct(w.shape, BF16)),
        in_specs=[HBM] * 5,
        out_specs=(VMEM,) * 6,
        scratch_shapes=[
            pltpu.VMEM(labels.shape, jnp.int32),
            pltpu.VMEM((1, slots.shape[0]), jnp.int32),
            pltpu.VMEM((rows, reach, chans), BF16),
            pltpu.VMEM((rows, reach, chans), BF16),
            pltpu.VMEM((chans // 128, rows * reach, 128), F32),
            pltpu.SemaphoreType.DMA((10,)),
        ],
        compiler_params=params(16),
        name="start",
    )(*fixed)


def join_kernel(*refs, count):
    at = 0
    for ref in refs[:count]:
        refs[-1][at : at + ref.shape[0]] = ref[...]
        at += ref.shape[0]


def join(parts, after):
    shape = (sum(p.shape[0] for p in parts),) + parts[0].shape[1:]
    return pl.pallas_call(
        functools.partial(join_kernel, count=len(parts)),
        out_shape=jax.ShapeDtypeStruct(shape, F32),
        in_specs=[VMEM] * len(parts) + [ANY] * len(after),
        out_specs=VMEM,
        compiler_params=params(),
        name="join",
    )(*parts, *after)


def scale_rows(block, note_rows, sums):
    def exponent(values):
        top = None
        for v in values:
            one = jnp.max(jnp.max(jnp.abs(v), axis=0, keepdims=True), axis=1, keepdims=True)
            top = one if top is None else jnp.maximum(top, one)
        return jnp.ceil(jnp.log2(jnp.maximum(top, 1e-30)))

    power = exponent([block, note_rows])
    power_sums = exponent([sums])
    return power, power_sums


def note_block(bias, power, power_sums, width):
    row = lax.broadcasted_iota(jnp.int32, (NOTE, width), 0)
    bias = jnp.broadcast_to(bias, (NOTE, width))
    power = jnp.broadcast_to(power, (NOTE, width))
    power_sums = jnp.broadcast_to(power_sums, (NOTE, width))
    return jnp.where(row == 0, bias, jnp.where(row == 1, power, power_sums))


def read_note(part, at):
    note = part[at : at + NOTE]
    down = jnp.exp2(note[1:2] - 12.0)
    return note[0:1] * down, down, jnp.exp2(note[2:3] - 12.0)


def deep_kernel(
    own_ref, other_ref, edge_ref, w_ref, b_ref, lab_ref, taps, member, slope, sums_ref, wide,
    inside, *, block, entries
):
    _, cols, chans = own_ref.shape
    rows = lab_ref.shape[0]
    lanes = chans // 128
    width = w_ref.shape[-1]
    half = position()[0]
    taps[0] = jnp.zeros(taps.shape[1:], BF16)
    taps[rows + 1] = jnp.zeros(taps.shape[1:], BF16)

    def prepare(ref, base, i, slot):
        x = ref[i].astype(F32)
        r = base + i
        for t in range(lanes):
            s = slot * lanes + t
            at = t * 128
            wide[s, 8 : 8 + cols] = x[:, at : at + 128]
            for g, place in enumerate((7, 8, 7 + cols, 8 + cols)):
                wide[s, place : place + 1] = edge_ref[g, t, pl.ds(r, 1), :]
        for tap in range(3):
            for t in range(lanes):
                piece = wide[slot * lanes + t, 7 + tap : 7 + tap + cols, :]
                at = (tap * lanes + t) * 128
                taps[r + 1, :, at : at + 128] = piece.astype(BF16)

    first, second = shares(rows)
    times = math.gcd(first, second)

    def prepare_all(even_ref, odd_ref):
        def prepare_rows(k, carry):
            for q in range(rows // times):
                ref, base = (even_ref, 0) if q < first // times else (odd_ref, first)
                prepare(ref, base, q * times - base + k, q)
            return carry

        lax.fori_loop(0, times, prepare_rows, 0)

    @pl.when(half == 0)
    def _():
        prepare_all(own_ref, other_ref)

    @pl.when(half != 0)
    def _():
        prepare_all(other_ref, own_ref)

    lab = jnp.transpose(lab_ref[...].astype(F32))
    lane = lax.broadcasted_iota(jnp.int32, (cols, 128), 1)
    want = jnp.where(lane < 3 * entries, lane % entries, -1).astype(F32)
    for r in range(rows):
        member[r] = (lab[:, r : r + 1] == want).astype(BF16)
    bias = b_ref[...]
    size = block * cols

    flat = jnp.concatenate([lab_ref[r : r + 1, :] for r in range(rows)], axis=1)
    entry = lax.broadcasted_iota(jnp.int32, (entries, rows * cols), 0)
    inside[...] = jnp.where(jnp.broadcast_to(flat, entry.shape) == entry, 1.0, 0.0).astype(BF16)

    def step(k, sums):
        r0 = k * block
        lhs = jnp.concatenate([taps[pl.ds(r0 + dr, block)] for dr in range(3)], axis=-1)
        v = jnp.dot(lhs.reshape(size, 9 * chans), w_ref[...], preferred_element_type=F32) + bias
        sig = sigmoid(v)
        features = (v * sig).astype(BF16)
        slope[pl.ds(k * size, size)] = sig * (1.0 + v * (1.0 - sig))
        mine = inside[:, pl.ds(pl.multiple_of(k * size, 128), size)]
        return sums + jnp.dot(mine, features, preferred_element_type=F32)

    sums_ref[...] = lax.fori_loop(0, rows // block, step, jnp.zeros((entries, width), F32))


def deep_forward(own, other, edges, w, b, labels, entries):
    _, cols, chans = own.shape
    rows, width = labels.shape[0], w.shape[-1]
    block = next(k for k in (8, 4, 2, 1) if rows % k == 0)
    first, second = shares(rows)
    slots = rows // math.gcd(first, second)
    return pl.pallas_call(
        functools.partial(deep_kernel, block=block, entries=entries),
        out_shape=(
            jax.ShapeDtypeStruct((rows + 2, cols, 3 * chans), BF16),
            jax.ShapeDtypeStruct((rows, cols, 128), BF16),
            jax.ShapeDtypeStruct((rows * cols, width), F32),
            jax.ShapeDtypeStruct((entries, width), F32),
        ),
        in_specs=[VMEM] * 6,
        out_specs=(VMEM,) * 4,
        scratch_shapes=[
            pltpu.VMEM((slots * (chans // 128), cols + 16, 128), F32),
            pltpu.VMEM((entries, rows * cols), BF16),
        ],
        compiler_params=params(16),
        cost_estimate=pl.CostEstimate(
            flops=4 * rows * cols * 9 * chans * width, bytes_accessed=8 << 20, transcendentals=0
        ),
        name="deep_forward",
    )(own, other, edges, w, b, labels)


def grad_kernel(
    taps, member, slope, sums_ref, *refs, n_parts, chunk
):
    part_refs = refs[:n_parts]
    out_refs, weight = refs[n_parts:-1], refs[-1]
    rows, cols, depth = member.shape[0], taps.shape[1], taps.shape[2]
    width = slope.shape[-1]
    me = position()[3]
    entries = sums_ref.shape[0]
    owned = part_refs[0].shape[1] - SIDE
    own_ids = jnp.broadcast_to(part_refs[0][0, owned : owned + 1, :entries], (entries, entries))
    across = lax.broadcasted_iota(jnp.int32, (entries, entries), 1)
    down = lax.broadcasted_iota(jnp.int32, (entries, entries), 0)
    ids = jnp.sum(jnp.where(across == down, own_ids, 0.0), axis=1, keepdims=True).astype(jnp.int32)
    total = jnp.zeros((entries, 1), F32)
    entry_grad = jnp.zeros((entries, width), F32)
    owner, inner = ids // owned, ids % owned
    spot = lax.broadcasted_iota(jnp.int32, (entries, owned), 1)
    for m, ref, k in relative(part_refs):
        there = ref[k, owned : owned + 1, :entries] == ids.astype(F32)
        counts = ref[k, owned + 1 : owned + 2, :entries]
        total += jnp.sum(jnp.where(there, counts, 0.0), axis=1, keepdims=True)
        hot = ((owner ^ me) == m) & (inner == spot)
        entry_grad += jnp.dot(
            hot.astype(F32), ref[k, :owned], precision=lax.Precision.HIGHEST, preferred_element_type=F32
        )
    entry_grad = entry_grad / jnp.maximum(total, 1.0)
    high = entry_grad.astype(BF16)
    rest = entry_grad - high.astype(F32)
    mid = rest.astype(BF16)
    low = (rest - mid.astype(F32)).astype(BF16)
    terms = jnp.concatenate([high, mid, low, jnp.zeros((128 - 3 * entries, width), BF16)], axis=0)
    pixel = jnp.dot(member[...].reshape(rows * cols, 128), terms, preferred_element_type=F32)
    dg = (pixel * slope[...]).astype(BF16)
    turned = jnp.transpose(dg)
    bias_sum = jnp.sum(dg.astype(F32), axis=0, keepdims=True)
    for dr in range(3):
        window = taps[dr : dr + rows].reshape(rows * cols, depth)
        out = jnp.dot(turned, window, preferred_element_type=F32)
        weight[dr * depth : (dr + 1) * depth] = jnp.transpose(out)
    if weight.shape[0] > 3 * depth:
        weight[3 * depth :] = jnp.zeros((weight.shape[0] - 3 * depth, width), F32)
    sums = sums_ref[...]
    power, power_sums = scale_rows(weight[...], bias_sum, sums)
    up = jnp.exp2(12.0 - power)
    note = note_block(bias_sum * up, power, power_sums, width)
    ways = 8
    digit = lax.rem(me, ways)
    heads = weight.shape[0] // chunk // ways
    sums = sums * jnp.exp2(12.0 - power_sums)
    for out_ref, (members, with_sums) in zip(out_refs, PAYLOADS):
        at = 0
        for m, hi in itertools.product(members, range(heads)):
            j = hi * ways + (digit ^ m)
            out_ref[at : at + chunk] = weight[pl.ds(pl.multiple_of(j * chunk, 8), chunk)] * up
            at += chunk
        out_ref[at : at + NOTE] = note
        if with_sums:
            out_ref[at + NOTE :] = sums


def deep_backward(forward, parts, chunk, count):
    taps, _, slope, sums = forward
    width, entries = slope.shape[-1], sums.shape[0]
    size = count // 8 * chunk
    return pl.pallas_call(
        functools.partial(grad_kernel, n_parts=len(parts), chunk=chunk),
        out_shape=tuple(
            jax.ShapeDtypeStruct((len(members) * size + NOTE + with_sums * entries, width), F32)
            for members, with_sums in PAYLOADS
        ),
        in_specs=[VMEM] * (4 + len(parts)),
        out_specs=(VMEM,) * len(PAYLOADS),
        scratch_shapes=[pltpu.VMEM((count * chunk, width), F32)],
        compiler_params=params(16),
        cost_estimate=pl.CostEstimate(
            flops=4 * slope.shape[0] * 3 * taps.shape[2] * width, bytes_accessed=8 << 20, transcendentals=0
        ),
        name="deep_backward",
    )(*forward, *parts)


def pair_kernel(own_ref, got_ref, *refs, size, entries, got_at, got_note, with_own):
    out_ref = refs[-1]
    own, got = own_ref[size : size + NOTE], got_ref[got_note : got_note + NOTE]
    power = jnp.maximum(own[1:2], got[1:2]) + 1.0
    power_sums = jnp.maximum(own[2:3], got[2:3])
    own_down, got_down = jnp.exp2(own[1:2] - power), jnp.exp2(got[1:2] - power)
    out_ref[:size] = own_ref[:size] * own_down + got_ref[got_at : got_at + size] * got_down
    bias = own[0:1] * own_down + got[0:1] * got_down
    out_ref[size : size + NOTE] = note_block(bias, power, power_sums, own.shape[-1])
    at = size + NOTE
    if with_own:
        sums = refs[0][at : at + entries] * jnp.exp2(own[2:3] - power_sums)
        out_ref[at : at + entries] = sums
        at += entries
    sums = got_ref[got_note + NOTE : got_note + NOTE + entries] * jnp.exp2(got[2:3] - power_sums)
    out_ref[at : at + entries] = sums


def merge_pair(own, got, own_sums, size, entries, got_at, got_note, after):
    width = own.shape[-1]
    rows = size + NOTE + (1 + len(own_sums)) * entries
    return pl.pallas_call(
        functools.partial(
            pair_kernel,
            size=size,
            entries=entries,
            got_at=got_at,
            got_note=got_note,
            with_own=bool(own_sums),
        ),
        out_shape=jax.ShapeDtypeStruct((rows, width), F32),
        in_specs=[VMEM] * (2 + len(own_sums)) + [ANY] * len(after),
        out_specs=VMEM,
        compiler_params=params(),
        name="merge_pair",
    )(own, got, *own_sums, *after)


def merge_kernel(*refs, plan, chunk, heads, entries, shift, next_ways):
    n_parts = len(plan)
    part_refs, out_refs, sums_ref = refs[:n_parts], refs[n_parts:-1], refs[-1]
    width = part_refs[0].shape[-1]
    size = heads * chunk
    total, bias = jnp.zeros((size, width), F32), jnp.zeros((1, width), F32)
    for ref, (added, note_at, members) in zip(part_refs, plan):
        more, down, down_sums = read_note(ref, note_at)
        if added:
            total, bias = total + ref[:size] * down, bias + more
        for k, m in enumerate(members):
            at = note_at + NOTE + k * entries
            sums_ref[m * entries : (m + 1) * entries] = ref[at : at + entries] * down_sums
    sums = sums_ref[...]
    power, power_sums = scale_rows(total, bias, sums)
    up = jnp.exp2(12.0 - power)
    note = note_block(bias * up, power, power_sums, width)
    total = total * up
    if next_ways == 1:
        out_refs[0][:size] = total
        out_refs[0][size:] = note
        return
    sums = sums * jnp.exp2(12.0 - power_sums)
    digit = lax.rem(position()[3] >> shift, next_ways)
    for m in range(next_ways):
        for hi in range(heads // next_ways):
            piece = jnp.zeros((chunk, width), F32)
            for d in range(next_ways):
                at = (hi * next_ways + d) * chunk
                piece = jnp.where((digit ^ m) == d, total[at : at + chunk], piece)
            out_refs[m][hi * chunk : (hi + 1) * chunk] = piece
        at = heads // next_ways * chunk
        out_refs[m][at : at + NOTE] = note
        out_refs[m][at + NOTE :] = sums


def merge(parts, chunk, heads, entries, shift, next_ways):
    width = parts[0][0].shape[-1]
    sums_rows = sum(len(members) for _, _, _, members in parts) * entries
    if next_ways == 1:
        outs = (jax.ShapeDtypeStruct((heads * chunk + NOTE, width), F32),)
    else:
        rows = heads // next_ways * chunk + NOTE + sums_rows
        outs = (jax.ShapeDtypeStruct((rows, width), F32),) * next_ways
    outs = outs + (jax.ShapeDtypeStruct((sums_rows, width), F32),)
    out = pl.pallas_call(
        functools.partial(
            merge_kernel,
            plan=tuple((added, at, tuple(members)) for _, added, at, members in parts),
            chunk=chunk,
            heads=heads,
            entries=entries,
            shift=shift,
            next_ways=next_ways,
        ),
        out_shape=outs,
        in_specs=[VMEM] * len(parts),
        out_specs=(VMEM,) * len(outs),
        compiler_params=params(),
        name="merge",
    )(*(part for part, _, _, _ in parts))
    return out[:-1], out[-1]


def embed_kernel(sums_ref, *refs, entries):
    part_refs, out_ref = refs[:-1], refs[-1]
    owned, width = out_ref.shape
    own = (position()[3] * owned + lax.broadcasted_iota(jnp.int32, (owned, entries), 0)).astype(F32)
    sums, counts = jnp.zeros((owned, width), F32), jnp.zeros((owned, 1), F32)
    for m, ref, k in relative(part_refs):
        there = ref[k, owned : owned + 1, :entries] == own
        count = ref[k, owned + 1 : owned + 2, :entries]
        counts += jnp.sum(jnp.where(there, count, 0.0), axis=1, keepdims=True)
        sums += jnp.dot(
            there.astype(F32),
            sums_ref[m * entries : (m + 1) * entries],
            precision=lax.Precision.HIGHEST,
            preferred_element_type=F32,
        )
    out_ref[...] = sums / jnp.maximum(counts, 1.0)


def spread_kernel(*refs, chunk, rows, members):
    part_refs, weight_ref, bias_ref, place = refs[:-3], refs[-3], refs[-2], refs[-1]
    me = position()[3]
    count = len(members)
    for p, k in itertools.product(range(count), range(part_refs[0].shape[0])):
        bias, down, _ = read_note(part_refs[p][k], chunk)
        j = me ^ (members[p] + k * count)
        target = weight_ref if rows == place.shape[0] else place
        target[pl.ds(pl.multiple_of(j * chunk, 8), chunk)] = part_refs[p][k, :chunk] * down

        @pl.when(j == 0)
        def _():
            bias_ref[...] = bias

    if rows != place.shape[0]:
        weight_ref[...] = place[:rows]


def spread(parts, chunk, count, rows):
    parts = {m: part.astype(F32) for m, part in parts.items()}
    width = parts[0].shape[-1]
    return pl.pallas_call(
        functools.partial(spread_kernel, chunk=chunk, rows=rows, members=tuple(parts)),
        out_shape=(jax.ShapeDtypeStruct((rows, width), F32), jax.ShapeDtypeStruct((1, width), F32)),
        in_specs=[VMEM] * len(parts),
        out_specs=(VMEM, VMEM),
        scratch_shapes=[pltpu.VMEM((count * chunk, width), F32)],
        compiler_params=params(),
        name="spread",
    )(*parts.values())


def body(
    section_input, conv_weight, conv_bias, deep_weight, deep_bias, labels, slot_ids, embed_grad
):
    chan_count = lax.axis_size("chan")
    strip_count = lax.axis_size("strip")
    channels = section_input.shape[-1]
    entries = slot_ids.shape[0]
    owned, width = embed_grad.shape
    conv_w = conv_weight.reshape(9 * channels, -1)
    conv_b = conv_bias.reshape(1, -1)

    side, head, tail, sent, near_rows, near_w = start(
        section_input, conv_w, embed_grad, slot_ids, labels
    )
    pairs = []
    for s in range(strip_count):
        for c in range(chan_count):
            to = s + 1 - 2 * (c & 1)
            if 0 <= to < strip_count:
                pairs.append((s * chan_count + c, to * chan_count + c))
    got = lax.ppermute(sent, ("strip", "chan"), pairs)

    steps = [(at + 1, 1) for at in range(min(2, strip_count.bit_length() - 2))]
    steps += [(at, min(3, strip_count.bit_length() - 1 - at)) for at in range(3, strip_count.bit_length() - 1, 3)]
    ahead = gather_step(side, "strip", steps[0])
    taps = windows(near_rows, section_input.shape[0])
    shared = join(ahead, [taps])
    got, shared = lax.optimization_barrier((got, shared))
    traded = swap(got, "chan", 1)
    ahead = gather_step(shared, "strip", steps[1])
    pooled = conv_pool(taps, near_w, conv_b, section_input.shape[0] // 4, [shared, got])
    pooled, shared = lax.optimization_barrier((pooled, join(ahead, [pooled])))
    other = swap(pooled, "chan", 1)
    for step in steps[2:]:
        shared = join(gather_step(shared, "strip", step), [])
    shared = [shared, swap(shared, "strip", 1)]
    edges = conv_edges(near_w, conv_b, got, traded, head, tail, [pooled])

    chunk = -(-9 * channels // strip_count // 8) * 8
    bits = strip_count.bit_length() - 1
    ways = 8
    forward = deep_forward(
                pooled,
        other,
        edges,
        deep_weight.reshape(9 * channels, width),
        deep_bias.reshape(1, width),
        labels,
        entries,
    )
    heads = strip_count // ways
    size = heads * chunk

    def sent(part, mask):
        return swap(part.astype(F16), "strip", mask).astype(F32)

    kept, beside, near, across, paired, pair, far = deep_backward(
        forward, shared, chunk, strip_count
    )
    got_far, got_pair = sent(far, 6), sent(pair, 1)
    onward = merge_pair(paired, got_pair, [pair], size, entries, 0, size, [])
    beside = merge_pair(beside, got_far, [], size, entries, size, 2 * size, [onward])
    parts = [
        (kept, True, size, []),
        (sent(beside, 1), True, size, [7]),
        (sent(near, 2), True, size, [2]),
        (sent(across, 3), True, size, [3]),
        (sent(onward, 4), True, size, [4, 5]),
        (got_far, True, 2 * size, [6]),
        (pair, False, size, [0]),
        (got_pair, False, size, [1]),
    ]
    held, shift = ways, 3
    while True:
        step = min(3, bits - shift)
        send, sums = merge(parts, chunk, heads, entries, shift, 1 << step)
        if step == 0:
            break
        more = 1 << step
        heads //= more
        arrived = [send[0]] + [sent(send[m], m << shift) for m in range(1, more)]
        parts = [
            (part, True, heads * chunk, list(range(m * held, (m + 1) * held)))
            for m, part in enumerate(arrived)
        ]
        held *= more
        shift += step
    embeddings = pl.pallas_call(
        functools.partial(embed_kernel, entries=entries),
        out_shape=jax.ShapeDtypeStruct((owned, width), F32),
        in_specs=[VMEM] * (1 + len(shared)),
        out_specs=VMEM,
        compiler_params=params(),
        name="embed",
    )(sums, *shared)
    own = send[0].astype(F16)[None]
    for at in range(3, bits, 3):
        own = jnp.concatenate(gather_step(own, "strip", (at, min(3, bits - at))), axis=0)
    gathered = {m: swap(own, "strip", m) if m else own for m in range(4)}
    for k in (2, 3):
        gathered[2 * k] = swap(own, "strip", 2 * k)
    late = {2 * k + 1: swap(gathered[2 * k], "strip", 1) for k in (2, 3)}
    weight_rows, bias_row = spread(
        {**gathered, **late}, chunk, strip_count, 9 * channels
    )
    return (embeddings, weight_rows.reshape(3, 3, channels, width), bias_row[0])


def solution(mesh):
    placed = (
        P(None, "strip", None),
        P(),
        P(),
        P(None, None, None, "chan"),
        P("chan"),
        P(None, "strip"),
        P("strip"),
        P("strip", "chan"),
    )
    return jax.shard_map(
        body,
        mesh=mesh,
        in_specs=placed,
        out_specs=(P("strip", "chan"), P(None, None, None, "chan"), P("chan")),
        check_vma=False,
    )
```

```python
import functools
import itertools
import math

import jax
import jax.numpy as jnp
from jax import lax
from jax.experimental import pallas as pl
from jax.experimental.pallas import tpu as pltpu
from jax.sharding import PartitionSpec as P

F32, BF16, F16 = jnp.float32, jnp.bfloat16, jnp.float16
VMEM = pl.BlockSpec(memory_space=pltpu.VMEM)
HBM = pl.BlockSpec(memory_space=pltpu.HBM)
ANY = pl.BlockSpec(memory_space=pl.ANY)
SIDE = 8
WIDTH = 3
PIECE = 4
STEP = 6
PAYLOADS = (((0,), 0), ((1,), 0), ((2,), 1), ((3,), 1), ((4,), 0), ((5,), 1), ((6, 7), 1))
NOTE = 8


def params(mib=8):
    return pltpu.CompilerParams(vmem_limit_bytes=mib << 20)


def position():
    strip = lax.axis_index("strip")
    last = lax.axis_size("strip") - 1
    return (
        lax.axis_index("chan") & 1,
        (strip == 0).astype(jnp.int32),
        (strip == last).astype(jnp.int32),
        strip,
    )


def swap(value, axis, mask):
    count = lax.axis_size(axis)
    return lax.ppermute(value, axis, [(i, i ^ mask) for i in range(count)])


def gather_step(held, axis, step):
    shift, size = step
    return [held] + [swap(held, axis, m << shift) for m in range(1, 1 << size)]


def relative(refs):
    half = len(refs) // 2
    for low in range(2):
        m = low
        for ref in refs[low * half : (low + 1) * half]:
            for k in range(ref.shape[0]):
                yield m, ref, k
                m += 2


def sigmoid(v):
    return jax.nn.sigmoid(v)


def shares(pooled_rows):
    first = pooled_rows // 2
    return first, pooled_rows - first


def pick(half, pair):
    return jnp.where(half == 0, pair[0], pair[1])


def share_rows(half, rows):
    first, second = shares(rows // 2)
    most = -(-(2 * max(first, second) + 1) // PIECE) * PIECE
    return most, pick(half, (0, rows - most)), pick(half, (-1, 2 * first - 1 - (rows - most)))


def window_kernel(rows_ref, *refs, rows):
    taps, wide = refs[-2:]
    most, cols, chans = rows_ref.shape
    half_cols = cols // 2
    half = position()[0]
    _, _, before = share_rows(half, rows)
    shift = PIECE - before
    lanes = chans // 128
    border = jnp.zeros((8, 128), F32)
    for t in range(wide.shape[0]):
        wide[t, 0:8] = border
        wide[t, cols + 8 : cols + 16] = border

    def prepare(k, carry):
        for slot in range(PIECE):
            r = k * PIECE + slot
            x = rows_ref[r].astype(F32)
            for t in range(lanes):
                wide[slot * lanes + t, 8 : 8 + cols] = x[:, t * 128 : (t + 1) * 128]
            for tap in range(4):
                for t in range(lanes):
                    part = wide[slot * lanes + t, pl.ds(7 + tap, half_cols, stride=2), :]
                    at = (tap * lanes + t) * 128
                    taps[r + shift, :, at : at + 128] = part.astype(BF16)
        return carry

    lax.fori_loop(0, most // PIECE, prepare, 0)
    second = shares(rows // 2)[1]
    outside = pick(half, (PIECE, PIECE + 2 * second + 1))
    taps[outside] = jnp.zeros(taps.shape[1:], BF16)


def windows(near_rows, rows, after):
    most, cols, chans = near_rows.shape
    return pl.pallas_call(
        functools.partial(window_kernel, rows=rows),
        out_shape=jax.ShapeDtypeStruct((most + 2 * PIECE, cols // 2, 4 * chans), BF16),
        in_specs=[VMEM] + [ANY] * len(after),
        out_specs=VMEM,
        scratch_shapes=[pltpu.VMEM((PIECE * (chans // 128), cols + 16, 128), F32)],
        compiler_params=params(16),
        cost_estimate=pl.CostEstimate(flops=0, bytes_accessed=12 << 20, transcendentals=0),
        name="windows",
    )(near_rows, *after)


def edge_part(pairs, w_ref, bias, edge_ref, acc):
    rows = pairs[0].shape[0]
    chans = w_ref.shape[1]
    lanes = chans // 128
    depth = 3 * chans
    lhs = jnp.concatenate(
        [
            pairs[s][:, (2 * j + phase) * chans : (2 * j + phase + 3) * chans]
            for s in range(2)
            for j in range(2)
            for phase in range(2)
        ],
        axis=0,
    )
    pad = rows + 16
    for dr in range(3):
        part = jnp.dot(lhs, w_ref[dr * depth : (dr + 1) * depth], preferred_element_type=F32)
        for g in range(8):
            own = part[g * rows : (g + 1) * rows]
            for t in range(lanes):
                at = 9 - dr
                piece = own[:, t * 128 : (t + 1) * 128]
                if dr == 0:
                    acc[g * lanes + t, 0:8] = jnp.zeros((8, 128), F32)
                    acc[g * lanes + t, 8 + rows : pad] = jnp.zeros((8, 128), F32)
                    acc[g * lanes + t, 8:9] = jnp.zeros((1, 128), F32)
                    acc[g * lanes + t, at : at + rows] = piece
                else:
                    acc[g * lanes + t, at : at + rows] += piece
    for g in range(4):
        for t in range(lanes):
            total = None
            for phase in range(2):
                at = (2 * g + phase) * lanes + t
                v = acc[at, 8 : 8 + rows] + bias[:, t * 128 : (t + 1) * 128]
                acc[at, 8 : 8 + rows] = v * sigmoid(v)
                both = (
                    acc[at, pl.ds(8, rows // 2, stride=2), :]
                    + acc[at, pl.ds(9, rows // 2, stride=2), :]
                )
                total = both if total is None else total + both
            lost = jnp.where(g == 0, position()[1], jnp.where(g == 3, position()[2], 0))
            keep = jnp.where(lost > 0, 0.0, 0.25)
            edge_ref[g, t] = (total * keep).astype(BF16).astype(F32)


def conv_kernel(taps, w_ref, b_ref, *refs):
    out_ref = refs[-1]
    assert out_ref.shape[0] % STEP == 0
    half_cols, chans = taps.shape[1], taps.shape[2] // 4
    bias = b_ref[...]

    def step(k, carry):
        r0 = PIECE + k * 2 * STEP
        total = None
        for phase in range(2):
            lhs = jnp.concatenate(
                [
                    taps[pl.ds(r0 + dr, 2 * STEP), :, phase * chans : (phase + 3) * chans]
                    for dr in range(3)
                ],
                axis=-1,
            ).reshape(2 * STEP * half_cols, 9 * chans)
            v = jnp.dot(lhs, w_ref[...], preferred_element_type=F32) + bias
            h = (v * sigmoid(v)).reshape(STEP, 2, half_cols, chans)
            h = h[:, 0] + h[:, 1]
            total = h if total is None else total + h
        out_ref[pl.ds(k * STEP, STEP)] = (total * 0.25).astype(BF16)
        return carry

    for k in range(out_ref.shape[0] // STEP):
        step(k, 0)


def conv_pool(taps, w, b, pooled_rows, after):
    _, half_cols, width = taps.shape
    chans = width // 4
    return pl.pallas_call(
        conv_kernel,
        out_shape=jax.ShapeDtypeStruct((pooled_rows, half_cols, chans), BF16),
        in_specs=[VMEM] * 3 + [ANY] * len(after),
        out_specs=VMEM,
        compiler_params=params(16),
        cost_estimate=pl.CostEstimate(
            flops=8 * pooled_rows * half_cols * 9 * chans * chans,
            bytes_accessed=8 << 20,
            transcendentals=0,
        ),
        name="conv_pool",
    )(taps, w, b, *after)


def edge_kernel(w_ref, b_ref, got_ref, traded_ref, head_ref, tail_ref, *refs):
    edge_ref, acc = refs[-2:]
    half = position()[0]
    got, traded = got_ref[...], traded_ref[...]
    left = jnp.concatenate([jnp.where(half == 0, got, traded), head_ref[...]], axis=-1)
    right = jnp.concatenate([tail_ref[...], jnp.where(half == 0, traded, got)], axis=-1)
    edge_part((left, right), w_ref, b_ref[...], edge_ref, acc)


def conv_edges(w, b, got, traded, head, tail, after):
    rows, lanes = head.shape[0], w.shape[1] // 128
    return pl.pallas_call(
        edge_kernel,
        out_shape=jax.ShapeDtypeStruct((4, lanes, rows // 2, 128), F32),
        in_specs=[VMEM] * 6 + [ANY] * len(after),
        out_specs=VMEM,
        scratch_shapes=[pltpu.VMEM((8 * lanes, rows + 16, 128), F32)],
        compiler_params=params(),
        cost_estimate=pl.CostEstimate(flops=0, bytes_accessed=4 << 20, transcendentals=0),
        name="conv_edges",
    )(w, b, got, traded, head, tail, *after)


def side_kernel(grad_hbm, labels_hbm, slots_hbm, side_ref, labels_ref, slots_ref, sems):
    owned, width = grad_hbm.shape
    entries = slots_ref.shape[1]
    copies = [
        pltpu.make_async_copy(labels_hbm, labels_ref, sems.at[0]),
        pltpu.make_async_copy(slots_hbm, slots_ref, sems.at[1]),
        pltpu.make_async_copy(grad_hbm, side_ref.at[0, pl.ds(0, owned)], sems.at[2]),
    ]
    for copy in copies:
        copy.start()
    lane = lax.broadcasted_iota(jnp.int32, (1, width), 1)
    copies[0].wait()
    labels = labels_ref[...]
    counts = jnp.zeros((1, width), F32)
    for e in range(entries):
        hit = jnp.where(labels == e, 1.0, 0.0)
        hit = jnp.sum(jnp.sum(hit, axis=0, keepdims=True), axis=1, keepdims=True)
        counts = jnp.where(lane == e, hit, counts)
    copies[1].wait()
    ids = jnp.concatenate(
        [slots_ref[...].astype(F32), jnp.zeros((1, width - entries), F32)], axis=1
    )
    row = lax.broadcasted_iota(jnp.int32, (SIDE, width), 0)
    side_ref[0, owned:] = jnp.where(row == 0, ids, jnp.where(row == 1, counts, 0.0))
    copies[2].wait()


def pack_side(grad, slots, labels):
    owned, width = grad.shape
    fixed = [
        pltpu.with_memory_space_constraint(a, pltpu.HBM)
        for a in (grad, labels, slots.reshape(1, -1))
    ]
    return pl.pallas_call(
        side_kernel,
        out_shape=jax.ShapeDtypeStruct((1, owned + SIDE, width), F32),
        in_specs=[HBM] * 3,
        out_specs=VMEM,
        scratch_shapes=[
            pltpu.VMEM(labels.shape, jnp.int32),
            pltpu.VMEM((1, slots.shape[0]), jnp.int32),
            pltpu.SemaphoreType.DMA((3,)),
        ],
        compiler_params=params(),
        name="pack_side",
    )(*fixed)


def columns_kernel(x_hbm, w_hbm, head_ref, tail_ref, send_ref, near_ref, w_ref, left, right, wide, sems):
    rows, cols, chans = x_hbm.shape
    reach = left.shape[1]
    half = position()[0]
    most, first, _ = share_rows(half, rows)
    size = most // 4
    copies = [
        pltpu.make_async_copy(x_hbm.at[:, pl.ds(0, reach)], left, sems.at[0]),
        pltpu.make_async_copy(x_hbm.at[:, pl.ds(cols - reach, reach)], right, sems.at[1]),
    ]
    for k in range(4):
        source = x_hbm.at[pl.ds(first + k * size, size)]
        copies.append(
            pltpu.make_async_copy(source, near_ref.at[pl.ds(k * size, size)], sems.at[2 + k])
        )
    copies.append(pltpu.make_async_copy(w_hbm, w_ref, sems.at[6]))
    for copy in copies:
        copy.start()
    lanes = chans // 128
    sides = ((left, head_ref, 0), (right, tail_ref, reach - WIDTH))
    for copy, (ref, out_ref, at) in zip(copies, sides):
        copy.wait()
        x = ref[...].astype(F32).reshape(rows * reach, chans)
        for t in range(lanes):
            wide[t] = x[:, t * 128 : (t + 1) * 128]
        for c in range(WIDTH):
            for t in range(lanes):
                part = wide[t, pl.ds(at + c, rows, stride=reach), :].astype(BF16)
                place = (c * lanes + t) * 128
                out_ref[:, place : place + 128] = part
    send_ref[...] = jnp.where(half == 0, tail_ref[...], head_ref[...])
    for copy in copies[2:]:
        copy.wait()


def columns(x, w):
    rows, cols, chans = x.shape
    reach = 16
    most = share_rows(0, rows)[0]
    border = jax.ShapeDtypeStruct((rows, WIDTH * chans), BF16)
    return pl.pallas_call(
        columns_kernel,
        out_shape=(border,) * 3
        + (jax.ShapeDtypeStruct((most, cols, chans), BF16), jax.ShapeDtypeStruct(w.shape, BF16)),
        in_specs=[HBM] * 2,
        out_specs=(VMEM,) * 5,
        scratch_shapes=[
            pltpu.VMEM((rows, reach, chans), BF16),
            pltpu.VMEM((rows, reach, chans), BF16),
            pltpu.VMEM((chans // 128, rows * reach, 128), F32),
            pltpu.SemaphoreType.DMA((7,)),
        ],
        compiler_params=params(16),
        name="columns",
    )(*(pltpu.with_memory_space_constraint(a, pltpu.HBM) for a in (x, w)))


def join_kernel(*refs, count):
    at = 0
    for ref in refs[:count]:
        refs[-1][at : at + ref.shape[0]] = ref[...]
        at += ref.shape[0]


def join(parts, after):
    shape = (sum(p.shape[0] for p in parts),) + parts[0].shape[1:]
    return pl.pallas_call(
        functools.partial(join_kernel, count=len(parts)),
        out_shape=jax.ShapeDtypeStruct(shape, F32),
        in_specs=[VMEM] * len(parts) + [ANY] * len(after),
        out_specs=VMEM,
        compiler_params=params(),
        name="join",
    )(*parts, *after)


def scale_rows(block, note_rows, sums):
    def exponent(values):
        top = None
        for v in values:
            one = jnp.max(jnp.max(jnp.abs(v), axis=0, keepdims=True), axis=1, keepdims=True)
            top = one if top is None else jnp.maximum(top, one)
        return jnp.ceil(jnp.log2(jnp.maximum(top, 1e-30)))

    power = exponent([block, note_rows])
    power_sums = exponent([sums])
    return power, power_sums


def note_block(bias, power, power_sums, width):
    row = lax.broadcasted_iota(jnp.int32, (NOTE, width), 0)
    bias = jnp.broadcast_to(bias, (NOTE, width))
    power = jnp.broadcast_to(power, (NOTE, width))
    power_sums = jnp.broadcast_to(power_sums, (NOTE, width))
    return jnp.where(row == 0, bias, jnp.where(row == 1, power, power_sums))


def read_note(part, at):
    note = part[at : at + NOTE]
    down = jnp.exp2(note[1:2] - 12.0)
    return note[0:1] * down, down, jnp.exp2(note[2:3] - 12.0)


def deep_kernel(
    own_ref, other_ref, edge_ref, w_ref, b_ref, lab_ref, taps, member, slope, sums_ref, wide,
    inside, *, block, entries
):
    _, cols, chans = own_ref.shape
    rows = lab_ref.shape[0]
    lanes = chans // 128
    width = w_ref.shape[-1]
    half = position()[0]
    taps[0] = jnp.zeros(taps.shape[1:], BF16)
    taps[rows + 1] = jnp.zeros(taps.shape[1:], BF16)

    def prepare(ref, base, i, slot):
        x = ref[i].astype(F32)
        r = base + i
        for t in range(lanes):
            s = slot * lanes + t
            at = t * 128
            wide[s, 8 : 8 + cols] = x[:, at : at + 128]
            for g, place in enumerate((7, 8, 7 + cols, 8 + cols)):
                wide[s, place : place + 1] = edge_ref[g, t, pl.ds(r, 1), :]
        for tap in range(3):
            for t in range(lanes):
                piece = wide[slot * lanes + t, 7 + tap : 7 + tap + cols, :]
                at = (tap * lanes + t) * 128
                taps[r + 1, :, at : at + 128] = piece.astype(BF16)

    first, second = shares(rows)
    times = math.gcd(first, second)

    def prepare_all(even_ref, odd_ref):
        def prepare_rows(k, carry):
            for q in range(rows // times):
                ref, base = (even_ref, 0) if q < first // times else (odd_ref, first)
                prepare(ref, base, q * times - base + k, q)
            return carry

        lax.fori_loop(0, times, prepare_rows, 0)

    @pl.when(half == 0)
    def _():
        prepare_all(own_ref, other_ref)

    @pl.when(half != 0)
    def _():
        prepare_all(other_ref, own_ref)

    lab = jnp.transpose(lab_ref[...].astype(F32))
    lane = lax.broadcasted_iota(jnp.int32, (cols, 128), 1)
    want = jnp.where(lane < 3 * entries, lane % entries, -1).astype(F32)
    for r in range(rows):
        member[r] = (lab[:, r : r + 1] == want).astype(BF16)
    bias = b_ref[...]
    size = block * cols

    flat = jnp.concatenate([lab_ref[r : r + 1, :] for r in range(rows)], axis=1)
    entry = lax.broadcasted_iota(jnp.int32, (entries, rows * cols), 0)
    inside[...] = jnp.where(jnp.broadcast_to(flat, entry.shape) == entry, 1.0, 0.0).astype(BF16)

    def step(k, sums):
        r0 = k * block
        lhs = jnp.concatenate([taps[pl.ds(r0 + dr, block)] for dr in range(3)], axis=-1)
        v = jnp.dot(lhs.reshape(size, 9 * chans), w_ref[...], preferred_element_type=F32) + bias
        sig = sigmoid(v)
        features = (v * sig).astype(BF16)
        slope[pl.ds(k * size, size)] = sig * (1.0 + v * (1.0 - sig))
        mine = inside[:, pl.ds(pl.multiple_of(k * size, 128), size)]
        return sums + jnp.dot(mine, features, preferred_element_type=F32)

    sums_ref[...] = lax.fori_loop(0, rows // block, step, jnp.zeros((entries, width), F32))


def deep_forward(own, other, edges, w, b, labels, entries):
    _, cols, chans = own.shape
    rows, width = labels.shape[0], w.shape[-1]
    block = next(k for k in (8, 4, 2, 1) if rows % k == 0)
    first, second = shares(rows)
    slots = rows // math.gcd(first, second)
    return pl.pallas_call(
        functools.partial(deep_kernel, block=block, entries=entries),
        out_shape=(
            jax.ShapeDtypeStruct((rows + 2, cols, 3 * chans), BF16),
            jax.ShapeDtypeStruct((rows, cols, 128), BF16),
            jax.ShapeDtypeStruct((rows * cols, width), F32),
            jax.ShapeDtypeStruct((entries, width), F32),
        ),
        in_specs=[VMEM] * 6,
        out_specs=(VMEM,) * 4,
        scratch_shapes=[
            pltpu.VMEM((slots * (chans // 128), cols + 16, 128), F32),
            pltpu.VMEM((entries, rows * cols), BF16),
        ],
        compiler_params=params(16),
        cost_estimate=pl.CostEstimate(
            flops=4 * rows * cols * 9 * chans * width, bytes_accessed=8 << 20, transcendentals=0
        ),
        name="deep_forward",
    )(own, other, edges, w, b, labels)


def grad_kernel(
    taps, member, slope, sums_ref, *refs, n_parts, chunk
):
    part_refs = refs[:n_parts]
    out_refs, weight = refs[n_parts:-1], refs[-1]
    rows, cols, depth = member.shape[0], taps.shape[1], taps.shape[2]
    width = slope.shape[-1]
    me = position()[3]
    entries = sums_ref.shape[0]
    owned = part_refs[0].shape[1] - SIDE
    own_ids = jnp.broadcast_to(part_refs[0][0, owned : owned + 1, :entries], (entries, entries))
    across = lax.broadcasted_iota(jnp.int32, (entries, entries), 1)
    down = lax.broadcasted_iota(jnp.int32, (entries, entries), 0)
    ids = jnp.sum(jnp.where(across == down, own_ids, 0.0), axis=1, keepdims=True).astype(jnp.int32)
    total = jnp.zeros((entries, 1), F32)
    entry_grad = jnp.zeros((entries, width), F32)
    owner, inner = ids // owned, ids % owned
    spot = lax.broadcasted_iota(jnp.int32, (entries, owned), 1)
    for m, ref, k in relative(part_refs):
        there = ref[k, owned : owned + 1, :entries] == ids.astype(F32)
        counts = ref[k, owned + 1 : owned + 2, :entries]
        total += jnp.sum(jnp.where(there, counts, 0.0), axis=1, keepdims=True)
        hot = ((owner ^ me) == m) & (inner == spot)
        entry_grad += jnp.dot(
            hot.astype(F32), ref[k, :owned], precision=lax.Precision.HIGHEST, preferred_element_type=F32
        )
    entry_grad = entry_grad / jnp.maximum(total, 1.0)
    high = entry_grad.astype(BF16)
    rest = entry_grad - high.astype(F32)
    mid = rest.astype(BF16)
    low = (rest - mid.astype(F32)).astype(BF16)
    terms = jnp.concatenate([high, mid, low, jnp.zeros((128 - 3 * entries, width), BF16)], axis=0)
    pixel = jnp.dot(member[...].reshape(rows * cols, 128), terms, preferred_element_type=F32)
    dg = (pixel * slope[...]).astype(BF16)
    turned = jnp.transpose(dg)
    bias_sum = jnp.sum(dg.astype(F32), axis=0, keepdims=True)
    for dr in range(3):
        window = taps[dr : dr + rows].reshape(rows * cols, depth)
        out = jnp.dot(turned, window, preferred_element_type=F32)
        weight[dr * depth : (dr + 1) * depth] = jnp.transpose(out)
    if weight.shape[0] > 3 * depth:
        weight[3 * depth :] = jnp.zeros((weight.shape[0] - 3 * depth, width), F32)
    sums = sums_ref[...]
    power, power_sums = scale_rows(weight[...], bias_sum, sums)
    up = jnp.exp2(12.0 - power)
    note = note_block(bias_sum * up, power, power_sums, width)
    ways = 8
    digit = lax.rem(me, ways)
    heads = weight.shape[0] // chunk // ways
    sums = sums * jnp.exp2(12.0 - power_sums)
    for out_ref, (members, with_sums) in zip(out_refs, PAYLOADS):
        at = 0
        for m, hi in itertools.product(members, range(heads)):
            j = hi * ways + (digit ^ m)
            out_ref[at : at + chunk] = weight[pl.ds(pl.multiple_of(j * chunk, 8), chunk)] * up
            at += chunk
        out_ref[at : at + NOTE] = note
        if with_sums:
            out_ref[at + NOTE :] = sums


def deep_backward(forward, parts, chunk, count):
    taps, _, slope, sums = forward
    width, entries = slope.shape[-1], sums.shape[0]
    size = count // 8 * chunk
    return pl.pallas_call(
        functools.partial(grad_kernel, n_parts=len(parts), chunk=chunk),
        out_shape=tuple(
            jax.ShapeDtypeStruct((len(members) * size + NOTE + with_sums * entries, width), F32)
            for members, with_sums in PAYLOADS
        ),
        in_specs=[VMEM] * (4 + len(parts)),
        out_specs=(VMEM,) * len(PAYLOADS),
        scratch_shapes=[pltpu.VMEM((count * chunk, width), F32)],
        compiler_params=params(16),
        cost_estimate=pl.CostEstimate(
            flops=4 * slope.shape[0] * 3 * taps.shape[2] * width, bytes_accessed=8 << 20, transcendentals=0
        ),
        name="deep_backward",
    )(*forward, *parts)


def pair_kernel(own_ref, got_ref, *refs, size, entries, got_at, got_note, with_own):
    out_ref = refs[-1]
    own, got = own_ref[size : size + NOTE], got_ref[got_note : got_note + NOTE]
    power = jnp.maximum(own[1:2], got[1:2]) + 1.0
    power_sums = jnp.maximum(own[2:3], got[2:3])
    own_down, got_down = jnp.exp2(own[1:2] - power), jnp.exp2(got[1:2] - power)
    out_ref[:size] = own_ref[:size] * own_down + got_ref[got_at : got_at + size] * got_down
    bias = own[0:1] * own_down + got[0:1] * got_down
    out_ref[size : size + NOTE] = note_block(bias, power, power_sums, own.shape[-1])
    at = size + NOTE
    if with_own:
        sums = refs[0][at : at + entries] * jnp.exp2(own[2:3] - power_sums)
        out_ref[at : at + entries] = sums
        at += entries
    sums = got_ref[got_note + NOTE : got_note + NOTE + entries] * jnp.exp2(got[2:3] - power_sums)
    out_ref[at : at + entries] = sums


def merge_pair(own, got, own_sums, size, entries, got_at, got_note, after):
    width = own.shape[-1]
    rows = size + NOTE + (1 + len(own_sums)) * entries
    return pl.pallas_call(
        functools.partial(
            pair_kernel,
            size=size,
            entries=entries,
            got_at=got_at,
            got_note=got_note,
            with_own=bool(own_sums),
        ),
        out_shape=jax.ShapeDtypeStruct((rows, width), F32),
        in_specs=[VMEM] * (2 + len(own_sums)) + [ANY] * len(after),
        out_specs=VMEM,
        compiler_params=params(),
        name="merge_pair",
    )(own, got, *own_sums, *after)


def merge_kernel(*refs, plan, chunk, heads, entries, shift, next_ways):
    n_parts = len(plan)
    part_refs, out_refs, sums_ref = refs[:n_parts], refs[n_parts:-1], refs[-1]
    width = part_refs[0].shape[-1]
    size = heads * chunk
    total, bias = jnp.zeros((size, width), F32), jnp.zeros((1, width), F32)
    for ref, (added, note_at, members) in zip(part_refs, plan):
        more, down, down_sums = read_note(ref, note_at)
        if added:
            total, bias = total + ref[:size] * down, bias + more
        for k, m in enumerate(members):
            at = note_at + NOTE + k * entries
            sums_ref[m * entries : (m + 1) * entries] = ref[at : at + entries] * down_sums
    sums = sums_ref[...]
    power, power_sums = scale_rows(total, bias, sums)
    up = jnp.exp2(12.0 - power)
    note = note_block(bias * up, power, power_sums, width)
    total = total * up
    if next_ways == 1:
        out_refs[0][:size] = total
        out_refs[0][size:] = note
        return
    sums = sums * jnp.exp2(12.0 - power_sums)
    digit = lax.rem(position()[3] >> shift, next_ways)
    for m in range(next_ways):
        for hi in range(heads // next_ways):
            piece = jnp.zeros((chunk, width), F32)
            for d in range(next_ways):
                at = (hi * next_ways + d) * chunk
                piece = jnp.where((digit ^ m) == d, total[at : at + chunk], piece)
            out_refs[m][hi * chunk : (hi + 1) * chunk] = piece
        at = heads // next_ways * chunk
        out_refs[m][at : at + NOTE] = note
        out_refs[m][at + NOTE :] = sums


def merge(parts, chunk, heads, entries, shift, next_ways):
    width = parts[0][0].shape[-1]
    sums_rows = sum(len(members) for _, _, _, members in parts) * entries
    if next_ways == 1:
        outs = (jax.ShapeDtypeStruct((heads * chunk + NOTE, width), F32),)
    else:
        rows = heads // next_ways * chunk + NOTE + sums_rows
        outs = (jax.ShapeDtypeStruct((rows, width), F32),) * next_ways
    outs = outs + (jax.ShapeDtypeStruct((sums_rows, width), F32),)
    out = pl.pallas_call(
        functools.partial(
            merge_kernel,
            plan=tuple((added, at, tuple(members)) for _, added, at, members in parts),
            chunk=chunk,
            heads=heads,
            entries=entries,
            shift=shift,
            next_ways=next_ways,
        ),
        out_shape=outs,
        in_specs=[VMEM] * len(parts),
        out_specs=(VMEM,) * len(outs),
        compiler_params=params(),
        name="merge",
    )(*(part for part, _, _, _ in parts))
    return out[:-1], out[-1]


def embed_kernel(sums_ref, *refs, entries):
    part_refs, out_ref = refs[:-1], refs[-1]
    owned, width = out_ref.shape
    own = (position()[3] * owned + lax.broadcasted_iota(jnp.int32, (owned, entries), 0)).astype(F32)
    sums, counts = jnp.zeros((owned, width), F32), jnp.zeros((owned, 1), F32)
    for m, ref, k in relative(part_refs):
        there = ref[k, owned : owned + 1, :entries] == own
        count = ref[k, owned + 1 : owned + 2, :entries]
        counts += jnp.sum(jnp.where(there, count, 0.0), axis=1, keepdims=True)
        sums += jnp.dot(
            there.astype(F32),
            sums_ref[m * entries : (m + 1) * entries],
            precision=lax.Precision.HIGHEST,
            preferred_element_type=F32,
        )
    out_ref[...] = sums / jnp.maximum(counts, 1.0)


def spread_kernel(*refs, chunk, rows, members):
    part_refs, weight_ref, bias_ref, place = refs[:-3], refs[-3], refs[-2], refs[-1]
    me = position()[3]
    count = len(members)
    for p, k in itertools.product(range(count), range(part_refs[0].shape[0])):
        bias, down, _ = read_note(part_refs[p][k], chunk)
        j = me ^ (members[p] + k * count)
        target = weight_ref if rows == place.shape[0] else place
        target[pl.ds(pl.multiple_of(j * chunk, 8), chunk)] = part_refs[p][k, :chunk] * down

        @pl.when(j == 0)
        def _():
            bias_ref[...] = bias

    if rows != place.shape[0]:
        weight_ref[...] = place[:rows]


def spread(parts, chunk, count, rows):
    parts = {m: part.astype(F32) for m, part in parts.items()}
    width = parts[0].shape[-1]
    return pl.pallas_call(
        functools.partial(spread_kernel, chunk=chunk, rows=rows, members=tuple(parts)),
        out_shape=(jax.ShapeDtypeStruct((rows, width), F32), jax.ShapeDtypeStruct((1, width), F32)),
        in_specs=[VMEM] * len(parts),
        out_specs=(VMEM, VMEM),
        scratch_shapes=[pltpu.VMEM((count * chunk, width), F32)],
        compiler_params=params(),
        name="spread",
    )(*parts.values())


def body(
    section_input, conv_weight, conv_bias, deep_weight, deep_bias, labels, slot_ids, embed_grad
):
    chan_count = lax.axis_size("chan")
    strip_count = lax.axis_size("strip")
    channels = section_input.shape[-1]
    entries = slot_ids.shape[0]
    owned, width = embed_grad.shape
    conv_w = conv_weight.reshape(9 * channels, -1)
    conv_b = conv_bias.reshape(1, -1)

    side = pack_side(embed_grad, slot_ids, labels)
    head, tail, border, near_rows, near_w = columns(section_input, conv_w)
    pairs = []
    for s in range(strip_count):
        for c in range(chan_count):
            to = s + 1 - 2 * (c & 1)
            if 0 <= to < strip_count:
                pairs.append((s * chan_count + c, to * chan_count + c))
    got = lax.ppermute(border, ("strip", "chan"), pairs)

    steps = [(at + 1, 1) for at in range(min(2, strip_count.bit_length() - 2))]
    steps += [(at, min(3, strip_count.bit_length() - 1 - at)) for at in range(3, strip_count.bit_length() - 1, 3)]
    ahead = gather_step(side, "strip", steps[0])
    shared = join(ahead, [border])
    taps = windows(near_rows, section_input.shape[0], [shared])
    ahead = gather_step(shared, "strip", steps[1])
    pooled = conv_pool(taps, near_w, conv_b, section_input.shape[0] // 4, [shared])
    pooled, got, shared = lax.optimization_barrier((pooled, got, join(ahead, [pooled])))
    other = swap(pooled, "chan", 1)
    traded = swap(got, "chan", 1)
    for step in steps[2:]:
        shared = join(gather_step(shared, "strip", step), [])
    shared = [shared, swap(shared, "strip", 1)]
    edges = conv_edges(near_w, conv_b, got, traded, head, tail, [pooled])

    chunk = -(-9 * channels // strip_count // 8) * 8
    bits = strip_count.bit_length() - 1
    ways = 8
    forward = deep_forward(
                pooled,
        other,
        edges,
        deep_weight.reshape(9 * channels, width),
        deep_bias.reshape(1, width),
        labels,
        entries,
    )
    heads = strip_count // ways
    size = heads * chunk

    def sent(part, mask):
        return swap(part.astype(F16), "strip", mask).astype(F32)

    kept, beside, near, across, paired, pair, far = deep_backward(
        forward, shared, chunk, strip_count
    )
    got_far, got_pair = sent(far, 6), sent(pair, 1)
    onward = merge_pair(paired, got_pair, [pair], size, entries, 0, size, [])
    beside = merge_pair(beside, got_far, [], size, entries, size, 2 * size, [onward])
    parts = [
        (kept, True, size, []),
        (sent(beside, 1), True, size, [7]),
        (sent(near, 2), True, size, [2]),
        (sent(across, 3), True, size, [3]),
        (sent(onward, 4), True, size, [4, 5]),
        (got_far, True, 2 * size, [6]),
        (pair, False, size, [0]),
        (got_pair, False, size, [1]),
    ]
    held, shift = ways, 3
    while True:
        step = min(3, bits - shift)
        send, sums = merge(parts, chunk, heads, entries, shift, 1 << step)
        if step == 0:
            break
        more = 1 << step
        heads //= more
        arrived = [send[0]] + [sent(send[m], m << shift) for m in range(1, more)]
        parts = [
            (part, True, heads * chunk, list(range(m * held, (m + 1) * held)))
            for m, part in enumerate(arrived)
        ]
        held *= more
        shift += step
    embeddings = pl.pallas_call(
        functools.partial(embed_kernel, entries=entries),
        out_shape=jax.ShapeDtypeStruct((owned, width), F32),
        in_specs=[VMEM] * (1 + len(shared)),
        out_specs=VMEM,
        compiler_params=params(),
        name="embed",
    )(sums, *shared)
    own = send[0].astype(F16)[None]
    for at in range(3, bits, 3):
        own = jnp.concatenate(gather_step(own, "strip", (at, min(3, bits - at))), axis=0)
    gathered = {m: swap(own, "strip", m) if m else own for m in range(4)}
    for k in (2, 3):
        gathered[2 * k] = swap(own, "strip", 2 * k)
    late = {2 * k + 1: swap(gathered[2 * k], "strip", 1) for k in (2, 3)}
    weight_rows, bias_row = spread(
        {**gathered, **late}, chunk, strip_count, 9 * channels
    )
    return (embeddings, weight_rows.reshape(3, 3, channels, width), bias_row[0])


def solution(mesh):
    placed = (
        P(None, "strip", None),
        P(),
        P(),
        P(None, None, None, "chan"),
        P("chan"),
        P(None, "strip"),
        P("strip"),
        P("strip", "chan"),
    )
    return jax.shard_map(
        body,
        mesh=mesh,
        in_specs=placed,
        out_specs=(P("strip", "chan"), P(None, None, None, "chan"), P("chan")),
        check_vma=False,
    )
```

```python
import functools
import itertools
import math

import jax
import jax.numpy as jnp
from jax import lax
from jax.experimental import pallas as pl
from jax.experimental.pallas import tpu as pltpu
from jax.sharding import PartitionSpec as P

F32, BF16, F16 = jnp.float32, jnp.bfloat16, jnp.float16
VMEM = pl.BlockSpec(memory_space=pltpu.VMEM)
HBM = pl.BlockSpec(memory_space=pltpu.HBM)
ANY = pl.BlockSpec(memory_space=pl.ANY)
SIDE = 8
WIDTH = 3
PIECE = 4
STEP = 6
PAYLOADS = (
    ((0,), 0, 0),
    ((1,), 0, 0),
    ((2,), 1, 40),
    ((3,), 1, 40),
    ((4,), 0, 0),
    ((5,), 1, 48),
    ((6, 7), 1, 0),
)
NOTE = 8


def params(mib=8):
    return pltpu.CompilerParams(vmem_limit_bytes=mib << 20)


def position():
    strip = lax.axis_index("strip")
    last = lax.axis_size("strip") - 1
    return (
        lax.axis_index("chan") & 1,
        (strip == 0).astype(jnp.int32),
        (strip == last).astype(jnp.int32),
        strip,
    )


def swap(value, axis, mask):
    count = lax.axis_size(axis)
    return lax.ppermute(value, axis, [(i, i ^ mask) for i in range(count)])


def gather_step(held, axis, step):
    shift, size = step
    return [held] + [swap(held, axis, m << shift) for m in range(1, 1 << size)]


def relative(refs):
    half = len(refs) // 2
    for low in range(2):
        m = low
        for ref in refs[low * half : (low + 1) * half]:
            for k in range(ref.shape[0]):
                yield m, ref, k
                m += 2


def sigmoid(v):
    return jax.nn.sigmoid(v)


def shares(pooled_rows):
    first = pooled_rows // 2
    return first, pooled_rows - first


def pick(half, pair):
    return jnp.where(half == 0, pair[0], pair[1])


def share_rows(half, rows):
    first, second = shares(rows // 2)
    most = -(-(2 * max(first, second) + 1) // PIECE) * PIECE
    return most, pick(half, (0, rows - most)), pick(half, (-1, 2 * first - 1 - (rows - most)))


def window_kernel(rows_ref, *refs, rows):
    taps, wide = refs[-2:]
    most, cols, chans = rows_ref.shape
    half_cols = cols // 2
    half = position()[0]
    _, _, before = share_rows(half, rows)
    shift = PIECE - before
    lanes = chans // 128
    border = jnp.zeros((8, 128), F32)
    for t in range(wide.shape[0]):
        wide[t, 0:8] = border
        wide[t, cols + 8 : cols + 16] = border

    def prepare(k, carry):
        for slot in range(PIECE):
            r = k * PIECE + slot
            x = rows_ref[r].astype(F32)
            for t in range(lanes):
                wide[slot * lanes + t, 8 : 8 + cols] = x[:, t * 128 : (t + 1) * 128]
            for tap in range(4):
                for t in range(lanes):
                    part = wide[slot * lanes + t, pl.ds(7 + tap, half_cols, stride=2), :]
                    at = (tap * lanes + t) * 128
                    taps[r + shift, :, at : at + 128] = part.astype(BF16)
        return carry

    lax.fori_loop(0, most // PIECE, prepare, 0)
    second = shares(rows // 2)[1]
    outside = pick(half, (PIECE, PIECE + 2 * second + 1))
    taps[outside] = jnp.zeros(taps.shape[1:], BF16)


def windows(near_rows, rows, after):
    most, cols, chans = near_rows.shape
    return pl.pallas_call(
        functools.partial(window_kernel, rows=rows),
        out_shape=jax.ShapeDtypeStruct((most + 2 * PIECE, cols // 2, 4 * chans), BF16),
        in_specs=[VMEM] + [ANY] * len(after),
        out_specs=VMEM,
        scratch_shapes=[pltpu.VMEM((PIECE * (chans // 128), cols + 16, 128), F32)],
        compiler_params=params(16),
        cost_estimate=pl.CostEstimate(flops=0, bytes_accessed=12 << 20, transcendentals=0),
        name="windows",
    )(near_rows, *after)


def edge_part(pairs, w_ref, bias, edge_ref, acc):
    rows = pairs[0].shape[0]
    chans = w_ref.shape[1]
    lanes = chans // 128
    depth = 3 * chans
    lhs = jnp.concatenate(
        [
            pairs[s][:, (2 * j + phase) * chans : (2 * j + phase + 3) * chans]
            for s in range(2)
            for j in range(2)
            for phase in range(2)
        ],
        axis=0,
    )
    pad = rows + 16
    for dr in range(3):
        part = jnp.dot(lhs, w_ref[dr * depth : (dr + 1) * depth], preferred_element_type=F32)
        for g in range(8):
            own = part[g * rows : (g + 1) * rows]
            for t in range(lanes):
                at = 9 - dr
                piece = own[:, t * 128 : (t + 1) * 128]
                if dr == 0:
                    acc[g * lanes + t, 0:8] = jnp.zeros((8, 128), F32)
                    acc[g * lanes + t, 8 + rows : pad] = jnp.zeros((8, 128), F32)
                    acc[g * lanes + t, 8:9] = jnp.zeros((1, 128), F32)
                    acc[g * lanes + t, at : at + rows] = piece
                else:
                    acc[g * lanes + t, at : at + rows] += piece
    for g in range(4):
        for t in range(lanes):
            total = None
            for phase in range(2):
                at = (2 * g + phase) * lanes + t
                v = acc[at, 8 : 8 + rows] + bias[:, t * 128 : (t + 1) * 128]
                acc[at, 8 : 8 + rows] = v * sigmoid(v)
                both = (
                    acc[at, pl.ds(8, rows // 2, stride=2), :]
                    + acc[at, pl.ds(9, rows // 2, stride=2), :]
                )
                total = both if total is None else total + both
            lost = jnp.where(g == 0, position()[1], jnp.where(g == 3, position()[2], 0))
            keep = jnp.where(lost > 0, 0.0, 0.25)
            edge_ref[g, t] = (total * keep).astype(BF16).astype(F32)


def conv_kernel(taps, w_ref, b_ref, *refs):
    out_ref = refs[-1]
    assert out_ref.shape[0] % STEP == 0
    half_cols, chans = taps.shape[1], taps.shape[2] // 4
    bias = b_ref[...]

    def step(k, carry):
        r0 = PIECE + k * 2 * STEP
        total = None
        for phase in range(2):
            lhs = jnp.concatenate(
                [
                    taps[pl.ds(r0 + dr, 2 * STEP), :, phase * chans : (phase + 3) * chans]
                    for dr in range(3)
                ],
                axis=-1,
            ).reshape(2 * STEP * half_cols, 9 * chans)
            v = jnp.dot(lhs, w_ref[...], preferred_element_type=F32) + bias
            h = (v * sigmoid(v)).reshape(STEP, 2, half_cols, chans)
            h = h[:, 0] + h[:, 1]
            total = h if total is None else total + h
        out_ref[pl.ds(k * STEP, STEP)] = (total * 0.25).astype(BF16)
        return carry

    for k in range(out_ref.shape[0] // STEP):
        step(k, 0)


def conv_pool(taps, w, b, pooled_rows, after):
    _, half_cols, width = taps.shape
    chans = width // 4
    return pl.pallas_call(
        conv_kernel,
        out_shape=jax.ShapeDtypeStruct((pooled_rows, half_cols, chans), BF16),
        in_specs=[VMEM] * 3 + [ANY] * len(after),
        out_specs=VMEM,
        compiler_params=params(16),
        cost_estimate=pl.CostEstimate(
            flops=8 * pooled_rows * half_cols * 9 * chans * chans,
            bytes_accessed=8 << 20,
            transcendentals=0,
        ),
        name="conv_pool",
    )(taps, w, b, *after)


def edge_kernel(w_ref, b_ref, got_ref, traded_ref, head_ref, tail_ref, *refs):
    edge_ref, acc = refs[-2:]
    half = position()[0]
    got, traded = got_ref[...], traded_ref[...]
    left = jnp.concatenate([jnp.where(half == 0, got, traded), head_ref[...]], axis=-1)
    right = jnp.concatenate([tail_ref[...], jnp.where(half == 0, traded, got)], axis=-1)
    edge_part((left, right), w_ref, b_ref[...], edge_ref, acc)


def conv_edges(w, b, got, traded, head, tail, after):
    rows, lanes = head.shape[0], w.shape[1] // 128
    return pl.pallas_call(
        edge_kernel,
        out_shape=jax.ShapeDtypeStruct((4, lanes, rows // 2, 128), F32),
        in_specs=[VMEM] * 6 + [ANY] * len(after),
        out_specs=VMEM,
        scratch_shapes=[pltpu.VMEM((8 * lanes, rows + 16, 128), F32)],
        compiler_params=params(),
        cost_estimate=pl.CostEstimate(flops=0, bytes_accessed=4 << 20, transcendentals=0),
        name="conv_edges",
    )(w, b, got, traded, head, tail, *after)


def side_kernel(grad_hbm, labels_hbm, slots_hbm, side_ref, labels_ref, slots_ref, sems):
    owned, width = grad_hbm.shape
    entries = slots_ref.shape[1]
    copies = [
        pltpu.make_async_copy(labels_hbm, labels_ref, sems.at[0]),
        pltpu.make_async_copy(slots_hbm, slots_ref, sems.at[1]),
        pltpu.make_async_copy(grad_hbm, side_ref.at[0, pl.ds(0, owned)], sems.at[2]),
    ]
    for copy in copies:
        copy.start()
    lane = lax.broadcasted_iota(jnp.int32, (1, width), 1)
    copies[0].wait()
    labels = labels_ref[...]
    counts = jnp.zeros((1, width), F32)
    for e in range(entries):
        hit = jnp.where(labels == e, 1.0, 0.0)
        hit = jnp.sum(jnp.sum(hit, axis=0, keepdims=True), axis=1, keepdims=True)
        counts = jnp.where(lane == e, hit, counts)
    copies[1].wait()
    ids = jnp.concatenate(
        [slots_ref[...].astype(F32), jnp.zeros((1, width - entries), F32)], axis=1
    )
    row = lax.broadcasted_iota(jnp.int32, (SIDE, width), 0)
    side_ref[0, owned:] = jnp.where(row == 0, ids, jnp.where(row == 1, counts, 0.0))
    copies[2].wait()


def pack_side(grad, slots, labels):
    owned, width = grad.shape
    fixed = [
        pltpu.with_memory_space_constraint(a, pltpu.HBM)
        for a in (grad, labels, slots.reshape(1, -1))
    ]
    return pl.pallas_call(
        side_kernel,
        out_shape=jax.ShapeDtypeStruct((1, owned + SIDE, width), F32),
        in_specs=[HBM] * 3,
        out_specs=VMEM,
        scratch_shapes=[
            pltpu.VMEM(labels.shape, jnp.int32),
            pltpu.VMEM((1, slots.shape[0]), jnp.int32),
            pltpu.SemaphoreType.DMA((3,)),
        ],
        compiler_params=params(),
        name="pack_side",
    )(*fixed)


def columns_kernel(x_hbm, w_hbm, head_ref, tail_ref, send_ref, near_ref, w_ref, left, right, wide, sems):
    rows, cols, chans = x_hbm.shape
    reach = left.shape[1]
    half = position()[0]
    most, first, _ = share_rows(half, rows)
    size = most // 4
    copies = [
        pltpu.make_async_copy(x_hbm.at[:, pl.ds(0, reach)], left, sems.at[0]),
        pltpu.make_async_copy(x_hbm.at[:, pl.ds(cols - reach, reach)], right, sems.at[1]),
    ]
    for k in range(4):
        source = x_hbm.at[pl.ds(first + k * size, size)]
        copies.append(
            pltpu.make_async_copy(source, near_ref.at[pl.ds(k * size, size)], sems.at[2 + k])
        )
    copies.append(pltpu.make_async_copy(w_hbm, w_ref, sems.at[6]))
    for copy in copies:
        copy.start()
    lanes = chans // 128
    sides = ((left, head_ref, 0), (right, tail_ref, reach - WIDTH))
    for copy, (ref, out_ref, at) in zip(copies, sides):
        copy.wait()
        x = ref[...].astype(F32).reshape(rows * reach, chans)
        for t in range(lanes):
            wide[t] = x[:, t * 128 : (t + 1) * 128]
        for c in range(WIDTH):
            for t in range(lanes):
                part = wide[t, pl.ds(at + c, rows, stride=reach), :].astype(BF16)
                place = (c * lanes + t) * 128
                out_ref[:, place : place + 128] = part
    send_ref[...] = jnp.where(half == 0, tail_ref[...], head_ref[...])
    for copy in copies[2:]:
        copy.wait()


def columns(x, w):
    rows, cols, chans = x.shape
    reach = 16
    most = share_rows(0, rows)[0]
    border = jax.ShapeDtypeStruct((rows, WIDTH * chans), BF16)
    return pl.pallas_call(
        columns_kernel,
        out_shape=(border,) * 3
        + (jax.ShapeDtypeStruct((most, cols, chans), BF16), jax.ShapeDtypeStruct(w.shape, BF16)),
        in_specs=[HBM] * 2,
        out_specs=(VMEM,) * 5,
        scratch_shapes=[
            pltpu.VMEM((rows, reach, chans), BF16),
            pltpu.VMEM((rows, reach, chans), BF16),
            pltpu.VMEM((chans // 128, rows * reach, 128), F32),
            pltpu.SemaphoreType.DMA((7,)),
        ],
        compiler_params=params(16),
        name="columns",
    )(*(pltpu.with_memory_space_constraint(a, pltpu.HBM) for a in (x, w)))


def join_kernel(*refs, count):
    at = 0
    for ref in refs[:count]:
        refs[-1][at : at + ref.shape[0]] = ref[...]
        at += ref.shape[0]


def join(parts, after):
    shape = (sum(p.shape[0] for p in parts),) + parts[0].shape[1:]
    return pl.pallas_call(
        functools.partial(join_kernel, count=len(parts)),
        out_shape=jax.ShapeDtypeStruct(shape, F32),
        in_specs=[VMEM] * len(parts) + [ANY] * len(after),
        out_specs=VMEM,
        compiler_params=params(),
        name="join",
    )(*parts, *after)


def scale_rows(block, note_rows, sums):
    def exponent(values):
        top = None
        for v in values:
            one = jnp.max(jnp.max(jnp.abs(v), axis=0, keepdims=True), axis=1, keepdims=True)
            top = one if top is None else jnp.maximum(top, one)
        return jnp.ceil(jnp.log2(jnp.maximum(top, 1e-30)))

    power = exponent([block, note_rows])
    power_sums = exponent([sums])
    return power, power_sums


def note_block(bias, power, power_sums, width):
    row = lax.broadcasted_iota(jnp.int32, (NOTE, width), 0)
    bias = jnp.broadcast_to(bias, (NOTE, width))
    power = jnp.broadcast_to(power, (NOTE, width))
    power_sums = jnp.broadcast_to(power_sums, (NOTE, width))
    return jnp.where(row == 0, bias, jnp.where(row == 1, power, power_sums))


def read_note(part, at):
    note = part[at : at + NOTE]
    down = jnp.exp2(note[1:2] - 12.0)
    return note[0:1] * down, down, jnp.exp2(note[2:3] - 12.0)


def deep_kernel(
    own_ref, other_ref, edge_ref, w_ref, b_ref, lab_ref, taps, member, slope, sums_ref, wide,
    inside, *, block, entries
):
    _, cols, chans = own_ref.shape
    rows = lab_ref.shape[0]
    lanes = chans // 128
    width = w_ref.shape[-1]
    half = position()[0]
    taps[0] = jnp.zeros(taps.shape[1:], BF16)
    taps[rows + 1] = jnp.zeros(taps.shape[1:], BF16)

    def prepare(ref, base, i, slot):
        x = ref[i].astype(F32)
        r = base + i
        for t in range(lanes):
            s = slot * lanes + t
            at = t * 128
            wide[s, 8 : 8 + cols] = x[:, at : at + 128]
            for g, place in enumerate((7, 8, 7 + cols, 8 + cols)):
                wide[s, place : place + 1] = edge_ref[g, t, pl.ds(r, 1), :]
        for tap in range(3):
            for t in range(lanes):
                piece = wide[slot * lanes + t, 7 + tap : 7 + tap + cols, :]
                at = (tap * lanes + t) * 128
                taps[r + 1, :, at : at + 128] = piece.astype(BF16)

    first, second = shares(rows)
    times = math.gcd(first, second)

    def prepare_all(even_ref, odd_ref):
        def prepare_rows(k, carry):
            for q in range(rows // times):
                ref, base = (even_ref, 0) if q < first // times else (odd_ref, first)
                prepare(ref, base, q * times - base + k, q)
            return carry

        lax.fori_loop(0, times, prepare_rows, 0)

    @pl.when(half == 0)
    def _():
        prepare_all(own_ref, other_ref)

    @pl.when(half != 0)
    def _():
        prepare_all(other_ref, own_ref)

    lab = jnp.transpose(lab_ref[...].astype(F32))
    lane = lax.broadcasted_iota(jnp.int32, (cols, 128), 1)
    want = jnp.where(lane < 3 * entries, lane % entries, -1).astype(F32)
    for r in range(rows):
        member[r] = (lab[:, r : r + 1] == want).astype(BF16)
    bias = b_ref[...]
    size = block * cols

    flat = jnp.concatenate([lab_ref[r : r + 1, :] for r in range(rows)], axis=1)
    entry = lax.broadcasted_iota(jnp.int32, (entries, rows * cols), 0)
    inside[...] = jnp.where(jnp.broadcast_to(flat, entry.shape) == entry, 1.0, 0.0).astype(BF16)

    def step(k, sums):
        r0 = k * block
        lhs = jnp.concatenate([taps[pl.ds(r0 + dr, block)] for dr in range(3)], axis=-1)
        v = jnp.dot(lhs.reshape(size, 9 * chans), w_ref[...], preferred_element_type=F32) + bias
        sig = sigmoid(v)
        features = (v * sig).astype(BF16)
        slope[pl.ds(k * size, size)] = sig * (1.0 + v * (1.0 - sig))
        mine = inside[:, pl.ds(pl.multiple_of(k * size, 128), size)]
        return sums + jnp.dot(mine, features, preferred_element_type=F32)

    sums_ref[...] = lax.fori_loop(0, rows // block, step, jnp.zeros((entries, width), F32))


def deep_forward(own, other, edges, w, b, labels, entries):
    _, cols, chans = own.shape
    rows, width = labels.shape[0], w.shape[-1]
    block = next(k for k in (8, 4, 2, 1) if rows % k == 0)
    first, second = shares(rows)
    slots = rows // math.gcd(first, second)
    return pl.pallas_call(
        functools.partial(deep_kernel, block=block, entries=entries),
        out_shape=(
            jax.ShapeDtypeStruct((rows + 2, cols, 3 * chans), BF16),
            jax.ShapeDtypeStruct((rows, cols, 128), BF16),
            jax.ShapeDtypeStruct((rows * cols, width), F32),
            jax.ShapeDtypeStruct((entries, width), F32),
        ),
        in_specs=[VMEM] * 6,
        out_specs=(VMEM,) * 4,
        scratch_shapes=[
            pltpu.VMEM((slots * (chans // 128), cols + 16, 128), F32),
            pltpu.VMEM((entries, rows * cols), BF16),
        ],
        compiler_params=params(16),
        cost_estimate=pl.CostEstimate(
            flops=4 * rows * cols * 9 * chans * width, bytes_accessed=8 << 20, transcendentals=0
        ),
        name="deep_forward",
    )(own, other, edges, w, b, labels)


def grad_kernel(
    taps, member, slope, sums_ref, *refs, n_parts, chunk
):
    part_refs = refs[:n_parts]
    out_refs, weight = refs[n_parts:-1], refs[-1]
    rows, cols, depth = member.shape[0], taps.shape[1], taps.shape[2]
    width = slope.shape[-1]
    me = position()[3]
    entries = sums_ref.shape[0]
    owned = part_refs[0].shape[1] - SIDE
    own_ids = jnp.broadcast_to(part_refs[0][0, owned : owned + 1, :entries], (entries, entries))
    across = lax.broadcasted_iota(jnp.int32, (entries, entries), 1)
    down = lax.broadcasted_iota(jnp.int32, (entries, entries), 0)
    ids = jnp.sum(jnp.where(across == down, own_ids, 0.0), axis=1, keepdims=True).astype(jnp.int32)
    total = jnp.zeros((entries, 1), F32)
    entry_grad = jnp.zeros((entries, width), F32)
    owner, inner = ids // owned, ids % owned
    spot = lax.broadcasted_iota(jnp.int32, (entries, owned), 1)
    for m, ref, k in relative(part_refs):
        there = ref[k, owned : owned + 1, :entries] == ids.astype(F32)
        counts = ref[k, owned + 1 : owned + 2, :entries]
        total += jnp.sum(jnp.where(there, counts, 0.0), axis=1, keepdims=True)
        hot = ((owner ^ me) == m) & (inner == spot)
        entry_grad += jnp.dot(
            hot.astype(F32), ref[k, :owned], precision=lax.Precision.HIGHEST, preferred_element_type=F32
        )
    entry_grad = entry_grad / jnp.maximum(total, 1.0)
    high = entry_grad.astype(BF16)
    rest = entry_grad - high.astype(F32)
    mid = rest.astype(BF16)
    low = (rest - mid.astype(F32)).astype(BF16)
    terms = jnp.concatenate([high, mid, low, jnp.zeros((128 - 3 * entries, width), BF16)], axis=0)
    pixel = jnp.dot(member[...].reshape(rows * cols, 128), terms, preferred_element_type=F32)
    dg = (pixel * slope[...]).astype(BF16)
    turned = jnp.transpose(dg)
    bias_sum = jnp.sum(dg.astype(F32), axis=0, keepdims=True)
    for dr in range(3):
        window = taps[dr : dr + rows].reshape(rows * cols, depth)
        out = jnp.dot(turned, window, preferred_element_type=F32)
        weight[dr * depth : (dr + 1) * depth] = jnp.transpose(out)
    if weight.shape[0] > 3 * depth:
        weight[3 * depth :] = jnp.zeros((weight.shape[0] - 3 * depth, width), F32)
    sums = sums_ref[...]
    power, power_sums = scale_rows(weight[...], bias_sum, sums)
    up = jnp.exp2(12.0 - power)
    note = note_block(bias_sum * up, power, power_sums, width)
    ways = 8
    digit = lax.rem(me, ways)
    heads = weight.shape[0] // chunk // ways
    sums = sums * jnp.exp2(12.0 - power_sums)
    for out_ref, (members, with_sums, spare) in zip(out_refs, PAYLOADS):
        at = 0
        for m, hi in itertools.product(members, range(heads)):
            j = hi * ways + (digit ^ m)
            out_ref[at : at + chunk] = weight[pl.ds(pl.multiple_of(j * chunk, 8), chunk)] * up
            at += chunk
        out_ref[at : at + NOTE] = note
        at += NOTE
        if with_sums:
            out_ref[at : at + entries] = sums
        if spare:
            out_ref[at + entries :] = jnp.zeros((spare, width), F32)


def deep_backward(forward, parts, chunk, count):
    taps, _, slope, sums = forward
    width, entries = slope.shape[-1], sums.shape[0]
    size = count // 8 * chunk
    return pl.pallas_call(
        functools.partial(grad_kernel, n_parts=len(parts), chunk=chunk),
        out_shape=tuple(
            jax.ShapeDtypeStruct(
                (len(members) * size + NOTE + with_sums * entries + spare, width), F32
            )
            for members, with_sums, spare in PAYLOADS
        ),
        in_specs=[VMEM] * (4 + len(parts)),
        out_specs=(VMEM,) * len(PAYLOADS),
        scratch_shapes=[pltpu.VMEM((count * chunk, width), F32)],
        compiler_params=params(16),
        cost_estimate=pl.CostEstimate(
            flops=4 * slope.shape[0] * 3 * taps.shape[2] * width, bytes_accessed=8 << 20, transcendentals=0
        ),
        name="deep_backward",
    )(*forward, *parts)


def pair_kernel(own_ref, got_ref, *refs, size, entries, got_at, got_note, with_own):
    out_ref = refs[-1]
    own, got = own_ref[size : size + NOTE], got_ref[got_note : got_note + NOTE]
    power = jnp.maximum(own[1:2], got[1:2]) + 1.0
    power_sums = jnp.maximum(own[2:3], got[2:3])
    own_down, got_down = jnp.exp2(own[1:2] - power), jnp.exp2(got[1:2] - power)
    out_ref[:size] = own_ref[:size] * own_down + got_ref[got_at : got_at + size] * got_down
    bias = own[0:1] * own_down + got[0:1] * got_down
    out_ref[size : size + NOTE] = note_block(bias, power, power_sums, own.shape[-1])
    at = size + NOTE
    if with_own:
        sums = refs[0][at : at + entries] * jnp.exp2(own[2:3] - power_sums)
        out_ref[at : at + entries] = sums
        at += entries
    sums = got_ref[got_note + NOTE : got_note + NOTE + entries] * jnp.exp2(got[2:3] - power_sums)
    out_ref[at : at + entries] = sums


def merge_pair(own, got, own_sums, size, entries, got_at, got_note, after):
    width = own.shape[-1]
    rows = size + NOTE + (1 + len(own_sums)) * entries
    return pl.pallas_call(
        functools.partial(
            pair_kernel,
            size=size,
            entries=entries,
            got_at=got_at,
            got_note=got_note,
            with_own=bool(own_sums),
        ),
        out_shape=jax.ShapeDtypeStruct((rows, width), F32),
        in_specs=[VMEM] * (2 + len(own_sums)) + [ANY] * len(after),
        out_specs=VMEM,
        compiler_params=params(),
        name="merge_pair",
    )(own, got, *own_sums, *after)


def merge_kernel(*refs, plan, chunk, heads, entries, shift, next_ways):
    n_parts = len(plan)
    part_refs, out_refs, sums_ref = refs[:n_parts], refs[n_parts:-1], refs[-1]
    width = part_refs[0].shape[-1]
    size = heads * chunk
    total, bias = jnp.zeros((size, width), F32), jnp.zeros((1, width), F32)
    for ref, (added, note_at, members) in zip(part_refs, plan):
        more, down, down_sums = read_note(ref, note_at)
        if added:
            total, bias = total + ref[:size] * down, bias + more
        for k, m in enumerate(members):
            at = note_at + NOTE + k * entries
            sums_ref[m * entries : (m + 1) * entries] = ref[at : at + entries] * down_sums
    sums = sums_ref[...]
    power, power_sums = scale_rows(total, bias, sums)
    up = jnp.exp2(12.0 - power)
    note = note_block(bias * up, power, power_sums, width)
    total = total * up
    if next_ways == 1:
        out_refs[0][:size] = total
        out_refs[0][size:] = note
        return
    sums = sums * jnp.exp2(12.0 - power_sums)
    digit = lax.rem(position()[3] >> shift, next_ways)
    for m in range(next_ways):
        for hi in range(heads // next_ways):
            piece = jnp.zeros((chunk, width), F32)
            for d in range(next_ways):
                at = (hi * next_ways + d) * chunk
                piece = jnp.where((digit ^ m) == d, total[at : at + chunk], piece)
            out_refs[m][hi * chunk : (hi + 1) * chunk] = piece
        at = heads // next_ways * chunk
        out_refs[m][at : at + NOTE] = note
        out_refs[m][at + NOTE :] = sums


def merge(parts, chunk, heads, entries, shift, next_ways):
    width = parts[0][0].shape[-1]
    sums_rows = sum(len(members) for _, _, _, members in parts) * entries
    if next_ways == 1:
        outs = (jax.ShapeDtypeStruct((heads * chunk + NOTE, width), F32),)
    else:
        rows = heads // next_ways * chunk + NOTE + sums_rows
        outs = (jax.ShapeDtypeStruct((rows, width), F32),) * next_ways
    outs = outs + (jax.ShapeDtypeStruct((sums_rows, width), F32),)
    out = pl.pallas_call(
        functools.partial(
            merge_kernel,
            plan=tuple((added, at, tuple(members)) for _, added, at, members in parts),
            chunk=chunk,
            heads=heads,
            entries=entries,
            shift=shift,
            next_ways=next_ways,
        ),
        out_shape=outs,
        in_specs=[VMEM] * len(parts),
        out_specs=(VMEM,) * len(outs),
        compiler_params=params(),
        name="merge",
    )(*(part for part, _, _, _ in parts))
    return out[:-1], out[-1]


def embed_kernel(sums_ref, *refs, entries):
    part_refs, out_ref = refs[:-1], refs[-1]
    owned, width = out_ref.shape
    own = (position()[3] * owned + lax.broadcasted_iota(jnp.int32, (owned, entries), 0)).astype(F32)
    sums, counts = jnp.zeros((owned, width), F32), jnp.zeros((owned, 1), F32)
    for m, ref, k in relative(part_refs):
        there = ref[k, owned : owned + 1, :entries] == own
        count = ref[k, owned + 1 : owned + 2, :entries]
        counts += jnp.sum(jnp.where(there, count, 0.0), axis=1, keepdims=True)
        sums += jnp.dot(
            there.astype(F32),
            sums_ref[m * entries : (m + 1) * entries],
            precision=lax.Precision.HIGHEST,
            preferred_element_type=F32,
        )
    out_ref[...] = sums / jnp.maximum(counts, 1.0)


def spread_kernel(*refs, chunk, rows, members):
    part_refs, weight_ref, bias_ref, place = refs[:-3], refs[-3], refs[-2], refs[-1]
    me = position()[3]
    count = len(members)
    for p, k in itertools.product(range(count), range(part_refs[0].shape[0])):
        bias, down, _ = read_note(part_refs[p][k], chunk)
        j = me ^ (members[p] + k * count)
        target = weight_ref if rows == place.shape[0] else place
        target[pl.ds(pl.multiple_of(j * chunk, 8), chunk)] = part_refs[p][k, :chunk] * down

        @pl.when(j == 0)
        def _():
            bias_ref[...] = bias

    if rows != place.shape[0]:
        weight_ref[...] = place[:rows]


def spread(parts, chunk, count, rows):
    parts = {m: part.astype(F32) for m, part in parts.items()}
    width = parts[0].shape[-1]
    return pl.pallas_call(
        functools.partial(spread_kernel, chunk=chunk, rows=rows, members=tuple(parts)),
        out_shape=(jax.ShapeDtypeStruct((rows, width), F32), jax.ShapeDtypeStruct((1, width), F32)),
        in_specs=[VMEM] * len(parts),
        out_specs=(VMEM, VMEM),
        scratch_shapes=[pltpu.VMEM((count * chunk, width), F32)],
        compiler_params=params(),
        name="spread",
    )(*parts.values())


def body(
    section_input, conv_weight, conv_bias, deep_weight, deep_bias, labels, slot_ids, embed_grad
):
    chan_count = lax.axis_size("chan")
    strip_count = lax.axis_size("strip")
    channels = section_input.shape[-1]
    entries = slot_ids.shape[0]
    owned, width = embed_grad.shape
    conv_w = conv_weight.reshape(9 * channels, -1)
    conv_b = conv_bias.reshape(1, -1)

    side = pack_side(embed_grad, slot_ids, labels)
    head, tail, border, near_rows, near_w = columns(section_input, conv_w)
    pairs = []
    for s in range(strip_count):
        for c in range(chan_count):
            to = s + 1 - 2 * (c & 1)
            if 0 <= to < strip_count:
                pairs.append((s * chan_count + c, to * chan_count + c))
    got = lax.ppermute(border, ("strip", "chan"), pairs)

    steps = [(at + 1, 1) for at in range(min(2, strip_count.bit_length() - 2))]
    steps += [(at, min(3, strip_count.bit_length() - 1 - at)) for at in range(3, strip_count.bit_length() - 1, 3)]
    ahead = gather_step(side, "strip", steps[0])
    shared = join(ahead, [border])
    taps = windows(near_rows, section_input.shape[0], [shared])
    ahead = gather_step(shared, "strip", steps[1])
    pooled = conv_pool(taps, near_w, conv_b, section_input.shape[0] // 4, [shared])
    pooled, got, shared = lax.optimization_barrier((pooled, got, join(ahead, [pooled])))
    other = swap(pooled, "chan", 1)
    traded = swap(got, "chan", 1)
    for step in steps[2:]:
        shared = join(gather_step(shared, "strip", step), [])
    shared = [shared, swap(shared, "strip", 1)]
    edges = conv_edges(near_w, conv_b, got, traded, head, tail, [pooled])

    chunk = -(-9 * channels // strip_count // 8) * 8
    bits = strip_count.bit_length() - 1
    ways = 8
    forward = deep_forward(
                pooled,
        other,
        edges,
        deep_weight.reshape(9 * channels, width),
        deep_bias.reshape(1, width),
        labels,
        entries,
    )
    heads = strip_count // ways
    size = heads * chunk

    def sent(part, mask):
        return swap(part.astype(F16), "strip", mask).astype(F32)

    kept, beside, near, across, paired, pair, far = deep_backward(
        forward, shared, chunk, strip_count
    )
    got_far, got_pair = sent(far, 6), sent(pair, 1)
    onward = merge_pair(paired, got_pair, [pair], size, entries, 0, size, [])
    beside = merge_pair(beside, got_far, [], size, entries, size, 2 * size, [onward])
    parts = [
        (kept, True, size, []),
        (sent(beside, 1), True, size, [7]),
        (sent(near, 2), True, size, [2]),
        (sent(across, 3), True, size, [3]),
        (sent(onward, 4), True, size, [4, 5]),
        (got_far, True, 2 * size, [6]),
        (pair, False, size, [0]),
        (got_pair, False, size, [1]),
    ]
    held, shift = ways, 3
    while True:
        step = min(3, bits - shift)
        send, sums = merge(parts, chunk, heads, entries, shift, 1 << step)
        if step == 0:
            break
        more = 1 << step
        heads //= more
        arrived = [send[0]] + [sent(send[m], m << shift) for m in range(1, more)]
        parts = [
            (part, True, heads * chunk, list(range(m * held, (m + 1) * held)))
            for m, part in enumerate(arrived)
        ]
        held *= more
        shift += step
    embeddings = pl.pallas_call(
        functools.partial(embed_kernel, entries=entries),
        out_shape=jax.ShapeDtypeStruct((owned, width), F32),
        in_specs=[VMEM] * (1 + len(shared)),
        out_specs=VMEM,
        compiler_params=params(),
        name="embed",
    )(sums, *shared)
    own = send[0].astype(F16)[None]
    for at in range(3, bits, 3):
        own = jnp.concatenate(gather_step(own, "strip", (at, min(3, bits - at))), axis=0)
    gathered = {m: swap(own, "strip", m) if m else own for m in range(4)}
    for k in (2, 3):
        gathered[2 * k] = swap(own, "strip", 2 * k)
    late = {2 * k + 1: swap(gathered[2 * k], "strip", 1) for k in (2, 3)}
    weight_rows, bias_row = spread(
        {**gathered, **late}, chunk, strip_count, 9 * channels
    )
    return (embeddings, weight_rows.reshape(3, 3, channels, width), bias_row[0])


def solution(mesh):
    placed = (
        P(None, "strip", None),
        P(),
        P(),
        P(None, None, None, "chan"),
        P("chan"),
        P(None, "strip"),
        P("strip"),
        P("strip", "chan"),
    )
    return jax.shard_map(
        body,
        mesh=mesh,
        in_specs=placed,
        out_specs=(P("strip", "chan"), P(None, None, None, "chan"), P("chan")),
        check_vma=False,
    )
```

```python
import functools
import itertools
import math

import jax
import jax.numpy as jnp
from jax import lax
from jax.experimental import pallas as pl
from jax.experimental.pallas import tpu as pltpu
from jax.sharding import PartitionSpec as P

F32, BF16, F16 = jnp.float32, jnp.bfloat16, jnp.float16
VMEM = pl.BlockSpec(memory_space=pltpu.VMEM)
HBM = pl.BlockSpec(memory_space=pltpu.HBM)
ANY = pl.BlockSpec(memory_space=pl.ANY)
SIDE = 8
WIDTH = 3
PIECE = 4
STEP = 6
PAYLOADS = (
    ((0,), 0, 0),
    ((1,), 0, 0),
    ((2,), 1, 40),
    ((3,), 1, 40),
    ((4,), 0, 0),
    ((5,), 1, 48),
    ((6, 7), 1, 0),
)
SPARE = (0, 16, 0)
NOTE = 8


def params(mib=8):
    return pltpu.CompilerParams(vmem_limit_bytes=mib << 20)


def position():
    strip = lax.axis_index("strip")
    last = lax.axis_size("strip") - 1
    return (
        lax.axis_index("chan") & 1,
        (strip == 0).astype(jnp.int32),
        (strip == last).astype(jnp.int32),
        strip,
    )


def swap(value, axis, mask):
    count = lax.axis_size(axis)
    return lax.ppermute(value, axis, [(i, i ^ mask) for i in range(count)])


def gather_step(held, axis, step):
    shift, size = step
    return [held] + [swap(held, axis, m << shift) for m in range(1, 1 << size)]


def relative(refs):
    half = len(refs) // 2
    for low in range(2):
        m = low
        for ref in refs[low * half : (low + 1) * half]:
            for k in range(ref.shape[0]):
                yield m, ref, k
                m += 2


def sigmoid(v):
    return jax.nn.sigmoid(v)


def shares(pooled_rows):
    first = pooled_rows // 2
    return first, pooled_rows - first


def pick(half, pair):
    return jnp.where(half == 0, pair[0], pair[1])


def share_rows(half, rows):
    first, second = shares(rows // 2)
    most = -(-(2 * max(first, second) + 1) // PIECE) * PIECE
    return most, pick(half, (0, rows - most)), pick(half, (-1, 2 * first - 1 - (rows - most)))


def window_kernel(rows_ref, *refs, rows):
    taps, wide = refs[-2:]
    most, cols, chans = rows_ref.shape
    half_cols = cols // 2
    half = position()[0]
    _, _, before = share_rows(half, rows)
    shift = PIECE - before
    lanes = chans // 128
    border = jnp.zeros((8, 128), F32)
    for t in range(wide.shape[0]):
        wide[t, 0:8] = border
        wide[t, cols + 8 : cols + 16] = border

    def prepare(k, carry):
        for slot in range(PIECE):
            r = k * PIECE + slot
            x = rows_ref[r].astype(F32)
            for t in range(lanes):
                wide[slot * lanes + t, 8 : 8 + cols] = x[:, t * 128 : (t + 1) * 128]
            for tap in range(4):
                for t in range(lanes):
                    part = wide[slot * lanes + t, pl.ds(7 + tap, half_cols, stride=2), :]
                    at = (tap * lanes + t) * 128
                    taps[r + shift, :, at : at + 128] = part.astype(BF16)
        return carry

    lax.fori_loop(0, most // PIECE, prepare, 0)
    second = shares(rows // 2)[1]
    outside = pick(half, (PIECE, PIECE + 2 * second + 1))
    taps[outside] = jnp.zeros(taps.shape[1:], BF16)


def windows(near_rows, rows, after):
    most, cols, chans = near_rows.shape
    return pl.pallas_call(
        functools.partial(window_kernel, rows=rows),
        out_shape=jax.ShapeDtypeStruct((most + 2 * PIECE, cols // 2, 4 * chans), BF16),
        in_specs=[VMEM] + [ANY] * len(after),
        out_specs=VMEM,
        scratch_shapes=[pltpu.VMEM((PIECE * (chans // 128), cols + 16, 128), F32)],
        compiler_params=params(16),
        cost_estimate=pl.CostEstimate(flops=0, bytes_accessed=12 << 20, transcendentals=0),
        name="windows",
    )(near_rows, *after)


def edge_part(pairs, w_ref, bias, edge_ref, acc):
    rows = pairs[0].shape[0]
    chans = w_ref.shape[1]
    lanes = chans // 128
    depth = 3 * chans
    lhs = jnp.concatenate(
        [
            pairs[s][:, (2 * j + phase) * chans : (2 * j + phase + 3) * chans]
            for s in range(2)
            for j in range(2)
            for phase in range(2)
        ],
        axis=0,
    )
    pad = rows + 16
    for dr in range(3):
        part = jnp.dot(lhs, w_ref[dr * depth : (dr + 1) * depth], preferred_element_type=F32)
        for g in range(8):
            own = part[g * rows : (g + 1) * rows]
            for t in range(lanes):
                at = 9 - dr
                piece = own[:, t * 128 : (t + 1) * 128]
                if dr == 0:
                    acc[g * lanes + t, 0:8] = jnp.zeros((8, 128), F32)
                    acc[g * lanes + t, 8 + rows : pad] = jnp.zeros((8, 128), F32)
                    acc[g * lanes + t, 8:9] = jnp.zeros((1, 128), F32)
                    acc[g * lanes + t, at : at + rows] = piece
                else:
                    acc[g * lanes + t, at : at + rows] += piece
    for g in range(4):
        for t in range(lanes):
            total = None
            for phase in range(2):
                at = (2 * g + phase) * lanes + t
                v = acc[at, 8 : 8 + rows] + bias[:, t * 128 : (t + 1) * 128]
                acc[at, 8 : 8 + rows] = v * sigmoid(v)
                both = (
                    acc[at, pl.ds(8, rows // 2, stride=2), :]
                    + acc[at, pl.ds(9, rows // 2, stride=2), :]
                )
                total = both if total is None else total + both
            lost = jnp.where(g == 0, position()[1], jnp.where(g == 3, position()[2], 0))
            keep = jnp.where(lost > 0, 0.0, 0.25)
            edge_ref[g, t] = (total * keep).astype(BF16).astype(F32)


def conv_kernel(taps, w_ref, b_ref, *refs):
    out_ref = refs[-1]
    assert out_ref.shape[0] % STEP == 0
    half_cols, chans = taps.shape[1], taps.shape[2] // 4
    bias = b_ref[...]

    def step(k, carry):
        r0 = PIECE + k * 2 * STEP
        total = None
        for phase in range(2):
            lhs = jnp.concatenate(
                [
                    taps[pl.ds(r0 + dr, 2 * STEP), :, phase * chans : (phase + 3) * chans]
                    for dr in range(3)
                ],
                axis=-1,
            ).reshape(2 * STEP * half_cols, 9 * chans)
            v = jnp.dot(lhs, w_ref[...], preferred_element_type=F32) + bias
            h = (v * sigmoid(v)).reshape(STEP, 2, half_cols, chans)
            h = h[:, 0] + h[:, 1]
            total = h if total is None else total + h
        out_ref[pl.ds(k * STEP, STEP)] = (total * 0.25).astype(BF16)
        return carry

    for k in range(out_ref.shape[0] // STEP):
        step(k, 0)


def conv_pool(taps, w, b, pooled_rows, after):
    _, half_cols, width = taps.shape
    chans = width // 4
    return pl.pallas_call(
        conv_kernel,
        out_shape=jax.ShapeDtypeStruct((pooled_rows, half_cols, chans), BF16),
        in_specs=[VMEM] * 3 + [ANY] * len(after),
        out_specs=VMEM,
        compiler_params=params(16),
        cost_estimate=pl.CostEstimate(
            flops=8 * pooled_rows * half_cols * 9 * chans * chans,
            bytes_accessed=8 << 20,
            transcendentals=0,
        ),
        name="conv_pool",
    )(taps, w, b, *after)


def edge_kernel(w_ref, b_ref, got_ref, traded_ref, head_ref, tail_ref, *refs):
    edge_ref, acc = refs[-2:]
    half = position()[0]
    got, traded = got_ref[...], traded_ref[...]
    left = jnp.concatenate([jnp.where(half == 0, got, traded), head_ref[...]], axis=-1)
    right = jnp.concatenate([tail_ref[...], jnp.where(half == 0, traded, got)], axis=-1)
    edge_part((left, right), w_ref, b_ref[...], edge_ref, acc)


def conv_edges(w, b, got, traded, head, tail, after):
    rows, lanes = head.shape[0], w.shape[1] // 128
    return pl.pallas_call(
        edge_kernel,
        out_shape=jax.ShapeDtypeStruct((4, lanes, rows // 2, 128), F32),
        in_specs=[VMEM] * 6 + [ANY] * len(after),
        out_specs=VMEM,
        scratch_shapes=[pltpu.VMEM((8 * lanes, rows + 16, 128), F32)],
        compiler_params=params(),
        cost_estimate=pl.CostEstimate(flops=0, bytes_accessed=4 << 20, transcendentals=0),
        name="conv_edges",
    )(w, b, got, traded, head, tail, *after)


def side_kernel(grad_hbm, labels_hbm, slots_hbm, side_ref, labels_ref, slots_ref, sems):
    owned, width = grad_hbm.shape
    entries = slots_ref.shape[1]
    copies = [
        pltpu.make_async_copy(labels_hbm, labels_ref, sems.at[0]),
        pltpu.make_async_copy(slots_hbm, slots_ref, sems.at[1]),
        pltpu.make_async_copy(grad_hbm, side_ref.at[0, pl.ds(0, owned)], sems.at[2]),
    ]
    for copy in copies:
        copy.start()
    lane = lax.broadcasted_iota(jnp.int32, (1, width), 1)
    copies[0].wait()
    labels = labels_ref[...]
    counts = jnp.zeros((1, width), F32)
    for e in range(entries):
        hit = jnp.where(labels == e, 1.0, 0.0)
        hit = jnp.sum(jnp.sum(hit, axis=0, keepdims=True), axis=1, keepdims=True)
        counts = jnp.where(lane == e, hit, counts)
    copies[1].wait()
    ids = jnp.concatenate(
        [slots_ref[...].astype(F32), jnp.zeros((1, width - entries), F32)], axis=1
    )
    row = lax.broadcasted_iota(jnp.int32, (SIDE, width), 0)
    side_ref[0, owned:] = jnp.where(row == 0, ids, jnp.where(row == 1, counts, 0.0))
    copies[2].wait()


def pack_side(grad, slots, labels):
    owned, width = grad.shape
    fixed = [
        pltpu.with_memory_space_constraint(a, pltpu.HBM)
        for a in (grad, labels, slots.reshape(1, -1))
    ]
    return pl.pallas_call(
        side_kernel,
        out_shape=jax.ShapeDtypeStruct((1, owned + SIDE, width), F32),
        in_specs=[HBM] * 3,
        out_specs=VMEM,
        scratch_shapes=[
            pltpu.VMEM(labels.shape, jnp.int32),
            pltpu.VMEM((1, slots.shape[0]), jnp.int32),
            pltpu.SemaphoreType.DMA((3,)),
        ],
        compiler_params=params(),
        name="pack_side",
    )(*fixed)


def columns_kernel(x_hbm, w_hbm, head_ref, tail_ref, send_ref, near_ref, w_ref, left, right, wide, sems):
    rows, cols, chans = x_hbm.shape
    reach = left.shape[1]
    half = position()[0]
    most, first, _ = share_rows(half, rows)
    size = most // 4
    copies = [
        pltpu.make_async_copy(x_hbm.at[:, pl.ds(0, reach)], left, sems.at[0]),
        pltpu.make_async_copy(x_hbm.at[:, pl.ds(cols - reach, reach)], right, sems.at[1]),
    ]
    for k in range(4):
        source = x_hbm.at[pl.ds(first + k * size, size)]
        copies.append(
            pltpu.make_async_copy(source, near_ref.at[pl.ds(k * size, size)], sems.at[2 + k])
        )
    copies.append(pltpu.make_async_copy(w_hbm, w_ref, sems.at[6]))
    for copy in copies:
        copy.start()
    lanes = chans // 128
    sides = ((left, head_ref, 0), (right, tail_ref, reach - WIDTH))
    for copy, (ref, out_ref, at) in zip(copies, sides):
        copy.wait()
        x = ref[...].astype(F32).reshape(rows * reach, chans)
        for t in range(lanes):
            wide[t] = x[:, t * 128 : (t + 1) * 128]
        for c in range(WIDTH):
            for t in range(lanes):
                part = wide[t, pl.ds(at + c, rows, stride=reach), :].astype(BF16)
                place = (c * lanes + t) * 128
                out_ref[:, place : place + 128] = part
    send_ref[...] = jnp.where(half == 0, tail_ref[...], head_ref[...])
    for copy in copies[2:]:
        copy.wait()


def columns(x, w):
    rows, cols, chans = x.shape
    reach = 16
    most = share_rows(0, rows)[0]
    border = jax.ShapeDtypeStruct((rows, WIDTH * chans), BF16)
    return pl.pallas_call(
        columns_kernel,
        out_shape=(border,) * 3
        + (jax.ShapeDtypeStruct((most, cols, chans), BF16), jax.ShapeDtypeStruct(w.shape, BF16)),
        in_specs=[HBM] * 2,
        out_specs=(VMEM,) * 5,
        scratch_shapes=[
            pltpu.VMEM((rows, reach, chans), BF16),
            pltpu.VMEM((rows, reach, chans), BF16),
            pltpu.VMEM((chans // 128, rows * reach, 128), F32),
            pltpu.SemaphoreType.DMA((7,)),
        ],
        compiler_params=params(16),
        name="columns",
    )(*(pltpu.with_memory_space_constraint(a, pltpu.HBM) for a in (x, w)))


def join_kernel(*refs, count):
    at = 0
    for ref in refs[:count]:
        refs[-1][at : at + ref.shape[0]] = ref[...]
        at += ref.shape[0]


def join(parts, after):
    shape = (sum(p.shape[0] for p in parts),) + parts[0].shape[1:]
    return pl.pallas_call(
        functools.partial(join_kernel, count=len(parts)),
        out_shape=jax.ShapeDtypeStruct(shape, F32),
        in_specs=[VMEM] * len(parts) + [ANY] * len(after),
        out_specs=VMEM,
        compiler_params=params(),
        name="join",
    )(*parts, *after)


def scale_rows(block, note_rows, sums):
    def exponent(values):
        top = None
        for v in values:
            one = jnp.max(jnp.max(jnp.abs(v), axis=0, keepdims=True), axis=1, keepdims=True)
            top = one if top is None else jnp.maximum(top, one)
        return jnp.ceil(jnp.log2(jnp.maximum(top, 1e-30)))

    power = exponent([block, note_rows])
    power_sums = exponent([sums])
    return power, power_sums


def note_block(bias, power, power_sums, width):
    row = lax.broadcasted_iota(jnp.int32, (NOTE, width), 0)
    bias = jnp.broadcast_to(bias, (NOTE, width))
    power = jnp.broadcast_to(power, (NOTE, width))
    power_sums = jnp.broadcast_to(power_sums, (NOTE, width))
    return jnp.where(row == 0, bias, jnp.where(row == 1, power, power_sums))


def read_note(part, at):
    note = part[at : at + NOTE]
    down = jnp.exp2(note[1:2] - 12.0)
    return note[0:1] * down, down, jnp.exp2(note[2:3] - 12.0)


def deep_kernel(
    own_ref, other_ref, edge_ref, w_ref, b_ref, lab_ref, taps, member, slope, sums_ref, wide,
    inside, *, block, entries
):
    _, cols, chans = own_ref.shape
    rows = lab_ref.shape[0]
    lanes = chans // 128
    width = w_ref.shape[-1]
    half = position()[0]
    taps[0] = jnp.zeros(taps.shape[1:], BF16)
    taps[rows + 1] = jnp.zeros(taps.shape[1:], BF16)

    def prepare(ref, base, i, slot):
        x = ref[i].astype(F32)
        r = base + i
        for t in range(lanes):
            s = slot * lanes + t
            at = t * 128
            wide[s, 8 : 8 + cols] = x[:, at : at + 128]
            for g, place in enumerate((7, 8, 7 + cols, 8 + cols)):
                wide[s, place : place + 1] = edge_ref[g, t, pl.ds(r, 1), :]
        for tap in range(3):
            for t in range(lanes):
                piece = wide[slot * lanes + t, 7 + tap : 7 + tap + cols, :]
                at = (tap * lanes + t) * 128
                taps[r + 1, :, at : at + 128] = piece.astype(BF16)

    first, second = shares(rows)
    times = math.gcd(first, second)

    def prepare_all(even_ref, odd_ref):
        def prepare_rows(k, carry):
            for q in range(rows // times):
                ref, base = (even_ref, 0) if q < first // times else (odd_ref, first)
                prepare(ref, base, q * times - base + k, q)
            return carry

        lax.fori_loop(0, times, prepare_rows, 0)

    @pl.when(half == 0)
    def _():
        prepare_all(own_ref, other_ref)

    @pl.when(half != 0)
    def _():
        prepare_all(other_ref, own_ref)

    lab = jnp.transpose(lab_ref[...].astype(F32))
    lane = lax.broadcasted_iota(jnp.int32, (cols, 128), 1)
    want = jnp.where(lane < 3 * entries, lane % entries, -1).astype(F32)
    for r in range(rows):
        member[r] = (lab[:, r : r + 1] == want).astype(BF16)
    bias = b_ref[...]
    size = block * cols

    flat = jnp.concatenate([lab_ref[r : r + 1, :] for r in range(rows)], axis=1)
    entry = lax.broadcasted_iota(jnp.int32, (entries, rows * cols), 0)
    inside[...] = jnp.where(jnp.broadcast_to(flat, entry.shape) == entry, 1.0, 0.0).astype(BF16)

    def step(k, sums):
        r0 = k * block
        lhs = jnp.concatenate([taps[pl.ds(r0 + dr, block)] for dr in range(3)], axis=-1)
        v = jnp.dot(lhs.reshape(size, 9 * chans), w_ref[...], preferred_element_type=F32) + bias
        sig = sigmoid(v)
        features = (v * sig).astype(BF16)
        slope[pl.ds(k * size, size)] = sig * (1.0 + v * (1.0 - sig))
        mine = inside[:, pl.ds(pl.multiple_of(k * size, 128), size)]
        return sums + jnp.dot(mine, features, preferred_element_type=F32)

    sums_ref[...] = lax.fori_loop(0, rows // block, step, jnp.zeros((entries, width), F32))


def deep_forward(own, other, edges, w, b, labels, entries):
    _, cols, chans = own.shape
    rows, width = labels.shape[0], w.shape[-1]
    block = next(k for k in (8, 4, 2, 1) if rows % k == 0)
    first, second = shares(rows)
    slots = rows // math.gcd(first, second)
    return pl.pallas_call(
        functools.partial(deep_kernel, block=block, entries=entries),
        out_shape=(
            jax.ShapeDtypeStruct((rows + 2, cols, 3 * chans), BF16),
            jax.ShapeDtypeStruct((rows, cols, 128), BF16),
            jax.ShapeDtypeStruct((rows * cols, width), F32),
            jax.ShapeDtypeStruct((entries, width), F32),
        ),
        in_specs=[VMEM] * 6,
        out_specs=(VMEM,) * 4,
        scratch_shapes=[
            pltpu.VMEM((slots * (chans // 128), cols + 16, 128), F32),
            pltpu.VMEM((entries, rows * cols), BF16),
        ],
        compiler_params=params(16),
        cost_estimate=pl.CostEstimate(
            flops=4 * rows * cols * 9 * chans * width, bytes_accessed=8 << 20, transcendentals=0
        ),
        name="deep_forward",
    )(own, other, edges, w, b, labels)


def grad_kernel(
    taps, member, slope, sums_ref, *refs, n_parts, chunk
):
    part_refs = refs[:n_parts]
    out_refs, weight = refs[n_parts:-1], refs[-1]
    rows, cols, depth = member.shape[0], taps.shape[1], taps.shape[2]
    width = slope.shape[-1]
    me = position()[3]
    entries = sums_ref.shape[0]
    owned = part_refs[0].shape[1] - SIDE
    own_ids = jnp.broadcast_to(part_refs[0][0, owned : owned + 1, :entries], (entries, entries))
    across = lax.broadcasted_iota(jnp.int32, (entries, entries), 1)
    down = lax.broadcasted_iota(jnp.int32, (entries, entries), 0)
    ids = jnp.sum(jnp.where(across == down, own_ids, 0.0), axis=1, keepdims=True).astype(jnp.int32)
    total = jnp.zeros((entries, 1), F32)
    entry_grad = jnp.zeros((entries, width), F32)
    owner, inner = ids // owned, ids % owned
    spot = lax.broadcasted_iota(jnp.int32, (entries, owned), 1)
    for m, ref, k in relative(part_refs):
        there = ref[k, owned : owned + 1, :entries] == ids.astype(F32)
        counts = ref[k, owned + 1 : owned + 2, :entries]
        total += jnp.sum(jnp.where(there, counts, 0.0), axis=1, keepdims=True)
        hot = ((owner ^ me) == m) & (inner == spot)
        entry_grad += jnp.dot(
            hot.astype(F32), ref[k, :owned], precision=lax.Precision.HIGHEST, preferred_element_type=F32
        )
    entry_grad = entry_grad / jnp.maximum(total, 1.0)
    high = entry_grad.astype(BF16)
    rest = entry_grad - high.astype(F32)
    mid = rest.astype(BF16)
    low = (rest - mid.astype(F32)).astype(BF16)
    terms = jnp.concatenate([high, mid, low, jnp.zeros((128 - 3 * entries, width), BF16)], axis=0)
    pixel = jnp.dot(member[...].reshape(rows * cols, 128), terms, preferred_element_type=F32)
    dg = (pixel * slope[...]).astype(BF16)
    turned = jnp.transpose(dg)
    bias_sum = jnp.sum(dg.astype(F32), axis=0, keepdims=True)
    for dr in range(3):
        window = taps[dr : dr + rows].reshape(rows * cols, depth)
        out = jnp.dot(turned, window, preferred_element_type=F32)
        weight[dr * depth : (dr + 1) * depth] = jnp.transpose(out)
    if weight.shape[0] > 3 * depth:
        weight[3 * depth :] = jnp.zeros((weight.shape[0] - 3 * depth, width), F32)
    sums = sums_ref[...]
    power, power_sums = scale_rows(weight[...], bias_sum, sums)
    up = jnp.exp2(12.0 - power)
    note = note_block(bias_sum * up, power, power_sums, width)
    ways = 8
    digit = lax.rem(me, ways)
    heads = weight.shape[0] // chunk // ways
    sums = sums * jnp.exp2(12.0 - power_sums)
    for out_ref, (members, with_sums, spare) in zip(out_refs, PAYLOADS):
        at = 0
        for m, hi in itertools.product(members, range(heads)):
            j = hi * ways + (digit ^ m)
            out_ref[at : at + chunk] = weight[pl.ds(pl.multiple_of(j * chunk, 8), chunk)] * up
            at += chunk
        out_ref[at : at + NOTE] = note
        at += NOTE
        if with_sums:
            out_ref[at : at + entries] = sums
        if spare:
            out_ref[at + entries :] = jnp.zeros((spare, width), F32)


def deep_backward(forward, parts, chunk, count):
    taps, _, slope, sums = forward
    width, entries = slope.shape[-1], sums.shape[0]
    size = count // 8 * chunk
    return pl.pallas_call(
        functools.partial(grad_kernel, n_parts=len(parts), chunk=chunk),
        out_shape=tuple(
            jax.ShapeDtypeStruct(
                (len(members) * size + NOTE + with_sums * entries + spare, width), F32
            )
            for members, with_sums, spare in PAYLOADS
        ),
        in_specs=[VMEM] * (4 + len(parts)),
        out_specs=(VMEM,) * len(PAYLOADS),
        scratch_shapes=[pltpu.VMEM((count * chunk, width), F32)],
        compiler_params=params(16),
        cost_estimate=pl.CostEstimate(
            flops=4 * slope.shape[0] * 3 * taps.shape[2] * width, bytes_accessed=8 << 20, transcendentals=0
        ),
        name="deep_backward",
    )(*forward, *parts)


def pair_kernel(own_ref, got_ref, *refs, size, entries, got_at, got_note, with_own):
    out_ref = refs[-1]
    own, got = own_ref[size : size + NOTE], got_ref[got_note : got_note + NOTE]
    power = jnp.maximum(own[1:2], got[1:2]) + 1.0
    power_sums = jnp.maximum(own[2:3], got[2:3])
    own_down, got_down = jnp.exp2(own[1:2] - power), jnp.exp2(got[1:2] - power)
    out_ref[:size] = own_ref[:size] * own_down + got_ref[got_at : got_at + size] * got_down
    bias = own[0:1] * own_down + got[0:1] * got_down
    out_ref[size : size + NOTE] = note_block(bias, power, power_sums, own.shape[-1])
    at = size + NOTE
    if with_own:
        sums = refs[0][at : at + entries] * jnp.exp2(own[2:3] - power_sums)
        out_ref[at : at + entries] = sums
        at += entries
    sums = got_ref[got_note + NOTE : got_note + NOTE + entries] * jnp.exp2(got[2:3] - power_sums)
    out_ref[at : at + entries] = sums


def merge_pair(own, got, own_sums, size, entries, got_at, got_note, after):
    width = own.shape[-1]
    rows = size + NOTE + (1 + len(own_sums)) * entries
    return pl.pallas_call(
        functools.partial(
            pair_kernel,
            size=size,
            entries=entries,
            got_at=got_at,
            got_note=got_note,
            with_own=bool(own_sums),
        ),
        out_shape=jax.ShapeDtypeStruct((rows, width), F32),
        in_specs=[VMEM] * (2 + len(own_sums)) + [ANY] * len(after),
        out_specs=VMEM,
        compiler_params=params(),
        name="merge_pair",
    )(own, got, *own_sums, *after)


def merge_kernel(*refs, plan, chunk, heads, entries, shift, next_ways):
    n_parts = len(plan)
    part_refs, out_refs, sums_ref = refs[:n_parts], refs[n_parts:-1], refs[-1]
    width = part_refs[0].shape[-1]
    size = heads * chunk
    total, bias = jnp.zeros((size, width), F32), jnp.zeros((1, width), F32)
    for ref, (added, note_at, members) in zip(part_refs, plan):
        more, down, down_sums = read_note(ref, note_at)
        if added:
            total, bias = total + ref[:size] * down, bias + more
        for k, m in enumerate(members):
            at = note_at + NOTE + k * entries
            sums_ref[m * entries : (m + 1) * entries] = ref[at : at + entries] * down_sums
    sums = sums_ref[...]
    power, power_sums = scale_rows(total, bias, sums)
    up = jnp.exp2(12.0 - power)
    note = note_block(bias * up, power, power_sums, width)
    total = total * up
    if next_ways == 1:
        for out_ref, spare in zip(out_refs, SPARE):
            out_ref[:size] = total
            out_ref[size : size + NOTE] = note
            if spare:
                out_ref[size + NOTE :] = jnp.zeros((spare, width), F32)
        return
    sums = sums * jnp.exp2(12.0 - power_sums)
    digit = lax.rem(position()[3] >> shift, next_ways)
    for m in range(next_ways):
        for hi in range(heads // next_ways):
            piece = jnp.zeros((chunk, width), F32)
            for d in range(next_ways):
                at = (hi * next_ways + d) * chunk
                piece = jnp.where((digit ^ m) == d, total[at : at + chunk], piece)
            out_refs[m][hi * chunk : (hi + 1) * chunk] = piece
        at = heads // next_ways * chunk
        out_refs[m][at : at + NOTE] = note
        out_refs[m][at + NOTE :] = sums


def merge(parts, chunk, heads, entries, shift, next_ways):
    width = parts[0][0].shape[-1]
    sums_rows = sum(len(members) for _, _, _, members in parts) * entries
    if next_ways == 1:
        outs = tuple(
            jax.ShapeDtypeStruct((heads * chunk + NOTE + spare, width), F32) for spare in SPARE
        )
    else:
        rows = heads // next_ways * chunk + NOTE + sums_rows
        outs = (jax.ShapeDtypeStruct((rows, width), F32),) * next_ways
    outs = outs + (jax.ShapeDtypeStruct((sums_rows, width), F32),)
    out = pl.pallas_call(
        functools.partial(
            merge_kernel,
            plan=tuple((added, at, tuple(members)) for _, added, at, members in parts),
            chunk=chunk,
            heads=heads,
            entries=entries,
            shift=shift,
            next_ways=next_ways,
        ),
        out_shape=outs,
        in_specs=[VMEM] * len(parts),
        out_specs=(VMEM,) * len(outs),
        compiler_params=params(),
        name="merge",
    )(*(part for part, _, _, _ in parts))
    return out[:-1], out[-1]


def embed_kernel(sums_ref, *refs, entries):
    part_refs, out_ref = refs[:-1], refs[-1]
    owned, width = out_ref.shape
    own = (position()[3] * owned + lax.broadcasted_iota(jnp.int32, (owned, entries), 0)).astype(F32)
    sums, counts = jnp.zeros((owned, width), F32), jnp.zeros((owned, 1), F32)
    for m, ref, k in relative(part_refs):
        there = ref[k, owned : owned + 1, :entries] == own
        count = ref[k, owned + 1 : owned + 2, :entries]
        counts += jnp.sum(jnp.where(there, count, 0.0), axis=1, keepdims=True)
        sums += jnp.dot(
            there.astype(F32),
            sums_ref[m * entries : (m + 1) * entries],
            precision=lax.Precision.HIGHEST,
            preferred_element_type=F32,
        )
    out_ref[...] = sums / jnp.maximum(counts, 1.0)


def spread_kernel(*refs, chunk, rows, members):
    part_refs, weight_ref, bias_ref, place = refs[:-3], refs[-3], refs[-2], refs[-1]
    me = position()[3]
    count = len(members)
    for p, k in itertools.product(range(count), range(part_refs[0].shape[0])):
        bias, down, _ = read_note(part_refs[p][k], chunk)
        j = me ^ (members[p] + k * count)
        target = weight_ref if rows == place.shape[0] else place
        target[pl.ds(pl.multiple_of(j * chunk, 8), chunk)] = part_refs[p][k, :chunk] * down

        @pl.when(j == 0)
        def _():
            bias_ref[...] = bias

    if rows != place.shape[0]:
        weight_ref[...] = place[:rows]


def spread(parts, chunk, count, rows):
    parts = {m: part.astype(F32) for m, part in parts.items()}
    width = parts[0].shape[-1]
    return pl.pallas_call(
        functools.partial(spread_kernel, chunk=chunk, rows=rows, members=tuple(parts)),
        out_shape=(jax.ShapeDtypeStruct((rows, width), F32), jax.ShapeDtypeStruct((1, width), F32)),
        in_specs=[VMEM] * len(parts),
        out_specs=(VMEM, VMEM),
        scratch_shapes=[pltpu.VMEM((count * chunk, width), F32)],
        compiler_params=params(),
        name="spread",
    )(*parts.values())


def body(
    section_input, conv_weight, conv_bias, deep_weight, deep_bias, labels, slot_ids, embed_grad
):
    chan_count = lax.axis_size("chan")
    strip_count = lax.axis_size("strip")
    channels = section_input.shape[-1]
    entries = slot_ids.shape[0]
    owned, width = embed_grad.shape
    conv_w = conv_weight.reshape(9 * channels, -1)
    conv_b = conv_bias.reshape(1, -1)

    side = pack_side(embed_grad, slot_ids, labels)
    head, tail, border, near_rows, near_w = columns(section_input, conv_w)
    pairs = []
    for s in range(strip_count):
        for c in range(chan_count):
            to = s + 1 - 2 * (c & 1)
            if 0 <= to < strip_count:
                pairs.append((s * chan_count + c, to * chan_count + c))
    got = lax.ppermute(border, ("strip", "chan"), pairs)

    steps = [(at + 1, 1) for at in range(min(2, strip_count.bit_length() - 2))]
    steps += [(at, min(3, strip_count.bit_length() - 1 - at)) for at in range(3, strip_count.bit_length() - 1, 3)]
    ahead = gather_step(side, "strip", steps[0])
    shared = join(ahead, [border])
    taps = windows(near_rows, section_input.shape[0], [shared])
    ahead = gather_step(shared, "strip", steps[1])
    pooled = conv_pool(taps, near_w, conv_b, section_input.shape[0] // 4, [shared])
    pooled, got, shared = lax.optimization_barrier((pooled, got, join(ahead, [pooled])))
    other = swap(pooled, "chan", 1)
    traded = swap(got, "chan", 1)
    for step in steps[2:]:
        shared = join(gather_step(shared, "strip", step), [])
    shared = [shared, swap(shared, "strip", 1)]
    edges = conv_edges(near_w, conv_b, got, traded, head, tail, [pooled])

    chunk = -(-9 * channels // strip_count // 8) * 8
    bits = strip_count.bit_length() - 1
    ways = 8
    forward = deep_forward(
                pooled,
        other,
        edges,
        deep_weight.reshape(9 * channels, width),
        deep_bias.reshape(1, width),
        labels,
        entries,
    )
    heads = strip_count // ways
    size = heads * chunk

    def sent(part, mask):
        return swap(part.astype(F16), "strip", mask).astype(F32)

    kept, beside, near, across, paired, pair, far = deep_backward(
        forward, shared, chunk, strip_count
    )
    got_far, got_pair = sent(far, 6), sent(pair, 1)
    onward = merge_pair(paired, got_pair, [pair], size, entries, 0, size, [])
    beside = merge_pair(beside, got_far, [], size, entries, size, 2 * size, [onward])
    parts = [
        (kept, True, size, []),
        (sent(beside, 1), True, size, [7]),
        (sent(near, 2), True, size, [2]),
        (sent(across, 3), True, size, [3]),
        (sent(onward, 4), True, size, [4, 5]),
        (got_far, True, 2 * size, [6]),
        (pair, False, size, [0]),
        (got_pair, False, size, [1]),
    ]
    held, shift = ways, 3
    while True:
        step = min(3, bits - shift)
        send, sums = merge(parts, chunk, heads, entries, shift, 1 << step)
        if step == 0:
            break
        more = 1 << step
        heads //= more
        arrived = [send[0]] + [sent(send[m], m << shift) for m in range(1, more)]
        parts = [
            (part, True, heads * chunk, list(range(m * held, (m + 1) * held)))
            for m, part in enumerate(arrived)
        ]
        held *= more
        shift += step
    embeddings = pl.pallas_call(
        functools.partial(embed_kernel, entries=entries),
        out_shape=jax.ShapeDtypeStruct((owned, width), F32),
        in_specs=[VMEM] * (1 + len(shared)),
        out_specs=VMEM,
        compiler_params=params(),
        name="embed",
    )(sums, *shared)
    own, middle, long = (part.astype(F16)[None] for part in send)
    for at in range(3, bits, 3):
        own = jnp.concatenate(gather_step(own, "strip", (at, min(3, bits - at))), axis=0)
        middle = long = own
    gathered = {0: own, 1: swap(middle, "strip", 1), 2: swap(own, "strip", 2)}
    gathered[3] = swap(middle, "strip", 3)
    gathered[4], gathered[6] = swap(long, "strip", 4), swap(own, "strip", 6)
    late = {m + 1: swap(gathered[m], "strip", 1) for m in (4, 6)}
    weight_rows, bias_row = spread(
        {**gathered, **late}, chunk, strip_count, 9 * channels
    )
    return (embeddings, weight_rows.reshape(3, 3, channels, width), bias_row[0])


def solution(mesh):
    placed = (
        P(None, "strip", None),
        P(),
        P(),
        P(None, None, None, "chan"),
        P("chan"),
        P(None, "strip"),
        P("strip"),
        P("strip", "chan"),
    )
    return jax.shard_map(
        body,
        mesh=mesh,
        in_specs=placed,
        out_specs=(P("strip", "chan"), P(None, None, None, "chan"), P("chan")),
        check_vma=False,
    )
```

```python
import functools
import itertools
import math

import jax
import jax.numpy as jnp
from jax import lax
from jax.experimental import pallas as pl
from jax.experimental.pallas import tpu as pltpu
from jax.sharding import PartitionSpec as P

F32, BF16, F16 = jnp.float32, jnp.bfloat16, jnp.float16
VMEM = pl.BlockSpec(memory_space=pltpu.VMEM)
HBM = pl.BlockSpec(memory_space=pltpu.HBM)
ANY = pl.BlockSpec(memory_space=pl.ANY)
SIDE = 8
WIDTH = 3
PIECE = 4
STEP = 6
PAYLOADS = (((0,), 0), ((1,), 0), ((2,), 0), ((3,), 0), ((4,), 0), ((5,), 1), ((6, 7), 1))
SPARE = (0, 16, 0)
NOTE = 8


def params(mib=8):
    return pltpu.CompilerParams(vmem_limit_bytes=mib << 20)


def position():
    strip = lax.axis_index("strip")
    last = lax.axis_size("strip") - 1
    return (
        lax.axis_index("chan") & 1,
        (strip == 0).astype(jnp.int32),
        (strip == last).astype(jnp.int32),
        strip,
    )


def swap(value, axis, mask):
    count = lax.axis_size(axis)
    return lax.ppermute(value, axis, [(i, i ^ mask) for i in range(count)])


def gather_step(held, axis, step):
    shift, size = step
    return [held] + [swap(held, axis, m << shift) for m in range(1, 1 << size)]


def relative(refs):
    half = len(refs) // 2
    for low in range(2):
        m = low
        for ref in refs[low * half : (low + 1) * half]:
            for k in range(ref.shape[0]):
                yield m, ref, k
                m += 2


def sigmoid(v):
    return jax.nn.sigmoid(v)


def shares(pooled_rows):
    first = pooled_rows // 2
    return first, pooled_rows - first


def pick(half, pair):
    return jnp.where(half == 0, pair[0], pair[1])


def share_rows(half, rows):
    first, second = shares(rows // 2)
    most = -(-(2 * max(first, second) + 1) // PIECE) * PIECE
    return most, pick(half, (0, rows - most)), pick(half, (-1, 2 * first - 1 - (rows - most)))


def window_kernel(rows_ref, *refs, rows):
    taps, wide = refs[-2:]
    most, cols, chans = rows_ref.shape
    half_cols = cols // 2
    half = position()[0]
    _, _, before = share_rows(half, rows)
    shift = PIECE - before
    lanes = chans // 128
    border = jnp.zeros((8, 128), F32)
    for t in range(wide.shape[0]):
        wide[t, 0:8] = border
        wide[t, cols + 8 : cols + 16] = border

    def prepare(k, carry):
        for slot in range(PIECE):
            r = k * PIECE + slot
            x = rows_ref[r].astype(F32)
            for t in range(lanes):
                wide[slot * lanes + t, 8 : 8 + cols] = x[:, t * 128 : (t + 1) * 128]
            for tap in range(4):
                for t in range(lanes):
                    part = wide[slot * lanes + t, pl.ds(7 + tap, half_cols, stride=2), :]
                    at = (tap * lanes + t) * 128
                    taps[r + shift, :, at : at + 128] = part.astype(BF16)
        return carry

    lax.fori_loop(0, most // PIECE, prepare, 0)
    second = shares(rows // 2)[1]
    outside = pick(half, (PIECE, PIECE + 2 * second + 1))
    taps[outside] = jnp.zeros(taps.shape[1:], BF16)


def windows(near_rows, rows, after):
    most, cols, chans = near_rows.shape
    return pl.pallas_call(
        functools.partial(window_kernel, rows=rows),
        out_shape=jax.ShapeDtypeStruct((most + 2 * PIECE, cols // 2, 4 * chans), BF16),
        in_specs=[VMEM] + [ANY] * len(after),
        out_specs=VMEM,
        scratch_shapes=[pltpu.VMEM((PIECE * (chans // 128), cols + 16, 128), F32)],
        compiler_params=params(16),
        cost_estimate=pl.CostEstimate(flops=0, bytes_accessed=12 << 20, transcendentals=0),
        name="windows",
    )(near_rows, *after)


def edge_part(pairs, w_ref, bias, edge_ref, acc):
    rows = pairs[0].shape[0]
    chans = w_ref.shape[1]
    lanes = chans // 128
    depth = 3 * chans
    lhs = jnp.concatenate(
        [
            pairs[s][:, (2 * j + phase) * chans : (2 * j + phase + 3) * chans]
            for s in range(2)
            for j in range(2)
            for phase in range(2)
        ],
        axis=0,
    )
    pad = rows + 16
    for dr in range(3):
        part = jnp.dot(lhs, w_ref[dr * depth : (dr + 1) * depth], preferred_element_type=F32)
        for g in range(8):
            own = part[g * rows : (g + 1) * rows]
            for t in range(lanes):
                at = 9 - dr
                piece = own[:, t * 128 : (t + 1) * 128]
                if dr == 0:
                    acc[g * lanes + t, 0:8] = jnp.zeros((8, 128), F32)
                    acc[g * lanes + t, 8 + rows : pad] = jnp.zeros((8, 128), F32)
                    acc[g * lanes + t, 8:9] = jnp.zeros((1, 128), F32)
                    acc[g * lanes + t, at : at + rows] = piece
                else:
                    acc[g * lanes + t, at : at + rows] += piece
    for g in range(4):
        for t in range(lanes):
            total = None
            for phase in range(2):
                at = (2 * g + phase) * lanes + t
                v = acc[at, 8 : 8 + rows] + bias[:, t * 128 : (t + 1) * 128]
                acc[at, 8 : 8 + rows] = v * sigmoid(v)
                both = (
                    acc[at, pl.ds(8, rows // 2, stride=2), :]
                    + acc[at, pl.ds(9, rows // 2, stride=2), :]
                )
                total = both if total is None else total + both
            lost = jnp.where(g == 0, position()[1], jnp.where(g == 3, position()[2], 0))
            keep = jnp.where(lost > 0, 0.0, 0.25)
            edge_ref[g, t] = (total * keep).astype(BF16).astype(F32)


def conv_kernel(taps, w_ref, b_ref, *refs):
    out_ref = refs[-1]
    assert out_ref.shape[0] % STEP == 0
    half_cols, chans = taps.shape[1], taps.shape[2] // 4
    bias = b_ref[...]

    def step(k, carry):
        r0 = PIECE + k * 2 * STEP
        total = None
        for phase in range(2):
            lhs = jnp.concatenate(
                [
                    taps[pl.ds(r0 + dr, 2 * STEP), :, phase * chans : (phase + 3) * chans]
                    for dr in range(3)
                ],
                axis=-1,
            ).reshape(2 * STEP * half_cols, 9 * chans)
            v = jnp.dot(lhs, w_ref[...], preferred_element_type=F32) + bias
            h = (v * sigmoid(v)).reshape(STEP, 2, half_cols, chans)
            h = h[:, 0] + h[:, 1]
            total = h if total is None else total + h
        out_ref[pl.ds(k * STEP, STEP)] = (total * 0.25).astype(BF16)
        return carry

    for k in range(out_ref.shape[0] // STEP):
        step(k, 0)


def conv_pool(taps, w, b, pooled_rows, after):
    _, half_cols, width = taps.shape
    chans = width // 4
    return pl.pallas_call(
        conv_kernel,
        out_shape=jax.ShapeDtypeStruct((pooled_rows, half_cols, chans), BF16),
        in_specs=[VMEM] * 3 + [ANY] * len(after),
        out_specs=VMEM,
        compiler_params=params(16),
        cost_estimate=pl.CostEstimate(
            flops=8 * pooled_rows * half_cols * 9 * chans * chans,
            bytes_accessed=8 << 20,
            transcendentals=0,
        ),
        name="conv_pool",
    )(taps, w, b, *after)


def edge_kernel(w_ref, b_ref, got_ref, traded_ref, head_ref, tail_ref, *refs):
    edge_ref, acc = refs[-2:]
    half = position()[0]
    got, traded = got_ref[...], traded_ref[...]
    left = jnp.concatenate([jnp.where(half == 0, got, traded), head_ref[...]], axis=-1)
    right = jnp.concatenate([tail_ref[...], jnp.where(half == 0, traded, got)], axis=-1)
    edge_part((left, right), w_ref, b_ref[...], edge_ref, acc)


def conv_edges(w, b, got, traded, head, tail, after):
    rows, lanes = head.shape[0], w.shape[1] // 128
    return pl.pallas_call(
        edge_kernel,
        out_shape=jax.ShapeDtypeStruct((4, lanes, rows // 2, 128), F32),
        in_specs=[VMEM] * 6 + [ANY] * len(after),
        out_specs=VMEM,
        scratch_shapes=[pltpu.VMEM((8 * lanes, rows + 16, 128), F32)],
        compiler_params=params(),
        cost_estimate=pl.CostEstimate(flops=0, bytes_accessed=4 << 20, transcendentals=0),
        name="conv_edges",
    )(w, b, got, traded, head, tail, *after)


def side_kernel(grad_hbm, labels_hbm, slots_hbm, side_ref, labels_ref, slots_ref, sems):
    owned, width = grad_hbm.shape
    entries = slots_ref.shape[1]
    copies = [
        pltpu.make_async_copy(labels_hbm, labels_ref, sems.at[0]),
        pltpu.make_async_copy(slots_hbm, slots_ref, sems.at[1]),
        pltpu.make_async_copy(grad_hbm, side_ref.at[0, pl.ds(0, owned)], sems.at[2]),
    ]
    for copy in copies:
        copy.start()
    lane = lax.broadcasted_iota(jnp.int32, (1, width), 1)
    copies[0].wait()
    labels = labels_ref[...]
    counts = jnp.zeros((1, width), F32)
    for e in range(entries):
        hit = jnp.where(labels == e, 1.0, 0.0)
        hit = jnp.sum(jnp.sum(hit, axis=0, keepdims=True), axis=1, keepdims=True)
        counts = jnp.where(lane == e, hit, counts)
    copies[1].wait()
    ids = jnp.concatenate(
        [slots_ref[...].astype(F32), jnp.zeros((1, width - entries), F32)], axis=1
    )
    row = lax.broadcasted_iota(jnp.int32, (SIDE, width), 0)
    side_ref[0, owned:] = jnp.where(row == 0, ids, jnp.where(row == 1, counts, 0.0))
    copies[2].wait()


def pack_side(grad, slots, labels):
    owned, width = grad.shape
    fixed = [
        pltpu.with_memory_space_constraint(a, pltpu.HBM)
        for a in (grad, labels, slots.reshape(1, -1))
    ]
    return pl.pallas_call(
        side_kernel,
        out_shape=jax.ShapeDtypeStruct((1, owned + SIDE, width), F32),
        in_specs=[HBM] * 3,
        out_specs=VMEM,
        scratch_shapes=[
            pltpu.VMEM(labels.shape, jnp.int32),
            pltpu.VMEM((1, slots.shape[0]), jnp.int32),
            pltpu.SemaphoreType.DMA((3,)),
        ],
        compiler_params=params(),
        name="pack_side",
    )(*fixed)


def columns_kernel(x_hbm, w_hbm, head_ref, tail_ref, send_ref, near_ref, w_ref, left, right, wide, sems):
    rows, cols, chans = x_hbm.shape
    reach = left.shape[1]
    half = position()[0]
    most, first, _ = share_rows(half, rows)
    size = most // 4
    copies = [
        pltpu.make_async_copy(x_hbm.at[:, pl.ds(0, reach)], left, sems.at[0]),
        pltpu.make_async_copy(x_hbm.at[:, pl.ds(cols - reach, reach)], right, sems.at[1]),
    ]
    for k in range(4):
        source = x_hbm.at[pl.ds(first + k * size, size)]
        copies.append(
            pltpu.make_async_copy(source, near_ref.at[pl.ds(k * size, size)], sems.at[2 + k])
        )
    copies.append(pltpu.make_async_copy(w_hbm, w_ref, sems.at[6]))
    for copy in copies:
        copy.start()
    lanes = chans // 128
    sides = ((left, head_ref, 0), (right, tail_ref, reach - WIDTH))
    for copy, (ref, out_ref, at) in zip(copies, sides):
        copy.wait()
        x = ref[...].astype(F32).reshape(rows * reach, chans)
        for t in range(lanes):
            wide[t] = x[:, t * 128 : (t + 1) * 128]
        for c in range(WIDTH):
            for t in range(lanes):
                part = wide[t, pl.ds(at + c, rows, stride=reach), :].astype(BF16)
                place = (c * lanes + t) * 128
                out_ref[:, place : place + 128] = part
    send_ref[...] = jnp.where(half == 0, tail_ref[...], head_ref[...])
    for copy in copies[2:]:
        copy.wait()


def columns(x, w):
    rows, cols, chans = x.shape
    reach = 16
    most = share_rows(0, rows)[0]
    border = jax.ShapeDtypeStruct((rows, WIDTH * chans), BF16)
    return pl.pallas_call(
        columns_kernel,
        out_shape=(border,) * 3
        + (jax.ShapeDtypeStruct((most, cols, chans), BF16), jax.ShapeDtypeStruct(w.shape, BF16)),
        in_specs=[HBM] * 2,
        out_specs=(VMEM,) * 5,
        scratch_shapes=[
            pltpu.VMEM((rows, reach, chans), BF16),
            pltpu.VMEM((rows, reach, chans), BF16),
            pltpu.VMEM((chans // 128, rows * reach, 128), F32),
            pltpu.SemaphoreType.DMA((7,)),
        ],
        compiler_params=params(16),
        name="columns",
    )(*(pltpu.with_memory_space_constraint(a, pltpu.HBM) for a in (x, w)))


def join_kernel(*refs, count):
    at = 0
    for ref in refs[:count]:
        refs[-1][at : at + ref.shape[0]] = ref[...]
        at += ref.shape[0]


def join(parts, after):
    shape = (sum(p.shape[0] for p in parts),) + parts[0].shape[1:]
    return pl.pallas_call(
        functools.partial(join_kernel, count=len(parts)),
        out_shape=jax.ShapeDtypeStruct(shape, F32),
        in_specs=[VMEM] * len(parts) + [ANY] * len(after),
        out_specs=VMEM,
        compiler_params=params(),
        name="join",
    )(*parts, *after)


def scale_rows(block, note_rows, sums):
    def exponent(values):
        top = None
        for v in values:
            one = jnp.max(jnp.max(jnp.abs(v), axis=0, keepdims=True), axis=1, keepdims=True)
            top = one if top is None else jnp.maximum(top, one)
        return jnp.ceil(jnp.log2(jnp.maximum(top, 1e-30)))

    power = exponent([block, note_rows])
    power_sums = exponent([sums])
    return power, power_sums


def note_block(bias, power, power_sums, width):
    row = lax.broadcasted_iota(jnp.int32, (NOTE, width), 0)
    bias = jnp.broadcast_to(bias, (NOTE, width))
    power = jnp.broadcast_to(power, (NOTE, width))
    power_sums = jnp.broadcast_to(power_sums, (NOTE, width))
    return jnp.where(row == 0, bias, jnp.where(row == 1, power, power_sums))


def read_note(part, at):
    note = part[at : at + NOTE]
    down = jnp.exp2(note[1:2] - 12.0)
    return note[0:1] * down, down, jnp.exp2(note[2:3] - 12.0)


def deep_kernel(
    own_ref, other_ref, edge_ref, w_ref, b_ref, lab_ref, taps, member, slope, sums_ref, wide,
    inside, *, block, entries
):
    _, cols, chans = own_ref.shape
    rows = lab_ref.shape[0]
    lanes = chans // 128
    width = w_ref.shape[-1]
    half = position()[0]
    taps[0] = jnp.zeros(taps.shape[1:], BF16)
    taps[rows + 1] = jnp.zeros(taps.shape[1:], BF16)

    def prepare(ref, base, i, slot):
        x = ref[i].astype(F32)
        r = base + i
        for t in range(lanes):
            s = slot * lanes + t
            at = t * 128
            wide[s, 8 : 8 + cols] = x[:, at : at + 128]
            for g, place in enumerate((7, 8, 7 + cols, 8 + cols)):
                wide[s, place : place + 1] = edge_ref[g, t, pl.ds(r, 1), :]
        for tap in range(3):
            for t in range(lanes):
                piece = wide[slot * lanes + t, 7 + tap : 7 + tap + cols, :]
                at = (tap * lanes + t) * 128
                taps[r + 1, :, at : at + 128] = piece.astype(BF16)

    first, second = shares(rows)
    times = math.gcd(first, second)

    def prepare_all(even_ref, odd_ref):
        def prepare_rows(k, carry):
            for q in range(rows // times):
                ref, base = (even_ref, 0) if q < first // times else (odd_ref, first)
                prepare(ref, base, q * times - base + k, q)
            return carry

        lax.fori_loop(0, times, prepare_rows, 0)

    @pl.when(half == 0)
    def _():
        prepare_all(own_ref, other_ref)

    @pl.when(half != 0)
    def _():
        prepare_all(other_ref, own_ref)

    lab = jnp.transpose(lab_ref[...].astype(F32))
    lane = lax.broadcasted_iota(jnp.int32, (cols, 128), 1)
    want = jnp.where(lane < 3 * entries, lane % entries, -1).astype(F32)
    for r in range(rows):
        member[r] = (lab[:, r : r + 1] == want).astype(BF16)
    bias = b_ref[...]
    size = block * cols

    flat = jnp.concatenate([lab_ref[r : r + 1, :] for r in range(rows)], axis=1)
    entry = lax.broadcasted_iota(jnp.int32, (entries, rows * cols), 0)
    inside[...] = jnp.where(jnp.broadcast_to(flat, entry.shape) == entry, 1.0, 0.0).astype(BF16)

    def step(k, sums):
        r0 = k * block
        lhs = jnp.concatenate([taps[pl.ds(r0 + dr, block)] for dr in range(3)], axis=-1)
        v = jnp.dot(lhs.reshape(size, 9 * chans), w_ref[...], preferred_element_type=F32) + bias
        sig = sigmoid(v)
        features = (v * sig).astype(BF16)
        slope[pl.ds(k * size, size)] = sig * (1.0 + v * (1.0 - sig))
        mine = inside[:, pl.ds(pl.multiple_of(k * size, 128), size)]
        return sums + jnp.dot(mine, features, preferred_element_type=F32)

    sums_ref[...] = lax.fori_loop(0, rows // block, step, jnp.zeros((entries, width), F32))


def deep_forward(own, other, edges, w, b, labels, entries):
    _, cols, chans = own.shape
    rows, width = labels.shape[0], w.shape[-1]
    block = next(k for k in (8, 4, 2, 1) if rows % k == 0)
    first, second = shares(rows)
    slots = rows // math.gcd(first, second)
    return pl.pallas_call(
        functools.partial(deep_kernel, block=block, entries=entries),
        out_shape=(
            jax.ShapeDtypeStruct((rows + 2, cols, 3 * chans), BF16),
            jax.ShapeDtypeStruct((rows, cols, 128), BF16),
            jax.ShapeDtypeStruct((rows * cols, width), F32),
            jax.ShapeDtypeStruct((entries, width), F32),
        ),
        in_specs=[VMEM] * 6,
        out_specs=(VMEM,) * 4,
        scratch_shapes=[
            pltpu.VMEM((slots * (chans // 128), cols + 16, 128), F32),
            pltpu.VMEM((entries, rows * cols), BF16),
        ],
        compiler_params=params(16),
        cost_estimate=pl.CostEstimate(
            flops=4 * rows * cols * 9 * chans * width, bytes_accessed=8 << 20, transcendentals=0
        ),
        name="deep_forward",
    )(own, other, edges, w, b, labels)


def grad_kernel(
    taps, member, slope, sums_ref, *refs, n_parts, chunk
):
    part_refs = refs[:n_parts]
    out_refs, weight = refs[n_parts:-1], refs[-1]
    rows, cols, depth = member.shape[0], taps.shape[1], taps.shape[2]
    width = slope.shape[-1]
    me = position()[3]
    entries = sums_ref.shape[0]
    owned = part_refs[0].shape[1] - SIDE
    own_ids = jnp.broadcast_to(part_refs[0][0, owned : owned + 1, :entries], (entries, entries))
    across = lax.broadcasted_iota(jnp.int32, (entries, entries), 1)
    down = lax.broadcasted_iota(jnp.int32, (entries, entries), 0)
    ids = jnp.sum(jnp.where(across == down, own_ids, 0.0), axis=1, keepdims=True).astype(jnp.int32)
    total = jnp.zeros((entries, 1), F32)
    entry_grad = jnp.zeros((entries, width), F32)
    owner, inner = ids // owned, ids % owned
    spot = lax.broadcasted_iota(jnp.int32, (entries, owned), 1)
    for m, ref, k in relative(part_refs):
        there = ref[k, owned : owned + 1, :entries] == ids.astype(F32)
        counts = ref[k, owned + 1 : owned + 2, :entries]
        total += jnp.sum(jnp.where(there, counts, 0.0), axis=1, keepdims=True)
        hot = ((owner ^ me) == m) & (inner == spot)
        entry_grad += jnp.dot(
            hot.astype(F32), ref[k, :owned], precision=lax.Precision.HIGHEST, preferred_element_type=F32
        )
    entry_grad = entry_grad / jnp.maximum(total, 1.0)
    high = entry_grad.astype(BF16)
    rest = entry_grad - high.astype(F32)
    mid = rest.astype(BF16)
    low = (rest - mid.astype(F32)).astype(BF16)
    terms = jnp.concatenate([high, mid, low, jnp.zeros((128 - 3 * entries, width), BF16)], axis=0)
    pixel = jnp.dot(member[...].reshape(rows * cols, 128), terms, preferred_element_type=F32)
    dg = (pixel * slope[...]).astype(BF16)
    turned = jnp.transpose(dg)
    bias_sum = jnp.sum(dg.astype(F32), axis=0, keepdims=True)
    for dr in range(3):
        window = taps[dr : dr + rows].reshape(rows * cols, depth)
        out = jnp.dot(turned, window, preferred_element_type=F32)
        weight[dr * depth : (dr + 1) * depth] = jnp.transpose(out)
    if weight.shape[0] > 3 * depth:
        weight[3 * depth :] = jnp.zeros((weight.shape[0] - 3 * depth, width), F32)
    sums = sums_ref[...]
    power, power_sums = scale_rows(weight[...], bias_sum, sums)
    up = jnp.exp2(12.0 - power)
    note = note_block(bias_sum * up, power, power_sums, width)
    ways = 8
    digit = lax.rem(me, ways)
    heads = weight.shape[0] // chunk // ways
    sums = sums * jnp.exp2(12.0 - power_sums)
    for out_ref, (members, with_sums) in zip(out_refs, PAYLOADS):
        at = 0
        for m, hi in itertools.product(members, range(heads)):
            j = hi * ways + (digit ^ m)
            out_ref[at : at + chunk] = weight[pl.ds(pl.multiple_of(j * chunk, 8), chunk)] * up
            at += chunk
        out_ref[at : at + NOTE] = note
        if with_sums:
            out_ref[at + NOTE :] = sums


def deep_backward(forward, parts, chunk, count):
    taps, _, slope, sums = forward
    width, entries = slope.shape[-1], sums.shape[0]
    size = count // 8 * chunk
    return pl.pallas_call(
        functools.partial(grad_kernel, n_parts=len(parts), chunk=chunk),
        out_shape=tuple(
            jax.ShapeDtypeStruct((len(members) * size + NOTE + with_sums * entries, width), F32)
            for members, with_sums in PAYLOADS
        ),
        in_specs=[VMEM] * (4 + len(parts)),
        out_specs=(VMEM,) * len(PAYLOADS),
        scratch_shapes=[pltpu.VMEM((count * chunk, width), F32)],
        compiler_params=params(16),
        cost_estimate=pl.CostEstimate(
            flops=4 * slope.shape[0] * 3 * taps.shape[2] * width, bytes_accessed=8 << 20, transcendentals=0
        ),
        name="deep_backward",
    )(*forward, *parts)


def pair_kernel(own_ref, got_ref, *refs, size, entries, got_at, got_note, sums_notes):
    out_ref = refs[-1]
    own, got = own_ref[size : size + NOTE], got_ref[got_note : got_note + NOTE]
    power = jnp.maximum(own[1:2], got[1:2]) + 1.0
    own_down, got_down = jnp.exp2(own[1:2] - power), jnp.exp2(got[1:2] - power)
    out_ref[:size] = own_ref[:size] * own_down + got_ref[got_at : got_at + size] * got_down
    bias = own[0:1] * own_down + got[0:1] * got_down
    powers = [ref[at + 2 : at + 3] for ref, at in zip(refs, sums_notes)]
    power_sums = functools.reduce(jnp.maximum, powers)
    out_ref[size : size + NOTE] = note_block(bias, power, power_sums, own.shape[-1])
    place = size + NOTE
    for ref, at, one in zip(refs, sums_notes, powers):
        sums = ref[at + NOTE : at + NOTE + entries] * jnp.exp2(one - power_sums)
        out_ref[place : place + entries] = sums
        place += entries
    if place < out_ref.shape[0]:
        out_ref[place:] = jnp.zeros((out_ref.shape[0] - place, own.shape[-1]), F32)


def merge_pair(own, got, sums, size, entries, got_at, got_note, after, spare=0):
    width = own.shape[-1]
    return pl.pallas_call(
        functools.partial(
            pair_kernel,
            size=size,
            entries=entries,
            got_at=got_at,
            got_note=got_note,
            sums_notes=tuple(at for _, at in sums),
        ),
        out_shape=jax.ShapeDtypeStruct((size + NOTE + len(sums) * entries + spare, width), F32),
        in_specs=[VMEM] * (2 + len(sums)) + [ANY] * len(after),
        out_specs=VMEM,
        compiler_params=params(),
        name="merge_pair",
    )(own, got, *(part for part, _ in sums), *after)


def merge_kernel(*refs, plan, chunk, heads, entries, shift, next_ways):
    n_parts = len(plan)
    part_refs, out_refs, sums_ref = refs[:n_parts], refs[n_parts:-1], refs[-1]
    width = part_refs[0].shape[-1]
    size = heads * chunk
    total, bias = jnp.zeros((size, width), F32), jnp.zeros((1, width), F32)
    for ref, (added, note_at, members) in zip(part_refs, plan):
        more, down, down_sums = read_note(ref, note_at)
        if added:
            total, bias = total + ref[:size] * down, bias + more
        for k, m in enumerate(members):
            at = note_at + NOTE + k * entries
            sums_ref[m * entries : (m + 1) * entries] = ref[at : at + entries] * down_sums
    sums = sums_ref[...]
    power, power_sums = scale_rows(total, bias, sums)
    up = jnp.exp2(12.0 - power)
    note = note_block(bias * up, power, power_sums, width)
    total = total * up
    if next_ways == 1:
        for out_ref, spare in zip(out_refs, SPARE):
            out_ref[:size] = total
            out_ref[size : size + NOTE] = note
            if spare:
                out_ref[size + NOTE :] = jnp.zeros((spare, width), F32)
        return
    sums = sums * jnp.exp2(12.0 - power_sums)
    digit = lax.rem(position()[3] >> shift, next_ways)
    for m in range(next_ways):
        for hi in range(heads // next_ways):
            piece = jnp.zeros((chunk, width), F32)
            for d in range(next_ways):
                at = (hi * next_ways + d) * chunk
                piece = jnp.where((digit ^ m) == d, total[at : at + chunk], piece)
            out_refs[m][hi * chunk : (hi + 1) * chunk] = piece
        at = heads // next_ways * chunk
        out_refs[m][at : at + NOTE] = note
        out_refs[m][at + NOTE :] = sums


def merge(parts, chunk, heads, entries, shift, next_ways):
    width = parts[0][0].shape[-1]
    sums_rows = sum(len(members) for _, _, _, members in parts) * entries
    if next_ways == 1:
        outs = tuple(
            jax.ShapeDtypeStruct((heads * chunk + NOTE + spare, width), F32) for spare in SPARE
        )
    else:
        rows = heads // next_ways * chunk + NOTE + sums_rows
        outs = (jax.ShapeDtypeStruct((rows, width), F32),) * next_ways
    outs = outs + (jax.ShapeDtypeStruct((sums_rows, width), F32),)
    out = pl.pallas_call(
        functools.partial(
            merge_kernel,
            plan=tuple((added, at, tuple(members)) for _, added, at, members in parts),
            chunk=chunk,
            heads=heads,
            entries=entries,
            shift=shift,
            next_ways=next_ways,
        ),
        out_shape=outs,
        in_specs=[VMEM] * len(parts),
        out_specs=(VMEM,) * len(outs),
        compiler_params=params(),
        name="merge",
    )(*(part for part, _, _, _ in parts))
    return out[:-1], out[-1]


def embed_kernel(sums_ref, *refs, entries):
    part_refs, out_ref = refs[:-1], refs[-1]
    owned, width = out_ref.shape
    own = (position()[3] * owned + lax.broadcasted_iota(jnp.int32, (owned, entries), 0)).astype(F32)
    sums, counts = jnp.zeros((owned, width), F32), jnp.zeros((owned, 1), F32)
    for m, ref, k in relative(part_refs):
        there = ref[k, owned : owned + 1, :entries] == own
        count = ref[k, owned + 1 : owned + 2, :entries]
        counts += jnp.sum(jnp.where(there, count, 0.0), axis=1, keepdims=True)
        sums += jnp.dot(
            there.astype(F32),
            sums_ref[m * entries : (m + 1) * entries],
            precision=lax.Precision.HIGHEST,
            preferred_element_type=F32,
        )
    out_ref[...] = sums / jnp.maximum(counts, 1.0)


def spread_kernel(*refs, chunk, rows, members):
    part_refs, weight_ref, bias_ref, place = refs[:-3], refs[-3], refs[-2], refs[-1]
    me = position()[3]
    count = len(members)
    for p, k in itertools.product(range(count), range(part_refs[0].shape[0])):
        bias, down, _ = read_note(part_refs[p][k], chunk)
        j = me ^ (members[p] + k * count)
        target = weight_ref if rows == place.shape[0] else place
        target[pl.ds(pl.multiple_of(j * chunk, 8), chunk)] = part_refs[p][k, :chunk] * down

        @pl.when(j == 0)
        def _():
            bias_ref[...] = bias

    if rows != place.shape[0]:
        weight_ref[...] = place[:rows]


def spread(parts, chunk, count, rows):
    parts = {m: part.astype(F32) for m, part in parts.items()}
    width = parts[0].shape[-1]
    return pl.pallas_call(
        functools.partial(spread_kernel, chunk=chunk, rows=rows, members=tuple(parts)),
        out_shape=(jax.ShapeDtypeStruct((rows, width), F32), jax.ShapeDtypeStruct((1, width), F32)),
        in_specs=[VMEM] * len(parts),
        out_specs=(VMEM, VMEM),
        scratch_shapes=[pltpu.VMEM((count * chunk, width), F32)],
        compiler_params=params(),
        name="spread",
    )(*parts.values())


def body(
    section_input, conv_weight, conv_bias, deep_weight, deep_bias, labels, slot_ids, embed_grad
):
    chan_count = lax.axis_size("chan")
    strip_count = lax.axis_size("strip")
    channels = section_input.shape[-1]
    entries = slot_ids.shape[0]
    owned, width = embed_grad.shape
    conv_w = conv_weight.reshape(9 * channels, -1)
    conv_b = conv_bias.reshape(1, -1)

    side = pack_side(embed_grad, slot_ids, labels)
    head, tail, border, near_rows, near_w = columns(section_input, conv_w)
    pairs = []
    for s in range(strip_count):
        for c in range(chan_count):
            to = s + 1 - 2 * (c & 1)
            if 0 <= to < strip_count:
                pairs.append((s * chan_count + c, to * chan_count + c))
    got = lax.ppermute(border, ("strip", "chan"), pairs)

    steps = [(at + 1, 1) for at in range(min(2, strip_count.bit_length() - 2))]
    steps += [(at, min(3, strip_count.bit_length() - 1 - at)) for at in range(3, strip_count.bit_length() - 1, 3)]
    ahead = gather_step(side, "strip", steps[0])
    shared = join(ahead, [border])
    taps = windows(near_rows, section_input.shape[0], [shared])
    ahead = gather_step(shared, "strip", steps[1])
    pooled = conv_pool(taps, near_w, conv_b, section_input.shape[0] // 4, [shared])
    pooled, got, shared = lax.optimization_barrier((pooled, got, join(ahead, [pooled])))
    other = swap(pooled, "chan", 1)
    traded = swap(got, "chan", 1)
    for step in steps[2:]:
        shared = join(gather_step(shared, "strip", step), [])
    shared = [shared, swap(shared, "strip", 1)]
    edges = conv_edges(near_w, conv_b, got, traded, head, tail, [pooled])

    chunk = -(-9 * channels // strip_count // 8) * 8
    bits = strip_count.bit_length() - 1
    ways = 8
    forward = deep_forward(
                pooled,
        other,
        edges,
        deep_weight.reshape(9 * channels, width),
        deep_bias.reshape(1, width),
        labels,
        entries,
    )
    heads = strip_count // ways
    size = heads * chunk

    def sent(part, mask):
        return swap(part.astype(F16), "strip", mask).astype(F32)

    kept, beside, near, near_pair, paired, pair, far = deep_backward(
        forward, shared, chunk, strip_count
    )
    got_far, got_pair, got_near = sent(far, 6), sent(pair, 1), sent(near_pair, 1)
    both = [(pair, size), (got_pair, size)]
    onward = merge_pair(paired, got_pair, both, size, entries, 0, size, [], spare=8)
    near = merge_pair(near, got_near, both, size, entries, 0, size, [onward])
    last = [(got_far, 2 * size)]
    beside = merge_pair(beside, got_far, last, size, entries, size, 2 * size, [near])
    parts = [
        (kept, True, size, []),
        (sent(beside, 1), True, size, [7]),
        (sent(near, 2), True, size, [2, 3]),
        (sent(onward, 4), True, size, [4, 5]),
        (got_far, True, 2 * size, [6]),
        (pair, False, size, [0]),
        (got_pair, False, size, [1]),
    ]
    held, shift = ways, 3
    while True:
        step = min(3, bits - shift)
        send, sums = merge(parts, chunk, heads, entries, shift, 1 << step)
        if step == 0:
            break
        more = 1 << step
        heads //= more
        arrived = [send[0]] + [sent(send[m], m << shift) for m in range(1, more)]
        parts = [
            (part, True, heads * chunk, list(range(m * held, (m + 1) * held)))
            for m, part in enumerate(arrived)
        ]
        held *= more
        shift += step
    embeddings = pl.pallas_call(
        functools.partial(embed_kernel, entries=entries),
        out_shape=jax.ShapeDtypeStruct((owned, width), F32),
        in_specs=[VMEM] * (1 + len(shared)),
        out_specs=VMEM,
        compiler_params=params(),
        name="embed",
    )(sums, *shared)
    own, middle, long = (part.astype(F16)[None] for part in send)
    for at in range(3, bits, 3):
        own = jnp.concatenate(gather_step(own, "strip", (at, min(3, bits - at))), axis=0)
        middle = long = own
    gathered = {0: own, 1: swap(middle, "strip", 1), 2: swap(own, "strip", 2)}
    gathered[3] = swap(middle, "strip", 3)
    gathered[4], gathered[6] = swap(long, "strip", 4), swap(own, "strip", 6)
    late = {m + 1: swap(gathered[m], "strip", 1) for m in (4, 6)}
    weight_rows, bias_row = spread(
        {**gathered, **late}, chunk, strip_count, 9 * channels
    )
    return (embeddings, weight_rows.reshape(3, 3, channels, width), bias_row[0])


def solution(mesh):
    placed = (
        P(None, "strip", None),
        P(),
        P(),
        P(None, None, None, "chan"),
        P("chan"),
        P(None, "strip"),
        P("strip"),
        P("strip", "chan"),
    )
    return jax.shard_map(
        body,
        mesh=mesh,
        in_specs=placed,
        out_specs=(P("strip", "chan"), P(None, None, None, "chan"), P("chan")),
        check_vma=False,
    )
```

```python
import functools
import itertools
import math

import jax
import jax.numpy as jnp
from jax import lax
from jax.experimental import pallas as pl
from jax.experimental.pallas import tpu as pltpu
from jax.sharding import PartitionSpec as P

F32, BF16, F16 = jnp.float32, jnp.bfloat16, jnp.float16
VMEM = pl.BlockSpec(memory_space=pltpu.VMEM)
HBM = pl.BlockSpec(memory_space=pltpu.HBM)
ANY = pl.BlockSpec(memory_space=pl.ANY)
SIDE = 8
WIDTH = 3
PIECE = 4
STEP = 6
PAYLOADS = (((0,), 0), ((1,), 0), ((2,), 0), ((3,), 0), ((4,), 0), ((5,), 1), ((6, 7), 1))
SPARE = (0, 16, 0)
NOTE = 8


def params(mib=8):
    return pltpu.CompilerParams(vmem_limit_bytes=mib << 20)


def position():
    strip = lax.axis_index("strip")
    last = lax.axis_size("strip") - 1
    return (
        lax.axis_index("chan") & 1,
        (strip == 0).astype(jnp.int32),
        (strip == last).astype(jnp.int32),
        strip,
    )


def swap(value, axis, mask):
    count = lax.axis_size(axis)
    return lax.ppermute(value, axis, [(i, i ^ mask) for i in range(count)])


def gather_step(held, axis, step):
    shift, size = step
    return [held] + [swap(held, axis, m << shift) for m in range(1, 1 << size)]


def relative(refs):
    half = len(refs) // 2
    for low in range(2):
        m = low
        for ref in refs[low * half : (low + 1) * half]:
            for k in range(ref.shape[0]):
                yield m, ref, k
                m += 2


def sigmoid(v):
    return jax.nn.sigmoid(v)


def shares(pooled_rows):
    first = pooled_rows // 2
    return first, pooled_rows - first


def pick(half, pair):
    return jnp.where(half == 0, pair[0], pair[1])


def share_rows(half, rows):
    first, second = shares(rows // 2)
    most = -(-(2 * max(first, second) + 1) // PIECE) * PIECE
    return most, pick(half, (0, rows - most)), pick(half, (-1, 2 * first - 1 - (rows - most)))


def window_kernel(rows_ref, *refs, rows):
    taps, wide = refs[-2:]
    most, cols, chans = rows_ref.shape
    half_cols = cols // 2
    half = position()[0]
    _, _, before = share_rows(half, rows)
    shift = PIECE - before
    lanes = chans // 128
    border = jnp.zeros((8, 128), F32)
    for t in range(wide.shape[0]):
        wide[t, 0:8] = border
        wide[t, cols + 8 : cols + 16] = border

    def prepare(k, carry):
        for slot in range(PIECE):
            r = k * PIECE + slot
            x = rows_ref[r].astype(F32)
            for t in range(lanes):
                wide[slot * lanes + t, 8 : 8 + cols] = x[:, t * 128 : (t + 1) * 128]
            for tap in range(4):
                for t in range(lanes):
                    part = wide[slot * lanes + t, pl.ds(7 + tap, half_cols, stride=2), :]
                    at = (tap * lanes + t) * 128
                    taps[r + shift, :, at : at + 128] = part.astype(BF16)
        return carry

    lax.fori_loop(0, most // PIECE, prepare, 0)
    second = shares(rows // 2)[1]
    outside = pick(half, (PIECE, PIECE + 2 * second + 1))
    taps[outside] = jnp.zeros(taps.shape[1:], BF16)


def windows(near_rows, rows, after):
    most, cols, chans = near_rows.shape
    return pl.pallas_call(
        functools.partial(window_kernel, rows=rows),
        out_shape=jax.ShapeDtypeStruct((most + 2 * PIECE, cols // 2, 4 * chans), BF16),
        in_specs=[VMEM] + [ANY] * len(after),
        out_specs=VMEM,
        scratch_shapes=[pltpu.VMEM((PIECE * (chans // 128), cols + 16, 128), F32)],
        compiler_params=params(16),
        cost_estimate=pl.CostEstimate(flops=0, bytes_accessed=12 << 20, transcendentals=0),
        name="windows",
    )(near_rows, *after)


def edge_part(pairs, w_ref, bias, edge_ref, acc):
    rows = pairs[0].shape[0]
    chans = w_ref.shape[1]
    lanes = chans // 128
    depth = 3 * chans
    lhs = jnp.concatenate(
        [
            pairs[s][:, (2 * j + phase) * chans : (2 * j + phase + 3) * chans]
            for s in range(2)
            for j in range(2)
            for phase in range(2)
        ],
        axis=0,
    )
    pad = rows + 16
    for dr in range(3):
        part = jnp.dot(lhs, w_ref[dr * depth : (dr + 1) * depth], preferred_element_type=F32)
        for g in range(8):
            own = part[g * rows : (g + 1) * rows]
            for t in range(lanes):
                at = 9 - dr
                piece = own[:, t * 128 : (t + 1) * 128]
                if dr == 0:
                    acc[g * lanes + t, 0:8] = jnp.zeros((8, 128), F32)
                    acc[g * lanes + t, 8 + rows : pad] = jnp.zeros((8, 128), F32)
                    acc[g * lanes + t, 8:9] = jnp.zeros((1, 128), F32)
                    acc[g * lanes + t, at : at + rows] = piece
                else:
                    acc[g * lanes + t, at : at + rows] += piece
    for g in range(4):
        for t in range(lanes):
            total = None
            for phase in range(2):
                at = (2 * g + phase) * lanes + t
                v = acc[at, 8 : 8 + rows] + bias[:, t * 128 : (t + 1) * 128]
                acc[at, 8 : 8 + rows] = v * sigmoid(v)
                both = (
                    acc[at, pl.ds(8, rows // 2, stride=2), :]
                    + acc[at, pl.ds(9, rows // 2, stride=2), :]
                )
                total = both if total is None else total + both
            lost = jnp.where(g == 0, position()[1], jnp.where(g == 3, position()[2], 0))
            keep = jnp.where(lost > 0, 0.0, 0.25)
            edge_ref[g, t] = (total * keep).astype(BF16).astype(F32)


def conv_kernel(taps, w_ref, b_ref, *refs):
    out_ref = refs[-1]
    assert out_ref.shape[0] % STEP == 0
    half_cols, chans = taps.shape[1], taps.shape[2] // 4
    bias = b_ref[...]

    def step(k, carry):
        r0 = PIECE + k * 2 * STEP
        total = None
        for phase in range(2):
            lhs = jnp.concatenate(
                [
                    taps[pl.ds(r0 + dr, 2 * STEP), :, phase * chans : (phase + 3) * chans]
                    for dr in range(3)
                ],
                axis=-1,
            ).reshape(2 * STEP * half_cols, 9 * chans)
            v = jnp.dot(lhs, w_ref[...], preferred_element_type=F32) + bias
            h = (v * sigmoid(v)).reshape(STEP, 2, half_cols, chans)
            h = h[:, 0] + h[:, 1]
            total = h if total is None else total + h
        out_ref[pl.ds(k * STEP, STEP)] = (total * 0.25).astype(BF16)
        return carry

    for k in range(out_ref.shape[0] // STEP):
        step(k, 0)


def conv_pool(taps, w, b, pooled_rows, after):
    _, half_cols, width = taps.shape
    chans = width // 4
    return pl.pallas_call(
        conv_kernel,
        out_shape=jax.ShapeDtypeStruct((pooled_rows, half_cols, chans), BF16),
        in_specs=[VMEM] * 3 + [ANY] * len(after),
        out_specs=VMEM,
        compiler_params=params(16),
        cost_estimate=pl.CostEstimate(
            flops=8 * pooled_rows * half_cols * 9 * chans * chans,
            bytes_accessed=8 << 20,
            transcendentals=0,
        ),
        name="conv_pool",
    )(taps, w, b, *after)


def edge_kernel(w_ref, b_ref, got_ref, traded_ref, head_ref, tail_ref, *refs):
    edge_ref, acc = refs[-2:]
    half = position()[0]
    got, traded = got_ref[...], traded_ref[...]
    left = jnp.concatenate([jnp.where(half == 0, got, traded), head_ref[...]], axis=-1)
    right = jnp.concatenate([tail_ref[...], jnp.where(half == 0, traded, got)], axis=-1)
    edge_part((left, right), w_ref, b_ref[...], edge_ref, acc)


def conv_edges(w, b, got, traded, head, tail, after):
    rows, lanes = head.shape[0], w.shape[1] // 128
    return pl.pallas_call(
        edge_kernel,
        out_shape=jax.ShapeDtypeStruct((4, lanes, rows // 2, 128), F32),
        in_specs=[VMEM] * 6 + [ANY] * len(after),
        out_specs=VMEM,
        scratch_shapes=[pltpu.VMEM((8 * lanes, rows + 16, 128), F32)],
        compiler_params=params(),
        cost_estimate=pl.CostEstimate(flops=0, bytes_accessed=4 << 20, transcendentals=0),
        name="conv_edges",
    )(w, b, got, traded, head, tail, *after)


def side_kernel(grad_hbm, labels_hbm, slots_hbm, side_ref, labels_ref, slots_ref, sems):
    owned, width = grad_hbm.shape
    entries = slots_ref.shape[1]
    copies = [
        pltpu.make_async_copy(labels_hbm, labels_ref, sems.at[0]),
        pltpu.make_async_copy(slots_hbm, slots_ref, sems.at[1]),
        pltpu.make_async_copy(grad_hbm, side_ref.at[0, pl.ds(0, owned)], sems.at[2]),
    ]
    for copy in copies:
        copy.start()
    lane = lax.broadcasted_iota(jnp.int32, (1, width), 1)
    copies[0].wait()
    labels = labels_ref[...]
    counts = jnp.zeros((1, width), F32)
    for e in range(entries):
        hit = jnp.where(labels == e, 1.0, 0.0)
        hit = jnp.sum(jnp.sum(hit, axis=0, keepdims=True), axis=1, keepdims=True)
        counts = jnp.where(lane == e, hit, counts)
    copies[1].wait()
    ids = jnp.concatenate(
        [slots_ref[...].astype(F32), jnp.zeros((1, width - entries), F32)], axis=1
    )
    row = lax.broadcasted_iota(jnp.int32, (SIDE, width), 0)
    side_ref[0, owned:] = jnp.where(row == 0, ids, jnp.where(row == 1, counts, 0.0))
    copies[2].wait()


def pack_side(grad, slots, labels):
    owned, width = grad.shape
    fixed = [
        pltpu.with_memory_space_constraint(a, pltpu.HBM)
        for a in (grad, labels, slots.reshape(1, -1))
    ]
    return pl.pallas_call(
        side_kernel,
        out_shape=jax.ShapeDtypeStruct((1, owned + SIDE, width), F32),
        in_specs=[HBM] * 3,
        out_specs=VMEM,
        scratch_shapes=[
            pltpu.VMEM(labels.shape, jnp.int32),
            pltpu.VMEM((1, slots.shape[0]), jnp.int32),
            pltpu.SemaphoreType.DMA((3,)),
        ],
        compiler_params=params(),
        name="pack_side",
    )(*fixed)


def columns_kernel(x_hbm, w_hbm, head_ref, tail_ref, send_ref, near_ref, w_ref, left, right, wide, sems):
    rows, cols, chans = x_hbm.shape
    reach = left.shape[1]
    half = position()[0]
    most, first, _ = share_rows(half, rows)
    size = most // 4
    copies = [
        pltpu.make_async_copy(x_hbm.at[:, pl.ds(0, reach)], left, sems.at[0]),
        pltpu.make_async_copy(x_hbm.at[:, pl.ds(cols - reach, reach)], right, sems.at[1]),
    ]
    for k in range(4):
        source = x_hbm.at[pl.ds(first + k * size, size)]
        copies.append(
            pltpu.make_async_copy(source, near_ref.at[pl.ds(k * size, size)], sems.at[2 + k])
        )
    copies.append(pltpu.make_async_copy(w_hbm, w_ref, sems.at[6]))
    for copy in copies:
        copy.start()
    lanes = chans // 128
    sides = ((left, head_ref, 0), (right, tail_ref, reach - WIDTH))
    for copy, (ref, out_ref, at) in zip(copies, sides):
        copy.wait()
        x = ref[...].astype(F32).reshape(rows * reach, chans)
        for t in range(lanes):
            wide[t, : rows * reach] = x[:, t * 128 : (t + 1) * 128]
        for c in range(WIDTH):
            for t in range(lanes):
                part = wide[t, pl.ds(at + c, rows, stride=reach), :].astype(BF16)
                place = (c * lanes + t) * 128
                out_ref[:, place : place + 128] = part
    send_ref[...] = jnp.where(half == 0, tail_ref[...], head_ref[...])
    for copy in copies[2:]:
        copy.wait()


def columns(x, w):
    rows, cols, chans = x.shape
    reach = 16
    most = share_rows(0, rows)[0]
    border = jax.ShapeDtypeStruct((rows, WIDTH * chans), BF16)
    return pl.pallas_call(
        columns_kernel,
        out_shape=(border,) * 3
        + (jax.ShapeDtypeStruct((most, cols, chans), BF16), jax.ShapeDtypeStruct(w.shape, BF16)),
        in_specs=[HBM] * 2,
        out_specs=(VMEM,) * 5,
        scratch_shapes=[
            pltpu.VMEM((rows, reach, chans), BF16),
            pltpu.VMEM((rows, reach, chans), BF16),
            pltpu.VMEM((chans // 128, (rows + 1) * reach, 128), F32),
            pltpu.SemaphoreType.DMA((7,)),
        ],
        compiler_params=params(16),
        name="columns",
    )(*(pltpu.with_memory_space_constraint(a, pltpu.HBM) for a in (x, w)))


def join_kernel(*refs, count):
    at = 0
    for ref in refs[:count]:
        refs[-1][at : at + ref.shape[0]] = ref[...]
        at += ref.shape[0]


def join(parts, after):
    shape = (sum(p.shape[0] for p in parts),) + parts[0].shape[1:]
    return pl.pallas_call(
        functools.partial(join_kernel, count=len(parts)),
        out_shape=jax.ShapeDtypeStruct(shape, F32),
        in_specs=[VMEM] * len(parts) + [ANY] * len(after),
        out_specs=VMEM,
        compiler_params=params(),
        name="join",
    )(*parts, *after)


def scale_rows(block, note_rows, sums):
    def exponent(values):
        top = None
        for v in values:
            one = jnp.max(jnp.max(jnp.abs(v), axis=0, keepdims=True), axis=1, keepdims=True)
            top = one if top is None else jnp.maximum(top, one)
        return jnp.ceil(jnp.log2(jnp.maximum(top, 1e-30)))

    power = exponent([block, note_rows])
    power_sums = exponent([sums])
    return power, power_sums


def note_block(bias, power, power_sums, width):
    row = lax.broadcasted_iota(jnp.int32, (NOTE, width), 0)
    bias = jnp.broadcast_to(bias, (NOTE, width))
    power = jnp.broadcast_to(power, (NOTE, width))
    power_sums = jnp.broadcast_to(power_sums, (NOTE, width))
    return jnp.where(row == 0, bias, jnp.where(row == 1, power, power_sums))


def read_note(part, at):
    note = part[at : at + NOTE]
    down = jnp.exp2(note[1:2] - 12.0)
    return note[0:1] * down, down, jnp.exp2(note[2:3] - 12.0)


def deep_kernel(
    own_ref, other_ref, edge_ref, w_ref, b_ref, lab_ref, taps, member, slope, sums_ref, wide,
    inside, *, block, entries
):
    _, cols, chans = own_ref.shape
    rows = lab_ref.shape[0]
    lanes = chans // 128
    width = w_ref.shape[-1]
    half = position()[0]
    taps[0] = jnp.zeros(taps.shape[1:], BF16)
    taps[rows + 1] = jnp.zeros(taps.shape[1:], BF16)

    def prepare(ref, base, i, slot):
        x = ref[i].astype(F32)
        r = base + i
        for t in range(lanes):
            s = slot * lanes + t
            at = t * 128
            wide[s, 8 : 8 + cols] = x[:, at : at + 128]
            for g, place in enumerate((7, 8, 7 + cols, 8 + cols)):
                wide[s, place : place + 1] = edge_ref[g, t, pl.ds(r, 1), :]
        for tap in range(3):
            for t in range(lanes):
                piece = wide[slot * lanes + t, 7 + tap : 7 + tap + cols, :]
                at = (tap * lanes + t) * 128
                taps[r + 1, :, at : at + 128] = piece.astype(BF16)

    first, second = shares(rows)
    times = math.gcd(first, second)

    def prepare_all(even_ref, odd_ref):
        def prepare_rows(k, carry):
            for q in range(rows // times):
                ref, base = (even_ref, 0) if q < first // times else (odd_ref, first)
                prepare(ref, base, q * times - base + k, q)
            return carry

        lax.fori_loop(0, times, prepare_rows, 0)

    @pl.when(half == 0)
    def _():
        prepare_all(own_ref, other_ref)

    @pl.when(half != 0)
    def _():
        prepare_all(other_ref, own_ref)

    lab = jnp.transpose(lab_ref[...].astype(F32))
    lane = lax.broadcasted_iota(jnp.int32, (cols, 128), 1)
    want = jnp.where(lane < 3 * entries, lane % entries, -1).astype(F32)
    for r in range(rows):
        member[r] = (lab[:, r : r + 1] == want).astype(BF16)
    bias = b_ref[...]
    size = block * cols

    flat = jnp.concatenate([lab_ref[r : r + 1, :] for r in range(rows)], axis=1)
    entry = lax.broadcasted_iota(jnp.int32, (entries, rows * cols), 0)
    inside[...] = jnp.where(jnp.broadcast_to(flat, entry.shape) == entry, 1.0, 0.0).astype(BF16)

    def step(k, sums):
        r0 = k * block
        lhs = jnp.concatenate([taps[pl.ds(r0 + dr, block)] for dr in range(3)], axis=-1)
        v = jnp.dot(lhs.reshape(size, 9 * chans), w_ref[...], preferred_element_type=F32) + bias
        sig = sigmoid(v)
        features = (v * sig).astype(BF16)
        slope[pl.ds(k * size, size)] = sig * (1.0 + v * (1.0 - sig))
        mine = inside[:, pl.ds(pl.multiple_of(k * size, 128), size)]
        return sums + jnp.dot(mine, features, preferred_element_type=F32)

    sums_ref[...] = lax.fori_loop(0, rows // block, step, jnp.zeros((entries, width), F32))


def deep_forward(own, other, edges, w, b, labels, entries):
    _, cols, chans = own.shape
    rows, width = labels.shape[0], w.shape[-1]
    block = next(k for k in (8, 4, 2, 1) if rows % k == 0)
    first, second = shares(rows)
    slots = rows // math.gcd(first, second)
    return pl.pallas_call(
        functools.partial(deep_kernel, block=block, entries=entries),
        out_shape=(
            jax.ShapeDtypeStruct((rows + 2, cols, 3 * chans), BF16),
            jax.ShapeDtypeStruct((rows, cols, 128), BF16),
            jax.ShapeDtypeStruct((rows * cols, width), F32),
            jax.ShapeDtypeStruct((entries, width), F32),
        ),
        in_specs=[VMEM] * 6,
        out_specs=(VMEM,) * 4,
        scratch_shapes=[
            pltpu.VMEM((slots * (chans // 128), cols + 16, 128), F32),
            pltpu.VMEM((entries, rows * cols), BF16),
        ],
        compiler_params=params(16),
        cost_estimate=pl.CostEstimate(
            flops=4 * rows * cols * 9 * chans * width, bytes_accessed=8 << 20, transcendentals=0
        ),
        name="deep_forward",
    )(own, other, edges, w, b, labels)


def grad_kernel(
    taps, member, slope, sums_ref, *refs, n_parts, chunk
):
    part_refs = refs[:n_parts]
    out_refs, weight = refs[n_parts:-1], refs[-1]
    rows, cols, depth = member.shape[0], taps.shape[1], taps.shape[2]
    width = slope.shape[-1]
    me = position()[3]
    entries = sums_ref.shape[0]
    owned = part_refs[0].shape[1] - SIDE
    own_ids = jnp.broadcast_to(part_refs[0][0, owned : owned + 1, :entries], (entries, entries))
    across = lax.broadcasted_iota(jnp.int32, (entries, entries), 1)
    down = lax.broadcasted_iota(jnp.int32, (entries, entries), 0)
    ids = jnp.sum(jnp.where(across == down, own_ids, 0.0), axis=1, keepdims=True).astype(jnp.int32)
    total = jnp.zeros((entries, 1), F32)
    entry_grad = jnp.zeros((entries, width), F32)
    owner, inner = ids // owned, ids % owned
    spot = lax.broadcasted_iota(jnp.int32, (entries, owned), 1)
    for m, ref, k in relative(part_refs):
        there = ref[k, owned : owned + 1, :entries] == ids.astype(F32)
        counts = ref[k, owned + 1 : owned + 2, :entries]
        total += jnp.sum(jnp.where(there, counts, 0.0), axis=1, keepdims=True)
        hot = ((owner ^ me) == m) & (inner == spot)
        entry_grad += jnp.dot(
            hot.astype(F32), ref[k, :owned], precision=lax.Precision.HIGHEST, preferred_element_type=F32
        )
    entry_grad = entry_grad / jnp.maximum(total, 1.0)
    high = entry_grad.astype(BF16)
    rest = entry_grad - high.astype(F32)
    mid = rest.astype(BF16)
    low = (rest - mid.astype(F32)).astype(BF16)
    terms = jnp.concatenate([high, mid, low, jnp.zeros((128 - 3 * entries, width), BF16)], axis=0)
    pixel = jnp.dot(member[...].reshape(rows * cols, 128), terms, preferred_element_type=F32)
    dg = (pixel * slope[...]).astype(BF16)
    turned = jnp.transpose(dg)
    bias_sum = jnp.sum(dg.astype(F32), axis=0, keepdims=True)
    for dr in range(3):
        window = taps[dr : dr + rows].reshape(rows * cols, depth)
        out = jnp.dot(turned, window, preferred_element_type=F32)
        weight[dr * depth : (dr + 1) * depth] = jnp.transpose(out)
    if weight.shape[0] > 3 * depth:
        weight[3 * depth :] = jnp.zeros((weight.shape[0] - 3 * depth, width), F32)
    sums = sums_ref[...]
    power, power_sums = scale_rows(weight[...], bias_sum, sums)
    up = jnp.exp2(12.0 - power)
    note = note_block(bias_sum * up, power, power_sums, width)
    ways = 8
    digit = lax.rem(me, ways)
    heads = weight.shape[0] // chunk // ways
    sums = sums * jnp.exp2(12.0 - power_sums)
    for out_ref, (members, with_sums) in zip(out_refs, PAYLOADS):
        at = 0
        for m, hi in itertools.product(members, range(heads)):
            j = hi * ways + (digit ^ m)
            out_ref[at : at + chunk] = weight[pl.ds(pl.multiple_of(j * chunk, 8), chunk)] * up
            at += chunk
        out_ref[at : at + NOTE] = note
        if with_sums:
            out_ref[at + NOTE :] = sums


def deep_backward(forward, parts, chunk, count):
    taps, _, slope, sums = forward
    width, entries = slope.shape[-1], sums.shape[0]
    size = count // 8 * chunk
    return pl.pallas_call(
        functools.partial(grad_kernel, n_parts=len(parts), chunk=chunk),
        out_shape=tuple(
            jax.ShapeDtypeStruct((len(members) * size + NOTE + with_sums * entries, width), F32)
            for members, with_sums in PAYLOADS
        ),
        in_specs=[VMEM] * (4 + len(parts)),
        out_specs=(VMEM,) * len(PAYLOADS),
        scratch_shapes=[pltpu.VMEM((count * chunk, width), F32)],
        compiler_params=params(16),
        cost_estimate=pl.CostEstimate(
            flops=4 * slope.shape[0] * 3 * taps.shape[2] * width, bytes_accessed=8 << 20, transcendentals=0
        ),
        name="deep_backward",
    )(*forward, *parts)


def pair_kernel(own_ref, got_ref, *refs, size, entries, got_at, got_note, sums_notes):
    out_ref = refs[-1]
    own, got = own_ref[size : size + NOTE], got_ref[got_note : got_note + NOTE]
    power = jnp.maximum(own[1:2], got[1:2]) + 1.0
    own_down, got_down = jnp.exp2(own[1:2] - power), jnp.exp2(got[1:2] - power)
    out_ref[:size] = own_ref[:size] * own_down + got_ref[got_at : got_at + size] * got_down
    bias = own[0:1] * own_down + got[0:1] * got_down
    powers = [ref[at + 2 : at + 3] for ref, at in zip(refs, sums_notes)]
    power_sums = functools.reduce(jnp.maximum, powers)
    out_ref[size : size + NOTE] = note_block(bias, power, power_sums, own.shape[-1])
    place = size + NOTE
    for ref, at, one in zip(refs, sums_notes, powers):
        sums = ref[at + NOTE : at + NOTE + entries] * jnp.exp2(one - power_sums)
        out_ref[place : place + entries] = sums
        place += entries
    if place < out_ref.shape[0]:
        out_ref[place:] = jnp.zeros((out_ref.shape[0] - place, own.shape[-1]), F32)


def merge_pair(own, got, sums, size, entries, got_at, got_note, after, spare=0):
    width = own.shape[-1]
    return pl.pallas_call(
        functools.partial(
            pair_kernel,
            size=size,
            entries=entries,
            got_at=got_at,
            got_note=got_note,
            sums_notes=tuple(at for _, at in sums),
        ),
        out_shape=jax.ShapeDtypeStruct((size + NOTE + len(sums) * entries + spare, width), F32),
        in_specs=[VMEM] * (2 + len(sums)) + [ANY] * len(after),
        out_specs=VMEM,
        compiler_params=params(),
        name="merge_pair",
    )(own, got, *(part for part, _ in sums), *after)


def merge_kernel(*refs, plan, chunk, heads, entries, shift, next_ways):
    n_parts = len(plan)
    part_refs, out_refs, sums_ref = refs[:n_parts], refs[n_parts:-1], refs[-1]
    width = part_refs[0].shape[-1]
    size = heads * chunk
    total, bias = jnp.zeros((size, width), F32), jnp.zeros((1, width), F32)
    for ref, (added, note_at, members) in zip(part_refs, plan):
        more, down, down_sums = read_note(ref, note_at)
        if added:
            total, bias = total + ref[:size] * down, bias + more
        for k, m in enumerate(members):
            at = note_at + NOTE + k * entries
            sums_ref[m * entries : (m + 1) * entries] = ref[at : at + entries] * down_sums
    sums = sums_ref[...]
    power, power_sums = scale_rows(total, bias, sums)
    up = jnp.exp2(12.0 - power)
    note = note_block(bias * up, power, power_sums, width)
    total = total * up
    if next_ways == 1:
        for out_ref, spare in zip(out_refs, SPARE):
            out_ref[:size] = total
            out_ref[size : size + NOTE] = note
            if spare:
                out_ref[size + NOTE :] = jnp.zeros((spare, width), F32)
        return
    sums = sums * jnp.exp2(12.0 - power_sums)
    digit = lax.rem(position()[3] >> shift, next_ways)
    for m in range(next_ways):
        for hi in range(heads // next_ways):
            piece = jnp.zeros((chunk, width), F32)
            for d in range(next_ways):
                at = (hi * next_ways + d) * chunk
                piece = jnp.where((digit ^ m) == d, total[at : at + chunk], piece)
            out_refs[m][hi * chunk : (hi + 1) * chunk] = piece
        at = heads // next_ways * chunk
        out_refs[m][at : at + NOTE] = note
        out_refs[m][at + NOTE :] = sums


def merge(parts, chunk, heads, entries, shift, next_ways):
    width = parts[0][0].shape[-1]
    sums_rows = sum(len(members) for _, _, _, members in parts) * entries
    if next_ways == 1:
        outs = tuple(
            jax.ShapeDtypeStruct((heads * chunk + NOTE + spare, width), F32) for spare in SPARE
        )
    else:
        rows = heads // next_ways * chunk + NOTE + sums_rows
        outs = (jax.ShapeDtypeStruct((rows, width), F32),) * next_ways
    outs = outs + (jax.ShapeDtypeStruct((sums_rows, width), F32),)
    out = pl.pallas_call(
        functools.partial(
            merge_kernel,
            plan=tuple((added, at, tuple(members)) for _, added, at, members in parts),
            chunk=chunk,
            heads=heads,
            entries=entries,
            shift=shift,
            next_ways=next_ways,
        ),
        out_shape=outs,
        in_specs=[VMEM] * len(parts),
        out_specs=(VMEM,) * len(outs),
        compiler_params=params(),
        name="merge",
    )(*(part for part, _, _, _ in parts))
    return out[:-1], out[-1]


def embed_kernel(sums_ref, *refs, entries):
    part_refs, out_ref = refs[:-1], refs[-1]
    owned, width = out_ref.shape
    own = (position()[3] * owned + lax.broadcasted_iota(jnp.int32, (owned, entries), 0)).astype(F32)
    sums, counts = jnp.zeros((owned, width), F32), jnp.zeros((owned, 1), F32)
    for m, ref, k in relative(part_refs):
        there = ref[k, owned : owned + 1, :entries] == own
        count = ref[k, owned + 1 : owned + 2, :entries]
        counts += jnp.sum(jnp.where(there, count, 0.0), axis=1, keepdims=True)
        sums += jnp.dot(
            there.astype(F32),
            sums_ref[m * entries : (m + 1) * entries],
            precision=lax.Precision.HIGHEST,
            preferred_element_type=F32,
        )
    out_ref[...] = sums / jnp.maximum(counts, 1.0)


def spread_kernel(*refs, chunk, rows, members):
    part_refs, weight_ref, bias_ref, place = refs[:-3], refs[-3], refs[-2], refs[-1]
    me = position()[3]
    count = len(members)
    for p, k in itertools.product(range(count), range(part_refs[0].shape[0])):
        bias, down, _ = read_note(part_refs[p][k], chunk)
        j = me ^ (members[p] + k * count)
        target = weight_ref if rows == place.shape[0] else place
        target[pl.ds(pl.multiple_of(j * chunk, 8), chunk)] = part_refs[p][k, :chunk] * down

        @pl.when(j == 0)
        def _():
            bias_ref[...] = bias

    if rows != place.shape[0]:
        weight_ref[...] = place[:rows]


def spread(parts, chunk, count, rows):
    parts = {m: part.astype(F32) for m, part in parts.items()}
    width = parts[0].shape[-1]
    return pl.pallas_call(
        functools.partial(spread_kernel, chunk=chunk, rows=rows, members=tuple(parts)),
        out_shape=(jax.ShapeDtypeStruct((rows, width), F32), jax.ShapeDtypeStruct((1, width), F32)),
        in_specs=[VMEM] * len(parts),
        out_specs=(VMEM, VMEM),
        scratch_shapes=[pltpu.VMEM((count * chunk, width), F32)],
        compiler_params=params(),
        name="spread",
    )(*parts.values())


def body(
    section_input, conv_weight, conv_bias, deep_weight, deep_bias, labels, slot_ids, embed_grad
):
    chan_count = lax.axis_size("chan")
    strip_count = lax.axis_size("strip")
    channels = section_input.shape[-1]
    entries = slot_ids.shape[0]
    owned, width = embed_grad.shape
    conv_w = conv_weight.reshape(9 * channels, -1)
    conv_b = conv_bias.reshape(1, -1)

    side = pack_side(embed_grad, slot_ids, labels)
    head, tail, border, near_rows, near_w = columns(section_input, conv_w)
    pairs = []
    for s in range(strip_count):
        for c in range(chan_count):
            to = s + 1 - 2 * (c & 1)
            if 0 <= to < strip_count:
                pairs.append((s * chan_count + c, to * chan_count + c))
    got = lax.ppermute(border, ("strip", "chan"), pairs)

    steps = [(at + 1, 1) for at in range(min(2, strip_count.bit_length() - 2))]
    steps += [(at, min(3, strip_count.bit_length() - 1 - at)) for at in range(3, strip_count.bit_length() - 1, 3)]
    ahead = gather_step(side, "strip", steps[0])
    shared = join(ahead, [border])
    taps = windows(near_rows, section_input.shape[0], [shared])
    ahead = gather_step(shared, "strip", steps[1])
    pooled = conv_pool(taps, near_w, conv_b, section_input.shape[0] // 4, [shared])
    pooled, got, shared = lax.optimization_barrier((pooled, got, join(ahead, [pooled])))
    other = swap(pooled, "chan", 1)
    traded = swap(got, "chan", 1)
    for step in steps[2:]:
        shared = join(gather_step(shared, "strip", step), [])
    shared = [shared, swap(shared, "strip", 1)]
    edges = conv_edges(near_w, conv_b, got, traded, head, tail, [pooled])

    chunk = -(-9 * channels // strip_count // 8) * 8
    bits = strip_count.bit_length() - 1
    ways = 8
    forward = deep_forward(
                pooled,
        other,
        edges,
        deep_weight.reshape(9 * channels, width),
        deep_bias.reshape(1, width),
        labels,
        entries,
    )
    heads = strip_count // ways
    size = heads * chunk

    def sent(part, mask):
        return swap(part.astype(F16), "strip", mask).astype(F32)

    kept, beside, near, near_pair, paired, pair, far = deep_backward(
        forward, shared, chunk, strip_count
    )
    got_far, got_pair, got_near = sent(far, 6), sent(pair, 1), sent(near_pair, 1)
    both = [(pair, size), (got_pair, size)]
    onward = merge_pair(paired, got_pair, both, size, entries, 0, size, [], spare=8)
    near = merge_pair(near, got_near, both, size, entries, 0, size, [onward])
    last = [(got_far, 2 * size)]
    beside = merge_pair(beside, got_far, last, size, entries, size, 2 * size, [near])
    parts = [
        (kept, True, size, []),
        (sent(beside, 1), True, size, [7]),
        (sent(near, 2), True, size, [2, 3]),
        (sent(onward, 4), True, size, [4, 5]),
        (got_far, True, 2 * size, [6]),
        (pair, False, size, [0]),
        (got_pair, False, size, [1]),
    ]
    held, shift = ways, 3
    while True:
        step = min(3, bits - shift)
        send, sums = merge(parts, chunk, heads, entries, shift, 1 << step)
        if step == 0:
            break
        more = 1 << step
        heads //= more
        arrived = [send[0]] + [sent(send[m], m << shift) for m in range(1, more)]
        parts = [
            (part, True, heads * chunk, list(range(m * held, (m + 1) * held)))
            for m, part in enumerate(arrived)
        ]
        held *= more
        shift += step
    embeddings = pl.pallas_call(
        functools.partial(embed_kernel, entries=entries),
        out_shape=jax.ShapeDtypeStruct((owned, width), F32),
        in_specs=[VMEM] * (1 + len(shared)),
        out_specs=VMEM,
        compiler_params=params(),
        name="embed",
    )(sums, *shared)
    own, middle, long = (part.astype(F16)[None] for part in send)
    for at in range(3, bits, 3):
        own = jnp.concatenate(gather_step(own, "strip", (at, min(3, bits - at))), axis=0)
        middle = long = own
    gathered = {0: own, 1: swap(middle, "strip", 1), 2: swap(own, "strip", 2)}
    gathered[3] = swap(middle, "strip", 3)
    gathered[4], gathered[6] = swap(long, "strip", 4), swap(own, "strip", 6)
    late = {m + 1: swap(gathered[m], "strip", 1) for m in (4, 6)}
    weight_rows, bias_row = spread(
        {**gathered, **late}, chunk, strip_count, 9 * channels
    )
    return (embeddings, weight_rows.reshape(3, 3, channels, width), bias_row[0])


def solution(mesh):
    placed = (
        P(None, "strip", None),
        P(),
        P(),
        P(None, None, None, "chan"),
        P("chan"),
        P(None, "strip"),
        P("strip"),
        P("strip", "chan"),
    )
    return jax.shard_map(
        body,
        mesh=mesh,
        in_specs=placed,
        out_specs=(P("strip", "chan"), P(None, None, None, "chan"), P("chan")),
        check_vma=False,
    )
```

```python
import functools
import itertools
import math

import jax
import jax.numpy as jnp
from jax import lax
from jax.experimental import pallas as pl
from jax.experimental.pallas import tpu as pltpu
from jax.sharding import PartitionSpec as P

F32, BF16, F16 = jnp.float32, jnp.bfloat16, jnp.float16
VMEM = pl.BlockSpec(memory_space=pltpu.VMEM)
HBM = pl.BlockSpec(memory_space=pltpu.HBM)
ANY = pl.BlockSpec(memory_space=pl.ANY)
SIDE = 8
WIDTH = 3
PIECE = 4
STEP = 6
PAYLOADS = (((0,), 0), ((1,), 0), ((2,), 0), ((3,), 0), ((4,), 0), ((5,), 1), ((6, 7), 1))
SPARE = (0, 16, 0)
NOTE = 8


def params(mib=8):
    return pltpu.CompilerParams(vmem_limit_bytes=mib << 20)


def position():
    strip = lax.axis_index("strip")
    last = lax.axis_size("strip") - 1
    return (
        lax.axis_index("chan") & 1,
        (strip == 0).astype(jnp.int32),
        (strip == last).astype(jnp.int32),
        strip,
    )


def swap(value, axis, mask):
    count = lax.axis_size(axis)
    return lax.ppermute(value, axis, [(i, i ^ mask) for i in range(count)])


def gather_step(held, axis, step):
    shift, size = step
    return [held] + [swap(held, axis, m << shift) for m in range(1, 1 << size)]


def relative(refs):
    half = len(refs) // 2
    for low in range(2):
        m = low
        for ref in refs[low * half : (low + 1) * half]:
            for k in range(ref.shape[0]):
                yield m, ref, k
                m += 2


def sigmoid(v):
    return jax.nn.sigmoid(v)


def shares(pooled_rows):
    first = pooled_rows // 2
    return first, pooled_rows - first


def pick(half, pair):
    return jnp.where(half == 0, pair[0], pair[1])


def share_rows(half, rows):
    first, second = shares(rows // 2)
    most = -(-(2 * max(first, second) + 1) // PIECE) * PIECE
    return most, pick(half, (0, rows - most)), pick(half, (-1, 2 * first - 1 - (rows - most)))


def window_kernel(rows_ref, *refs, rows):
    taps, wide = refs[-2:]
    most, cols, chans = rows_ref.shape
    half_cols = cols // 2
    half = position()[0]
    _, _, before = share_rows(half, rows)
    shift = PIECE - before
    lanes = chans // 128
    border = jnp.zeros((8, 128), F32)
    for t in range(wide.shape[0]):
        wide[t, 0:8] = border
        wide[t, cols + 8 : cols + 16] = border

    def prepare(k, carry):
        for slot in range(PIECE):
            r = k * PIECE + slot
            x = rows_ref[r].astype(F32)
            for t in range(lanes):
                wide[slot * lanes + t, 8 : 8 + cols] = x[:, t * 128 : (t + 1) * 128]
            for tap in range(4):
                for t in range(lanes):
                    part = wide[slot * lanes + t, pl.ds(7 + tap, half_cols, stride=2), :]
                    at = (tap * lanes + t) * 128
                    taps[r + shift, :, at : at + 128] = part.astype(BF16)
        return carry

    lax.fori_loop(0, most // PIECE, prepare, 0)
    second = shares(rows // 2)[1]
    outside = pick(half, (PIECE, PIECE + 2 * second + 1))
    taps[outside] = jnp.zeros(taps.shape[1:], BF16)


def windows(near_rows, rows, after):
    most, cols, chans = near_rows.shape
    return pl.pallas_call(
        functools.partial(window_kernel, rows=rows),
        out_shape=jax.ShapeDtypeStruct((most + 2 * PIECE, cols // 2, 4 * chans), BF16),
        in_specs=[VMEM] + [ANY] * len(after),
        out_specs=VMEM,
        scratch_shapes=[pltpu.VMEM((PIECE * (chans // 128), cols + 16, 128), F32)],
        compiler_params=params(16),
        cost_estimate=pl.CostEstimate(flops=0, bytes_accessed=12 << 20, transcendentals=0),
        name="windows",
    )(near_rows, *after)


def edge_part(pairs, w_ref, bias, edge_ref, acc):
    rows = pairs[0].shape[0]
    chans = w_ref.shape[1]
    lanes = chans // 128
    depth = 3 * chans
    lhs = jnp.concatenate(
        [
            pairs[s][:, (2 * j + phase) * chans : (2 * j + phase + 3) * chans]
            for s in range(2)
            for j in range(2)
            for phase in range(2)
        ],
        axis=0,
    )
    pad = rows + 16
    for dr in range(3):
        part = jnp.dot(lhs, w_ref[dr * depth : (dr + 1) * depth], preferred_element_type=F32)
        for g in range(8):
            own = part[g * rows : (g + 1) * rows]
            for t in range(lanes):
                at = 9 - dr
                piece = own[:, t * 128 : (t + 1) * 128]
                if dr == 0:
                    acc[g * lanes + t, 0:8] = jnp.zeros((8, 128), F32)
                    acc[g * lanes + t, 8 + rows : pad] = jnp.zeros((8, 128), F32)
                    acc[g * lanes + t, 8:9] = jnp.zeros((1, 128), F32)
                    acc[g * lanes + t, at : at + rows] = piece
                else:
                    acc[g * lanes + t, at : at + rows] += piece
    for g in range(4):
        for t in range(lanes):
            total = None
            for phase in range(2):
                at = (2 * g + phase) * lanes + t
                v = acc[at, 8 : 8 + rows] + bias[:, t * 128 : (t + 1) * 128]
                acc[at, 8 : 8 + rows] = v * sigmoid(v)
                both = (
                    acc[at, pl.ds(8, rows // 2, stride=2), :]
                    + acc[at, pl.ds(9, rows // 2, stride=2), :]
                )
                total = both if total is None else total + both
            lost = jnp.where(g == 0, position()[1], jnp.where(g == 3, position()[2], 0))
            keep = jnp.where(lost > 0, 0.0, 0.25)
            edge_ref[g, t] = (total * keep).astype(BF16).astype(F32)


def conv_kernel(taps, w_ref, b_ref, *refs):
    out_ref = refs[-1]
    assert out_ref.shape[0] % STEP == 0
    half_cols, chans = taps.shape[1], taps.shape[2] // 4
    bias = b_ref[...]

    def step(k, carry):
        r0 = PIECE + k * 2 * STEP
        total = None
        for phase in range(2):
            lhs = jnp.concatenate(
                [
                    taps[pl.ds(r0 + dr, 2 * STEP), :, phase * chans : (phase + 3) * chans]
                    for dr in range(3)
                ],
                axis=-1,
            ).reshape(2 * STEP * half_cols, 9 * chans)
            v = jnp.dot(lhs, w_ref[...], preferred_element_type=F32) + bias
            h = (v * sigmoid(v)).reshape(STEP, 2, half_cols, chans)
            h = h[:, 0] + h[:, 1]
            total = h if total is None else total + h
        out_ref[pl.ds(k * STEP, STEP)] = (total * 0.25).astype(BF16)
        return carry

    for k in range(out_ref.shape[0] // STEP):
        step(k, 0)


def conv_pool(taps, w, b, pooled_rows, after):
    _, half_cols, width = taps.shape
    chans = width // 4
    return pl.pallas_call(
        conv_kernel,
        out_shape=jax.ShapeDtypeStruct((pooled_rows, half_cols, chans), BF16),
        in_specs=[VMEM] * 3 + [ANY] * len(after),
        out_specs=VMEM,
        compiler_params=params(16),
        cost_estimate=pl.CostEstimate(
            flops=8 * pooled_rows * half_cols * 9 * chans * chans,
            bytes_accessed=8 << 20,
            transcendentals=0,
        ),
        name="conv_pool",
    )(taps, w, b, *after)


def edge_kernel(w_ref, b_ref, got_ref, traded_ref, head_ref, tail_ref, *refs):
    edge_ref, acc = refs[-2:]
    half = position()[0]
    got, traded = got_ref[...], traded_ref[...]
    left = jnp.concatenate([jnp.where(half == 0, got, traded), head_ref[...]], axis=-1)
    right = jnp.concatenate([tail_ref[...], jnp.where(half == 0, traded, got)], axis=-1)
    edge_part((left, right), w_ref, b_ref[...], edge_ref, acc)


def conv_edges(w, b, got, traded, head, tail, after):
    rows, lanes = head.shape[0], w.shape[1] // 128
    return pl.pallas_call(
        edge_kernel,
        out_shape=jax.ShapeDtypeStruct((4, lanes, rows // 2, 128), F32),
        in_specs=[VMEM] * 6 + [ANY] * len(after),
        out_specs=VMEM,
        scratch_shapes=[pltpu.VMEM((8 * lanes, rows + 16, 128), F32)],
        compiler_params=params(),
        cost_estimate=pl.CostEstimate(flops=0, bytes_accessed=4 << 20, transcendentals=0),
        name="conv_edges",
    )(w, b, got, traded, head, tail, *after)


def side_kernel(grad_hbm, labels_hbm, slots_hbm, side_ref, labels_ref, slots_ref, sems):
    owned, width = grad_hbm.shape
    entries = slots_ref.shape[1]
    copies = [
        pltpu.make_async_copy(labels_hbm, labels_ref, sems.at[0]),
        pltpu.make_async_copy(slots_hbm, slots_ref, sems.at[1]),
        pltpu.make_async_copy(grad_hbm, side_ref.at[0, pl.ds(0, owned)], sems.at[2]),
    ]
    for copy in copies:
        copy.start()
    lane = lax.broadcasted_iota(jnp.int32, (1, width), 1)
    copies[0].wait()
    labels = labels_ref[...]
    counts = jnp.zeros((1, width), F32)
    for e in range(entries):
        hit = jnp.where(labels == e, 1.0, 0.0)
        hit = jnp.sum(jnp.sum(hit, axis=0, keepdims=True), axis=1, keepdims=True)
        counts = jnp.where(lane == e, hit, counts)
    copies[1].wait()
    ids = jnp.concatenate(
        [slots_ref[...].astype(F32), jnp.zeros((1, width - entries), F32)], axis=1
    )
    row = lax.broadcasted_iota(jnp.int32, (SIDE, width), 0)
    side_ref[0, owned:] = jnp.where(row == 0, ids, jnp.where(row == 1, counts, 0.0))
    copies[2].wait()


def pack_side(grad, slots, labels):
    owned, width = grad.shape
    fixed = [
        pltpu.with_memory_space_constraint(a, pltpu.HBM)
        for a in (grad, labels, slots.reshape(1, -1))
    ]
    return pl.pallas_call(
        side_kernel,
        out_shape=jax.ShapeDtypeStruct((1, owned + SIDE, width), F32),
        in_specs=[HBM] * 3,
        out_specs=VMEM,
        scratch_shapes=[
            pltpu.VMEM(labels.shape, jnp.int32),
            pltpu.VMEM((1, slots.shape[0]), jnp.int32),
            pltpu.SemaphoreType.DMA((3,)),
        ],
        compiler_params=params(),
        name="pack_side",
    )(*fixed)


def columns_kernel(x_hbm, w_hbm, head_ref, tail_ref, send_ref, near_ref, w_ref, left, right, wide, sems):
    rows, cols, chans = x_hbm.shape
    reach = left.shape[1]
    half = position()[0]
    most, first, _ = share_rows(half, rows)
    size = most // 4
    copies = [
        pltpu.make_async_copy(x_hbm.at[:, pl.ds(0, reach)], left, sems.at[0]),
        pltpu.make_async_copy(x_hbm.at[:, pl.ds(cols - reach, reach)], right, sems.at[1]),
    ]
    for k in range(4):
        source = x_hbm.at[pl.ds(first + k * size, size)]
        copies.append(
            pltpu.make_async_copy(source, near_ref.at[pl.ds(k * size, size)], sems.at[2 + k])
        )
    copies.append(pltpu.make_async_copy(w_hbm, w_ref, sems.at[6]))
    for copy in copies:
        copy.start()
    lanes = chans // 128
    sides = ((left, head_ref, 0), (right, tail_ref, reach - WIDTH))
    for copy, (ref, out_ref, at) in zip(copies, sides):
        copy.wait()
        x = ref[...].astype(F32).reshape(rows * reach, chans)
        for t in range(lanes):
            wide[t, : rows * reach] = x[:, t * 128 : (t + 1) * 128]
        for c in range(WIDTH):
            for t in range(lanes):
                part = wide[t, pl.ds(at + c, rows, stride=reach), :].astype(BF16)
                place = (c * lanes + t) * 128
                out_ref[:, place : place + 128] = part
    send_ref[...] = jnp.where(half == 0, tail_ref[...], head_ref[...])
    for copy in copies[2:]:
        copy.wait()


def columns(x, w):
    rows, cols, chans = x.shape
    reach = 16
    most = share_rows(0, rows)[0]
    border = jax.ShapeDtypeStruct((rows, WIDTH * chans), BF16)
    return pl.pallas_call(
        columns_kernel,
        out_shape=(border,) * 3
        + (jax.ShapeDtypeStruct((most, cols, chans), BF16), jax.ShapeDtypeStruct(w.shape, BF16)),
        in_specs=[HBM] * 2,
        out_specs=(VMEM,) * 5,
        scratch_shapes=[
            pltpu.VMEM((rows, reach, chans), BF16),
            pltpu.VMEM((rows, reach, chans), BF16),
            pltpu.VMEM((chans // 128, (rows + 1) * reach, 128), F32),
            pltpu.SemaphoreType.DMA((7,)),
        ],
        compiler_params=params(16),
        name="columns",
    )(*(pltpu.with_memory_space_constraint(a, pltpu.HBM) for a in (x, w)))


def join_kernel(*refs, count):
    at = 0
    for ref in refs[:count]:
        refs[-1][at : at + ref.shape[0]] = ref[...]
        at += ref.shape[0]


def join(parts, after):
    shape = (sum(p.shape[0] for p in parts),) + parts[0].shape[1:]
    return pl.pallas_call(
        functools.partial(join_kernel, count=len(parts)),
        out_shape=jax.ShapeDtypeStruct(shape, F32),
        in_specs=[VMEM] * len(parts) + [ANY] * len(after),
        out_specs=VMEM,
        compiler_params=params(),
        name="join",
    )(*parts, *after)


def scale_rows(block, note_rows, sums):
    def exponent(values):
        top = None
        for v in values:
            one = jnp.max(jnp.max(jnp.abs(v), axis=0, keepdims=True), axis=1, keepdims=True)
            top = one if top is None else jnp.maximum(top, one)
        return jnp.ceil(jnp.log2(jnp.maximum(top, 1e-30)))

    power = exponent([block, note_rows])
    power_sums = exponent([sums])
    return power, power_sums


def note_block(bias, power, power_sums, width):
    row = lax.broadcasted_iota(jnp.int32, (NOTE, width), 0)
    bias = jnp.broadcast_to(bias, (NOTE, width))
    power = jnp.broadcast_to(power, (NOTE, width))
    power_sums = jnp.broadcast_to(power_sums, (NOTE, width))
    return jnp.where(row == 0, bias, jnp.where(row == 1, power, power_sums))


def read_note(part, at):
    note = part[at : at + NOTE]
    down = jnp.exp2(note[1:2] - 12.0)
    return note[0:1] * down, down, jnp.exp2(note[2:3] - 12.0)


def deep_kernel(
    own_ref, other_ref, edge_ref, w_ref, b_ref, lab_ref, taps, member, slope, sums_ref, wide,
    inside, *, block, entries
):
    _, cols, chans = own_ref.shape
    rows = lab_ref.shape[0]
    lanes = chans // 128
    width = w_ref.shape[-1]
    half = position()[0]
    taps[0] = jnp.zeros(taps.shape[1:], BF16)
    taps[rows + 1] = jnp.zeros(taps.shape[1:], BF16)

    def prepare(ref, base, i, slot):
        x = ref[i].astype(F32)
        r = base + i
        for t in range(lanes):
            s = slot * lanes + t
            at = t * 128
            wide[s, 8 : 8 + cols] = x[:, at : at + 128]
            for g, place in enumerate((7, 8, 7 + cols, 8 + cols)):
                wide[s, place : place + 1] = edge_ref[g, t, pl.ds(r, 1), :]
        for tap in range(3):
            for t in range(lanes):
                piece = wide[slot * lanes + t, 7 + tap : 7 + tap + cols, :]
                at = (tap * lanes + t) * 128
                taps[r + 1, :, at : at + 128] = piece.astype(BF16)

    first, second = shares(rows)
    times = math.gcd(first, second)

    def prepare_all(even_ref, odd_ref):
        def prepare_rows(k, carry):
            for q in range(rows // times):
                ref, base = (even_ref, 0) if q < first // times else (odd_ref, first)
                prepare(ref, base, q * times - base + k, q)
            return carry

        lax.fori_loop(0, times, prepare_rows, 0)

    @pl.when(half == 0)
    def _():
        prepare_all(own_ref, other_ref)

    @pl.when(half != 0)
    def _():
        prepare_all(other_ref, own_ref)

    lab = jnp.transpose(lab_ref[...].astype(F32))
    lane = lax.broadcasted_iota(jnp.int32, (cols, 128), 1)
    want = jnp.where(lane < 3 * entries, lane % entries, -1).astype(F32)
    for r in range(rows):
        member[r] = (lab[:, r : r + 1] == want).astype(BF16)
    bias = b_ref[...]
    size = block * cols

    flat = jnp.concatenate([lab_ref[r : r + 1, :] for r in range(rows)], axis=1)
    entry = lax.broadcasted_iota(jnp.int32, (entries, rows * cols), 0)
    inside[...] = jnp.where(jnp.broadcast_to(flat, entry.shape) == entry, 1.0, 0.0).astype(BF16)

    def step(k, sums):
        r0 = k * block
        lhs = jnp.concatenate([taps[pl.ds(r0 + dr, block)] for dr in range(3)], axis=-1)
        v = jnp.dot(lhs.reshape(size, 9 * chans), w_ref[...], preferred_element_type=F32) + bias
        sig = sigmoid(v)
        features = (v * sig).astype(BF16)
        slope[pl.ds(k * size, size)] = sig * (1.0 + v * (1.0 - sig))
        mine = inside[:, pl.ds(pl.multiple_of(k * size, 128), size)]
        return sums + jnp.dot(mine, features, preferred_element_type=F32)

    sums_ref[...] = lax.fori_loop(0, rows // block, step, jnp.zeros((entries, width), F32))


def deep_forward(own, other, edges, w, b, labels, entries):
    _, cols, chans = own.shape
    rows, width = labels.shape[0], w.shape[-1]
    block = next(k for k in (8, 4, 2, 1) if rows % k == 0)
    first, second = shares(rows)
    slots = rows // math.gcd(first, second)
    return pl.pallas_call(
        functools.partial(deep_kernel, block=block, entries=entries),
        out_shape=(
            jax.ShapeDtypeStruct((rows + 2, cols, 3 * chans), BF16),
            jax.ShapeDtypeStruct((rows, cols, 128), BF16),
            jax.ShapeDtypeStruct((rows * cols, width), F32),
            jax.ShapeDtypeStruct((entries, width), F32),
        ),
        in_specs=[VMEM] * 6,
        out_specs=(VMEM,) * 4,
        scratch_shapes=[
            pltpu.VMEM((slots * (chans // 128), cols + 16, 128), F32),
            pltpu.VMEM((entries, rows * cols), BF16),
        ],
        compiler_params=params(16),
        cost_estimate=pl.CostEstimate(
            flops=4 * rows * cols * 9 * chans * width, bytes_accessed=8 << 20, transcendentals=0
        ),
        name="deep_forward",
    )(own, other, edges, w, b, labels)


def three_terms(value, axis):
    high = value.astype(BF16)
    rest = value - high.astype(F32)
    mid = rest.astype(BF16)
    low = (rest - mid.astype(F32)).astype(BF16)
    return jnp.concatenate([high, mid, low], axis=axis)


def grad_kernel(
    taps, member, slope, sums_ref, *refs, n_parts, chunk
):
    part_refs = refs[:n_parts]
    out_refs, weight = refs[n_parts:-1], refs[-1]
    rows, cols, depth = member.shape[0], taps.shape[1], taps.shape[2]
    width = slope.shape[-1]
    me = position()[3]
    entries = sums_ref.shape[0]
    owned = part_refs[0].shape[1] - SIDE
    own_ids = jnp.broadcast_to(part_refs[0][0, owned : owned + 1, :entries], (entries, entries))
    across = lax.broadcasted_iota(jnp.int32, (entries, entries), 1)
    down = lax.broadcasted_iota(jnp.int32, (entries, entries), 0)
    ids = jnp.sum(jnp.where(across == down, own_ids, 0.0), axis=1, keepdims=True).astype(jnp.int32)
    total = jnp.zeros((entries, 1), F32)
    entry_grad = jnp.zeros((entries, width), F32)
    owner, inner = ids // owned, ids % owned
    spot = lax.broadcasted_iota(jnp.int32, (entries, owned), 1)
    for m, ref, k in relative(part_refs):
        there = ref[k, owned : owned + 1, :entries] == ids.astype(F32)
        counts = ref[k, owned + 1 : owned + 2, :entries]
        total += jnp.sum(jnp.where(there, counts, 0.0), axis=1, keepdims=True)
        hot = ((owner ^ me) == m) & (inner == spot)
        picked = jnp.dot(
            hot.astype(BF16), three_terms(ref[k, :owned], 1), preferred_element_type=F32
        )
        entry_grad += picked[:, :width] + picked[:, width : 2 * width] + picked[:, 2 * width :]
    entry_grad = entry_grad / jnp.maximum(total, 1.0)
    spare = jnp.zeros((128 - 3 * entries, width), BF16)
    terms = jnp.concatenate([three_terms(entry_grad, 0), spare], axis=0)
    pixel = jnp.dot(member[...].reshape(rows * cols, 128), terms, preferred_element_type=F32)
    dg = (pixel * slope[...]).astype(BF16)
    turned = jnp.transpose(dg)
    bias_sum = jnp.sum(dg.astype(F32), axis=0, keepdims=True)
    for dr in range(3):
        window = taps[dr : dr + rows].reshape(rows * cols, depth)
        out = jnp.dot(turned, window, preferred_element_type=F32)
        weight[dr * depth : (dr + 1) * depth] = jnp.transpose(out)
    if weight.shape[0] > 3 * depth:
        weight[3 * depth :] = jnp.zeros((weight.shape[0] - 3 * depth, width), F32)
    sums = sums_ref[...]
    power, power_sums = scale_rows(weight[...], bias_sum, sums)
    up = jnp.exp2(12.0 - power)
    note = note_block(bias_sum * up, power, power_sums, width)
    ways = 8
    digit = lax.rem(me, ways)
    heads = weight.shape[0] // chunk // ways
    sums = sums * jnp.exp2(12.0 - power_sums)
    for out_ref, (members, with_sums) in zip(out_refs, PAYLOADS):
        at = 0
        for m, hi in itertools.product(members, range(heads)):
            j = hi * ways + (digit ^ m)
            out_ref[at : at + chunk] = weight[pl.ds(pl.multiple_of(j * chunk, 8), chunk)] * up
            at += chunk
        out_ref[at : at + NOTE] = note
        if with_sums:
            out_ref[at + NOTE :] = sums


def deep_backward(forward, parts, chunk, count):
    taps, _, slope, sums = forward
    width, entries = slope.shape[-1], sums.shape[0]
    size = count // 8 * chunk
    return pl.pallas_call(
        functools.partial(grad_kernel, n_parts=len(parts), chunk=chunk),
        out_shape=tuple(
            jax.ShapeDtypeStruct((len(members) * size + NOTE + with_sums * entries, width), F32)
            for members, with_sums in PAYLOADS
        ),
        in_specs=[VMEM] * (4 + len(parts)),
        out_specs=(VMEM,) * len(PAYLOADS),
        scratch_shapes=[pltpu.VMEM((count * chunk, width), F32)],
        compiler_params=params(16),
        cost_estimate=pl.CostEstimate(
            flops=4 * slope.shape[0] * 3 * taps.shape[2] * width, bytes_accessed=8 << 20, transcendentals=0
        ),
        name="deep_backward",
    )(*forward, *parts)


def pair_kernel(own_ref, got_ref, *refs, size, entries, got_at, got_note, sums_notes):
    out_ref = refs[-1]
    own, got = own_ref[size : size + NOTE], got_ref[got_note : got_note + NOTE]
    power = jnp.maximum(own[1:2], got[1:2]) + 1.0
    own_down, got_down = jnp.exp2(own[1:2] - power), jnp.exp2(got[1:2] - power)
    out_ref[:size] = own_ref[:size] * own_down + got_ref[got_at : got_at + size] * got_down
    bias = own[0:1] * own_down + got[0:1] * got_down
    powers = [ref[at + 2 : at + 3] for ref, at in zip(refs, sums_notes)]
    power_sums = functools.reduce(jnp.maximum, powers)
    out_ref[size : size + NOTE] = note_block(bias, power, power_sums, own.shape[-1])
    place = size + NOTE
    for ref, at, one in zip(refs, sums_notes, powers):
        sums = ref[at + NOTE : at + NOTE + entries] * jnp.exp2(one - power_sums)
        out_ref[place : place + entries] = sums
        place += entries
    if place < out_ref.shape[0]:
        out_ref[place:] = jnp.zeros((out_ref.shape[0] - place, own.shape[-1]), F32)


def merge_pair(own, got, sums, size, entries, got_at, got_note, after, spare=0):
    width = own.shape[-1]
    return pl.pallas_call(
        functools.partial(
            pair_kernel,
            size=size,
            entries=entries,
            got_at=got_at,
            got_note=got_note,
            sums_notes=tuple(at for _, at in sums),
        ),
        out_shape=jax.ShapeDtypeStruct((size + NOTE + len(sums) * entries + spare, width), F32),
        in_specs=[VMEM] * (2 + len(sums)) + [ANY] * len(after),
        out_specs=VMEM,
        compiler_params=params(),
        name="merge_pair",
    )(own, got, *(part for part, _ in sums), *after)


def merge_kernel(*refs, plan, chunk, heads, entries, shift, next_ways):
    n_parts = len(plan)
    part_refs, out_refs, sums_ref = refs[:n_parts], refs[n_parts:-1], refs[-1]
    width = part_refs[0].shape[-1]
    size = heads * chunk
    total, bias = jnp.zeros((size, width), F32), jnp.zeros((1, width), F32)
    for ref, (added, note_at, members) in zip(part_refs, plan):
        more, down, down_sums = read_note(ref, note_at)
        if added:
            total, bias = total + ref[:size] * down, bias + more
        for k, m in enumerate(members):
            at = note_at + NOTE + k * entries
            sums_ref[m * entries : (m + 1) * entries] = ref[at : at + entries] * down_sums
    sums = sums_ref[...]
    power, power_sums = scale_rows(total, bias, sums)
    up = jnp.exp2(12.0 - power)
    note = note_block(bias * up, power, power_sums, width)
    total = total * up
    if next_ways == 1:
        for out_ref, spare in zip(out_refs, SPARE):
            out_ref[:size] = total
            out_ref[size : size + NOTE] = note
            if spare:
                out_ref[size + NOTE :] = jnp.zeros((spare, width), F32)
        return
    sums = sums * jnp.exp2(12.0 - power_sums)
    digit = lax.rem(position()[3] >> shift, next_ways)
    for m in range(next_ways):
        for hi in range(heads // next_ways):
            piece = jnp.zeros((chunk, width), F32)
            for d in range(next_ways):
                at = (hi * next_ways + d) * chunk
                piece = jnp.where((digit ^ m) == d, total[at : at + chunk], piece)
            out_refs[m][hi * chunk : (hi + 1) * chunk] = piece
        at = heads // next_ways * chunk
        out_refs[m][at : at + NOTE] = note
        out_refs[m][at + NOTE :] = sums


def merge(parts, chunk, heads, entries, shift, next_ways):
    width = parts[0][0].shape[-1]
    sums_rows = sum(len(members) for _, _, _, members in parts) * entries
    if next_ways == 1:
        outs = tuple(
            jax.ShapeDtypeStruct((heads * chunk + NOTE + spare, width), F32) for spare in SPARE
        )
    else:
        rows = heads // next_ways * chunk + NOTE + sums_rows
        outs = (jax.ShapeDtypeStruct((rows, width), F32),) * next_ways
    outs = outs + (jax.ShapeDtypeStruct((sums_rows, width), F32),)
    out = pl.pallas_call(
        functools.partial(
            merge_kernel,
            plan=tuple((added, at, tuple(members)) for _, added, at, members in parts),
            chunk=chunk,
            heads=heads,
            entries=entries,
            shift=shift,
            next_ways=next_ways,
        ),
        out_shape=outs,
        in_specs=[VMEM] * len(parts),
        out_specs=(VMEM,) * len(outs),
        compiler_params=params(),
        name="merge",
    )(*(part for part, _, _, _ in parts))
    return out[:-1], out[-1]


def embed_kernel(sums_ref, *refs, entries):
    part_refs, out_ref = refs[:-1], refs[-1]
    owned, width = out_ref.shape
    own = (position()[3] * owned + lax.broadcasted_iota(jnp.int32, (owned, entries), 0)).astype(F32)
    sums, counts = jnp.zeros((owned, width), F32), jnp.zeros((owned, 1), F32)
    for m, ref, k in relative(part_refs):
        there = ref[k, owned : owned + 1, :entries] == own
        count = ref[k, owned + 1 : owned + 2, :entries]
        counts += jnp.sum(jnp.where(there, count, 0.0), axis=1, keepdims=True)
        sums += jnp.dot(
            there.astype(F32),
            sums_ref[m * entries : (m + 1) * entries],
            precision=lax.Precision.HIGHEST,
            preferred_element_type=F32,
        )
    out_ref[...] = sums / jnp.maximum(counts, 1.0)


def spread_kernel(*refs, chunk, rows, members):
    part_refs, weight_ref, bias_ref, place = refs[:-3], refs[-3], refs[-2], refs[-1]
    me = position()[3]
    count = len(members)
    for p, k in itertools.product(range(count), range(part_refs[0].shape[0])):
        bias, down, _ = read_note(part_refs[p][k], chunk)
        j = me ^ (members[p] + k * count)
        target = weight_ref if rows == place.shape[0] else place
        target[pl.ds(pl.multiple_of(j * chunk, 8), chunk)] = part_refs[p][k, :chunk] * down

        @pl.when(j == 0)
        def _():
            bias_ref[...] = bias

    if rows != place.shape[0]:
        weight_ref[...] = place[:rows]


def spread(parts, chunk, count, rows):
    parts = {m: part.astype(F32) for m, part in parts.items()}
    width = parts[0].shape[-1]
    return pl.pallas_call(
        functools.partial(spread_kernel, chunk=chunk, rows=rows, members=tuple(parts)),
        out_shape=(jax.ShapeDtypeStruct((rows, width), F32), jax.ShapeDtypeStruct((1, width), F32)),
        in_specs=[VMEM] * len(parts),
        out_specs=(VMEM, VMEM),
        scratch_shapes=[pltpu.VMEM((count * chunk, width), F32)],
        compiler_params=params(),
        name="spread",
    )(*parts.values())


def body(
    section_input, conv_weight, conv_bias, deep_weight, deep_bias, labels, slot_ids, embed_grad
):
    chan_count = lax.axis_size("chan")
    strip_count = lax.axis_size("strip")
    channels = section_input.shape[-1]
    entries = slot_ids.shape[0]
    owned, width = embed_grad.shape
    conv_w = conv_weight.reshape(9 * channels, -1)
    conv_b = conv_bias.reshape(1, -1)

    side = pack_side(embed_grad, slot_ids, labels)
    head, tail, border, near_rows, near_w = columns(section_input, conv_w)
    pairs = []
    for s in range(strip_count):
        for c in range(chan_count):
            to = s + 1 - 2 * (c & 1)
            if 0 <= to < strip_count:
                pairs.append((s * chan_count + c, to * chan_count + c))
    got = lax.ppermute(border, ("strip", "chan"), pairs)

    steps = [(at + 1, 1) for at in range(min(2, strip_count.bit_length() - 2))]
    steps += [(at, min(3, strip_count.bit_length() - 1 - at)) for at in range(3, strip_count.bit_length() - 1, 3)]
    ahead = gather_step(side, "strip", steps[0])
    shared = join(ahead, [border])
    taps = windows(near_rows, section_input.shape[0], [shared])
    ahead = gather_step(shared, "strip", steps[1])
    pooled = conv_pool(taps, near_w, conv_b, section_input.shape[0] // 4, [shared])
    pooled, got, shared = lax.optimization_barrier((pooled, got, join(ahead, [pooled])))
    other = swap(pooled, "chan", 1)
    traded = swap(got, "chan", 1)
    for step in steps[2:]:
        shared = join(gather_step(shared, "strip", step), [])
    shared = [shared, swap(shared, "strip", 1)]
    edges = conv_edges(near_w, conv_b, got, traded, head, tail, [pooled])

    chunk = -(-9 * channels // strip_count // 8) * 8
    bits = strip_count.bit_length() - 1
    ways = 8
    forward = deep_forward(
                pooled,
        other,
        edges,
        deep_weight.reshape(9 * channels, width),
        deep_bias.reshape(1, width),
        labels,
        entries,
    )
    heads = strip_count // ways
    size = heads * chunk

    def sent(part, mask):
        return swap(part.astype(F16), "strip", mask).astype(F32)

    kept, beside, near, near_pair, paired, pair, far = deep_backward(
        forward, shared, chunk, strip_count
    )
    got_far, got_pair, got_near = sent(far, 6), sent(pair, 1), sent(near_pair, 1)
    both = [(pair, size), (got_pair, size)]
    onward = merge_pair(paired, got_pair, both, size, entries, 0, size, [], spare=8)
    near = merge_pair(near, got_near, both, size, entries, 0, size, [onward])
    last = [(got_far, 2 * size)]
    beside = merge_pair(beside, got_far, last, size, entries, size, 2 * size, [near])
    parts = [
        (kept, True, size, []),
        (sent(beside, 1), True, size, [7]),
        (sent(near, 2), True, size, [2, 3]),
        (sent(onward, 4), True, size, [4, 5]),
        (got_far, True, 2 * size, [6]),
        (pair, False, size, [0]),
        (got_pair, False, size, [1]),
    ]
    held, shift = ways, 3
    while True:
        step = min(3, bits - shift)
        send, sums = merge(parts, chunk, heads, entries, shift, 1 << step)
        if step == 0:
            break
        more = 1 << step
        heads //= more
        arrived = [send[0]] + [sent(send[m], m << shift) for m in range(1, more)]
        parts = [
            (part, True, heads * chunk, list(range(m * held, (m + 1) * held)))
            for m, part in enumerate(arrived)
        ]
        held *= more
        shift += step
    embeddings = pl.pallas_call(
        functools.partial(embed_kernel, entries=entries),
        out_shape=jax.ShapeDtypeStruct((owned, width), F32),
        in_specs=[VMEM] * (1 + len(shared)),
        out_specs=VMEM,
        compiler_params=params(),
        name="embed",
    )(sums, *shared)
    own, middle, long = (part.astype(F16)[None] for part in send)
    for at in range(3, bits, 3):
        own = jnp.concatenate(gather_step(own, "strip", (at, min(3, bits - at))), axis=0)
        middle = long = own
    gathered = {0: own, 1: swap(middle, "strip", 1), 2: swap(own, "strip", 2)}
    gathered[3] = swap(middle, "strip", 3)
    gathered[4], gathered[6] = swap(long, "strip", 4), swap(own, "strip", 6)
    late = {m + 1: swap(gathered[m], "strip", 1) for m in (4, 6)}
    weight_rows, bias_row = spread(
        {**gathered, **late}, chunk, strip_count, 9 * channels
    )
    return (embeddings, weight_rows.reshape(3, 3, channels, width), bias_row[0])


def solution(mesh):
    placed = (
        P(None, "strip", None),
        P(),
        P(),
        P(None, None, None, "chan"),
        P("chan"),
        P(None, "strip"),
        P("strip"),
        P("strip", "chan"),
    )
    return jax.shard_map(
        body,
        mesh=mesh,
        in_specs=placed,
        out_specs=(P("strip", "chan"), P(None, None, None, "chan"), P("chan")),
        check_vma=False,
    )
```
